32 devices in a mesh: grp: 2 (over x), blk: 8 (over z, y), cls: 2 (over core).
Axes of the slice: x: 2, y: 2, z: 4, core: 2. Of those that a mesh axis runs over, the one named last changes fastest.
Arguments:
- particles: bfloat16 [32768, 8192], P(('grp', 'blk', 'cls')), parts along dimension 0, may hold values from -11 to 11
- significant: int32 [16, 32768], P(None, ('grp', 'blk', 'cls')), parts along dimension 1, may hold values from 0 to 511, as said below
- templates: bfloat16 [1024, 8192], P(('grp', 'blk')), parts along dimension 0, may hold values from -0.2 to 0.2
- template_class: int32 [1024], P(('grp', 'blk')), parts along dimension 0, may hold values from 0 to 7
- class_counts: int32 [16], P('grp'), parts along dimension 0, may hold values from 1024 to 4096
- inv_noise: float32 [8192], replicated, may hold values from 0.3 to 3
Outputs:
- loglik: float32 [32768], P(('grp', 'blk', 'cls')), parts along dimension 0
- class_avg: float32 [16, 8192], P(('grp', 'cls'), 'blk'), parts along dimension 0
The draws below stay inside these ranges and needn't reach their ends.
There are 2 independent parts, one for each index of `grp`. The reference program is written for one: setup_inputs(seed, part) draws one part's arguments, and reference() takes and returns one part's arrays. A program takes and returns all parts, laid end to end along the dimension named above; an argument that names none is the same for every part. Nothing has to cross between parts.
Inputs may be any that keep to these rules, and one draw needn't show every extreme that they name: `significant`: the 16 templates of a particle are distinct; taking template ids around a circle of 512 from an offset of the particle's own, its k-th template lies in the k-th of 16 equal arcs.
All inputs are finite; a program needn't handle non-finite values.
Results may differ from the reference program's by a relative error of at most 0.0012.
Values may be sent and summed in bfloat16 or wider, within the bound.
No kernel may reach another device: no remote copies, remote signals or barrier semaphores. Data moves between devices by JAX's collectives and lax.ppermute only.
A program may use at most 128 MiB of HBM per device.

```python
import math
import jax
import jax.numpy as jnp

F = 8192
C = 8
K = 16
NT = 512
NP = 16384


def draw_particles(key, part):
    key = jax.random.fold_in(key, 101)
    key_mean, key_noise = jax.random.split(key, 2)
    mean_row = jnp.clip(jax.random.normal(key_mean, (F,), jnp.float32), -3.0, 3.0)
    noise = jnp.clip(jax.random.normal(key_noise, (NP, F), jnp.float32), -3.0, 3.0)
    values = mean_row[None, :] + 0.8 * noise
    return values.astype(jnp.bfloat16)


def draw_templates(key, part):
    key = jax.random.fold_in(key, 202)
    key_rows = jax.random.fold_in(key, 0)
    values = 0.04 * jnp.clip(jax.random.normal(key_rows, (NT, F), jnp.float32), -4.0, 4.0)
    return values.astype(jnp.bfloat16)


def draw_significant(key, part):
    key = jax.random.fold_in(key, 303)
    key_start, key_jitter = jax.random.split(key)
    offset = NT // K
    start_ids = jax.random.randint(key_start, (NP,), 0, NT)
    jitter = jax.random.randint(key_jitter, (K, NP), 0, offset)
    index = jnp.arange(NP)
    spacing = max(NP // 8, 1)
    aligned = (index % spacing == 0) & (index // spacing < 8)
    start_ids = jnp.where(aligned, index // spacing * (NT // 8), start_ids)
    leading = jnp.arange(K)[:, None] < 2
    jitter = jnp.where(leading & aligned[None, :], 0, jitter)
    slots = start_ids[None, :] + jnp.arange(K)[:, None] * offset + jitter
    return (slots % NT).astype(jnp.int32)


def plant(array, stream_key, low, top_value):
    longest = array.shape.index(max(array.shape))
    spots = []
    for shift in (0, 1):
        where = [jax.random.randint(jax.random.fold_in(stream_key, axis), (), 0, length) for axis, length in enumerate(array.shape)]
        where[longest] = (where[longest] + shift) % array.shape[longest]
        spots.append(tuple(where))
    return array.at[spots[0]].set(low).at[spots[1]].set(top_value)


def setup_inputs(seed: int = 0, part: int = 0) -> dict:
    key_list = jax.random.split(jax.random.key(seed), 7)
    own_keys = jax.random.split(jax.random.fold_in(key_list[6], part), 7)
    particles = draw_particles(jax.random.fold_in(jax.random.fold_in(key_list[6], part), 71), part)
    significant = draw_significant(jax.random.fold_in(jax.random.fold_in(key_list[6], part), 71), part)
    templates = draw_templates(jax.random.fold_in(jax.random.fold_in(key_list[6], part), 71), part)
    template_class = plant(jax.random.randint(own_keys[3], (NT,), 0, C), jax.random.fold_in(own_keys[3], 1), 0, C - 1).astype(jnp.int32)
    class_counts = plant(jax.random.randint(own_keys[4], (C,), NP // (2 * C), 2 * NP // C + 1), jax.random.fold_in(own_keys[4], 1), NP // (2 * C), (2 * NP // C + 1) - 1).astype(jnp.int32)
    inv_noise = jnp.clip(jnp.exp(jax.random.uniform(key_list[5], (F,), jnp.float32, math.log(0.3), math.log(3.0))), 0.3, 3.0)
    return {"particles": particles, "significant": significant, "templates": templates, "template_class": template_class, "class_counts": class_counts, "inv_noise": inv_noise}


def reference(particles, significant, templates, template_class, class_counts, inv_noise):
    widened = templates.astype(jnp.float32)
    weighted = (widened * inv_noise[None, :]).astype(jnp.bfloat16)
    energy = 0.5 * jnp.sum(inv_noise[None, :] * widened * widened, axis=1)
    log_counts = jnp.log(class_counts.astype(jnp.float32))
    prior = log_counts[template_class]
    scores = jnp.dot(weighted, particles.T, preferred_element_type=jnp.float32)
    scores = scores - energy[:, None] + prior[:, None]
    top_all = jnp.max(scores, axis=0)
    loglik = top_all + jnp.log(jnp.sum(jnp.exp(scores - top_all[None, :]), axis=0))
    picked = jnp.take_along_axis(scores, significant, axis=0)
    picked_class = template_class[significant]
    sig_max = jnp.max(picked, axis=0)
    sig_exp = jnp.exp(picked - sig_max[None, :])
    posterior = sig_exp / jnp.sum(sig_exp, axis=0)[None, :]
    class_ids = jnp.arange(C, dtype=jnp.int32)
    hits = picked_class[:, None, :] == class_ids[None, :, None]
    class_weights = jnp.sum(jnp.where(hits, posterior[:, None, :], jnp.float32(0.0)), axis=0)
    rounded = class_weights.astype(jnp.bfloat16)
    class_sums = jnp.dot(rounded, particles, preferred_element_type=jnp.float32)
    class_totals = jnp.sum(class_weights, axis=1)
    class_avg = class_sums / (class_totals + class_counts.astype(jnp.float32))[:, None]
    return loglik, class_avg
```

```python
import functools

import jax
import jax.numpy as jnp
from jax import lax
from jax.experimental import pallas as pl
from jax.experimental.pallas import tpu as pltpu
from jax.sharding import PartitionSpec as P

LOWEST = -1e30
STEPS = 8
SUBS = 2
LANES = 128
STATE_ROWS = 8
VMEM_LIMIT = 48 * 1024 * 1024


def ring_order(blocks):
    if blocks <= 8:
        return list(range(0, blocks, 2)) + list(range(blocks - 1, 0, -2))
    return list(range(blocks))


def score_kernel(layout, base_ref, logs_ref, sig_ref, state_ref, noise_ref, part_ref, *rest):
    groups = []
    at = 0
    for subs in layout:
        groups.append((rest[at], rest[at + 1 : at + 1 + subs]))
        at += 1 + subs
    out_ref, acc, energy = rest[at:]
    step = pl.program_id(0)
    steps = pl.num_programs(0)

    @pl.when(step == 0)
    def _():
        acc[...] = jnp.zeros_like(acc)
        energy[...] = jnp.zeros_like(energy)

    def add(which):
        rows = [refs[which if len(refs) > 1 else 0][...] for _, refs in groups]
        widened = jnp.concatenate(rows, axis=0).astype(jnp.float32)
        product = widened * noise_ref[...]
        square = product * widened
        folded = square[:, :LANES]
        for lane in range(LANES, square.shape[1], LANES):
            folded = folded + square[:, lane : lane + LANES]
        energy[...] += folded
        acc[...] += lax.dot_general(
            product.astype(jnp.bfloat16),
            part_ref[...],
            (((1,), (1,)), ((), ())),
            preferred_element_type=jnp.float32,
        )

    most = max(layout)
    for which in range(most):
        pl.when(step * most // steps == which)(functools.partial(add, which))

    @pl.when(step == steps - 1)
    def _():
        classes = logs_ref.shape[0]
        tags = jnp.concatenate([ref[...] for ref, _ in groups], axis=0).astype(jnp.float32)
        row_ids = []
        for group, (ref, _) in enumerate(groups):
            row_ids.append(
                base_ref[group] + lax.broadcasted_iota(jnp.int32, (ref.shape[0], 1), 0)
            )
        ids = jnp.concatenate(row_ids, axis=0)
        prior = jnp.zeros_like(tags[:, :1])
        for tag in range(classes):
            prior = jnp.where(tags[:, :1] == tag, logs_ref[tag], prior)
        bias = prior - 0.5 * jnp.sum(energy[...], axis=1, keepdims=True)
        scores = acc[...] + bias
        old_max = state_ref[0:1, :]
        old_sum = state_ref[1:2, :]
        new_max = jnp.maximum(old_max, jnp.max(scores, axis=0, keepdims=True))
        new_sum = old_sum * jnp.exp(old_max - new_max) + jnp.sum(
            jnp.exp(scores - new_max), axis=0, keepdims=True
        )
        hit = sig_ref[0:1, :] == ids
        for pick in range(1, sig_ref.shape[0]):
            hit = hit | (sig_ref[pick : pick + 1, :] == ids)
        old_top = state_ref[2:3, :]
        new_top = jnp.maximum(
            old_top, jnp.max(jnp.where(hit, scores, LOWEST), axis=0, keepdims=True)
        )
        value = jnp.where(hit, jnp.exp(scores - new_top), 0.0)
        lane = lax.broadcasted_iota(jnp.int32, tags.shape, 1).astype(jnp.float32)
        onehot = jnp.transpose(jnp.where(tags == lane, 1.0, 0.0))[:classes, :].astype(jnp.bfloat16)
        weights = state_ref[STATE_ROWS:, :] * jnp.exp(old_top - new_top)
        left = value
        for _ in range(3):
            piece = left.astype(jnp.bfloat16)
            left = left - piece.astype(jnp.float32)
            weights = weights + jnp.dot(onehot, piece, preferred_element_type=jnp.float32)
        out_ref[0:1, :] = new_max
        out_ref[1:2, :] = new_sum
        out_ref[2:3, :] = new_top
        out_ref[3:STATE_ROWS, :] = jnp.zeros_like(out_ref[3:STATE_ROWS, :])
        out_ref[STATE_ROWS:, :] = weights


def score_groups(groups, bases, logs, significant, state, noise, particles):
    per_device, freqs = particles.shape
    width = freqs // STEPS
    specs = [
        pl.BlockSpec(memory_space=pltpu.SMEM),
        pl.BlockSpec(memory_space=pltpu.SMEM),
        pl.BlockSpec(significant.shape, lambda j: (0, 0)),
        pl.BlockSpec(state.shape, lambda j: (0, 0)),
        pl.BlockSpec((1, width), lambda j: (0, j)),
        pl.BlockSpec((per_device, width), lambda j: (0, j)),
    ]
    arrays = [bases, logs, significant, state, noise, particles]
    layout = []
    rows = 0
    for tags, column, parts in groups:
        height = parts[0].shape[0]
        rows += height
        layout.append(len(parts))
        specs.append(pl.BlockSpec((height, LANES), lambda j, column=column: (0, column)))
        arrays.append(tags)
        share = STEPS // len(parts)
        for index, part in enumerate(parts):
            specs.append(
                pl.BlockSpec(
                    (height, width),
                    lambda j, low=index * share, share=share: (
                        0,
                        jnp.clip(j - low, 0, share - 1),
                    ),
                )
            )
            arrays.append(part)
    return pl.pallas_call(
        functools.partial(score_kernel, tuple(layout)),
        grid=(STEPS,),
        in_specs=specs,
        out_specs=pl.BlockSpec(state.shape, lambda j: (0, 0)),
        out_shape=jax.ShapeDtypeStruct(state.shape, jnp.float32),
        scratch_shapes=[
            pltpu.VMEM((rows, per_device), jnp.float32),
            pltpu.VMEM((rows, LANES), jnp.float32),
        ],
        compiler_params=pltpu.CompilerParams(vmem_limit_bytes=VMEM_LIMIT),
        cost_estimate=pl.CostEstimate(
            flops=4 * 128 * per_device * freqs,
            bytes_accessed=2 * per_device * freqs,
            transcendentals=0,
        ),
    )(*arrays)


def sums_kernel(own_ref, state_ref, part_ref, loglik_ref, mine_ref, theirs_ref, rounded, totals):
    classes, per_owner = rounded.shape[0], mine_ref.shape[1]
    width = part_ref.shape[1]

    @pl.when(pl.program_id(0) == 0)
    def _():
        loglik_ref[...] = state_ref[0:1, :] + jnp.log(state_ref[1:2, :])
        weights = state_ref[STATE_ROWS:, :]
        weights = weights / jnp.sum(weights, axis=0, keepdims=True)
        turned = jnp.concatenate([weights[per_owner:], weights[:per_owner]], axis=0)
        weights = jnp.where(own_ref[0] == 0, weights, turned)
        rounded[...] = weights.astype(jnp.bfloat16)
        total = jnp.sum(weights, axis=1, keepdims=True)
        totals[...] = jnp.broadcast_to(total, totals.shape)

    sums = jnp.dot(rounded[...], part_ref[...], preferred_element_type=jnp.float32)
    mine_ref[0, :, :width] = sums[:per_owner]
    theirs_ref[0, :, :width] = sums[per_owner:classes]
    mine_ref[0, :, width:] = totals[:per_owner]
    theirs_ref[0, :, width:] = totals[per_owner:classes]


def class_sums(own, state, particles, blocks, classes, owners):
    per_device, freqs = particles.shape
    width = freqs // blocks
    per_owner = classes // owners
    piece = jax.ShapeDtypeStruct((blocks, per_owner, width + LANES), jnp.float32)
    piece_spec = pl.BlockSpec((1, per_owner, width + LANES), lambda j: (j, 0, 0))
    return pl.pallas_call(
        sums_kernel,
        grid=(blocks,),
        in_specs=[
            pl.BlockSpec(memory_space=pltpu.SMEM),
            pl.BlockSpec(state.shape, lambda j: (0, 0)),
            pl.BlockSpec((per_device, width), lambda j: (0, j)),
        ],
        out_specs=[pl.BlockSpec((1, per_device), lambda j: (0, 0)), piece_spec, piece_spec],
        out_shape=[jax.ShapeDtypeStruct((1, per_device), jnp.float32), piece, piece],
        scratch_shapes=[
            pltpu.VMEM((classes, per_device), jnp.bfloat16),
            pltpu.VMEM((classes, LANES), jnp.float32),
        ],
        compiler_params=pltpu.CompilerParams(vmem_limit_bytes=VMEM_LIMIT),
        cost_estimate=pl.CostEstimate(
            flops=2 * 128 * per_device * freqs,
            bytes_accessed=2 * per_device * freqs,
            transcendentals=0,
        ),
    )(own, state, particles)


def body(particles, significant, templates, template_class, class_counts, inv_noise):
    per_device, freqs = particles.shape
    height = templates.shape[0]
    classes = class_counts.shape[0]
    blocks = lax.axis_size("blk")
    owners = lax.axis_size("cls")
    half = height // owners
    order = ring_order(blocks)
    place = [order.index(block) for block in range(blocks)]
    block_id = lax.axis_index("blk")
    core = lax.axis_index("cls")
    at = jnp.asarray(place, jnp.int32)[block_id]
    order_table = jnp.asarray(order, jnp.int32)
    forward = [(order[i], order[(i + 1) % blocks]) for i in range(blocks)]
    backward = [(order[(i + 1) % blocks], order[i]) for i in range(blocks)]
    swap = [(i, owners - 1 - i) for i in range(owners)]

    noise = inv_noise[None, :]
    logs = jnp.log(class_counts.astype(jnp.float32))
    tags = jnp.broadcast_to(
        template_class.astype(jnp.bfloat16)[:, None], (height, LANES)
    )
    own_rows = lax.dynamic_slice_in_dim(templates, core * half, half, 0)
    own_tags = lax.dynamic_slice_in_dim(tags, core * half, half, 0)
    span = freqs // SUBS
    first = []
    for sub in range(SUBS):
        first.append(
            jnp.concatenate([own_rows[:, sub * span : (sub + 1) * span], own_tags], axis=1)
        )

    score = functools.partial(
        score_groups,
        logs=logs,
        significant=significant,
        noise=noise,
        particles=particles,
    )
    column = span // LANES

    state = jnp.concatenate(
        [
            jnp.full((1, per_device), LOWEST, jnp.float32),
            jnp.zeros((1, per_device), jnp.float32),
            jnp.full((1, per_device), LOWEST, jnp.float32),
            jnp.zeros((STATE_ROWS - 3 + classes, per_device), jnp.float32),
        ],
        axis=0,
    )
    last = blocks // 2
    held = {1: first, -1: first}
    for distance in range(last + 1):
        if distance == 0:
            groups = [(tags, 0, [templates])]
            bases = [block_id * height]
        else:
            groups, bases = [], []
            for way, pairs in ((1, forward), (-1, backward)):
                taken = list(range(SUBS))
                if distance == last:
                    taken = taken[: SUBS // 2] if way == 1 else taken[SUBS // 2 :]
                arrived = {sub: lax.ppermute(held[way][sub], "blk", pairs) for sub in taken}
                passed = {sub: lax.ppermute(arrived[sub], "cls", swap) for sub in taken}
                held[way] = arrived
                source = order_table[lax.rem(at - way * distance + blocks, blocks)]
                if distance == last and way == -1:
                    for sub in taken:
                        groups[0][2].append(arrived[sub])
                        groups[1][2].append(passed[sub])
                    continue
                parts = [arrived[sub] for sub in taken]
                others = [passed[sub] for sub in taken]
                groups.append((parts[0], column, parts))
                groups.append((others[0], column, others))
                bases.append(source * height + core * half)
                bases.append(source * height + (owners - 1 - core) * half)
        state = score(groups, jnp.stack(bases), state=state)

    loglik, mine, theirs = class_sums(
        core[None], state, particles, blocks, classes, owners
    )
    reduced = mine + lax.ppermute(theirs, "cls", swap)
    pieces = lax.all_to_all(reduced, "blk", split_axis=0, concat_axis=0, tiled=True)
    total = jnp.sum(pieces, axis=0)
    width = freqs // blocks
    per_owner = classes // owners
    counts = lax.dynamic_slice_in_dim(class_counts, core * per_owner, per_owner, 0)
    class_avg = total[:, :width] / (total[:, width] + counts.astype(jnp.float32))[:, None]
    return loglik[0], class_avg


def solution(mesh):
    placed = (
        P(("grp", "blk", "cls"), None),
        P(None, ("grp", "blk", "cls")),
        P(("grp", "blk"), None),
        P(("grp", "blk")),
        P("grp"),
        P(),
    )
    return jax.shard_map(
        body,
        mesh=mesh,
        in_specs=placed,
        out_specs=(P(("grp", "blk", "cls")), P(("grp", "cls"), "blk")),
        check_vma=False,
    )
```

```python
import functools

import jax
import jax.numpy as jnp
from jax import lax
from jax.experimental import pallas as pl
from jax.experimental.pallas import tpu as pltpu
from jax.sharding import PartitionSpec as P

LOWEST = -1e30
STEPS = 8
SUBS = 2
LANES = 128
STATE_ROWS = 8
VMEM_LIMIT = 16 * 1024 * 1024


def ring_order(blocks):
    if blocks <= 8:
        return list(range(0, blocks, 2)) + list(range(blocks - 1, 0, -2))
    return list(range(blocks))


def message_kernel(core_ref, tags_ref, rows_ref, *message_refs):
    span = message_refs[0].shape[1]
    half = rows_ref.shape[0]
    for index, ref in enumerate(message_refs):
        ref[:, :span] = rows_ref[:, index * span : (index + 1) * span]
    row = lax.broadcasted_iota(jnp.int32, (half, LANES), 0)
    tags = jnp.zeros((half, LANES), jnp.float32)
    for r in range(half):
        tag = tags_ref[core_ref[0] * half + r].astype(jnp.float32)
        tags = jnp.where(row == r, tag, tags)
    message_refs[-1][:, span:] = tags.astype(jnp.bfloat16)


def make_messages(core, template_class, templates, owners):
    height, freqs = templates.shape
    half = height // owners
    span = freqs // SUBS
    widths = [span] * (SUBS - 1) + [span + LANES]
    return pl.pallas_call(
        message_kernel,
        grid_spec=pltpu.PrefetchScalarGridSpec(
            num_scalar_prefetch=2,
            grid=(1,),
            in_specs=[pl.BlockSpec((half, freqs), lambda j, core, tags: (core[0], 0))],
            out_specs=[pl.BlockSpec((half, width), lambda j, core, tags: (0, 0)) for width in widths],
        ),
        out_shape=[jax.ShapeDtypeStruct((half, width), jnp.bfloat16) for width in widths],
        compiler_params=pltpu.CompilerParams(vmem_limit_bytes=VMEM_LIMIT),
    )(core, template_class, templates)


def add_scores(rows, noise, part, acc, energy):
    widened = rows.astype(jnp.float32)
    product = widened * noise
    square = product * widened
    folded = square[:, :LANES]
    for lane in range(LANES, square.shape[1], LANES):
        folded = folded + square[:, lane : lane + LANES]
    energy[...] += folded
    acc[...] += lax.dot_general(
        product.astype(jnp.bfloat16),
        part,
        (((1,), (1,)), ((), ())),
        preferred_element_type=jnp.float32,
    )


def add_rows(tags, ids, logs_ref, sig_ref, state, acc, energy):
    classes = logs_ref.shape[0]
    prior = jnp.zeros_like(tags[:, :1])
    for tag in range(classes):
        prior = jnp.where(tags[:, :1] == tag, logs_ref[tag], prior)
    bias = prior - 0.5 * jnp.sum(energy[...], axis=1, keepdims=True)
    scores = acc[...] + bias
    old_max, old_sum, old_top, weights = state
    new_max = jnp.maximum(old_max, jnp.max(scores, axis=0, keepdims=True))
    new_sum = old_sum * jnp.exp(old_max - new_max) + jnp.sum(
        jnp.exp(scores - new_max), axis=0, keepdims=True
    )
    hit = sig_ref[0:1, :] == ids
    for pick in range(1, sig_ref.shape[0]):
        hit = hit | (sig_ref[pick : pick + 1, :] == ids)
    new_top = jnp.maximum(
        old_top, jnp.max(jnp.where(hit, scores, LOWEST), axis=0, keepdims=True)
    )
    value = jnp.where(hit, jnp.exp(scores - new_top), 0.0)
    lane = lax.broadcasted_iota(jnp.int32, tags.shape, 1).astype(jnp.float32)
    onehot = jnp.transpose(jnp.where(tags == lane, 1.0, 0.0))[:classes, :].astype(jnp.bfloat16)
    weights = weights * jnp.exp(old_top - new_top)
    left = value
    for _ in range(3):
        piece = left.astype(jnp.bfloat16)
        left = left - piece.astype(jnp.float32)
        weights = weights + jnp.dot(onehot, piece, preferred_element_type=jnp.float32)
    return new_max, new_sum, new_top, weights


def put_state(state, out_ref):
    new_max, new_sum, new_top, weights = state
    out_ref[0:1, :] = new_max
    out_ref[1:2, :] = new_sum
    out_ref[2:3, :] = new_top
    out_ref[3:STATE_ROWS, :] = jnp.zeros_like(out_ref[3:STATE_ROWS, :])
    out_ref[STATE_ROWS:, :] = weights


def get_state(state_ref):
    return state_ref[0:1, :], state_ref[1:2, :], state_ref[2:3, :], state_ref[STATE_ROWS:, :]


def own_kernel(
    base_ref, logs_ref, tags_ref, sig_ref, noise_ref, tmpl_ref, far_ref,
    out_ref, near_ref, acc, energy, arrived,
):
    freqs = noise_ref.shape[1]
    height = tmpl_ref.shape[0]
    width = freqs // STEPS

    def copy(step):
        columns = pl.ds(pl.multiple_of(step * width, width), width)
        return pltpu.make_async_copy(
            far_ref.at[:, columns], near_ref.at[:, columns], arrived.at[step]
        )

    for step in range(STEPS):
        copy(step).start()
    acc[...] = jnp.zeros_like(acc)
    energy[...] = jnp.zeros_like(energy)

    @pl.loop(0, STEPS)
    def _(step):
        copy(step).wait()
        columns = pl.ds(pl.multiple_of(step * width, width), width)
        add_scores(
            tmpl_ref[:, columns], noise_ref[:, columns], near_ref[:, columns], acc, energy
        )

    row = lax.broadcasted_iota(jnp.int32, (height, LANES), 0)
    tags = jnp.zeros((height, LANES), jnp.float32)
    for r in range(height):
        tags = jnp.where(row == r, tags_ref[r].astype(jnp.float32), tags)
    ids = base_ref[0] + lax.broadcasted_iota(jnp.int32, (height, 1), 0)
    lowest = jnp.full((1, acc.shape[1]), LOWEST, jnp.float32)
    none = jnp.zeros((1, acc.shape[1]), jnp.float32)
    weights = jnp.zeros((logs_ref.shape[0], acc.shape[1]), jnp.float32)
    state = (lowest, none, lowest, weights)
    put_state(add_rows(tags, ids, logs_ref, sig_ref, state, acc, energy), out_ref)


def in_smem():
    return pl.BlockSpec(memory_space=pltpu.SMEM)


def in_vmem():
    return pl.BlockSpec(memory_space=pltpu.VMEM)


def score_own(base, logs, template_class, significant, noise, templates, particles):
    per_device, freqs = particles.shape
    height = templates.shape[0]
    rows = STATE_ROWS + logs.shape[0]
    return pl.pallas_call(
        own_kernel,
        in_specs=[in_smem()] * 3 + [in_vmem()] * 3 + [pl.BlockSpec(memory_space=pl.ANY)],
        out_specs=[in_vmem(), in_vmem()],
        out_shape=[
            jax.ShapeDtypeStruct((rows, per_device), jnp.float32),
            pltpu.VMEM(particles.shape, particles.dtype),
        ],
        scratch_shapes=[
            pltpu.VMEM((height, per_device), jnp.float32),
            pltpu.VMEM((height, LANES), jnp.float32),
            pltpu.SemaphoreType.DMA((STEPS,)),
        ],
        compiler_params=pltpu.CompilerParams(vmem_limit_bytes=VMEM_LIMIT),
        cost_estimate=pl.CostEstimate(
            flops=4 * 128 * per_device * freqs,
            bytes_accessed=2 * per_device * freqs,
            transcendentals=0,
        ),
    )(
        base, logs, template_class, significant, noise, templates,
        pltpu.with_memory_space_constraint(particles, pltpu.HBM),
    )


def ring_kernel(layout, base_ref, logs_ref, sig_ref, state_ref, noise_ref, part_ref, *rest):
    groups = []
    at = 0
    for subs in layout:
        groups.append(rest[at : at + subs])
        at += subs
    out_ref, acc, energy = rest[at:]
    freqs = noise_ref.shape[1]
    width = freqs // STEPS
    share = STEPS // layout[0]
    acc[...] = jnp.zeros_like(acc)
    energy[...] = jnp.zeros_like(energy)
    for which in range(layout[0]):

        @pl.loop(0, share)
        def _(step):
            near = pl.ds(pl.multiple_of(step * width, width), width)
            columns = pl.ds(pl.multiple_of((which * share + step) * width, width), width)
            rows = jnp.concatenate([refs[which][:, near] for refs in groups], axis=0)
            add_scores(rows, noise_ref[:, columns], part_ref[:, columns], acc, energy)

    span = freqs // layout[0]
    tags = jnp.concatenate([refs[-1][:, span:] for refs in groups], axis=0).astype(jnp.float32)
    row_ids = []
    for group, refs in enumerate(groups):
        height = refs[0].shape[0]
        row_ids.append(base_ref[group] + lax.broadcasted_iota(jnp.int32, (height, 1), 0))
    ids = jnp.concatenate(row_ids, axis=0)
    state = add_rows(tags, ids, logs_ref, sig_ref, get_state(state_ref), acc, energy)
    put_state(state, out_ref)


def score_groups(groups, bases, logs, significant, state, noise, particles):
    per_device, freqs = particles.shape
    parts = [part for group in groups for part in group]
    rows = sum(group[0].shape[0] for group in groups)
    return pl.pallas_call(
        functools.partial(ring_kernel, tuple(len(group) for group in groups)),
        in_specs=[in_smem()] * 2 + [in_vmem()] * (4 + len(parts)),
        out_specs=in_vmem(),
        out_shape=jax.ShapeDtypeStruct(state.shape, jnp.float32),
        scratch_shapes=[
            pltpu.VMEM((rows, per_device), jnp.float32),
            pltpu.VMEM((rows, LANES), jnp.float32),
        ],
        compiler_params=pltpu.CompilerParams(vmem_limit_bytes=VMEM_LIMIT),
        cost_estimate=pl.CostEstimate(
            flops=4 * 128 * per_device * freqs,
            bytes_accessed=2 * per_device * freqs,
            transcendentals=0,
        ),
    )(
        bases, logs, significant, state, noise,
        pltpu.with_memory_space_constraint(particles, pltpu.VMEM), *parts,
    )


def sums_kernel(own_ref, state_ref, part_ref, loglik_ref, mine_ref, theirs_ref):
    blocks, per_owner = mine_ref.shape[:2]
    width = part_ref.shape[1] // blocks
    _, _, _, weights = get_state(state_ref)
    loglik_ref[...] = state_ref[0:1, :] + jnp.log(state_ref[1:2, :])
    weights = weights / jnp.sum(weights, axis=0, keepdims=True)
    turned = jnp.concatenate([weights[per_owner:], weights[:per_owner]], axis=0)
    weights = jnp.where(own_ref[0] == 0, weights, turned)
    rounded = weights.astype(jnp.bfloat16)
    total = jnp.broadcast_to(
        jnp.sum(weights, axis=1, keepdims=True), (weights.shape[0], LANES)
    )

    @pl.loop(0, blocks)
    def _(block):
        columns = pl.ds(pl.multiple_of(block * width, width), width)
        sums = jnp.dot(rounded, part_ref[:, columns], preferred_element_type=jnp.float32)
        mine_ref[block, :, :width] = sums[:per_owner]
        theirs_ref[block, :, :width] = sums[per_owner:]
        mine_ref[block, :, width:] = total[:per_owner]
        theirs_ref[block, :, width:] = total[per_owner:]


def class_sums(own, state, particles, blocks, classes, owners):
    per_device, freqs = particles.shape
    width = freqs // blocks
    per_owner = classes // owners
    piece = jax.ShapeDtypeStruct((blocks, per_owner, width + LANES), jnp.float32)
    return pl.pallas_call(
        sums_kernel,
        in_specs=[in_smem(), in_vmem(), in_vmem()],
        out_specs=[in_vmem()] * 3,
        out_shape=[jax.ShapeDtypeStruct((1, per_device), jnp.float32), piece, piece],
        compiler_params=pltpu.CompilerParams(vmem_limit_bytes=VMEM_LIMIT),
        cost_estimate=pl.CostEstimate(
            flops=2 * 128 * per_device * freqs,
            bytes_accessed=2 * per_device * freqs,
            transcendentals=0,
        ),
    )(own, state, pltpu.with_memory_space_constraint(particles, pltpu.VMEM))


def scatter_sum(pieces, blocks, block_id):
    if blocks & (blocks - 1):
        pieces = lax.all_to_all(pieces, "blk", split_axis=0, concat_axis=0, tiled=True)
        return jnp.sum(pieces, axis=0)
    stride = blocks // 2
    while stride:
        bit = lax.rem(lax.div(block_id, stride), 2)
        keep = lax.dynamic_slice_in_dim(pieces, bit * stride, stride, 0)
        send = lax.dynamic_slice_in_dim(pieces, (1 - bit) * stride, stride, 0)
        pairs = [(i, i ^ stride) for i in range(blocks)]
        pieces = keep + lax.ppermute(send, "blk", pairs)
        stride //= 2
    return pieces[0]


def body(particles, significant, templates, template_class, class_counts, inv_noise):
    per_device, freqs = particles.shape
    height = templates.shape[0]
    classes = class_counts.shape[0]
    blocks = lax.axis_size("blk")
    owners = lax.axis_size("cls")
    half = height // owners
    order = ring_order(blocks)
    place = [order.index(block) for block in range(blocks)]
    block_id = lax.axis_index("blk")
    core = lax.axis_index("cls")
    at = jnp.asarray(place, jnp.int32)[block_id]
    order_table = jnp.asarray(order, jnp.int32)
    forward = [(order[i], order[(i + 1) % blocks]) for i in range(blocks)]
    backward = [(order[(i + 1) % blocks], order[i]) for i in range(blocks)]
    swap = [(i, owners - 1 - i) for i in range(owners)]

    noise = inv_noise[None, :]
    logs = jnp.log(class_counts.astype(jnp.float32))
    first = make_messages(core[None], template_class, templates, owners)
    base = (block_id * height)[None]
    state, near = score_own(
        base, logs, template_class, significant, noise, templates, particles
    )
    last = blocks // 2
    held = {1: first, -1: first}
    for distance in range(1, last + 1):
        groups, bases = [], []
        for way, pairs in ((1, forward), (-1, backward)):
            taken = list(range(SUBS))
            if distance == last:
                taken = taken[: SUBS // 2] if way == 1 else taken[SUBS // 2 :]
            arrived = {sub: lax.ppermute(held[way][sub], "blk", pairs) for sub in taken}
            passed = {sub: lax.ppermute(arrived[sub], "cls", swap) for sub in taken}
            held[way] = arrived
            if distance == last and way == -1:
                for sub in taken:
                    groups[0].append(arrived[sub])
                    groups[1].append(passed[sub])
                continue
            source = order_table[lax.rem(at - way * distance + blocks, blocks)]
            groups.append([arrived[sub] for sub in taken])
            groups.append([passed[sub] for sub in taken])
            bases.append(source * height + core * half)
            bases.append(source * height + (owners - 1 - core) * half)
        state = score_groups(groups, jnp.stack(bases), logs, significant, state, noise, near)

    loglik, mine, theirs = class_sums(core[None], state, near, blocks, classes, owners)
    reduced = mine + lax.ppermute(theirs, "cls", swap)
    total = scatter_sum(reduced, blocks, block_id)
    width = freqs // blocks
    per_owner = classes // owners
    counts = lax.dynamic_slice_in_dim(class_counts, core * per_owner, per_owner, 0)
    class_avg = total[:, :width] / (total[:, width] + counts.astype(jnp.float32))[:, None]
    return loglik[0], class_avg


def solution(mesh):
    placed = (
        P(("grp", "blk", "cls"), None),
        P(None, ("grp", "blk", "cls")),
        P(("grp", "blk"), None),
        P(("grp", "blk")),
        P("grp"),
        P(),
    )
    return jax.shard_map(
        body,
        mesh=mesh,
        in_specs=placed,
        out_specs=(P(("grp", "blk", "cls")), P(("grp", "cls"), "blk")),
        check_vma=False,
    )
```

```python
import functools

import jax
import jax.numpy as jnp
from jax import lax
from jax.experimental import pallas as pl
from jax.experimental.pallas import tpu as pltpu
from jax.sharding import PartitionSpec as P

LOWEST = -1e30
STEPS = 8
WIDTH = 1024
LANES = 128
STATE_ROWS = 8
VMEM_LIMIT = 16 * 1024 * 1024


def ring_order(blocks):
    if blocks <= 8:
        return list(range(0, blocks, 2)) + list(range(blocks - 1, 0, -2))
    return list(range(blocks))


def message_kernel(tags_ref, rows_ref, first_ref, second_ref, sent):
    height, span = first_ref.shape
    copies = [
        pltpu.make_async_copy(rows_ref.at[:, :span], first_ref, sent.at[0]),
        pltpu.make_async_copy(rows_ref.at[:, span:], second_ref.at[:, :span], sent.at[1]),
    ]
    for copy in copies:
        copy.start()
    second_ref[:, span:] = tag_rows(tags_ref, height).astype(jnp.bfloat16)
    for copy in copies:
        copy.wait()


def make_messages(template_class, templates):
    height, freqs = templates.shape
    span = freqs // 2
    return pl.pallas_call(
        message_kernel,
        in_specs=[in_smem(), pl.BlockSpec(memory_space=pl.ANY)],
        out_specs=[in_vmem(), in_vmem()],
        out_shape=[
            pltpu.VMEM((height, span), jnp.bfloat16),
            pltpu.VMEM((height, span + LANES), jnp.bfloat16),
        ],
        scratch_shapes=[pltpu.SemaphoreType.DMA((2,))],
        compiler_params=pltpu.CompilerParams(vmem_limit_bytes=VMEM_LIMIT),
    )(
        pltpu.with_memory_space_constraint(template_class, pltpu.HBM),
        pltpu.with_memory_space_constraint(templates, pltpu.HBM),
    )


def tag_rows(tags_ref, height):
    row = lax.broadcasted_iota(jnp.int32, (height, LANES), 0)
    tags = jnp.zeros((height, LANES), jnp.float32)
    for r in range(height):
        tags = jnp.where(row == r, tags_ref[r].astype(jnp.float32), tags)
    return tags


def in_smem():
    return pl.BlockSpec(memory_space=pltpu.SMEM)


def in_vmem():
    return pl.BlockSpec(memory_space=pltpu.VMEM)


def add_scores(rows, noise, part, acc, energy):
    widened = rows.astype(jnp.float32)
    product = widened * noise
    square = product * widened
    folded = square[:, :LANES]
    for lane in range(LANES, square.shape[1], LANES):
        folded = folded + square[:, lane : lane + LANES]
    energy[...] += folded
    acc[...] += lax.dot_general(
        part,
        product.astype(jnp.bfloat16),
        (((1,), (1,)), ((), ())),
        preferred_element_type=jnp.float32,
    )


def add_rows(tags, ids, logs_ref, sig_ref, state, acc, energy):
    classes = logs_ref.shape[0]
    prior = jnp.zeros_like(tags[:, :1])
    for tag in range(classes):
        prior = jnp.where(tags[:, :1] == tag, logs_ref[tag], prior)
    bias = prior - 0.5 * jnp.sum(energy[...], axis=1, keepdims=True)
    scores = jnp.transpose(acc[...]) + bias
    old_max, old_sum, old_top, weights = state
    new_max = jnp.maximum(old_max, jnp.max(scores, axis=0, keepdims=True))
    new_sum = old_sum * jnp.exp(old_max - new_max) + jnp.sum(
        jnp.exp(scores - new_max), axis=0, keepdims=True
    )
    hit = sig_ref[0:1, :] == ids
    for pick in range(1, sig_ref.shape[0]):
        hit = hit | (sig_ref[pick : pick + 1, :] == ids)
    new_top = jnp.maximum(
        old_top, jnp.max(jnp.where(hit, scores, LOWEST), axis=0, keepdims=True)
    )
    value = jnp.where(hit, jnp.exp(scores - new_top), 0.0)
    lane = lax.broadcasted_iota(jnp.int32, tags.shape, 1).astype(jnp.float32)
    onehot = jnp.transpose(jnp.where(tags == lane, 1.0, 0.0))[:classes, :].astype(jnp.bfloat16)
    weights = weights * jnp.exp(old_top - new_top)
    left = value
    for _ in range(3):
        piece = left.astype(jnp.bfloat16)
        left = left - piece.astype(jnp.float32)
        weights = weights + jnp.dot(onehot, piece, preferred_element_type=jnp.float32)
    return new_max, new_sum, new_top, weights


def put_state(state, out_ref):
    new_max, new_sum, new_top, weights = state
    out_ref[0:1, :] = new_max
    out_ref[1:2, :] = new_sum
    out_ref[2:3, :] = new_top
    out_ref[3:STATE_ROWS, :] = jnp.zeros_like(out_ref[3:STATE_ROWS, :])
    out_ref[STATE_ROWS:, :] = weights


def get_state(state_ref):
    return state_ref[0:1, :], state_ref[1:2, :], state_ref[2:3, :], state_ref[STATE_ROWS:, :]


def own_kernel(
    where_ref, logs_ref, tags_ref, sig_ref, noise_ref, tmpl_ref, far_ref,
    out_ref, near_ref, acc, energy, arrived,
):
    freqs = noise_ref.shape[1]
    height = tmpl_ref.shape[0]
    width = freqs // STEPS

    def copy(step):
        columns = pl.ds(pl.multiple_of(step * width, width), width)
        return pltpu.make_async_copy(
            far_ref.at[:, columns], near_ref.at[:, columns], arrived.at[step]
        )

    for step in range(STEPS):
        copy(step).start()
    acc[...] = jnp.zeros_like(acc)
    energy[...] = jnp.zeros_like(energy)

    @pl.loop(0, STEPS)
    def _(step):
        copy(step).wait()
        columns = pl.ds(pl.multiple_of(step * width, width), width)
        add_scores(
            tmpl_ref[:, columns], noise_ref[:, columns], near_ref[:, columns], acc, energy
        )

    tags = tag_rows(tags_ref, height)
    ids = where_ref[0] * height + lax.broadcasted_iota(jnp.int32, (height, 1), 0)
    lowest = jnp.full((1, acc.shape[0]), LOWEST, jnp.float32)
    none = jnp.zeros((1, acc.shape[0]), jnp.float32)
    weights = jnp.zeros((logs_ref.shape[0], acc.shape[0]), jnp.float32)
    state = (lowest, none, lowest, weights)
    put_state(add_rows(tags, ids, logs_ref, sig_ref, state, acc, energy), out_ref)


def score_own(where, logs, template_class, significant, noise, templates, particles):
    per_device, freqs = particles.shape
    height = templates.shape[0]
    rows = STATE_ROWS + logs.shape[0]
    return pl.pallas_call(
        own_kernel,
        in_specs=[in_smem()] * 3 + [in_vmem()] * 3 + [pl.BlockSpec(memory_space=pl.ANY)],
        out_specs=[in_vmem(), in_vmem()],
        out_shape=[
            jax.ShapeDtypeStruct((rows, per_device), jnp.float32),
            pltpu.VMEM(particles.shape, particles.dtype),
        ],
        scratch_shapes=[
            pltpu.VMEM((per_device, height), jnp.float32),
            pltpu.VMEM((height, LANES), jnp.float32),
            pltpu.SemaphoreType.DMA((STEPS,)),
        ],
        compiler_params=pltpu.CompilerParams(vmem_limit_bytes=VMEM_LIMIT),
        cost_estimate=pl.CostEstimate(
            flops=4 * 128 * per_device * freqs,
            bytes_accessed=2 * per_device * freqs,
            transcendentals=0,
        ),
    )(
        where,
        logs,
        *(
            pltpu.with_memory_space_constraint(x, pltpu.HBM)
            for x in (template_class, significant, noise, templates, particles)
        ),
    )


def ring_kernel(phase, ends, sources, where_ref, noise_ref, part_ref, own_ref, sib_ref, *rest):
    if phase == 0:
        acc, energy = rest
        acc[...] = jnp.zeros_like(acc)
        energy[...] = jnp.zeros_like(energy)
    else:
        acc_in, energy_in, logs_ref, sig_ref, state_ref, out_ref, acc, energy = rest
        acc[...] = acc_in[...]
        energy[...] = energy_in[...]
    freqs = noise_ref.shape[1]
    span = freqs // 4 if ends else freqs // 2
    core = where_ref[1]
    low = phase * (freqs // 2)
    if ends:
        pieces = [((own_ref,), low + core * span), ((sib_ref,), low + (1 - core) * span)]
    else:
        pieces = [((own_ref, sib_ref), low)]
    for refs, start in pieces:

        @pl.loop(0, span // WIDTH)
        def _(step):
            near = pl.ds(pl.multiple_of(step * WIDTH, WIDTH), WIDTH)
            columns = pl.ds(pl.multiple_of(start + step * WIDTH, WIDTH), WIDTH)
            rows = jnp.concatenate([ref[:, near] for ref in refs], axis=0)
            add_scores(rows, noise_ref[:, columns], part_ref[:, columns], acc, energy)

    if phase == 0:
        return
    height = own_ref.shape[0]
    tags = [ref[:, span:].astype(jnp.float32) for ref in (own_ref, sib_ref)]
    tags = jnp.where(core == 0, tags[1], tags[0]) if ends else jnp.concatenate(tags, axis=0)
    found = []
    for table in sources:
        source = jnp.int32(table[0])
        for block in range(1, len(table)):
            source = jnp.where(where_ref[0] == block, table[block], source)
        found.append(source)
    row = lax.broadcasted_iota(jnp.int32, (height, 1), 0)
    if ends:
        ids = found[0] * height + row
    else:
        own = jnp.where(core == 0, found[0], found[1])
        sib = jnp.where(core == 0, found[1], found[0])
        ids = jnp.concatenate([own * height + row, sib * height + row], axis=0)
    state = add_rows(tags, ids, logs_ref, sig_ref, get_state(state_ref), acc, energy)
    put_state(state, out_ref)


def ring_scores(phase, ends, sources, where, noise, particles, own, sib, rest):
    per_device, freqs = particles.shape
    rows = own.shape[0] * (1 if ends else 2)
    sums = [
        jax.ShapeDtypeStruct((per_device, rows), jnp.float32),
        jax.ShapeDtypeStruct((rows, LANES), jnp.float32),
    ]
    params = {}
    if phase == 0:
        params.update(out_specs=[in_vmem(), in_vmem()], out_shape=sums)
        rest_specs = []
    else:
        state = jax.ShapeDtypeStruct(rest[-1].shape, jnp.float32)
        scratch = [pltpu.VMEM(array.shape, array.dtype) for array in sums]
        params.update(out_specs=in_vmem(), out_shape=state, scratch_shapes=scratch)
        rest_specs = [in_vmem(), in_vmem(), in_smem(), in_vmem(), in_vmem()]
    return pl.pallas_call(
        functools.partial(ring_kernel, phase, ends, sources),
        in_specs=[in_smem()] + [in_vmem()] * 4 + rest_specs,
        compiler_params=pltpu.CompilerParams(vmem_limit_bytes=VMEM_LIMIT),
        cost_estimate=pl.CostEstimate(
            flops=2 * 128 * per_device * freqs,
            bytes_accessed=per_device * freqs,
            transcendentals=0,
        ),
        **params,
    )(
        where,
        noise,
        pltpu.with_memory_space_constraint(particles, pltpu.VMEM),
        own,
        sib,
        *rest,
    )


def sums_kernel(own_ref, state_ref, part_ref, loglik_ref, mine_ref, theirs_ref):
    blocks, per_owner = mine_ref.shape[:2]
    width = part_ref.shape[1] // blocks
    _, _, _, weights = get_state(state_ref)
    loglik_ref[...] = state_ref[0:1, :] + jnp.log(state_ref[1:2, :])
    weights = weights / jnp.sum(weights, axis=0, keepdims=True)
    turned = jnp.concatenate([weights[per_owner:], weights[:per_owner]], axis=0)
    weights = jnp.where(own_ref[0] == 0, weights, turned)
    rounded = weights.astype(jnp.bfloat16)
    total = jnp.broadcast_to(
        jnp.sum(weights, axis=1, keepdims=True), (weights.shape[0], LANES)
    )

    @pl.loop(0, blocks)
    def _(block):
        columns = pl.ds(pl.multiple_of(block * width, width), width)
        sums = jnp.dot(rounded, part_ref[:, columns], preferred_element_type=jnp.float32)
        mine_ref[block, :, :width] = sums[:per_owner]
        theirs_ref[block, :, :width] = sums[per_owner:]
        mine_ref[block, :, width:] = total[:per_owner]
        theirs_ref[block, :, width:] = total[per_owner:]


def class_sums(own, state, particles, blocks, classes, owners):
    per_device, freqs = particles.shape
    width = freqs // blocks
    per_owner = classes // owners
    piece = jax.ShapeDtypeStruct((blocks, per_owner, width + LANES), jnp.float32)
    return pl.pallas_call(
        sums_kernel,
        in_specs=[in_smem(), in_vmem(), in_vmem()],
        out_specs=[in_vmem()] * 3,
        out_shape=[jax.ShapeDtypeStruct((1, per_device), jnp.float32), piece, piece],
        compiler_params=pltpu.CompilerParams(vmem_limit_bytes=VMEM_LIMIT),
        cost_estimate=pl.CostEstimate(
            flops=2 * 128 * per_device * freqs,
            bytes_accessed=2 * per_device * freqs,
            transcendentals=0,
        ),
    )(own, state, pltpu.with_memory_space_constraint(particles, pltpu.VMEM))


def scatter_sum(pieces, blocks, block_id):
    if blocks & (blocks - 1):
        pieces = lax.all_to_all(pieces, "blk", split_axis=0, concat_axis=0, tiled=True)
        return jnp.sum(pieces, axis=0)
    steps = blocks.bit_length() - 1
    tail = pieces.shape[1:]
    for step in range(steps):
        stride = 1 << step
        bit = lax.rem(lax.div(block_id, stride), 2)
        pairs = pieces.reshape((-1, 2) + tail)
        keep = lax.dynamic_index_in_dim(pairs, bit, 1, keepdims=False)
        send = lax.dynamic_index_in_dim(pairs, 1 - bit, 1, keepdims=False)
        swaps = [(i, i ^ stride) for i in range(blocks)]
        pieces = keep + lax.ppermute(send, "blk", swaps)
    return pieces[0]


def body(particles, significant, templates, template_class, class_counts, inv_noise):
    per_device, freqs = particles.shape
    classes = class_counts.shape[0]
    blocks = lax.axis_size("blk")
    owners = lax.axis_size("cls")
    order = ring_order(blocks)
    place = [order.index(block) for block in range(blocks)]
    block_id = lax.axis_index("blk")
    core = lax.axis_index("cls")
    ring = [(2 * order[i], 2 * order[(i + 1) % blocks]) for i in range(blocks)]
    ring += [(2 * order[(i + 1) % blocks] + 1, 2 * order[i] + 1) for i in range(blocks)]
    swap = [(i, owners - 1 - i) for i in range(owners)]

    noise = inv_noise[None, :]
    logs = jnp.log(class_counts.astype(jnp.float32))
    held = make_messages(template_class, templates)
    where = jnp.stack([block_id, core])
    state, near = score_own(
        where, logs, template_class, significant, noise, templates, particles
    )
    last = blocks // 2
    gates = [state]
    for distance in range(1, last + 1):
        ends = distance == last
        sources = [
            tuple(order[(place[block] - sign * distance) % blocks] for block in range(blocks))
            for sign in (1, -1)
        ]
        arrived = []
        sums = ()
        for phase in range(2):
            message = held[phase]
            if ends:
                cut = freqs // 4
                message = lax.dynamic_slice_in_dim(
                    message, core * cut, message.shape[1] - cut, 1
                )
            own = lax.ppermute(message, ("blk", "cls"), ring)
            own, _ = lax.optimization_barrier((own, gates[max(len(gates) - 2, 0)]))
            sib = lax.ppermute(own, "cls", swap)
            rest = () if phase == 0 else (*sums, logs, significant, state)
            sums = ring_scores(phase, ends, sources, where, noise, near, own, sib, rest)
            gates.append(sums)
            if phase == 1:
                state = sums
            arrived.append(own)
        held = arrived

    loglik, mine, theirs = class_sums(core[None], state, near, blocks, classes, owners)
    reduced = mine + lax.ppermute(theirs, "cls", swap)
    total = scatter_sum(reduced, blocks, block_id)
    width = freqs // blocks
    per_owner = classes // owners
    counts = lax.dynamic_slice_in_dim(class_counts, core * per_owner, per_owner, 0)
    class_avg = total[:, :width] / (total[:, width] + counts.astype(jnp.float32))[:, None]
    return loglik[0], class_avg


def solution(mesh):
    placed = (
        P(("grp", "blk", "cls"), None),
        P(None, ("grp", "blk", "cls")),
        P(("grp", "blk"), None),
        P(("grp", "blk")),
        P("grp"),
        P(),
    )
    return jax.shard_map(
        body,
        mesh=mesh,
        in_specs=placed,
        out_specs=(P(("grp", "blk", "cls")), P(("grp", "cls"), "blk")),
        check_vma=False,
    )
```

```python
import functools

import jax
import jax.numpy as jnp
from jax import lax
from jax.experimental import pallas as pl
from jax.experimental.pallas import tpu as pltpu
from jax.sharding import PartitionSpec as P

LOWEST = -1e30
STEPS = 8
WIDTH = 1024
SLOTS = 3
STRIP = 256
LANES = 128
STATE_ROWS = 8
VMEM_LIMIT = 12 * 1024 * 1024


def ring_order(blocks):
    if blocks <= 8:
        return list(range(0, blocks, 2)) + list(range(blocks - 1, 0, -2))
    return list(range(blocks))


def message_kernel(tags_ref, rows_ref, first_ref, second_ref, sent):
    height, span = first_ref.shape
    copies = [
        pltpu.make_async_copy(rows_ref.at[:, :span], first_ref, sent.at[0]),
        pltpu.make_async_copy(rows_ref.at[:, span:], second_ref.at[:, :span], sent.at[1]),
    ]
    for copy in copies:
        copy.start()
    second_ref[:, span:] = tag_rows(tags_ref, height).astype(jnp.bfloat16)
    for copy in copies:
        copy.wait()


def make_messages(template_class, templates):
    height, freqs = templates.shape
    span = freqs // 2
    return pl.pallas_call(
        message_kernel,
        in_specs=[in_smem(), pl.BlockSpec(memory_space=pl.ANY)],
        out_specs=[in_vmem(), in_vmem()],
        out_shape=[
            pltpu.VMEM((height, span), jnp.bfloat16),
            pltpu.VMEM((height, span + LANES), jnp.bfloat16),
        ],
        scratch_shapes=[pltpu.SemaphoreType.DMA((2,))],
        compiler_params=pltpu.CompilerParams(vmem_limit_bytes=VMEM_LIMIT),
    )(
        pltpu.with_memory_space_constraint(template_class, pltpu.HBM),
        pltpu.with_memory_space_constraint(templates, pltpu.HBM),
    )


def tag_rows(tags_ref, height):
    row = lax.broadcasted_iota(jnp.int32, (height, LANES), 0)
    tags = jnp.zeros((height, LANES), jnp.float32)
    for r in range(height):
        tags = jnp.where(row == r, tags_ref[r].astype(jnp.float32), tags)
    return tags


def in_smem():
    return pl.BlockSpec(memory_space=pltpu.SMEM)


def in_vmem():
    return pl.BlockSpec(memory_space=pltpu.VMEM)


def add_scores(rows, noise, part, acc, energy):
    widened = rows.astype(jnp.float32)
    product = widened * noise
    square = product * widened
    folded = square[:, :LANES]
    for lane in range(LANES, square.shape[1], LANES):
        folded = folded + square[:, lane : lane + LANES]
    energy[...] += folded
    acc[...] += lax.dot_general(
        product.astype(jnp.bfloat16),
        part,
        (((1,), (0,)), ((), ())),
        preferred_element_type=jnp.float32,
    )


def pick_words(sig_ref, words_ref):
    word = lax.broadcasted_iota(jnp.int32, words_ref.shape, 0)
    words = jnp.zeros(words_ref.shape, jnp.int32)
    for pick in range(sig_ref.shape[0]):
        chosen = sig_ref[pick : pick + 1, :]
        bit = jnp.left_shift(1, jnp.bitwise_and(chosen, 31))
        words = words | jnp.where(jnp.right_shift(chosen, 5) == word, bit, 0)
    words_ref[...] = words


def picked_rows(words_ref, source, height):
    bit = jnp.left_shift(1, lax.broadcasted_iota(jnp.int32, (32, 1), 0))
    rows = []
    for word in range(height // 32):
        rows.append((words_ref[pl.ds(source * (height // 32) + word, 1), :] & bit) != 0)
    return jnp.concatenate(rows, axis=0)


def add_rows(tags, hit, logs_ref, state, acc, energy):
    classes = logs_ref.shape[0]
    prior = jnp.zeros_like(tags[:, :1])
    for tag in range(classes):
        prior = jnp.where(tags[:, :1] == tag, logs_ref[tag], prior)
    bias = prior - 0.5 * jnp.sum(energy[...], axis=1, keepdims=True)
    scores = acc[...] + bias
    old_max, old_sum, old_top, weights = state
    new_max = jnp.maximum(old_max, jnp.max(scores, axis=0, keepdims=True))
    new_sum = old_sum * jnp.exp(old_max - new_max) + jnp.sum(
        jnp.exp(scores - new_max), axis=0, keepdims=True
    )
    new_top = jnp.maximum(
        old_top, jnp.max(jnp.where(hit, scores, LOWEST), axis=0, keepdims=True)
    )
    value = jnp.where(hit, jnp.exp(scores - new_top), 0.0)
    lane = lax.broadcasted_iota(jnp.int32, tags.shape, 1).astype(jnp.float32)
    onehot = jnp.transpose(jnp.where(tags == lane, 1.0, 0.0))[:classes, :].astype(jnp.bfloat16)
    weights = weights * jnp.exp(old_top - new_top)
    left = value
    for _ in range(3):
        piece = left.astype(jnp.bfloat16)
        left = left - piece.astype(jnp.float32)
        weights = weights + jnp.dot(onehot, piece, preferred_element_type=jnp.float32)
    return new_max, new_sum, new_top, weights


def put_state(state, out_ref):
    new_max, new_sum, new_top, weights = state
    out_ref[0:1, :] = new_max
    out_ref[1:2, :] = new_sum
    out_ref[2:3, :] = new_top
    out_ref[3:STATE_ROWS, :] = jnp.zeros_like(out_ref[3:STATE_ROWS, :])
    out_ref[STATE_ROWS:, :] = weights


def get_state(state_ref):
    return state_ref[0:1, :], state_ref[1:2, :], state_ref[2:3, :], state_ref[STATE_ROWS:, :]


def own_kernel(
    where_ref, logs_ref, tags_ref, sig_ref, noise_ref, tmpl_ref, far_ref,
    out_ref, turned_ref, words_ref, acc, energy, slots, arrived,
):
    freqs = noise_ref.shape[1]
    height = tmpl_ref.shape[0]
    width = freqs // STEPS

    def copy(step):
        columns = pl.ds(pl.multiple_of(step * width, width), width)
        slot = lax.rem(step, SLOTS)
        return pltpu.make_async_copy(far_ref.at[:, columns], slots.at[slot], arrived.at[slot])

    for step in range(SLOTS):
        copy(step).start()
    pick_words(sig_ref, words_ref)
    acc[...] = jnp.zeros_like(acc)
    energy[...] = jnp.zeros_like(energy)

    @pl.loop(0, STEPS)
    def _(step):
        copy(step).wait()
        columns = pl.ds(pl.multiple_of(step * width, width), width)
        slot = lax.rem(step, SLOTS)

        @pl.loop(0, width // STRIP)
        def _(strip):
            some = pl.ds(pl.multiple_of(strip * STRIP, STRIP), STRIP)
            there = pl.ds(pl.multiple_of(step * width + strip * STRIP, STRIP), STRIP)
            turned_ref[there, :] = jnp.transpose(slots[slot, :, some])

        @pl.when(step + SLOTS < STEPS)
        def _():
            copy(step + SLOTS).start()

        add_scores(
            tmpl_ref[:, columns], noise_ref[:, columns], turned_ref[columns, :], acc, energy
        )

    tags = tag_rows(tags_ref, height)
    hit = picked_rows(words_ref, where_ref[0], height)
    lowest = jnp.full((1, acc.shape[1]), LOWEST, jnp.float32)
    none = jnp.zeros((1, acc.shape[1]), jnp.float32)
    weights = jnp.zeros((logs_ref.shape[0], acc.shape[1]), jnp.float32)
    state = (lowest, none, lowest, weights)
    put_state(add_rows(tags, hit, logs_ref, state, acc, energy), out_ref)


def score_own(where, logs, template_class, significant, noise, templates, particles, total):
    per_device, freqs = particles.shape
    height = templates.shape[0]
    rows = STATE_ROWS + logs.shape[0]
    return pl.pallas_call(
        own_kernel,
        in_specs=[in_smem()] * 3 + [in_vmem()] * 3 + [pl.BlockSpec(memory_space=pl.ANY)],
        out_specs=[in_vmem()] * 3,
        out_shape=[
            jax.ShapeDtypeStruct((rows, per_device), jnp.float32),
            pltpu.VMEM((freqs, per_device), particles.dtype),
            jax.ShapeDtypeStruct((total // 32, per_device), jnp.int32),
        ],
        scratch_shapes=[
            pltpu.VMEM((height, per_device), jnp.float32),
            pltpu.VMEM((height, LANES), jnp.float32),
            pltpu.VMEM((SLOTS, per_device, freqs // STEPS), particles.dtype),
            pltpu.SemaphoreType.DMA((SLOTS,)),
        ],
        compiler_params=pltpu.CompilerParams(vmem_limit_bytes=VMEM_LIMIT),
        cost_estimate=pl.CostEstimate(
            flops=4 * 128 * per_device * freqs,
            bytes_accessed=2 * per_device * freqs,
            transcendentals=0,
        ),
    )(
        where,
        logs,
        *(
            pltpu.with_memory_space_constraint(x, pltpu.HBM)
            for x in (template_class, significant, noise, templates, particles)
        ),
    )


def near_copies(far_ref, near, arrived):
    blocks, _, width = near.shape
    return [
        pltpu.make_async_copy(
            far_ref.at[:, block * width : (block + 1) * width], near.at[block], arrived.at[block]
        )
        for block in range(blocks)
    ]


def class_sums(state, core, near, copies, loglik_ref, mine_ref, theirs_ref):
    top, total, _, weights = state
    loglik_ref[...] = top + jnp.log(total)
    per_owner = mine_ref.shape[1]
    width = near.shape[2]
    weights = weights / jnp.sum(weights, axis=0, keepdims=True)
    turned = jnp.concatenate([weights[per_owner:], weights[:per_owner]], axis=0)
    weights = jnp.where(core == 0, weights, turned)
    rounded = weights.astype(jnp.bfloat16)
    totals = jnp.broadcast_to(
        jnp.sum(weights, axis=1, keepdims=True), (weights.shape[0], LANES)
    )
    for block, copy in enumerate(copies):
        copy.wait()
        sums = jnp.dot(rounded, near[block], preferred_element_type=jnp.float32)
        mine_ref[block, :, :width] = sums[:per_owner]
        theirs_ref[block, :, :width] = sums[per_owner:]
        mine_ref[block, :, width:] = totals[:per_owner]
        theirs_ref[block, :, width:] = totals[per_owner:]


def ring_kernel(phase, ends, sources, where_ref, noise_ref, part_ref, own_ref, sib_ref, *rest):
    if phase == 0:
        acc, energy = rest
        acc[...] = jnp.zeros_like(acc)
        energy[...] = jnp.zeros_like(energy)
    else:
        acc_in, energy_in, logs_ref, words_ref, state_ref, *rest = rest
        if ends:
            far_ref, loglik_ref, mine_ref, theirs_ref, acc, energy, near, arrived = rest
            copies = near_copies(far_ref, near, arrived)
            for copy in copies:
                copy.start()
        else:
            out_ref, acc, energy = rest
        acc[...] = acc_in[...]
        energy[...] = energy_in[...]
    freqs = noise_ref.shape[1]
    span = freqs // 4 if ends else freqs // 2
    core = where_ref[1]
    low = phase * (freqs // 2)
    if ends:
        pieces = [((own_ref,), low + core * span), ((sib_ref,), low + (1 - core) * span)]
    else:
        pieces = [((own_ref, sib_ref), low)]
    for refs, start in pieces:

        @pl.loop(0, span // WIDTH)
        def _(step):
            near = pl.ds(pl.multiple_of(step * WIDTH, WIDTH), WIDTH)
            columns = pl.ds(pl.multiple_of(start + step * WIDTH, WIDTH), WIDTH)
            rows = jnp.concatenate([ref[:, near] for ref in refs], axis=0)
            add_scores(rows, noise_ref[:, columns], part_ref[columns, :], acc, energy)

    if phase == 0:
        return
    height = own_ref.shape[0]
    tags = [ref[:, span:].astype(jnp.float32) for ref in (own_ref, sib_ref)]
    tags = jnp.where(core == 0, tags[1], tags[0]) if ends else jnp.concatenate(tags, axis=0)
    found = []
    for table in sources:
        source = jnp.int32(table[0])
        for block in range(1, len(table)):
            source = jnp.where(where_ref[0] == block, table[block], source)
        found.append(source)
    if ends:
        hit = picked_rows(words_ref, found[0], height)
    else:
        own = jnp.where(core == 0, found[0], found[1])
        sib = jnp.where(core == 0, found[1], found[0])
        hit = jnp.concatenate(
            [picked_rows(words_ref, source, height) for source in (own, sib)], axis=0
        )
    state = add_rows(tags, hit, logs_ref, get_state(state_ref), acc, energy)
    if ends:
        class_sums(state, core, near, copies, loglik_ref, mine_ref, theirs_ref)
    else:
        put_state(state, out_ref)


def ring_scores(phase, sources, where, noise, turned, own, sib, rest, blocks=0, owners=0):
    ends = blocks > 0
    freqs, per_device = turned.shape
    rows = own.shape[0] * (1 if ends else 2)
    sums = [
        jax.ShapeDtypeStruct((rows, per_device), jnp.float32),
        jax.ShapeDtypeStruct((rows, LANES), jnp.float32),
    ]
    scratch = [pltpu.VMEM(array.shape, array.dtype) for array in sums]
    limit = VMEM_LIMIT
    if phase == 0:
        shapes, scratch, rest_specs = sums, [], []
    else:
        logs, state = rest[2], rest[4]
        rest_specs = [in_vmem(), in_vmem(), in_smem(), in_vmem(), in_vmem()]
        if ends:
            width = freqs // blocks
            per_owner = logs.shape[0] // owners
            piece = jax.ShapeDtypeStruct((blocks, per_owner, width + LANES), jnp.float32)
            shapes = [jax.ShapeDtypeStruct((1, per_device), jnp.float32), piece, piece]
            scratch += [
                pltpu.VMEM((blocks, per_device, width), turned.dtype),
                pltpu.SemaphoreType.DMA((blocks,)),
            ]
            rest_specs.append(pl.BlockSpec(memory_space=pl.ANY))
            rest = (*rest[:-1], pltpu.with_memory_space_constraint(rest[-1], pltpu.HBM))
            limit += 2 * per_device * freqs
        else:
            shapes = [jax.ShapeDtypeStruct(state.shape, jnp.float32)]
    return pl.pallas_call(
        functools.partial(ring_kernel, phase, ends, sources),
        in_specs=[in_smem()] + [in_vmem()] * 4 + rest_specs,
        out_specs=[in_vmem()] * len(shapes),
        out_shape=shapes,
        scratch_shapes=scratch,
        compiler_params=pltpu.CompilerParams(vmem_limit_bytes=limit),
        cost_estimate=pl.CostEstimate(
            flops=2 * 128 * per_device * freqs,
            bytes_accessed=per_device * freqs,
            transcendentals=0,
        ),
    )(
        where,
        noise,
        pltpu.with_memory_space_constraint(turned, pltpu.VMEM),
        own,
        sib,
        *rest,
    )


def scatter_sum(pieces, blocks, block_id):
    if blocks & (blocks - 1):
        pieces = lax.all_to_all(pieces, "blk", split_axis=0, concat_axis=0, tiled=True)
        return jnp.sum(pieces, axis=0)
    steps = blocks.bit_length() - 1
    tail = pieces.shape[1:]
    for step in range(steps):
        stride = 1 << step
        bit = lax.rem(lax.div(block_id, stride), 2)
        pairs = pieces.reshape((-1, 2) + tail)
        keep = lax.dynamic_index_in_dim(pairs, bit, 1, keepdims=False)
        send = lax.dynamic_index_in_dim(pairs, 1 - bit, 1, keepdims=False)
        swaps = [(i, i ^ stride) for i in range(blocks)]
        pieces = keep + lax.ppermute(send, "blk", swaps)
    return pieces[0]


def body(particles, significant, templates, template_class, class_counts, inv_noise):
    per_device, freqs = particles.shape
    classes = class_counts.shape[0]
    blocks = lax.axis_size("blk")
    owners = lax.axis_size("cls")
    order = ring_order(blocks)
    place = [order.index(block) for block in range(blocks)]
    block_id = lax.axis_index("blk")
    core = lax.axis_index("cls")
    ring = [(2 * order[i], 2 * order[(i + 1) % blocks]) for i in range(blocks)]
    ring += [(2 * order[(i + 1) % blocks] + 1, 2 * order[i] + 1) for i in range(blocks)]
    swap = [(i, owners - 1 - i) for i in range(owners)]

    noise = inv_noise[None, :]
    logs = jnp.log(class_counts.astype(jnp.float32))
    held = make_messages(template_class, templates)
    where = jnp.stack([block_id, core])
    state, turned, words = score_own(
        where, logs, template_class, significant, noise, templates, particles,
        blocks * templates.shape[0],
    )
    last = blocks // 2
    gates = [state]
    for distance in range(1, last + 1):
        ends = distance == last
        sources = [
            tuple(order[(place[block] - sign * distance) % blocks] for block in range(blocks))
            for sign in (1, -1)
        ]
        arrived = []
        sums = ()
        for phase in range(2):
            message = held[phase]
            if ends:
                cut = freqs // 4
                message = lax.dynamic_slice_in_dim(
                    message, core * cut, message.shape[1] - cut, 1
                )
            own = lax.ppermute(message, ("blk", "cls"), ring)
            own, _ = lax.optimization_barrier((own, gates[max(len(gates) - 2, 0)]))
            sib = lax.ppermute(own, "cls", swap)
            rest = () if phase == 0 else (*sums, logs, words, state)
            if ends:
                rest += (particles,) if phase else ()
                sums = ring_scores(
                    phase, sources, where, noise, turned, own, sib, rest, blocks, owners
                )
            else:
                sums = ring_scores(phase, sources, where, noise, turned, own, sib, rest)
            gates.append(sums)
            arrived.append(own)
        held = arrived
        if not ends:
            (state,) = sums

    loglik, mine, theirs = sums
    reduced = mine + lax.ppermute(theirs, "cls", swap)
    total = scatter_sum(reduced, blocks, block_id)
    width = freqs // blocks
    per_owner = classes // owners
    counts = lax.dynamic_slice_in_dim(class_counts, core * per_owner, per_owner, 0)
    class_avg = total[:, :width] / (total[:, width] + counts.astype(jnp.float32))[:, None]
    return loglik[0], class_avg


def solution(mesh):
    placed = (
        P(("grp", "blk", "cls"), None),
        P(None, ("grp", "blk", "cls")),
        P(("grp", "blk"), None),
        P(("grp", "blk")),
        P("grp"),
        P(),
    )
    return jax.shard_map(
        body,
        mesh=mesh,
        in_specs=placed,
        out_specs=(P(("grp", "blk", "cls")), P(("grp", "cls"), "blk")),
        check_vma=False,
    )
```

```python
import functools

import jax
import jax.numpy as jnp
from jax import lax
from jax.experimental import pallas as pl
from jax.experimental.pallas import tpu as pltpu
from jax.sharding import PartitionSpec as P

LOWEST = -1e30
STEPS = 16
WIDTH = 1024
SLOTS = 4
STRIP = 256
LANES = 128
STATE_ROWS = 8
VMEM_LIMIT = 10 * 1024 * 1024
SMALL_LIMIT = 6 * 1024 * 1024


def ring_order(blocks):
    if blocks <= 8:
        return list(range(0, blocks, 2)) + list(range(blocks - 1, 0, -2))
    return list(range(blocks))


def message_kernel(tags_ref, rows_ref, first_ref, second_ref, tags, sent):
    height, span = first_ref.shape
    copies = [
        pltpu.make_async_copy(tags_ref, tags, sent.at[0]),
        pltpu.make_async_copy(rows_ref.at[:, :span], first_ref, sent.at[1]),
        pltpu.make_async_copy(rows_ref.at[:, span:], second_ref.at[:, :span], sent.at[2]),
    ]
    for copy in copies:
        copy.start()
    copies[0].wait()
    second_ref[:, span:] = tag_rows(tags, height).astype(jnp.bfloat16)
    for copy in copies[1:]:
        copy.wait()


def make_messages(tags, templates):
    height, freqs = templates.shape
    span = freqs // 2
    return pl.pallas_call(
        message_kernel,
        in_specs=[pl.BlockSpec(memory_space=pl.ANY)] * 2,
        out_specs=[in_vmem(), in_vmem()],
        out_shape=[
            pltpu.VMEM((height, span), jnp.bfloat16),
            pltpu.VMEM((height, span + LANES), jnp.bfloat16),
        ],
        scratch_shapes=[pltpu.VMEM(tags.shape, tags.dtype), pltpu.SemaphoreType.DMA((3,))],
        compiler_params=pltpu.CompilerParams(vmem_limit_bytes=SMALL_LIMIT),
    )(
        pltpu.with_memory_space_constraint(tags, pltpu.HBM),
        pltpu.with_memory_space_constraint(templates, pltpu.HBM),
    )


def tag_rows(tags_ref, height):
    row = lax.broadcasted_iota(jnp.int32, (height, height), 0)
    lane = lax.broadcasted_iota(jnp.int32, (height, height), 1)
    spread = jnp.where(row == lane, tags_ref[...].astype(jnp.float32), 0.0)
    return jnp.broadcast_to(jnp.sum(spread, axis=1, keepdims=True), (height, LANES))


def in_smem():
    return pl.BlockSpec(memory_space=pltpu.SMEM)


def in_vmem():
    return pl.BlockSpec(memory_space=pltpu.VMEM)


def weigh(rows, noise, energy):
    widened = rows.astype(jnp.float32)
    product = widened * noise
    square = product * widened
    folded = square[:, :LANES]
    for lane in range(LANES, square.shape[1], LANES):
        folded = folded + square[:, lane : lane + LANES]
    energy[...] += folded
    return product.astype(jnp.bfloat16)


def pick_words(sig_ref, words_ref):
    word = lax.broadcasted_iota(jnp.int32, words_ref.shape, 0)
    words = jnp.zeros(words_ref.shape, jnp.int32)
    for pick in range(sig_ref.shape[0]):
        chosen = sig_ref[pick : pick + 1, :]
        bit = jnp.left_shift(1, jnp.bitwise_and(chosen, 31))
        words = words | jnp.where(jnp.right_shift(chosen, 5) == word, bit, 0)
    words_ref[...] = words


def picked_rows(words_ref, source, height):
    bit = jnp.left_shift(1, lax.broadcasted_iota(jnp.int32, (32, 1), 0))
    rows = []
    for word in range(height // 32):
        rows.append((words_ref[pl.ds(source * (height // 32) + word, 1), :] & bit) != 0)
    return jnp.concatenate(rows, axis=0)


def add_rows(tags, hit, logs_ref, state, acc, energy):
    classes = logs_ref.shape[0]
    prior = jnp.zeros_like(tags[:, :1])
    for tag in range(classes):
        prior = jnp.where(tags[:, :1] == tag, logs_ref[tag], prior)
    bias = prior - 0.5 * jnp.sum(energy[...], axis=1, keepdims=True)
    scores = acc[...] + bias
    old_max, old_sum, old_top, weights = state
    new_max = jnp.maximum(old_max, jnp.max(scores, axis=0, keepdims=True))
    new_sum = old_sum * jnp.exp(old_max - new_max) + jnp.sum(
        jnp.exp(scores - new_max), axis=0, keepdims=True
    )
    new_top = jnp.maximum(
        old_top, jnp.max(jnp.where(hit, scores, LOWEST), axis=0, keepdims=True)
    )
    value = jnp.where(hit, jnp.exp(scores - new_top), 0.0)
    lane = lax.broadcasted_iota(jnp.int32, tags.shape, 1).astype(jnp.float32)
    onehot = jnp.transpose(jnp.where(tags == lane, 1.0, 0.0))[:classes, :].astype(jnp.bfloat16)
    weights = weights * jnp.exp(old_top - new_top)
    left = value
    for _ in range(3):
        piece = left.astype(jnp.bfloat16)
        left = left - piece.astype(jnp.float32)
        weights = weights + jnp.dot(onehot, piece, preferred_element_type=jnp.float32)
    return new_max, new_sum, new_top, weights


def put_state(state, out_ref):
    new_max, new_sum, new_top, weights = state
    out_ref[0:1, :] = new_max
    out_ref[1:2, :] = new_sum
    out_ref[2:3, :] = new_top
    out_ref[3:STATE_ROWS, :] = jnp.zeros_like(out_ref[3:STATE_ROWS, :])
    out_ref[STATE_ROWS:, :] = weights


def get_state(state_ref):
    return state_ref[0:1, :], state_ref[1:2, :], state_ref[2:3, :], state_ref[STATE_ROWS:, :]


def own_kernel(phase, where_ref, noise_ref, tmpl_ref, far_ref, *rest):
    if phase == 0:
        sig_ref, turned_ref, words_ref, acc, energy, slots, arrived = rest
    else:
        acc_in, energy_in, logs_ref, tags_ref, words_ref, *rest = rest
        turned_ref, out_ref, acc, energy, slots, arrived = rest
    span = turned_ref.shape[0]
    height = tmpl_ref.shape[0]
    width = slots.shape[2]
    steps = span // width
    low = phase * span

    def copy(step):
        columns = pl.ds(pl.multiple_of(low + step * width, width), width)
        slot = lax.rem(step, SLOTS)
        return pltpu.make_async_copy(far_ref.at[:, columns], slots.at[slot], arrived.at[slot])

    for step in range(SLOTS):
        copy(step).start()
    if phase == 0:
        pick_words(sig_ref, words_ref)
        acc[...] = jnp.zeros_like(acc)
        energy[...] = jnp.zeros_like(energy)
    else:
        acc[...] = acc_in[...]
        energy[...] = energy_in[...]
    across = lax.broadcasted_iota(jnp.int32, (STRIP, STRIP), 0)
    along = lax.broadcasted_iota(jnp.int32, (STRIP, STRIP), 1)
    identity = jnp.where(across == along, 1.0, 0.0).astype(jnp.bfloat16)

    @pl.loop(0, steps)
    def _(step):
        copy(step).wait()
        slot = lax.rem(step, SLOTS)
        for strip in range(0, width, STRIP):
            there = pl.ds(pl.multiple_of(step * width + strip, STRIP), STRIP)
            weighted = weigh(tmpl_ref[:, there], noise_ref[:, there], energy)
            both = lax.dot_general(
                jnp.concatenate([weighted, identity], axis=0),
                slots[slot, :, strip : strip + STRIP],
                (((1,), (1,)), ((), ())),
                preferred_element_type=jnp.float32,
            )
            acc[...] += both[:height]
            turned_ref[there, :] = both[height:].astype(jnp.bfloat16)

        @pl.when(step + SLOTS < steps)
        def _():
            copy(step + SLOTS).start()

    if phase == 0:
        return
    tags = tag_rows(tags_ref, height)
    hit = picked_rows(words_ref, where_ref[0], height)
    lowest = jnp.full((1, acc.shape[1]), LOWEST, jnp.float32)
    none = jnp.zeros((1, acc.shape[1]), jnp.float32)
    weights = jnp.zeros((logs_ref.shape[0], acc.shape[1]), jnp.float32)
    state = (lowest, none, lowest, weights)
    put_state(add_rows(tags, hit, logs_ref, state, acc, energy), out_ref)


def own_scores(phase, where, noise, templates, particles, rest, total=0):
    per_device, freqs = particles.shape
    height = templates.shape[0]
    width = freqs // STEPS
    sums = [
        jax.ShapeDtypeStruct((height, per_device), jnp.float32),
        jax.ShapeDtypeStruct((height, LANES), jnp.float32),
    ]
    shapes = [pltpu.VMEM((freqs // 2, per_device), particles.dtype)]
    scratch = [
        pltpu.VMEM((SLOTS, per_device, width), particles.dtype),
        pltpu.SemaphoreType.DMA((SLOTS,)),
    ]
    if phase == 0:
        shapes += [jax.ShapeDtypeStruct((total // 32, per_device), jnp.int32)] + sums
        rest_specs = [in_vmem()]
    else:
        rows = STATE_ROWS + rest[2].shape[0]
        shapes.append(jax.ShapeDtypeStruct((rows, per_device), jnp.float32))
        scratch = [pltpu.VMEM(array.shape, array.dtype) for array in sums] + scratch
        rest_specs = [in_vmem(), in_vmem(), in_smem(), in_vmem(), in_vmem()]
    return pl.pallas_call(
        functools.partial(own_kernel, phase),
        grid=(1,),
        in_specs=[
            in_smem(),
            pl.BlockSpec((1, freqs // 2), lambda j: (0, phase)),
            pl.BlockSpec((height, freqs // 2), lambda j: (0, phase)),
            pl.BlockSpec(memory_space=pl.ANY),
            *rest_specs,
        ],
        out_specs=[in_vmem()] * len(shapes),
        out_shape=shapes,
        scratch_shapes=scratch,
        compiler_params=pltpu.CompilerParams(vmem_limit_bytes=VMEM_LIMIT),
        cost_estimate=pl.CostEstimate(
            flops=2 * 128 * per_device * freqs,
            bytes_accessed=per_device * freqs,
            transcendentals=0,
        ),
    )(
        where,
        *(pltpu.with_memory_space_constraint(x, pltpu.HBM) for x in (noise, templates, particles)),
        *rest,
    )


def near_copies(far_ref, near, arrived):
    blocks, _, width = near.shape
    return [
        pltpu.make_async_copy(
            far_ref.at[:, block * width : (block + 1) * width], near.at[block], arrived.at[block]
        )
        for block in range(blocks)
    ]


def class_sums(state, core, near, copies, loglik_ref, mine_ref, theirs_ref):
    top, total, _, weights = state
    loglik_ref[...] = top + jnp.log(total)
    per_owner = mine_ref.shape[1]
    width = near.shape[2]
    weights = weights / jnp.sum(weights, axis=0, keepdims=True)
    turned = jnp.concatenate([weights[per_owner:], weights[:per_owner]], axis=0)
    weights = jnp.where(core == 0, weights, turned)
    rounded = weights.astype(jnp.bfloat16)
    totals = jnp.broadcast_to(
        jnp.sum(weights, axis=1, keepdims=True), (weights.shape[0], LANES)
    )
    for block, copy in enumerate(copies):
        copy.wait()
        sums = jnp.dot(rounded, near[block], preferred_element_type=jnp.float32)
        mine_ref[block, :, :width] = sums[:per_owner]
        theirs_ref[block, :, :width] = sums[per_owner:]
        mine_ref[block, :, width:] = totals[:per_owner]
        theirs_ref[block, :, width:] = totals[per_owner:]


def ring_kernel(phase, ends, sources, where_ref, noise_ref, part_ref, own_ref, sib_ref, *rest):
    if phase == 0:
        acc, energy = rest
        acc[...] = jnp.zeros_like(acc)
        energy[...] = jnp.zeros_like(energy)
    else:
        acc_in, energy_in, logs_ref, words_ref, state_ref, *rest = rest
        if ends:
            far_ref, loglik_ref, mine_ref, theirs_ref, acc, energy, near, arrived = rest
            copies = near_copies(far_ref, near, arrived)
            for copy in copies:
                copy.start()
        else:
            out_ref, acc, energy = rest
        acc[...] = acc_in[...]
        energy[...] = energy_in[...]
    half = part_ref.shape[0]
    span = half // 2 if ends else half
    core = where_ref[1]
    if ends:
        pieces = [((own_ref,), core * span), ((sib_ref,), (1 - core) * span)]
    else:
        pieces = [((own_ref, sib_ref), 0)]
    for refs, start in pieces:

        @pl.loop(0, span // WIDTH)
        def _(step):
            near = pl.ds(pl.multiple_of(step * WIDTH, WIDTH), WIDTH)
            there = pl.ds(pl.multiple_of(start + step * WIDTH, WIDTH), WIDTH)
            columns = pl.ds(pl.multiple_of(phase * half + start + step * WIDTH, WIDTH), WIDTH)
            rows = jnp.concatenate([ref[:, near] for ref in refs], axis=0)
            weighted = weigh(rows, noise_ref[:, columns], energy)
            acc[...] += jnp.dot(
                weighted, part_ref[there, :], preferred_element_type=jnp.float32
            )

    if phase == 0:
        return
    height = own_ref.shape[0]
    tags = [ref[:, span:].astype(jnp.float32) for ref in (own_ref, sib_ref)]
    tags = jnp.where(core == 0, tags[1], tags[0]) if ends else jnp.concatenate(tags, axis=0)
    found = []
    for table in sources:
        source = jnp.int32(table[0])
        for block in range(1, len(table)):
            source = jnp.where(where_ref[0] == block, table[block], source)
        found.append(source)
    if ends:
        hit = picked_rows(words_ref, found[0], height)
    else:
        own = jnp.where(core == 0, found[0], found[1])
        sib = jnp.where(core == 0, found[1], found[0])
        hit = jnp.concatenate(
            [picked_rows(words_ref, source, height) for source in (own, sib)], axis=0
        )
    state = add_rows(tags, hit, logs_ref, get_state(state_ref), acc, energy)
    if ends:
        class_sums(state, core, near, copies, loglik_ref, mine_ref, theirs_ref)
    else:
        put_state(state, out_ref)


def ring_scores(phase, sources, where, noise, turned, own, sib, rest, blocks=0, owners=0):
    ends = blocks > 0
    half, per_device = turned.shape
    freqs = 2 * half
    rows = own.shape[0] * (1 if ends else 2)
    sums = [
        jax.ShapeDtypeStruct((rows, per_device), jnp.float32),
        jax.ShapeDtypeStruct((rows, LANES), jnp.float32),
    ]
    scratch = [pltpu.VMEM(array.shape, array.dtype) for array in sums]
    limit = SMALL_LIMIT
    if phase == 0:
        shapes, scratch, rest_specs = sums, [], []
    else:
        logs, state = rest[2], rest[4]
        rest_specs = [in_vmem(), in_vmem(), in_smem(), in_vmem(), in_vmem()]
        if ends:
            width = freqs // blocks
            per_owner = logs.shape[0] // owners
            piece = jax.ShapeDtypeStruct((blocks, per_owner, width + LANES), jnp.float32)
            shapes = [jax.ShapeDtypeStruct((1, per_device), jnp.float32), piece, piece]
            scratch += [
                pltpu.VMEM((blocks, per_device, width), turned.dtype),
                pltpu.SemaphoreType.DMA((blocks,)),
            ]
            rest_specs.append(pl.BlockSpec(memory_space=pl.ANY))
            rest = (*rest[:-1], pltpu.with_memory_space_constraint(rest[-1], pltpu.HBM))
            limit += 2 * per_device * freqs
        else:
            shapes = [jax.ShapeDtypeStruct(state.shape, jnp.float32)]
    return pl.pallas_call(
        functools.partial(ring_kernel, phase, ends, sources),
        in_specs=[in_smem()] + [in_vmem()] * 4 + rest_specs,
        out_specs=[in_vmem()] * len(shapes),
        out_shape=shapes,
        scratch_shapes=scratch,
        compiler_params=pltpu.CompilerParams(vmem_limit_bytes=limit),
        cost_estimate=pl.CostEstimate(
            flops=2 * 128 * per_device * freqs,
            bytes_accessed=per_device * freqs,
            transcendentals=0,
        ),
    )(
        where,
        noise,
        pltpu.with_memory_space_constraint(turned, pltpu.VMEM),
        own,
        sib,
        *rest,
    )


def scatter_sum(pieces, blocks, block_id):
    if blocks & (blocks - 1):
        pieces = lax.all_to_all(pieces, "blk", split_axis=0, concat_axis=0, tiled=True)
        return jnp.sum(pieces, axis=0)
    steps = blocks.bit_length() - 1
    tail = pieces.shape[1:]
    for step in range(steps):
        stride = 1 << step
        bit = lax.rem(lax.div(block_id, stride), 2)
        pairs = pieces.reshape((-1, 2) + tail)
        keep = lax.dynamic_index_in_dim(pairs, bit, 1, keepdims=False)
        send = lax.dynamic_index_in_dim(pairs, 1 - bit, 1, keepdims=False)
        swaps = [(i, i ^ stride) for i in range(blocks)]
        pieces = keep + lax.ppermute(send, "blk", swaps)
    return pieces[0]


def body(particles, significant, templates, template_class, class_counts, inv_noise):
    per_device, freqs = particles.shape
    classes = class_counts.shape[0]
    blocks = lax.axis_size("blk")
    owners = lax.axis_size("cls")
    order = ring_order(blocks)
    place = [order.index(block) for block in range(blocks)]
    block_id = lax.axis_index("blk")
    core = lax.axis_index("cls")
    ring = [(2 * order[i], 2 * order[(i + 1) % blocks]) for i in range(blocks)]
    ring += [(2 * order[(i + 1) % blocks] + 1, 2 * order[i] + 1) for i in range(blocks)]
    swap = [(i, owners - 1 - i) for i in range(owners)]

    noise = inv_noise[None, :]
    logs = jnp.log(class_counts.astype(jnp.float32))
    tags = template_class[None, :]
    held = make_messages(tags, templates)
    where = jnp.stack([block_id, core])
    cut = freqs // 4
    where, cut_at = lax.optimization_barrier((where, core.astype(jnp.uint32) * cut))
    picks = pltpu.with_memory_space_constraint(significant, pltpu.HBM)
    first, words, *sums = own_scores(
        0, where, noise, templates, particles, (picks,), blocks * templates.shape[0]
    )
    second, state = own_scores(
        1, where, noise, templates, particles, (*sums, logs, tags, words)
    )
    turned = (first, second)
    last = blocks // 2
    gates = [sums, state]
    for distance in range(1, last + 1):
        ends = distance == last
        sources = [
            tuple(order[(place[block] - sign * distance) % blocks] for block in range(blocks))
            for sign in (1, -1)
        ]
        arrived = []
        sums = ()
        for phase in range(2):
            message = held[phase]
            if ends:
                message = lax.dynamic_slice(
                    message,
                    (jnp.uint32(0), cut_at),
                    (message.shape[0], message.shape[1] - cut),
                )
            own = lax.ppermute(message, ("blk", "cls"), ring)
            own, _ = lax.optimization_barrier((own, gates[len(gates) - 2]))
            sib = lax.ppermute(own, "cls", swap)
            rest = () if phase == 0 else (*sums, logs, words, state)
            if ends:
                rest += (particles,) if phase else ()
                sums = ring_scores(
                    phase, sources, where, noise, turned[phase], own, sib, rest, blocks, owners
                )
            else:
                sums = ring_scores(phase, sources, where, noise, turned[phase], own, sib, rest)
            gates.append(sums)
            arrived.append(own)
        held = arrived
        if not ends:
            (state,) = sums

    loglik, mine, theirs = sums
    reduced = mine + lax.ppermute(theirs, "cls", swap)
    total = scatter_sum(reduced, blocks, block_id)
    width = freqs // blocks
    per_owner = classes // owners
    counts = lax.dynamic_slice_in_dim(class_counts, core * per_owner, per_owner, 0)
    class_avg = total[:, :width] / (total[:, width] + counts.astype(jnp.float32))[:, None]
    return loglik[0], class_avg


def solution(mesh):
    placed = (
        P(("grp", "blk", "cls"), None),
        P(None, ("grp", "blk", "cls")),
        P(("grp", "blk"), None),
        P(("grp", "blk")),
        P("grp"),
        P(),
    )
    return jax.shard_map(
        body,
        mesh=mesh,
        in_specs=placed,
        out_specs=(P(("grp", "blk", "cls")), P(("grp", "cls"), "blk")),
        check_vma=False,
    )
```

```python
import functools

import jax
import jax.numpy as jnp
from jax import lax
from jax.experimental import pallas as pl
from jax.experimental.pallas import tpu as pltpu
from jax.sharding import PartitionSpec as P

LOWEST = -1e30
STEPS = 16
WIDTH = 1024
SLOTS = 4
STRIP = 256
LANES = 128
STATE_ROWS = 8
VMEM_LIMIT = 10 * 1024 * 1024
SMALL_LIMIT = 6 * 1024 * 1024


def ring_order(blocks):
    if blocks <= 8:
        return list(range(0, blocks, 2)) + list(range(blocks - 1, 0, -2))
    return list(range(blocks))


def message_kernel(tags_ref, rows_ref, out_ref, tags, sent):
    height, span = out_ref.shape[0], out_ref.shape[1] - LANES
    copies = [
        pltpu.make_async_copy(tags_ref, tags, sent.at[0]),
        pltpu.make_async_copy(rows_ref.at[:, span:], out_ref.at[:, :span], sent.at[1]),
    ]
    for copy in copies:
        copy.start()
    copies[0].wait()
    out_ref[:, span:] = tag_rows(tags, height).astype(jnp.bfloat16)
    copies[1].wait()


def tagged_message(tags, templates):
    height, freqs = templates.shape
    return pl.pallas_call(
        message_kernel,
        in_specs=[pl.BlockSpec(memory_space=pl.ANY)] * 2,
        out_specs=in_vmem(),
        out_shape=pltpu.VMEM((height, freqs // 2 + LANES), jnp.bfloat16),
        scratch_shapes=[pltpu.VMEM(tags.shape, tags.dtype), pltpu.SemaphoreType.DMA((2,))],
        compiler_params=pltpu.CompilerParams(vmem_limit_bytes=SMALL_LIMIT),
    )(
        pltpu.with_memory_space_constraint(tags, pltpu.HBM),
        pltpu.with_memory_space_constraint(templates, pltpu.HBM),
    )


def tag_rows(tags_ref, height):
    row = lax.broadcasted_iota(jnp.int32, (height, height), 0)
    lane = lax.broadcasted_iota(jnp.int32, (height, height), 1)
    spread = jnp.where(row == lane, tags_ref[...].astype(jnp.float32), 0.0)
    return jnp.broadcast_to(jnp.sum(spread, axis=1, keepdims=True), (height, LANES))


def in_smem():
    return pl.BlockSpec(memory_space=pltpu.SMEM)


def in_vmem():
    return pl.BlockSpec(memory_space=pltpu.VMEM)


def weigh(rows, noise, energy):
    widened = rows.astype(jnp.float32)
    product = widened * noise
    square = product * widened
    folded = square[:, :LANES]
    for lane in range(LANES, square.shape[1], LANES):
        folded = folded + square[:, lane : lane + LANES]
    energy[...] += folded
    return product.astype(jnp.bfloat16)


def pick_words(sig_ref, words_ref):
    word = lax.broadcasted_iota(jnp.int32, words_ref.shape, 0)
    words = jnp.zeros(words_ref.shape, jnp.int32)
    for pick in range(sig_ref.shape[0]):
        chosen = sig_ref[pick : pick + 1, :]
        bit = jnp.left_shift(1, jnp.bitwise_and(chosen, 31))
        words = words | jnp.where(jnp.right_shift(chosen, 5) == word, bit, 0)
    words_ref[...] = words


def picked_rows(words_ref, source, height):
    bit = jnp.left_shift(1, lax.broadcasted_iota(jnp.int32, (32, 1), 0))
    rows = []
    for word in range(height // 32):
        rows.append((words_ref[pl.ds(source * (height // 32) + word, 1), :] & bit) != 0)
    return jnp.concatenate(rows, axis=0)


def add_rows(tags, hit, logs_ref, state, acc, energy):
    classes = logs_ref.shape[0]
    prior = jnp.zeros_like(tags[:, :1])
    for tag in range(classes):
        prior = jnp.where(tags[:, :1] == tag, logs_ref[tag], prior)
    bias = prior - 0.5 * jnp.sum(energy[...], axis=1, keepdims=True)
    scores = acc[...] + bias
    old_max, old_sum, old_top, weights = state
    new_max = jnp.maximum(old_max, jnp.max(scores, axis=0, keepdims=True))
    new_sum = old_sum * jnp.exp(old_max - new_max) + jnp.sum(
        jnp.exp(scores - new_max), axis=0, keepdims=True
    )
    new_top = jnp.maximum(
        old_top, jnp.max(jnp.where(hit, scores, LOWEST), axis=0, keepdims=True)
    )
    value = jnp.where(hit, jnp.exp(scores - new_top), 0.0)
    lane = lax.broadcasted_iota(jnp.int32, tags.shape, 1).astype(jnp.float32)
    onehot = jnp.transpose(jnp.where(tags == lane, 1.0, 0.0))[:classes, :].astype(jnp.bfloat16)
    weights = weights * jnp.exp(old_top - new_top)
    left = value
    for _ in range(3):
        piece = left.astype(jnp.bfloat16)
        left = left - piece.astype(jnp.float32)
        weights = weights + jnp.dot(onehot, piece, preferred_element_type=jnp.float32)
    return new_max, new_sum, new_top, weights


def put_state(state, out_ref):
    new_max, new_sum, new_top, weights = state
    out_ref[0:1, :] = new_max
    out_ref[1:2, :] = new_sum
    out_ref[2:3, :] = new_top
    out_ref[3:STATE_ROWS, :] = jnp.zeros_like(out_ref[3:STATE_ROWS, :])
    out_ref[STATE_ROWS:, :] = weights


def get_state(state_ref):
    return state_ref[0:1, :], state_ref[1:2, :], state_ref[2:3, :], state_ref[STATE_ROWS:, :]


def own_kernel(phase, where_ref, noise_ref, tmpl_ref, far_ref, *rest):
    if phase == 0:
        sig_ref, turned_ref, words_ref, acc, energy, slots, arrived = rest
    else:
        acc_in, energy_in, logs_ref, tags_ref, words_ref, *rest = rest
        turned_ref, out_ref, acc, energy, slots, arrived = rest
    span = turned_ref.shape[0]
    height = tmpl_ref.shape[0]
    width = slots.shape[2]
    steps = span // width
    low = phase * span

    def copy(step):
        columns = pl.ds(pl.multiple_of(low + step * width, width), width)
        slot = lax.rem(step, SLOTS)
        return pltpu.make_async_copy(far_ref.at[:, columns], slots.at[slot], arrived.at[slot])

    for step in range(SLOTS):
        copy(step).start()
    if phase == 0:
        pick_words(sig_ref, words_ref)
        acc[...] = jnp.zeros_like(acc)
        energy[...] = jnp.zeros_like(energy)
    else:
        acc[...] = acc_in[...]
        energy[...] = energy_in[...]
    @pl.loop(0, steps)
    def _(step):
        copy(step).wait()
        slot = lax.rem(step, SLOTS)
        for strip in range(0, width, STRIP):
            there = pl.ds(pl.multiple_of(step * width + strip, STRIP), STRIP)
            weighted = weigh(tmpl_ref[:, there], noise_ref[:, there], energy)
            turned = jnp.transpose(slots[slot, :, strip : strip + STRIP])
            turned_ref[there, :] = turned
            acc[...] += jnp.dot(weighted, turned, preferred_element_type=jnp.float32)

        @pl.when(step + SLOTS < steps)
        def _():
            copy(step + SLOTS).start()

    if phase == 0:
        return
    tags = tag_rows(tags_ref, height)
    hit = picked_rows(words_ref, where_ref[0], height)
    lowest = jnp.full((1, acc.shape[1]), LOWEST, jnp.float32)
    none = jnp.zeros((1, acc.shape[1]), jnp.float32)
    weights = jnp.zeros((logs_ref.shape[0], acc.shape[1]), jnp.float32)
    state = (lowest, none, lowest, weights)
    put_state(add_rows(tags, hit, logs_ref, state, acc, energy), out_ref)


def own_scores(phase, where, noise, templates, particles, rest, total=0):
    per_device, freqs = particles.shape
    height = templates.shape[0]
    width = freqs // STEPS
    sums = [
        jax.ShapeDtypeStruct((height, per_device), jnp.float32),
        jax.ShapeDtypeStruct((height, LANES), jnp.float32),
    ]
    shapes = [pltpu.VMEM((freqs // 2, per_device), particles.dtype)]
    scratch = [
        pltpu.VMEM((SLOTS, per_device, width), particles.dtype),
        pltpu.SemaphoreType.DMA((SLOTS,)),
    ]
    if phase == 0:
        shapes += [jax.ShapeDtypeStruct((total // 32, per_device), jnp.int32)] + sums
        rest_specs = [in_vmem()]
    else:
        rows = STATE_ROWS + rest[2].shape[0]
        shapes.append(jax.ShapeDtypeStruct((rows, per_device), jnp.float32))
        scratch = [pltpu.VMEM(array.shape, array.dtype) for array in sums] + scratch
        rest_specs = [in_vmem(), in_vmem(), in_smem(), in_vmem(), in_vmem()]
    return pl.pallas_call(
        functools.partial(own_kernel, phase),
        grid=(1,),
        in_specs=[
            in_smem(),
            pl.BlockSpec((1, freqs // 2), lambda j: (0, phase)),
            pl.BlockSpec((height, freqs // 2), lambda j: (0, phase)),
            pl.BlockSpec(memory_space=pl.ANY),
            *rest_specs,
        ],
        out_specs=[in_vmem()] * len(shapes),
        out_shape=shapes,
        scratch_shapes=scratch,
        compiler_params=pltpu.CompilerParams(vmem_limit_bytes=VMEM_LIMIT),
        cost_estimate=pl.CostEstimate(
            flops=2 * 128 * per_device * freqs,
            bytes_accessed=per_device * freqs,
            transcendentals=0,
        ),
    )(
        where,
        *(pltpu.with_memory_space_constraint(x, pltpu.HBM) for x in (noise, templates, particles)),
        *rest,
    )


def near_copies(far_ref, near, arrived):
    blocks, _, width = near.shape
    return [
        pltpu.make_async_copy(
            far_ref.at[:, block * width : (block + 1) * width], near.at[block], arrived.at[block]
        )
        for block in range(blocks)
    ]


def class_sums(state, core, near, copies, loglik_ref, mine_ref, theirs_ref):
    top, total, _, weights = state
    loglik_ref[...] = top + jnp.log(total)
    per_owner = mine_ref.shape[1]
    width = near.shape[2]
    weights = weights / jnp.sum(weights, axis=0, keepdims=True)
    turned = jnp.concatenate([weights[per_owner:], weights[:per_owner]], axis=0)
    weights = jnp.where(core == 0, weights, turned)
    rounded = weights.astype(jnp.bfloat16)
    totals = jnp.broadcast_to(
        jnp.sum(weights, axis=1, keepdims=True), (weights.shape[0], LANES)
    )
    for block, copy in enumerate(copies):
        copy.wait()
        sums = jnp.dot(rounded, near[block], preferred_element_type=jnp.float32)
        mine_ref[block, :, :width] = sums[:per_owner]
        theirs_ref[block, :, :width] = sums[per_owner:]
        mine_ref[block, :, width:] = totals[:per_owner]
        theirs_ref[block, :, width:] = totals[per_owner:]


def ring_kernel(phase, ends, sources, where_ref, noise_ref, part_ref, *rest):
    row_refs, rest = rest[: 2 * len(sources)], rest[2 * len(sources) :]
    if phase == 0:
        acc, energy = rest
        acc[...] = jnp.zeros_like(acc)
        energy[...] = jnp.zeros_like(energy)
    else:
        acc_in, energy_in, logs_ref, words_ref, state_ref, *rest = rest
        if ends:
            far_ref, loglik_ref, mine_ref, theirs_ref, acc, energy, near, arrived = rest
            copies = near_copies(far_ref, near, arrived)
            for copy in copies:
                copy.start()
        else:
            out_ref, acc, energy = rest
        acc[...] = acc_in[...]
        energy[...] = energy_in[...]
    half = part_ref.shape[0]
    span = half // 2 if ends else half
    core = where_ref[1]
    if ends:
        pieces = [(row_refs[:1], core * span), (row_refs[1:], (1 - core) * span)]
    else:
        pieces = [(row_refs, 0)]
    for refs, start in pieces:
        for step in range(span // WIDTH):
            here = pl.ds(step * WIDTH, WIDTH)
            there = pl.ds(pl.multiple_of(start + step * WIDTH, WIDTH), WIDTH)
            columns = pl.ds(pl.multiple_of(phase * half + start + step * WIDTH, WIDTH), WIDTH)
            rows = jnp.concatenate([ref[:, here] for ref in refs], axis=0)
            weighted = weigh(rows, noise_ref[:, columns], energy)
            acc[...] += jnp.dot(
                weighted, part_ref[there, :], preferred_element_type=jnp.float32
            )

    if phase == 0:
        return
    height = row_refs[0].shape[0]
    tags = [ref[:, span:].astype(jnp.float32) for ref in row_refs]
    tags = jnp.where(core == 0, tags[1], tags[0]) if ends else jnp.concatenate(tags, axis=0)
    found = []
    for tables in sources:
        for table in tables:
            source = jnp.int32(table[0])
            for block in range(1, len(table)):
                source = jnp.where(where_ref[0] == block, table[block], source)
            found.append(source)
    if ends:
        found = found[:1]
    else:
        for at in range(0, len(found), 2):
            front, back = found[at : at + 2]
            found[at] = jnp.where(core == 0, front, back)
            found[at + 1] = jnp.where(core == 0, back, front)
    hit = jnp.concatenate([picked_rows(words_ref, source, height) for source in found], axis=0)
    state = add_rows(tags, hit, logs_ref, get_state(state_ref), acc, energy)
    if ends:
        class_sums(state, core, near, copies, loglik_ref, mine_ref, theirs_ref)
    else:
        put_state(state, out_ref)


def ring_scores(phase, sources, where, noise, turned, arrays, rest, blocks=0, owners=0):
    ends = blocks > 0
    half, per_device = turned.shape
    freqs = 2 * half
    rows = arrays[0].shape[0] * (1 if ends else len(arrays))
    sums = [
        jax.ShapeDtypeStruct((rows, per_device), jnp.float32),
        jax.ShapeDtypeStruct((rows, LANES), jnp.float32),
    ]
    scratch = [pltpu.VMEM(array.shape, array.dtype) for array in sums]
    limit = SMALL_LIMIT
    if phase == 0:
        shapes, scratch, rest_specs = sums, [], []
    else:
        logs, state = rest[2], rest[4]
        rest_specs = [in_vmem(), in_vmem(), in_smem(), in_vmem(), in_vmem()]
        if ends:
            width = freqs // blocks
            per_owner = logs.shape[0] // owners
            piece = jax.ShapeDtypeStruct((blocks, per_owner, width + LANES), jnp.float32)
            shapes = [jax.ShapeDtypeStruct((1, per_device), jnp.float32), piece, piece]
            scratch += [
                pltpu.VMEM((blocks, per_device, width), turned.dtype),
                pltpu.SemaphoreType.DMA((blocks,)),
            ]
            rest_specs.append(pl.BlockSpec(memory_space=pl.ANY))
            rest = (*rest[:-1], pltpu.with_memory_space_constraint(rest[-1], pltpu.HBM))
            limit += 2 * per_device * freqs
        else:
            shapes = [jax.ShapeDtypeStruct(state.shape, jnp.float32)]
    return pl.pallas_call(
        functools.partial(ring_kernel, phase, ends, sources),
        in_specs=[in_smem()] + [in_vmem()] * (2 + len(arrays)) + rest_specs,
        out_specs=[in_vmem()] * len(shapes),
        out_shape=shapes,
        scratch_shapes=scratch,
        compiler_params=pltpu.CompilerParams(vmem_limit_bytes=limit),
        cost_estimate=pl.CostEstimate(
            flops=2 * 128 * per_device * freqs,
            bytes_accessed=per_device * freqs,
            transcendentals=0,
        ),
    )(
        where,
        noise,
        pltpu.with_memory_space_constraint(turned, pltpu.VMEM),
        *arrays,
        *rest,
    )


def scatter_sum(pieces, blocks, block_id):
    if blocks & (blocks - 1):
        pieces = lax.all_to_all(pieces, "blk", split_axis=0, concat_axis=0, tiled=True)
        return jnp.sum(pieces, axis=0)
    steps = blocks.bit_length() - 1
    tail = pieces.shape[1:]
    for step in range(steps):
        stride = 1 << step
        bit = lax.rem(lax.div(block_id, stride), 2)
        pairs = pieces.reshape((-1, 2) + tail)
        keep = lax.dynamic_index_in_dim(pairs, bit, 1, keepdims=False)
        send = lax.dynamic_index_in_dim(pairs, 1 - bit, 1, keepdims=False)
        swaps = [(i, i ^ stride) for i in range(blocks)]
        pieces = keep + lax.ppermute(send, "blk", swaps)
    return pieces[0]


def body(particles, significant, templates, template_class, class_counts, inv_noise):
    per_device, freqs = particles.shape
    classes = class_counts.shape[0]
    blocks = lax.axis_size("blk")
    owners = lax.axis_size("cls")
    order = ring_order(blocks)
    place = [order.index(block) for block in range(blocks)]
    block_id = lax.axis_index("blk")
    core = lax.axis_index("cls")
    ring = [(2 * order[i], 2 * order[(i + 1) % blocks]) for i in range(blocks)]
    ring += [(2 * order[(i + 1) % blocks] + 1, 2 * order[i] + 1) for i in range(blocks)]
    swap = [(i, owners - 1 - i) for i in range(owners)]

    noise = inv_noise[None, :]
    logs = jnp.log(class_counts.astype(jnp.float32))
    tags = template_class[None, :]
    head = templates[:, : freqs // 2]
    head, later = lax.optimization_barrier((head, templates))
    held = [head, tagged_message(tags, later)]
    where = jnp.stack([block_id, core])
    cut = freqs // 4
    where, cut_at = lax.optimization_barrier((where, core.astype(jnp.uint32) * cut))
    picks = pltpu.with_memory_space_constraint(significant, pltpu.HBM)
    first, words, *sums = own_scores(
        0, where, noise, templates, particles, (picks,), blocks * templates.shape[0]
    )
    second, state = own_scores(
        1, where, noise, templates, particles, (*sums, logs, tags, words)
    )
    turned = (first, second)
    last = blocks // 2
    gates = [sums, state]
    pairs, tables = ([], []), []
    for distance in range(1, last + 1):
        ends = distance == last
        tables.append(
            [
                tuple(order[(place[block] - sign * distance) % blocks] for block in range(blocks))
                for sign in (1, -1)
            ]
        )
        arrived = []
        for phase in range(2):
            message = held[phase]
            if ends:
                message = lax.dynamic_slice(
                    message,
                    (jnp.uint32(0), cut_at),
                    (message.shape[0], message.shape[1] - cut),
                )
            own = lax.ppermute(message, ("blk", "cls"), ring)
            own, _ = lax.optimization_barrier((own, gates[len(gates) - 2]))
            arrived.append(own)
            pairs[phase].extend((own, lax.ppermute(own, "cls", swap)))
            rest = () if phase == 0 else (*sums, logs, words, state)
            if ends:
                rest += (particles,) if phase else ()
                sums = ring_scores(
                    phase, tables, where, noise, turned[phase], pairs[phase], rest, blocks, owners
                )
            else:
                sums = ring_scores(phase, tables, where, noise, turned[phase], pairs[phase], rest)
            gates.append(sums)
        held = arrived
        pairs, tables = ([], []), []
        if not ends:
            (state,) = sums

    loglik, mine, theirs = sums
    reduced = mine + lax.ppermute(theirs, "cls", swap)
    total = scatter_sum(reduced, blocks, block_id)
    width = freqs // blocks
    per_owner = classes // owners
    counts = lax.dynamic_slice_in_dim(class_counts, core * per_owner, per_owner, 0)
    class_avg = total[:, :width] / (total[:, width] + counts.astype(jnp.float32))[:, None]
    return loglik[0], class_avg


def solution(mesh):
    placed = (
        P(("grp", "blk", "cls"), None),
        P(None, ("grp", "blk", "cls")),
        P(("grp", "blk"), None),
        P(("grp", "blk")),
        P("grp"),
        P(),
    )
    return jax.shard_map(
        body,
        mesh=mesh,
        in_specs=placed,
        out_specs=(P(("grp", "blk", "cls")), P(("grp", "cls"), "blk")),
        check_vma=False,
    )
```

```python
import functools

import jax
import jax.numpy as jnp
from jax import lax
from jax.experimental import pallas as pl
from jax.experimental.pallas import tpu as pltpu
from jax.sharding import PartitionSpec as P

LOWEST = -1e30
STEPS = 16
WIDTH = 1024
STRIP = 256
LANES = 128
STATE_ROWS = 8
VMEM_LIMIT = 14 * 1024 * 1024
SMALL_LIMIT = 6 * 1024 * 1024


def ring_order(blocks):
    if blocks <= 8:
        return list(range(0, blocks, 2)) + list(range(blocks - 1, 0, -2))
    return list(range(blocks))


def message_kernel(tags_ref, rows_ref, first_ref, second_ref, tags, sent):
    height, span = first_ref.shape
    copies = [
        pltpu.make_async_copy(tags_ref, tags, sent.at[0]),
        pltpu.make_async_copy(rows_ref.at[:, :span], first_ref, sent.at[1]),
        pltpu.make_async_copy(rows_ref.at[:, span:], second_ref.at[:, :span], sent.at[2]),
    ]
    for copy in copies:
        copy.start()
    copies[0].wait()
    second_ref[:, span:] = tag_rows(tags, height).astype(jnp.bfloat16)
    for copy in copies[1:]:
        copy.wait()


def make_messages(tags, templates):
    height, freqs = templates.shape
    span = freqs // 2
    return pl.pallas_call(
        message_kernel,
        in_specs=[pl.BlockSpec(memory_space=pl.ANY)] * 2,
        out_specs=[in_vmem(), in_vmem()],
        out_shape=[
            pltpu.VMEM((height, span), jnp.bfloat16),
            pltpu.VMEM((height, span + LANES), jnp.bfloat16),
        ],
        scratch_shapes=[pltpu.VMEM(tags.shape, tags.dtype), pltpu.SemaphoreType.DMA((3,))],
        compiler_params=pltpu.CompilerParams(vmem_limit_bytes=SMALL_LIMIT),
    )(
        pltpu.with_memory_space_constraint(tags, pltpu.HBM),
        pltpu.with_memory_space_constraint(templates, pltpu.HBM),
    )


def tag_rows(tags_ref, height):
    row = lax.broadcasted_iota(jnp.int32, (height, height), 0)
    lane = lax.broadcasted_iota(jnp.int32, (height, height), 1)
    spread = jnp.where(row == lane, tags_ref[...].astype(jnp.float32), 0.0)
    return jnp.broadcast_to(jnp.sum(spread, axis=1, keepdims=True), (height, LANES))


def in_smem():
    return pl.BlockSpec(memory_space=pltpu.SMEM)


def in_vmem():
    return pl.BlockSpec(memory_space=pltpu.VMEM)


def weigh(rows, noise, energy):
    widened = rows.astype(jnp.float32)
    product = widened * noise
    square = product * widened
    folded = square[:, :LANES]
    for lane in range(LANES, square.shape[1], LANES):
        folded = folded + square[:, lane : lane + LANES]
    energy[...] += folded
    return product.astype(jnp.bfloat16)


def pick_words(sig_ref, words_ref):
    word = lax.broadcasted_iota(jnp.int32, words_ref.shape, 0)
    words = jnp.zeros(words_ref.shape, jnp.int32)
    for pick in range(sig_ref.shape[0]):
        chosen = sig_ref[pick : pick + 1, :]
        bit = jnp.left_shift(1, jnp.bitwise_and(chosen, 31))
        words = words | jnp.where(jnp.right_shift(chosen, 5) == word, bit, 0)
    words_ref[...] = words


def picked_rows(words_ref, source, height):
    bit = jnp.left_shift(1, lax.broadcasted_iota(jnp.int32, (32, 1), 0))
    rows = []
    for word in range(height // 32):
        rows.append((words_ref[pl.ds(source * (height // 32) + word, 1), :] & bit) != 0)
    return jnp.concatenate(rows, axis=0)


def add_rows(tags, hit, logs_ref, state, acc, energy):
    classes = logs_ref.shape[0]
    prior = jnp.zeros_like(tags[:, :1])
    for tag in range(classes):
        prior = jnp.where(tags[:, :1] == tag, logs_ref[tag], prior)
    bias = prior - 0.5 * jnp.sum(energy[...], axis=1, keepdims=True)
    scores = acc[...] + bias
    old_max, old_sum, old_top, weights = state
    new_max = jnp.maximum(old_max, jnp.max(scores, axis=0, keepdims=True))
    new_sum = old_sum * jnp.exp(old_max - new_max) + jnp.sum(
        jnp.exp(scores - new_max), axis=0, keepdims=True
    )
    new_top = jnp.maximum(
        old_top, jnp.max(jnp.where(hit, scores, LOWEST), axis=0, keepdims=True)
    )
    value = jnp.where(hit, jnp.exp(scores - new_top), 0.0)
    lane = lax.broadcasted_iota(jnp.int32, tags.shape, 1).astype(jnp.float32)
    onehot = jnp.transpose(jnp.where(tags == lane, 1.0, 0.0))[:classes, :].astype(jnp.bfloat16)
    weights = weights * jnp.exp(old_top - new_top)
    left = value
    for _ in range(3):
        piece = left.astype(jnp.bfloat16)
        left = left - piece.astype(jnp.float32)
        weights = weights + jnp.dot(onehot, piece, preferred_element_type=jnp.float32)
    return new_max, new_sum, new_top, weights


def put_state(state, out_ref):
    new_max, new_sum, new_top, weights = state
    out_ref[0:1, :] = new_max
    out_ref[1:2, :] = new_sum
    out_ref[2:3, :] = new_top
    out_ref[3:STATE_ROWS, :] = jnp.zeros_like(out_ref[3:STATE_ROWS, :])
    out_ref[STATE_ROWS:, :] = weights


def get_state(state_ref):
    return state_ref[0:1, :], state_ref[1:2, :], state_ref[2:3, :], state_ref[STATE_ROWS:, :]


def own_kernel(phase, where_ref, noise_ref, tmpl_ref, far_ref, *rest):
    if phase == 0:
        sig_ref, turned_ref, words_ref, acc, energy, near, arrived = rest
    else:
        acc_in, energy_in, logs_ref, tags_ref, words_ref, *rest = rest
        turned_ref, out_ref, acc, energy, near, arrived = rest
    span = turned_ref.shape[0]
    height = tmpl_ref.shape[0]
    width = near.shape[2]
    steps = span // width
    low = phase * span

    def copy(step):
        columns = pl.ds(pl.multiple_of(low + step * width, width), width)
        return pltpu.make_async_copy(far_ref.at[:, columns], near.at[step], arrived.at[step])

    for step in range(steps):
        copy(step).start()
    if phase == 0:
        pick_words(sig_ref, words_ref)
        acc[...] = jnp.zeros_like(acc)
        energy[...] = jnp.zeros_like(energy)
    else:
        acc[...] = acc_in[...]
        energy[...] = energy_in[...]
    @pl.loop(0, steps)
    def _(step):
        copy(step).wait()
        for strip in range(0, width, STRIP):
            there = pl.ds(pl.multiple_of(step * width + strip, STRIP), STRIP)
            weighted = weigh(tmpl_ref[:, there], noise_ref[:, there], energy)
            turned = jnp.transpose(near[step, :, strip : strip + STRIP])
            turned_ref[there, :] = turned
            acc[...] += jnp.dot(weighted, turned, preferred_element_type=jnp.float32)

    if phase == 0:
        return
    tags = tag_rows(tags_ref, height)
    hit = picked_rows(words_ref, where_ref[0], height)
    lowest = jnp.full((1, acc.shape[1]), LOWEST, jnp.float32)
    none = jnp.zeros((1, acc.shape[1]), jnp.float32)
    weights = jnp.zeros((logs_ref.shape[0], acc.shape[1]), jnp.float32)
    state = (lowest, none, lowest, weights)
    put_state(add_rows(tags, hit, logs_ref, state, acc, energy), out_ref)


def own_scores(phase, where, noise, templates, particles, rest, total=0):
    per_device, freqs = particles.shape
    height = templates.shape[0]
    width = freqs // STEPS
    sums = [
        jax.ShapeDtypeStruct((height, per_device), jnp.float32),
        jax.ShapeDtypeStruct((height, LANES), jnp.float32),
    ]
    shapes = [pltpu.VMEM((freqs // 2, per_device), particles.dtype)]
    scratch = [
        pltpu.VMEM((STEPS // 2, per_device, width), particles.dtype),
        pltpu.SemaphoreType.DMA((STEPS // 2,)),
    ]
    if phase == 0:
        shapes += [jax.ShapeDtypeStruct((total // 32, per_device), jnp.int32)] + sums
        rest_specs = [in_vmem()]
    else:
        rows = STATE_ROWS + rest[2].shape[0]
        shapes.append(jax.ShapeDtypeStruct((rows, per_device), jnp.float32))
        scratch = [pltpu.VMEM(array.shape, array.dtype) for array in sums] + scratch
        rest_specs = [in_vmem(), in_vmem(), in_smem(), in_vmem(), in_vmem()]
    return pl.pallas_call(
        functools.partial(own_kernel, phase),
        grid=(1,),
        in_specs=[
            in_smem(),
            pl.BlockSpec((1, freqs // 2), lambda j: (0, phase)),
            pl.BlockSpec((height, freqs // 2), lambda j: (0, phase)),
            pl.BlockSpec(memory_space=pl.ANY),
            *rest_specs,
        ],
        out_specs=[in_vmem()] * len(shapes),
        out_shape=shapes,
        scratch_shapes=scratch,
        compiler_params=pltpu.CompilerParams(vmem_limit_bytes=VMEM_LIMIT),
        cost_estimate=pl.CostEstimate(
            flops=2 * 128 * per_device * freqs,
            bytes_accessed=per_device * freqs,
            transcendentals=0,
        ),
    )(
        where,
        *(pltpu.with_memory_space_constraint(x, pltpu.HBM) for x in (noise, templates, particles)),
        *rest,
    )


def near_copies(far_ref, near, arrived):
    blocks, _, width = near.shape
    return [
        pltpu.make_async_copy(
            far_ref.at[:, block * width : (block + 1) * width], near.at[block], arrived.at[block]
        )
        for block in range(blocks)
    ]


def class_sums(state, core, near, copies, loglik_ref, mine_ref, theirs_ref):
    top, total, _, weights = state
    loglik_ref[...] = top + jnp.log(total)
    per_owner = mine_ref.shape[1]
    width = near.shape[2]
    weights = weights / jnp.sum(weights, axis=0, keepdims=True)
    turned = jnp.concatenate([weights[per_owner:], weights[:per_owner]], axis=0)
    weights = jnp.where(core == 0, weights, turned)
    rounded = weights.astype(jnp.bfloat16)
    totals = jnp.broadcast_to(
        jnp.sum(weights, axis=1, keepdims=True), (weights.shape[0], LANES)
    )
    for block, copy in enumerate(copies):
        copy.wait()
        sums = jnp.dot(rounded, near[block], preferred_element_type=jnp.float32)
        mine_ref[block, :, :width] = sums[:per_owner]
        theirs_ref[block, :, :width] = sums[per_owner:]
        mine_ref[block, :, width:] = totals[:per_owner]
        theirs_ref[block, :, width:] = totals[per_owner:]


def ring_kernel(phase, ends, sources, where_ref, noise_ref, part_ref, *rest):
    row_refs, rest = rest[: 2 * len(sources)], rest[2 * len(sources) :]
    if phase == 0:
        acc, energy = rest
        acc[...] = jnp.zeros_like(acc)
        energy[...] = jnp.zeros_like(energy)
    else:
        acc_in, energy_in, logs_ref, words_ref, state_ref, *rest = rest
        if ends:
            far_ref, loglik_ref, mine_ref, theirs_ref, acc, energy, near, arrived = rest
            copies = near_copies(far_ref, near, arrived)
            for copy in copies:
                copy.start()
        else:
            out_ref, acc, energy = rest
        acc[...] = acc_in[...]
        energy[...] = energy_in[...]
    half = part_ref.shape[0]
    span = half // 2 if ends else half
    core = where_ref[1]
    if ends:
        pieces = [(row_refs[:1], core * span), (row_refs[1:], (1 - core) * span)]
    else:
        pieces = [(row_refs, 0)]
    for refs, start in pieces:

        def add(step):
            here = pl.ds(pl.multiple_of(step * WIDTH, WIDTH), WIDTH)
            there = pl.ds(pl.multiple_of(start + step * WIDTH, WIDTH), WIDTH)
            columns = pl.ds(pl.multiple_of(phase * half + start + step * WIDTH, WIDTH), WIDTH)
            rows = jnp.concatenate([ref[:, here] for ref in refs], axis=0)
            weighted = weigh(rows, noise_ref[:, columns], energy)
            acc[...] += jnp.dot(
                weighted, part_ref[there, :], preferred_element_type=jnp.float32
            )

        if ends and phase == 1:
            pl.loop(0, span // WIDTH)(add)
        else:
            for step in range(span // WIDTH):
                add(step)

    if phase == 0:
        return
    height = row_refs[0].shape[0]
    tags = [ref[:, span:].astype(jnp.float32) for ref in row_refs]
    tags = jnp.where(core == 0, tags[1], tags[0]) if ends else jnp.concatenate(tags, axis=0)
    found = []
    for tables in sources:
        for table in tables:
            source = jnp.int32(table[0])
            for block in range(1, len(table)):
                source = jnp.where(where_ref[0] == block, table[block], source)
            found.append(source)
    if ends:
        found = found[:1]
    else:
        for at in range(0, len(found), 2):
            front, back = found[at : at + 2]
            found[at] = jnp.where(core == 0, front, back)
            found[at + 1] = jnp.where(core == 0, back, front)
    hit = jnp.concatenate([picked_rows(words_ref, source, height) for source in found], axis=0)
    state = add_rows(tags, hit, logs_ref, get_state(state_ref), acc, energy)
    if ends:
        class_sums(state, core, near, copies, loglik_ref, mine_ref, theirs_ref)
    else:
        put_state(state, out_ref)


def ring_scores(phase, sources, where, noise, turned, arrays, rest, blocks=0, owners=0):
    ends = blocks > 0
    half, per_device = turned.shape
    freqs = 2 * half
    rows = arrays[0].shape[0] * (1 if ends else len(arrays))
    sums = [
        jax.ShapeDtypeStruct((rows, per_device), jnp.float32),
        jax.ShapeDtypeStruct((rows, LANES), jnp.float32),
    ]
    scratch = [pltpu.VMEM(array.shape, array.dtype) for array in sums]
    limit = SMALL_LIMIT
    if phase == 0:
        shapes, scratch, rest_specs = sums, [], []
    else:
        logs, state = rest[2], rest[4]
        rest_specs = [in_vmem(), in_vmem(), in_smem(), in_vmem(), in_vmem()]
        if ends:
            width = freqs // blocks
            per_owner = logs.shape[0] // owners
            piece = jax.ShapeDtypeStruct((blocks, per_owner, width + LANES), jnp.float32)
            shapes = [jax.ShapeDtypeStruct((1, per_device), jnp.float32), piece, piece]
            scratch += [
                pltpu.VMEM((blocks, per_device, width), turned.dtype),
                pltpu.SemaphoreType.DMA((blocks,)),
            ]
            rest_specs.append(pl.BlockSpec(memory_space=pl.ANY))
            rest = (*rest[:-1], pltpu.with_memory_space_constraint(rest[-1], pltpu.HBM))
            limit += 2 * per_device * freqs
        else:
            shapes = [jax.ShapeDtypeStruct(state.shape, jnp.float32)]
    return pl.pallas_call(
        functools.partial(ring_kernel, phase, ends, sources),
        in_specs=[in_smem()] + [in_vmem()] * (2 + len(arrays)) + rest_specs,
        out_specs=[in_vmem()] * len(shapes),
        out_shape=shapes,
        scratch_shapes=scratch,
        compiler_params=pltpu.CompilerParams(vmem_limit_bytes=limit),
        cost_estimate=pl.CostEstimate(
            flops=2 * 128 * per_device * freqs,
            bytes_accessed=per_device * freqs,
            transcendentals=0,
        ),
    )(
        where,
        noise,
        pltpu.with_memory_space_constraint(turned, pltpu.VMEM),
        *arrays,
        *rest,
    )


def scatter_sum(pieces, blocks, block_id):
    if blocks & (blocks - 1):
        pieces = lax.all_to_all(pieces, "blk", split_axis=0, concat_axis=0, tiled=True)
        return jnp.sum(pieces, axis=0)
    steps = blocks.bit_length() - 1
    tail = pieces.shape[1:]
    for step in range(steps):
        stride = 1 << step
        bit = lax.rem(lax.div(block_id, stride), 2)
        pairs = pieces.reshape((-1, 2) + tail)
        keep = lax.dynamic_index_in_dim(pairs, bit, 1, keepdims=False)
        send = lax.dynamic_index_in_dim(pairs, 1 - bit, 1, keepdims=False)
        swaps = [(i, i ^ stride) for i in range(blocks)]
        pieces = keep + lax.ppermute(send, "blk", swaps)
    return pieces[0]


def body(particles, significant, templates, template_class, class_counts, inv_noise):
    per_device, freqs = particles.shape
    classes = class_counts.shape[0]
    blocks = lax.axis_size("blk")
    owners = lax.axis_size("cls")
    order = ring_order(blocks)
    place = [order.index(block) for block in range(blocks)]
    block_id = lax.axis_index("blk")
    core = lax.axis_index("cls")
    ring = [(2 * order[i], 2 * order[(i + 1) % blocks]) for i in range(blocks)]
    ring += [(2 * order[(i + 1) % blocks] + 1, 2 * order[i] + 1) for i in range(blocks)]
    swap = [(i, owners - 1 - i) for i in range(owners)]

    noise = inv_noise[None, :]
    logs = jnp.log(class_counts.astype(jnp.float32))
    tags = template_class[None, :]
    held = make_messages(tags, templates)
    where = jnp.stack([block_id, core])
    cut = freqs // 4
    where, cut_at = lax.optimization_barrier((where, core.astype(jnp.uint32) * cut))
    picks = pltpu.with_memory_space_constraint(significant, pltpu.HBM)
    first, words, *sums = own_scores(
        0, where, noise, templates, particles, (picks,), blocks * templates.shape[0]
    )
    second, state = own_scores(
        1, where, noise, templates, particles, (*sums, logs, tags, words)
    )
    turned = (first, second)
    last = blocks // 2
    gates = [sums, state]
    pairs, tables = ([], []), []
    for distance in range(1, last + 1):
        ends = distance == last
        tables.append(
            [
                tuple(order[(place[block] - sign * distance) % blocks] for block in range(blocks))
                for sign in (1, -1)
            ]
        )
        arrived = []
        for phase in range(2):
            message = held[phase]
            if ends:
                message = lax.dynamic_slice(
                    message,
                    (jnp.uint32(0), cut_at),
                    (message.shape[0], message.shape[1] - cut),
                )
            own = lax.ppermute(message, ("blk", "cls"), ring)
            own, _ = lax.optimization_barrier((own, gates[len(gates) - 2]))
            arrived.append(own)
            pairs[phase].extend((own, lax.ppermute(own, "cls", swap)))
            rest = () if phase == 0 else (*sums, logs, words, state)
            if ends:
                rest += (particles,) if phase else ()
                sums = ring_scores(
                    phase, tables, where, noise, turned[phase], pairs[phase], rest, blocks, owners
                )
            else:
                sums = ring_scores(phase, tables, where, noise, turned[phase], pairs[phase], rest)
            gates.append(sums)
        held = arrived
        pairs, tables = ([], []), []
        if not ends:
            (state,) = sums

    loglik, mine, theirs = sums
    reduced = mine + lax.ppermute(theirs, "cls", swap)
    total = scatter_sum(reduced, blocks, block_id)
    width = freqs // blocks
    per_owner = classes // owners
    counts = lax.dynamic_slice_in_dim(class_counts, core * per_owner, per_owner, 0)
    class_avg = total[:, :width] / (total[:, width] + counts.astype(jnp.float32))[:, None]
    return loglik[0], class_avg


def solution(mesh):
    placed = (
        P(("grp", "blk", "cls"), None),
        P(None, ("grp", "blk", "cls")),
        P(("grp", "blk"), None),
        P(("grp", "blk")),
        P("grp"),
        P(),
    )
    return jax.shard_map(
        body,
        mesh=mesh,
        in_specs=placed,
        out_specs=(P(("grp", "blk", "cls")), P(("grp", "cls"), "blk")),
        check_vma=False,
    )
```

```python
import functools

import jax
import jax.numpy as jnp
from jax import lax
from jax.experimental import pallas as pl
from jax.experimental.pallas import tpu as pltpu
from jax.sharding import PartitionSpec as P

LOWEST = -1e30
STEPS = 16
WIDTH = 1024
STRIP = 256
LANES = 128
STATE_ROWS = 8
VMEM_LIMIT = 16 * 1024 * 1024
SMALL_LIMIT = 6 * 1024 * 1024


def ring_order(blocks):
    if blocks <= 8:
        return list(range(0, blocks, 2)) + list(range(blocks - 1, 0, -2))
    return list(range(blocks))


def message_kernel(tags_ref, rows_ref, first_ref, second_ref, tags, sent):
    height, span = first_ref.shape
    copies = [
        pltpu.make_async_copy(tags_ref, tags, sent.at[0]),
        pltpu.make_async_copy(rows_ref.at[:, :span], first_ref, sent.at[1]),
        pltpu.make_async_copy(rows_ref.at[:, span:], second_ref.at[:, :span], sent.at[2]),
    ]
    for copy in copies:
        copy.start()
    copies[0].wait()
    second_ref[:, span:] = tag_rows(tags, height).astype(jnp.bfloat16)
    for copy in copies[1:]:
        copy.wait()


def make_messages(tags, templates):
    height, freqs = templates.shape
    span = freqs // 2
    return pl.pallas_call(
        message_kernel,
        in_specs=[pl.BlockSpec(memory_space=pl.ANY)] * 2,
        out_specs=[in_vmem(), in_vmem()],
        out_shape=[
            pltpu.VMEM((height, span), jnp.bfloat16),
            pltpu.VMEM((height, span + LANES), jnp.bfloat16),
        ],
        scratch_shapes=[pltpu.VMEM(tags.shape, tags.dtype), pltpu.SemaphoreType.DMA((3,))],
        compiler_params=pltpu.CompilerParams(vmem_limit_bytes=SMALL_LIMIT),
    )(
        pltpu.with_memory_space_constraint(tags, pltpu.HBM),
        pltpu.with_memory_space_constraint(templates, pltpu.HBM),
    )


def tag_rows(tags_ref, height):
    row = lax.broadcasted_iota(jnp.int32, (height, height), 0)
    lane = lax.broadcasted_iota(jnp.int32, (height, height), 1)
    spread = jnp.where(row == lane, tags_ref[...].astype(jnp.float32), 0.0)
    return jnp.broadcast_to(jnp.sum(spread, axis=1, keepdims=True), (height, LANES))


def in_smem():
    return pl.BlockSpec(memory_space=pltpu.SMEM)


def in_vmem():
    return pl.BlockSpec(memory_space=pltpu.VMEM)


def weigh(rows, noise, energy):
    widened = rows.astype(jnp.float32)
    product = widened * noise
    square = product * widened
    folded = square[:, :LANES]
    for lane in range(LANES, square.shape[1], LANES):
        folded = folded + square[:, lane : lane + LANES]
    energy[...] += folded
    return product.astype(jnp.bfloat16)


def pick_words(sig_ref, words_ref):
    word = lax.broadcasted_iota(jnp.int32, words_ref.shape, 0)
    words = jnp.zeros(words_ref.shape, jnp.int32)
    for pick in range(sig_ref.shape[0]):
        chosen = sig_ref[pick : pick + 1, :]
        bit = jnp.left_shift(1, jnp.bitwise_and(chosen, 31))
        words = words | jnp.where(jnp.right_shift(chosen, 5) == word, bit, 0)
    words_ref[...] = words


def picked_rows(words_ref, source, height):
    bit = jnp.left_shift(1, lax.broadcasted_iota(jnp.int32, (32, 1), 0))
    rows = []
    for word in range(height // 32):
        rows.append((words_ref[pl.ds(source * (height // 32) + word, 1), :] & bit) != 0)
    return jnp.concatenate(rows, axis=0)


def add_rows(tags, hit, logs_ref, state, acc, energy):
    classes = logs_ref.shape[0]
    prior = jnp.zeros_like(tags[:, :1])
    for tag in range(classes):
        prior = jnp.where(tags[:, :1] == tag, logs_ref[tag], prior)
    bias = prior - 0.5 * jnp.sum(energy[...], axis=1, keepdims=True)
    scores = acc[...] + bias
    old_max, old_sum, old_top, weights = state
    new_max = jnp.maximum(old_max, jnp.max(scores, axis=0, keepdims=True))
    new_sum = old_sum * jnp.exp(old_max - new_max) + jnp.sum(
        jnp.exp(scores - new_max), axis=0, keepdims=True
    )
    new_top = jnp.maximum(
        old_top, jnp.max(jnp.where(hit, scores, LOWEST), axis=0, keepdims=True)
    )
    value = jnp.where(hit, jnp.exp(scores - new_top), 0.0)
    lane = lax.broadcasted_iota(jnp.int32, tags.shape, 1).astype(jnp.float32)
    onehot = jnp.transpose(jnp.where(tags == lane, 1.0, 0.0))[:classes, :].astype(jnp.bfloat16)
    weights = weights * jnp.exp(old_top - new_top)
    left = value
    for _ in range(3):
        piece = left.astype(jnp.bfloat16)
        left = left - piece.astype(jnp.float32)
        weights = weights + jnp.dot(onehot, piece, preferred_element_type=jnp.float32)
    return new_max, new_sum, new_top, weights


def put_state(state, out_ref):
    new_max, new_sum, new_top, weights = state
    out_ref[0:1, :] = new_max
    out_ref[1:2, :] = new_sum
    out_ref[2:3, :] = new_top
    out_ref[3:STATE_ROWS, :] = jnp.zeros_like(out_ref[3:STATE_ROWS, :])
    out_ref[STATE_ROWS:, :] = weights


def get_state(state_ref):
    return state_ref[0:1, :], state_ref[1:2, :], state_ref[2:3, :], state_ref[STATE_ROWS:, :]


def own_kernel(first, last, low, where_ref, noise_ref, tmpl_ref, far_ref, *rest):
    if first:
        sig_ref, words_ref, acc, energy, *turned_refs, near, arrived = rest
        pick_words(sig_ref, words_ref)
        acc[...] = jnp.zeros_like(acc)
        energy[...] = jnp.zeros_like(energy)
    else:
        acc_in, energy_in, *rest = rest
        if last:
            logs_ref, tags_ref, words_ref, out_ref, *turned_refs, acc, energy, near, arrived = rest
        else:
            acc, energy, *turned_refs, near, arrived = rest
        acc[...] = acc_in[...]
        energy[...] = energy_in[...]
    span, height, width = turned_refs[0].shape[0], tmpl_ref.shape[0], near.shape[2]
    steps = near.shape[0]

    def copy(step):
        columns = pl.ds(pl.multiple_of(low + step * width, width), width)
        return pltpu.make_async_copy(far_ref.at[:, columns], near.at[step], arrived.at[step])

    for step in range(steps):
        copy(step).start()
    for quarter, turned_ref in enumerate(turned_refs):

        @pl.loop(0, span // width)
        def _(inner):
            step = quarter * (span // width) + inner
            copy(step).wait()
            for strip in range(0, width, STRIP):
                there = pl.ds(pl.multiple_of(inner * width + strip, STRIP), STRIP)
                columns = pl.ds(pl.multiple_of(low + step * width + strip, STRIP), STRIP)
                weighted = weigh(tmpl_ref[:, columns], noise_ref[:, columns], energy)
                turned = jnp.transpose(near[step, :, strip : strip + STRIP])
                turned_ref[there, :] = turned
                acc[...] += jnp.dot(weighted, turned, preferred_element_type=jnp.float32)

    if not last:
        return
    tags = tag_rows(tags_ref, height)
    hit = picked_rows(words_ref, where_ref[0], height)
    lowest = jnp.full((1, acc.shape[1]), LOWEST, jnp.float32)
    none = jnp.zeros((1, acc.shape[1]), jnp.float32)
    weights = jnp.zeros((logs_ref.shape[0], acc.shape[1]), jnp.float32)
    state = (lowest, none, lowest, weights)
    put_state(add_rows(tags, hit, logs_ref, state, acc, energy), out_ref)


def own_scores(quarters, where, noise, templates, particles, rest, total=0):
    per_device, freqs = particles.shape
    height = templates.shape[0]
    width = freqs // STEPS
    span = freqs // 4
    steps = len(quarters) * span // width
    first, last = quarters[0] == 0, quarters[-1] == 3
    sums = [
        jax.ShapeDtypeStruct((height, per_device), jnp.float32),
        jax.ShapeDtypeStruct((height, LANES), jnp.float32),
    ]
    turned = [pltpu.VMEM((span, per_device), particles.dtype)] * len(quarters)
    scratch = [
        pltpu.VMEM((steps, per_device, width), particles.dtype),
        pltpu.SemaphoreType.DMA((steps,)),
    ]
    if first:
        shapes = [jax.ShapeDtypeStruct((total // 32, per_device), jnp.int32)] + sums
        rest_specs = [in_vmem()]
    elif last:
        rows = STATE_ROWS + rest[2].shape[0]
        shapes = [jax.ShapeDtypeStruct((rows, per_device), jnp.float32)]
        rest_specs = [in_vmem(), in_vmem(), in_smem(), in_vmem(), in_vmem()]
    else:
        shapes = sums
        rest_specs = [in_vmem(), in_vmem()]
    if last:
        scratch = [pltpu.VMEM(array.shape, array.dtype) for array in sums] + scratch
    return pl.pallas_call(
        functools.partial(own_kernel, first, last, quarters[0] * span),
        in_specs=[in_smem(), in_vmem(), in_vmem(), pl.BlockSpec(memory_space=pl.ANY)] + rest_specs,
        out_specs=[in_vmem()] * (len(shapes) + len(turned)),
        out_shape=shapes + turned,
        scratch_shapes=scratch,
        compiler_params=pltpu.CompilerParams(vmem_limit_bytes=VMEM_LIMIT),
        cost_estimate=pl.CostEstimate(
            flops=2 * 128 * per_device * freqs,
            bytes_accessed=per_device * freqs,
            transcendentals=0,
        ),
    )(
        where,
        *(pltpu.with_memory_space_constraint(x, pltpu.HBM) for x in (noise, templates, particles)),
        *rest,
    )


def near_copy(block, far_ref, near, arrived):
    width = near.shape[2]
    columns = pl.ds(pl.multiple_of(block * width, width), width)
    return pltpu.make_async_copy(far_ref.at[:, columns], near.at[block], arrived.at[block])


def class_sums(state, core, far_ref, near, arrived, loglik_ref, mine_ref, theirs_ref):
    top, total, _, weights = state
    loglik_ref[...] = top + jnp.log(total)
    blocks, per_owner = mine_ref.shape[:2]
    width = near.shape[2]
    weights = weights / jnp.sum(weights, axis=0, keepdims=True)
    turned = jnp.concatenate([weights[per_owner:], weights[:per_owner]], axis=0)
    weights = jnp.where(core == 0, weights, turned)
    rounded = weights.astype(jnp.bfloat16)
    totals = jnp.broadcast_to(
        jnp.sum(weights, axis=1, keepdims=True), (weights.shape[0], LANES)
    )

    @pl.loop(0, blocks)
    def _(block):
        near_copy(block, far_ref, near, arrived).wait()
        sums = jnp.dot(rounded, near[block], preferred_element_type=jnp.float32)
        mine_ref[block, :, :width] = sums[:per_owner]
        theirs_ref[block, :, :width] = sums[per_owner:]
        mine_ref[block, :, width:] = totals[:per_owner]
        theirs_ref[block, :, width:] = totals[per_owner:]


def ring_kernel(phase, ends, sources, where_ref, noise_ref, low_ref, high_ref, *rest):
    row_refs, rest = rest[: 2 * len(sources)], rest[2 * len(sources) :]
    if phase == 0:
        acc, energy = rest
        acc[...] = jnp.zeros_like(acc)
        energy[...] = jnp.zeros_like(energy)
    else:
        acc_in, energy_in, logs_ref, words_ref, state_ref, *rest = rest
        if ends:
            far_ref, loglik_ref, mine_ref, theirs_ref, acc, energy, near, arrived = rest
            for block in range(near.shape[0]):
                near_copy(block, far_ref, near, arrived).start()
        else:
            out_ref, acc, energy = rest
        acc[...] = acc_in[...]
        energy[...] = energy_in[...]
    quarter = low_ref.shape[0]
    core = where_ref[1]

    def add(refs, part_ref, at, step, start):
        here = pl.ds(pl.multiple_of(start + step * WIDTH, WIDTH), WIDTH)
        there = pl.ds(pl.multiple_of(step * WIDTH, WIDTH), WIDTH)
        columns = pl.ds((2 * phase + at) * quarter + step * WIDTH, WIDTH)
        rows = jnp.concatenate([ref[:, here] for ref in refs], axis=0)
        weighted = weigh(rows, noise_ref[:, columns], energy)
        acc[...] += jnp.dot(weighted, part_ref[there, :], preferred_element_type=jnp.float32)

    for at, part_ref in enumerate((low_ref, high_ref)):
        for step in range(quarter // WIDTH):
            if ends:
                for own, ref in ((True, row_refs[0]), (False, row_refs[1])):
                    pl.when((core == at) == own)(
                        functools.partial(add, [ref], part_ref, at, step, 0)
                    )
            else:
                add(row_refs, part_ref, at, step, at * quarter)

    if phase == 0:
        return
    height = row_refs[0].shape[0]
    span = quarter if ends else 2 * quarter
    tags = [ref[:, span:].astype(jnp.float32) for ref in row_refs]
    tags = jnp.where(core == 0, tags[1], tags[0]) if ends else jnp.concatenate(tags, axis=0)
    found = []
    for tables in sources:
        for table in tables:
            source = jnp.int32(table[0])
            for block in range(1, len(table)):
                source = jnp.where(where_ref[0] == block, table[block], source)
            found.append(source)
    if ends:
        found = found[:1]
    else:
        for at in range(0, len(found), 2):
            front, back = found[at : at + 2]
            found[at] = jnp.where(core == 0, front, back)
            found[at + 1] = jnp.where(core == 0, back, front)
    hit = jnp.concatenate([picked_rows(words_ref, source, height) for source in found], axis=0)
    state = add_rows(tags, hit, logs_ref, get_state(state_ref), acc, energy)
    if ends:
        class_sums(state, core, far_ref, near, arrived, loglik_ref, mine_ref, theirs_ref)
    else:
        put_state(state, out_ref)


def ring_scores(phase, sources, where, noise, turned, arrays, rest, blocks=0, owners=0):
    ends = blocks > 0
    quarter, per_device = turned[0].shape
    freqs = 4 * quarter
    rows = arrays[0].shape[0] * (1 if ends else len(arrays))
    sums = [
        jax.ShapeDtypeStruct((rows, per_device), jnp.float32),
        jax.ShapeDtypeStruct((rows, LANES), jnp.float32),
    ]
    scratch = [pltpu.VMEM(array.shape, array.dtype) for array in sums]
    limit = SMALL_LIMIT
    if phase == 0:
        shapes, scratch, rest_specs = sums, [], []
    else:
        logs, state = rest[2], rest[4]
        rest_specs = [in_vmem(), in_vmem(), in_smem(), in_vmem(), in_vmem()]
        if ends:
            width = freqs // blocks
            per_owner = logs.shape[0] // owners
            piece = jax.ShapeDtypeStruct((blocks, per_owner, width + LANES), jnp.float32)
            shapes = [jax.ShapeDtypeStruct((1, per_device), jnp.float32), piece, piece]
            scratch += [
                pltpu.VMEM((blocks, per_device, width), turned[0].dtype),
                pltpu.SemaphoreType.DMA((blocks,)),
            ]
            rest_specs.append(pl.BlockSpec(memory_space=pl.ANY))
            rest = (*rest[:-1], pltpu.with_memory_space_constraint(rest[-1], pltpu.HBM))
            limit += 2 * per_device * freqs
        else:
            shapes = [jax.ShapeDtypeStruct(state.shape, jnp.float32)]
    return pl.pallas_call(
        functools.partial(ring_kernel, phase, ends, sources),
        in_specs=[in_smem()] + [in_vmem()] * (3 + len(arrays)) + rest_specs,
        out_specs=[in_vmem()] * len(shapes),
        out_shape=shapes,
        scratch_shapes=scratch,
        compiler_params=pltpu.CompilerParams(vmem_limit_bytes=limit),
        cost_estimate=pl.CostEstimate(
            flops=2 * 128 * per_device * freqs,
            bytes_accessed=per_device * freqs,
            transcendentals=0,
        ),
    )(
        where,
        noise,
        *(pltpu.with_memory_space_constraint(part, pltpu.VMEM) for part in turned),
        *arrays,
        *rest,
    )


def scatter_sum(pieces, blocks, block_id):
    if blocks & (blocks - 1):
        pieces = lax.all_to_all(pieces, "blk", split_axis=0, concat_axis=0, tiled=True)
        return jnp.sum(pieces, axis=0)
    steps = blocks.bit_length() - 1
    tail = pieces.shape[1:]
    for step in range(steps):
        stride = 1 << step
        bit = lax.rem(lax.div(block_id, stride), 2)
        pairs = pieces.reshape((-1, 2) + tail)
        keep = lax.dynamic_index_in_dim(pairs, bit, 1, keepdims=False)
        send = lax.dynamic_index_in_dim(pairs, 1 - bit, 1, keepdims=False)
        swaps = [(i, i ^ stride) for i in range(blocks)]
        pieces = keep + lax.ppermute(send, "blk", swaps)
    return pieces[0]


def body(particles, significant, templates, template_class, class_counts, inv_noise):
    per_device, freqs = particles.shape
    classes = class_counts.shape[0]
    blocks = lax.axis_size("blk")
    owners = lax.axis_size("cls")
    order = ring_order(blocks)
    place = [order.index(block) for block in range(blocks)]
    block_id = lax.axis_index("blk")
    core = lax.axis_index("cls")
    ring = [(2 * order[i], 2 * order[(i + 1) % blocks]) for i in range(blocks)]
    ring += [(2 * order[(i + 1) % blocks] + 1, 2 * order[i] + 1) for i in range(blocks)]
    swap = [(i, owners - 1 - i) for i in range(owners)]

    noise = inv_noise[None, :]
    logs = jnp.log(class_counts.astype(jnp.float32))
    tags = template_class[None, :]
    held = make_messages(tags, templates)
    where = jnp.stack([block_id, core])
    cut = freqs // 4
    where, cut_at = lax.optimization_barrier((where, core.astype(jnp.uint32) * cut))
    picks = pltpu.with_memory_space_constraint(significant, pltpu.HBM)
    own = functools.partial(
        own_scores, where=where, noise=noise, templates=templates, particles=particles
    )
    words, *sums, low, high = own([0, 1], rest=(picks,), total=blocks * templates.shape[0])
    turned = [(low, high)]
    gates = [sums]
    *sums, low = own([2], rest=tuple(sums))
    gates.append(sums)
    state, high = own([3], rest=(*sums, logs, tags, words))
    turned.append((low, high))
    gates.append(state)
    last = blocks // 2
    pairs, tables = ([], []), []
    for distance in range(1, last + 1):
        ends = distance == last
        tables.append(
            [
                tuple(order[(place[block] - sign * distance) % blocks] for block in range(blocks))
                for sign in (1, -1)
            ]
        )
        arrived = []
        for phase in range(2):
            message = held[phase]
            if ends:
                message = lax.dynamic_slice(
                    message,
                    (jnp.uint32(0), cut_at),
                    (message.shape[0], message.shape[1] - cut),
                )
            own = lax.ppermute(message, ("blk", "cls"), ring)
            gate = phase if distance == 1 else len(gates) - (3 if distance == 2 else 2)
            own, _ = lax.optimization_barrier((own, gates[gate]))
            arrived.append(own)
            pairs[phase].extend((own, lax.ppermute(own, "cls", swap)))
            rest = () if phase == 0 else (*sums, logs, words, state)
            if ends:
                rest += (particles,) if phase else ()
                sums = ring_scores(
                    phase, tables, where, noise, turned[phase], pairs[phase], rest, blocks, owners
                )
            else:
                sums = ring_scores(phase, tables, where, noise, turned[phase], pairs[phase], rest)
            gates.append(sums)
        held = arrived
        pairs, tables = ([], []), []
        if not ends:
            (state,) = sums

    loglik, mine, theirs = sums
    reduced = mine + lax.ppermute(theirs, "cls", swap)
    total = scatter_sum(reduced, blocks, block_id)
    width = freqs // blocks
    per_owner = classes // owners
    counts = lax.dynamic_slice_in_dim(class_counts, core * per_owner, per_owner, 0)
    class_avg = total[:, :width] / (total[:, width] + counts.astype(jnp.float32))[:, None]
    return loglik[0], class_avg


def solution(mesh):
    placed = (
        P(("grp", "blk", "cls"), None),
        P(None, ("grp", "blk", "cls")),
        P(("grp", "blk"), None),
        P(("grp", "blk")),
        P("grp"),
        P(),
    )
    return jax.shard_map(
        body,
        mesh=mesh,
        in_specs=placed,
        out_specs=(P(("grp", "blk", "cls")), P(("grp", "cls"), "blk")),
        check_vma=False,
    )
```

```python
import functools

import jax
import jax.numpy as jnp
from jax import lax
from jax.experimental import pallas as pl
from jax.experimental.pallas import tpu as pltpu
from jax.sharding import PartitionSpec as P

LOWEST = -1e30
STEPS = 16
WIDTH = 1024
STRIP = 256
LANES = 128
STATE_ROWS = 8
VMEM_LIMIT = 16 * 1024 * 1024
SMALL_LIMIT = 6 * 1024 * 1024


def ring_order(blocks):
    if blocks <= 8:
        return list(range(0, blocks, 2)) + list(range(blocks - 1, 0, -2))
    return list(range(blocks))


def message_kernel(
    tags_ref, noise_ref, sig_ref, rows_ref,
    first_ref, second_ref, near_noise_ref, near_sig_ref, tags, sent,
):
    height, span = first_ref.shape
    copies = [
        pltpu.make_async_copy(rows_ref.at[:, :span], first_ref, sent.at[0]),
        pltpu.make_async_copy(rows_ref.at[:, span:], second_ref.at[:, :span], sent.at[1]),
        pltpu.make_async_copy(tags_ref, tags, sent.at[2]),
        pltpu.make_async_copy(noise_ref, near_noise_ref, sent.at[3]),
        pltpu.make_async_copy(sig_ref, near_sig_ref, sent.at[4]),
    ]
    for copy in copies:
        copy.start()
    copies[2].wait()
    second_ref[:, span:] = tag_rows(tags, height).astype(jnp.bfloat16)
    for copy in copies[:2] + copies[3:]:
        copy.wait()


def make_messages(tags, noise, significant, templates):
    height, freqs = templates.shape
    span = freqs // 2
    return pl.pallas_call(
        message_kernel,
        in_specs=[pl.BlockSpec(memory_space=pl.ANY)] * 4,
        out_specs=[in_vmem()] * 4,
        out_shape=[
            pltpu.VMEM((height, span), jnp.bfloat16),
            pltpu.VMEM((height, span + LANES), jnp.bfloat16),
            pltpu.VMEM(noise.shape, noise.dtype),
            pltpu.VMEM(significant.shape, significant.dtype),
        ],
        scratch_shapes=[pltpu.VMEM(tags.shape, tags.dtype), pltpu.SemaphoreType.DMA((5,))],
        compiler_params=pltpu.CompilerParams(vmem_limit_bytes=SMALL_LIMIT),
    )(
        *(
            pltpu.with_memory_space_constraint(x, pltpu.HBM)
            for x in (tags, noise, significant, templates)
        )
    )


def tag_rows(tags_ref, height):
    row = lax.broadcasted_iota(jnp.int32, (height, height), 0)
    lane = lax.broadcasted_iota(jnp.int32, (height, height), 1)
    spread = jnp.where(row == lane, tags_ref[...].astype(jnp.float32), 0.0)
    return jnp.broadcast_to(jnp.sum(spread, axis=1, keepdims=True), (height, LANES))


def in_smem():
    return pl.BlockSpec(memory_space=pltpu.SMEM)


def in_vmem():
    return pl.BlockSpec(memory_space=pltpu.VMEM)


def weigh(rows, noise, energy):
    widened = rows.astype(jnp.float32)
    product = widened * noise
    square = product * widened
    folded = square[:, :LANES]
    for lane in range(LANES, square.shape[1], LANES):
        folded = folded + square[:, lane : lane + LANES]
    energy[...] += folded
    return product.astype(jnp.bfloat16)


def pick_words(sig_ref, words_ref):
    word = lax.broadcasted_iota(jnp.int32, words_ref.shape, 0)
    words = jnp.zeros(words_ref.shape, jnp.int32)
    for pick in range(sig_ref.shape[0]):
        chosen = sig_ref[pick : pick + 1, :]
        bit = jnp.left_shift(1, jnp.bitwise_and(chosen, 31))
        words = words | jnp.where(jnp.right_shift(chosen, 5) == word, bit, 0)
    words_ref[...] = words


def picked_rows(words_ref, source, height):
    bit = jnp.left_shift(1, lax.broadcasted_iota(jnp.int32, (32, 1), 0))
    rows = []
    for word in range(height // 32):
        rows.append((words_ref[pl.ds(source * (height // 32) + word, 1), :] & bit) != 0)
    return jnp.concatenate(rows, axis=0)


def add_rows(tags, hit, logs_ref, state, acc, energy):
    classes = logs_ref.shape[0]
    prior = jnp.zeros_like(tags[:, :1])
    for tag in range(classes):
        prior = jnp.where(tags[:, :1] == tag, logs_ref[tag], prior)
    bias = prior - 0.5 * jnp.sum(energy[...], axis=1, keepdims=True)
    scores = acc[...] + bias
    old_max, old_sum, old_top, weights = state
    new_max = jnp.maximum(old_max, jnp.max(scores, axis=0, keepdims=True))
    new_sum = old_sum * jnp.exp(old_max - new_max) + jnp.sum(
        jnp.exp(scores - new_max), axis=0, keepdims=True
    )
    new_top = jnp.maximum(
        old_top, jnp.max(jnp.where(hit, scores, LOWEST), axis=0, keepdims=True)
    )
    value = jnp.where(hit, jnp.exp(scores - new_top), 0.0)
    lane = lax.broadcasted_iota(jnp.int32, tags.shape, 1).astype(jnp.float32)
    onehot = jnp.transpose(jnp.where(tags == lane, 1.0, 0.0))[:classes, :].astype(jnp.bfloat16)
    weights = weights * jnp.exp(old_top - new_top)
    left = value
    for _ in range(3):
        piece = left.astype(jnp.bfloat16)
        left = left - piece.astype(jnp.float32)
        weights = weights + jnp.dot(onehot, piece, preferred_element_type=jnp.float32)
    return new_max, new_sum, new_top, weights


def put_state(state, out_ref):
    new_max, new_sum, new_top, weights = state
    out_ref[0:1, :] = new_max
    out_ref[1:2, :] = new_sum
    out_ref[2:3, :] = new_top
    out_ref[3:STATE_ROWS, :] = jnp.zeros_like(out_ref[3:STATE_ROWS, :])
    out_ref[STATE_ROWS:, :] = weights


def get_state(state_ref):
    return state_ref[0:1, :], state_ref[1:2, :], state_ref[2:3, :], state_ref[STATE_ROWS:, :]


def own_kernel(quarters, where_ref, noise_ref, tmpl_ref, far_ref, *rest):
    first, last = quarters[0] == 0, quarters[-1] == 3
    if first:
        sig_ref, words_ref, acc, energy, *turned_refs, next_ref, near, arrived, late = rest
    elif last:
        acc_in, energy_in, logs_ref, tags_ref, words_ref, near, out_ref, *rest = rest
        *turned_refs, acc, energy = rest
    else:
        acc_in, energy_in, near, acc, energy, *turned_refs, next_ref, late = rest
    span, height = turned_refs[0].shape[0], tmpl_ref.shape[0]
    steps, _, width = near.shape
    low = quarters[0] * span

    def copy(step):
        columns = pl.ds(pl.multiple_of(low + step * width, width), width)
        return pltpu.make_async_copy(far_ref.at[:, columns], near.at[step], arrived.at[step])

    def following(step):
        columns = pl.ds(low + (steps + step) * width, width)
        return pltpu.make_async_copy(far_ref.at[:, columns], next_ref.at[step], late.at[step])

    if first:
        for step in range(steps):
            copy(step).start()
    if not last:
        for step in range(next_ref.shape[0]):
            following(step).start()
    if first:
        pick_words(sig_ref, words_ref)
        acc[...] = jnp.zeros_like(acc)
        energy[...] = jnp.zeros_like(energy)
    else:
        acc[...] = acc_in[...]
        energy[...] = energy_in[...]
    for quarter, turned_ref in zip(quarters, turned_refs):

        @pl.loop(0, span // width)
        def _(inner):
            step = (quarter - quarters[0]) * (span // width) + inner
            if first:
                copy(step).wait()
            for strip in range(0, width, STRIP):
                there = pl.ds(pl.multiple_of(inner * width + strip, STRIP), STRIP)
                part = quarter % 2 * span + inner * width + strip
                here = pl.ds(pl.multiple_of(part, STRIP), STRIP)
                columns = pl.ds(pl.multiple_of(low + step * width + strip, STRIP), STRIP)
                weighted = weigh(tmpl_ref[:, here], noise_ref[:, columns], energy)
                turned = jnp.transpose(near[step, :, strip : strip + STRIP])
                turned_ref[there, :] = turned
                acc[...] += jnp.dot(weighted, turned, preferred_element_type=jnp.float32)

    if not last:
        for step in range(next_ref.shape[0]):
            following(step).wait()
        return
    tags = tag_rows(tags_ref, height)
    hit = picked_rows(words_ref, where_ref[0], height)
    lowest = jnp.full((1, acc.shape[1]), LOWEST, jnp.float32)
    none = jnp.zeros((1, acc.shape[1]), jnp.float32)
    weights = jnp.zeros((logs_ref.shape[0], acc.shape[1]), jnp.float32)
    state = (lowest, none, lowest, weights)
    put_state(add_rows(tags, hit, logs_ref, state, acc, energy), out_ref)


def own_scores(quarters, where, noise, particles, templates, rest, total=0):
    per_device, freqs = particles.shape
    height = templates.shape[0]
    width = freqs // STEPS
    span = freqs // 4
    steps = span // width
    first, last = quarters[0] == 0, quarters[-1] == 3
    sums = [
        jax.ShapeDtypeStruct((height, per_device), jnp.float32),
        jax.ShapeDtypeStruct((height, LANES), jnp.float32),
    ]
    turned = [pltpu.VMEM((span, per_device), particles.dtype)] * len(quarters)
    raw = pltpu.VMEM((steps, per_device, width), particles.dtype)
    if first:
        shapes = [jax.ShapeDtypeStruct((total // 32, per_device), jnp.int32)] + sums
        shapes += turned + [raw]
        rest_specs = [in_vmem()]
        scratch = [
            pltpu.VMEM((2 * steps, per_device, width), particles.dtype),
            pltpu.SemaphoreType.DMA((2 * steps,)),
            pltpu.SemaphoreType.DMA((steps,)),
        ]
    elif last:
        rows = STATE_ROWS + rest[2].shape[0]
        shapes = [jax.ShapeDtypeStruct((rows, per_device), jnp.float32)] + turned
        rest_specs = [in_vmem(), in_vmem(), in_smem(), in_vmem(), in_vmem(), in_vmem()]
        scratch = [pltpu.VMEM(array.shape, array.dtype) for array in sums]
    else:
        shapes = sums + turned + [raw]
        rest_specs = [in_vmem()] * 3
        scratch = [pltpu.SemaphoreType.DMA((steps,))]
    if not first:
        rest = (*rest[:-1], pltpu.with_memory_space_constraint(rest[-1], pltpu.VMEM))
    return pl.pallas_call(
        functools.partial(own_kernel, quarters),
        in_specs=[in_smem(), in_vmem(), in_vmem(), pl.BlockSpec(memory_space=pl.ANY)] + rest_specs,
        out_specs=[in_vmem()] * len(shapes),
        out_shape=shapes,
        scratch_shapes=scratch,
        compiler_params=pltpu.CompilerParams(vmem_limit_bytes=VMEM_LIMIT if first else SMALL_LIMIT),
        cost_estimate=pl.CostEstimate(
            flops=2 * 128 * per_device * freqs,
            bytes_accessed=per_device * freqs,
            transcendentals=0,
        ),
    )(where, noise, templates, pltpu.with_memory_space_constraint(particles, pltpu.HBM), *rest)


def near_copies(part, far_ref, near, arrived):
    blocks, _, width = near.shape
    return [
        pltpu.make_async_copy(
            far_ref.at[:, pl.ds((part * blocks + block) * width, width)],
            near.at[block],
            arrived.at[block],
        )
        for block in range(blocks)
    ]


def class_sums(state, core, nears, copies, loglik_ref, mine_ref, theirs_ref):
    top, total, _, weights = state
    loglik_ref[...] = top + jnp.log(total)
    per_owner = mine_ref.shape[1]
    blocks, _, width = nears[0].shape
    weights = weights / jnp.sum(weights, axis=0, keepdims=True)
    turned = jnp.concatenate([weights[per_owner:], weights[:per_owner]], axis=0)
    weights = jnp.where(core == 0, weights, turned)
    rounded = weights.astype(jnp.bfloat16)
    totals = jnp.broadcast_to(
        jnp.sum(weights, axis=1, keepdims=True), (weights.shape[0], LANES)
    )
    for part, near in enumerate(nears):
        if part == len(nears) - 1:
            for copy in copies:
                copy.wait()

        @pl.loop(0, blocks)
        def _(inner):
            block = part * blocks + inner
            sums = jnp.dot(rounded, near[inner], preferred_element_type=jnp.float32)
            mine_ref[block, :, :width] = sums[:per_owner]
            theirs_ref[block, :, :width] = sums[per_owner:]
            mine_ref[block, :, width:] = totals[:per_owner]
            theirs_ref[block, :, width:] = totals[per_owner:]


def ring_kernel(phase, ends, part, sources, where_ref, noise_ref, low_ref, high_ref, *rest):
    row_refs, rest = rest[: 2 * len(sources)], rest[2 * len(sources) :]
    far_ref = near = copies = None
    if part is not None:
        far_ref, *rest = rest
    if phase == 0:
        acc, energy, *rest = rest
    else:
        acc_in, energy_in, logs_ref, words_ref, state_ref, *rest = rest
        if ends:
            *nears, loglik_ref, mine_ref, theirs_ref, acc, energy = rest[:8]
            rest = rest[8:]
        else:
            out_ref, *rest = rest
            if part is not None:
                near, acc, energy, arrived = rest
            else:
                acc, energy = rest
    if part is not None:
        if phase == 0 or ends:
            near, arrived = rest
        copies = near_copies(part, far_ref, near, arrived)
        for copy in copies:
            copy.start()
    if phase == 0:
        acc[...] = jnp.zeros_like(acc)
        energy[...] = jnp.zeros_like(energy)
    else:
        acc[...] = acc_in[...]
        energy[...] = energy_in[...]
    quarter = low_ref.shape[0]
    core = where_ref[1]

    def add(refs, part_ref, at, step, start):
        here = pl.ds(pl.multiple_of(start + step * WIDTH, WIDTH), WIDTH)
        there = pl.ds(pl.multiple_of(step * WIDTH, WIDTH), WIDTH)
        columns = pl.ds((2 * phase + at) * quarter + step * WIDTH, WIDTH)
        rows = jnp.concatenate([ref[:, here] for ref in refs], axis=0)
        weighted = weigh(rows, noise_ref[:, columns], energy)
        acc[...] += jnp.dot(weighted, part_ref[there, :], preferred_element_type=jnp.float32)

    for at, part_ref in enumerate((low_ref, high_ref)):
        for step in range(quarter // WIDTH):
            if ends:
                for own, ref in ((True, row_refs[0]), (False, row_refs[1])):
                    pl.when((core == at) == own)(
                        functools.partial(add, [ref], part_ref, at, step, 0)
                    )
            else:
                add(row_refs, part_ref, at, step, at * quarter)

    if part is not None and not (ends and phase == 1):
        for copy in copies:
            copy.wait()
    if phase == 0:
        return
    height = row_refs[0].shape[0]
    span = quarter if ends else 2 * quarter
    tags = [ref[:, span:].astype(jnp.float32) for ref in row_refs]
    tags = jnp.where(core == 0, tags[1], tags[0]) if ends else jnp.concatenate(tags, axis=0)
    found = []
    for tables in sources:
        for table in tables:
            source = jnp.int32(table[0])
            for block in range(1, len(table)):
                source = jnp.where(where_ref[0] == block, table[block], source)
            found.append(source)
    if ends:
        found = found[:1]
    else:
        for at in range(0, len(found), 2):
            front, back = found[at : at + 2]
            found[at] = jnp.where(core == 0, front, back)
            found[at + 1] = jnp.where(core == 0, back, front)
    hit = jnp.concatenate([picked_rows(words_ref, source, height) for source in found], axis=0)
    state = add_rows(tags, hit, logs_ref, get_state(state_ref), acc, energy)
    if ends:
        class_sums(state, core, [*nears, near], copies, loglik_ref, mine_ref, theirs_ref)
    else:
        put_state(state, out_ref)


def ring_scores(phase, sources, where, noise, turned, arrays, rest, ends, particles, part, shape):
    quarter, per_device = turned[0].shape
    freqs = 4 * quarter
    rows = arrays[0].shape[0] * (1 if ends else len(arrays))
    sums = [
        jax.ShapeDtypeStruct((rows, per_device), jnp.float32),
        jax.ShapeDtypeStruct((rows, LANES), jnp.float32),
    ]
    scratch = [pltpu.VMEM(array.shape, array.dtype) for array in sums]
    blocks = shape[0] // 4
    raw = (blocks, per_device, freqs // shape[0])
    specs, inputs = [], []
    if part is not None:
        specs = [pl.BlockSpec(memory_space=pl.ANY)]
        inputs = [pltpu.with_memory_space_constraint(particles, pltpu.HBM)]
    if phase == 0:
        shapes, scratch = sums, []
    else:
        specs += [in_vmem(), in_vmem(), in_smem(), in_vmem(), in_vmem()]
        if ends:
            piece = jax.ShapeDtypeStruct(shape, jnp.float32)
            shapes = [jax.ShapeDtypeStruct((1, per_device), jnp.float32), piece, piece]
            specs += [in_vmem()] * 3
            nears = [pltpu.with_memory_space_constraint(x, pltpu.VMEM) for x in rest[5:]]
            rest = (*rest[:5], *nears)
        else:
            shapes = [jax.ShapeDtypeStruct(rest[4].shape, jnp.float32)]
    if part is not None:
        if ends and phase == 1:
            scratch.append(pltpu.VMEM(raw, particles.dtype))
        else:
            shapes.append(pltpu.VMEM(raw, particles.dtype))
        scratch.append(pltpu.SemaphoreType.DMA((blocks,)))
    return pl.pallas_call(
        functools.partial(ring_kernel, phase, ends, part, sources),
        in_specs=[in_smem()] + [in_vmem()] * (3 + len(arrays)) + specs,
        out_specs=[in_vmem()] * len(shapes),
        out_shape=shapes,
        scratch_shapes=scratch,
        compiler_params=pltpu.CompilerParams(vmem_limit_bytes=VMEM_LIMIT if ends else SMALL_LIMIT),
        cost_estimate=pl.CostEstimate(
            flops=2 * 128 * per_device * freqs,
            bytes_accessed=per_device * freqs,
            transcendentals=0,
        ),
    )(
        where,
        noise,
        *(pltpu.with_memory_space_constraint(part, pltpu.VMEM) for part in turned),
        *arrays,
        *inputs,
        *rest,
    )


def scatter_sum(pieces, blocks, block_id):
    tail = pieces.shape[1:]
    stride, left = 1, blocks
    while left > 1:
        radix = 4 if stride > 1 and left % 4 == 0 else 2
        digit = lax.rem(lax.div(block_id, jnp.uint32(stride)), jnp.uint32(radix))
        groups = pieces.reshape((-1, radix) + tail)
        total = lax.dynamic_index_in_dim(groups, digit, 1, keepdims=False)
        for change in range(1, radix):
            there = lax.bitwise_xor(digit, jnp.uint32(change))
            send = lax.dynamic_index_in_dim(groups, there, 1, keepdims=False)
            swaps = [(i, i ^ (change * stride)) for i in range(blocks)]
            total = total + lax.ppermute(send, "blk", swaps)
        pieces = total
        stride, left = stride * radix, left // radix
    return pieces[0]


def body(particles, significant, templates, template_class, class_counts, inv_noise):
    per_device, freqs = particles.shape
    classes = class_counts.shape[0]
    blocks = lax.axis_size("blk")
    owners = lax.axis_size("cls")
    order = ring_order(blocks)
    place = [order.index(block) for block in range(blocks)]
    block_id = lax.axis_index("blk")
    core = lax.axis_index("cls")
    ring = [(2 * order[i], 2 * order[(i + 1) % blocks]) for i in range(blocks)]
    ring += [(2 * order[(i + 1) % blocks] + 1, 2 * order[i] + 1) for i in range(blocks)]
    swap = [(i, owners - 1 - i) for i in range(owners)]

    noise = inv_noise[None, :]
    logs = jnp.log(class_counts.astype(jnp.float32))
    tags = template_class[None, :]
    *held, near_noise, picks = make_messages(tags, noise, significant, templates)
    where = jnp.stack([block_id, core])
    cut = freqs // 4
    where, cut_at = lax.optimization_barrier((where, core.astype(jnp.uint32) * cut))
    own = functools.partial(own_scores, where=where, noise=near_noise, particles=particles)
    total = blocks * templates.shape[0]
    words, *sums, low, high, raw = own([0, 1], templates=held[0], rest=(picks,), total=total)
    turned = [(low, high)]
    gates = [sums]
    *sums, low, raw = own([2], templates=held[1], rest=(*sums, raw))
    gates.append(sums)
    state, high = own([3], templates=held[1], rest=(*sums, logs, tags, words, raw))
    turned.append((low, high))
    gates.append(state)
    width = freqs // blocks
    per_owner = classes // owners
    shape = (blocks, per_owner, width + LANES)
    nears = []
    last = blocks // 2
    for distance in range(1, last + 1):
        ends = distance == last
        tables = [
            [
                tuple(order[(place[block] - sign * distance) % blocks] for block in range(blocks))
                for sign in (1, -1)
            ]
        ]
        arrived = []
        for phase in range(2):
            message = held[phase]
            if ends:
                message = lax.dynamic_slice(
                    message,
                    (jnp.uint32(0), cut_at),
                    (message.shape[0], message.shape[1] - cut),
                )
            own = lax.ppermute(message, ("blk", "cls"), ring)
            lag = 3 if distance == 2 else 2
            gate = phase if distance == 1 else len(gates) - lag
            own, _ = lax.optimization_barrier((own, gates[gate]))
            pair = (own, lax.ppermute(own, "cls", swap))
            arrived.append(own)
            rest = (*sums, logs, words, state) if phase else ()
            if ends and phase:
                rest += tuple(nears)
            part = 2 * (distance - last) + phase + 2
            part = part if part >= 0 else None
            sums = ring_scores(
                phase, tables, where, near_noise, turned[phase], pair, rest,
                ends, particles, part, shape,
            )
            gates.append(sums)
            if part is not None and part < 3:
                *sums, near = sums
                nears.append(near)
        held = arrived
        if not ends:
            (state,) = sums

    loglik, mine, theirs = sums
    reduced = mine + lax.ppermute(theirs, "cls", swap)
    total = scatter_sum(reduced, blocks, block_id.astype(jnp.uint32))
    counts = lax.dynamic_slice_in_dim(class_counts, core * per_owner, per_owner, 0)
    class_avg = total[:, :width] / (total[:, width] + counts.astype(jnp.float32))[:, None]
    return loglik[0], class_avg


def solution(mesh):
    placed = (
        P(("grp", "blk", "cls"), None),
        P(None, ("grp", "blk", "cls")),
        P(("grp", "blk"), None),
        P(("grp", "blk")),
        P("grp"),
        P(),
    )
    return jax.shard_map(
        body,
        mesh=mesh,
        in_specs=placed,
        out_specs=(P(("grp", "blk", "cls")), P(("grp", "cls"), "blk")),
        check_vma=False,
    )
```

```python
import functools

import jax
import jax.numpy as jnp
from jax import lax
from jax.experimental import pallas as pl
from jax.experimental.pallas import tpu as pltpu
from jax.sharding import PartitionSpec as P

LOWEST = -1e30
STEPS = 16
WIDTH = 1024
STRIP = 256
LANES = 128
STATE_ROWS = 8
VMEM_LIMIT = 16 * 1024 * 1024
SMALL_LIMIT = 6 * 1024 * 1024


def ring_order(blocks):
    if blocks <= 8:
        return list(range(0, blocks, 2)) + list(range(blocks - 1, 0, -2))
    return list(range(blocks))


def message_kernel(
    tags_ref, noise_ref, sig_ref, rows_ref,
    first_ref, second_ref, near_noise_ref, near_sig_ref, tags, sent,
):
    height, span = first_ref.shape
    copies = [
        pltpu.make_async_copy(rows_ref.at[:, :span], first_ref, sent.at[0]),
        pltpu.make_async_copy(rows_ref.at[:, span:], second_ref.at[:, :span], sent.at[1]),
        pltpu.make_async_copy(tags_ref, tags, sent.at[2]),
        pltpu.make_async_copy(noise_ref, near_noise_ref, sent.at[3]),
        pltpu.make_async_copy(sig_ref, near_sig_ref, sent.at[4]),
    ]
    for copy in copies:
        copy.start()
    copies[2].wait()
    second_ref[:, span:] = tag_rows(tags, height).astype(jnp.bfloat16)
    for copy in copies[:2] + copies[3:]:
        copy.wait()


def make_messages(tags, noise, significant, templates):
    height, freqs = templates.shape
    span = freqs // 2
    return pl.pallas_call(
        message_kernel,
        in_specs=[pl.BlockSpec(memory_space=pl.ANY)] * 4,
        out_specs=[in_vmem()] * 4,
        out_shape=[
            pltpu.VMEM((height, span), jnp.bfloat16),
            pltpu.VMEM((height, span + LANES), jnp.bfloat16),
            pltpu.VMEM(noise.shape, noise.dtype),
            pltpu.VMEM(significant.shape, significant.dtype),
        ],
        scratch_shapes=[pltpu.VMEM(tags.shape, tags.dtype), pltpu.SemaphoreType.DMA((5,))],
        compiler_params=pltpu.CompilerParams(vmem_limit_bytes=SMALL_LIMIT),
    )(
        *(
            pltpu.with_memory_space_constraint(x, pltpu.HBM)
            for x in (tags, noise, significant, templates)
        )
    )


def tag_rows(tags_ref, height):
    row = lax.broadcasted_iota(jnp.int32, (height, height), 0)
    lane = lax.broadcasted_iota(jnp.int32, (height, height), 1)
    spread = jnp.where(row == lane, tags_ref[...].astype(jnp.float32), 0.0)
    return jnp.broadcast_to(jnp.sum(spread, axis=1, keepdims=True), (height, LANES))


def in_smem():
    return pl.BlockSpec(memory_space=pltpu.SMEM)


def in_vmem():
    return pl.BlockSpec(memory_space=pltpu.VMEM)


def weigh(rows, noise, energy):
    widened = rows.astype(jnp.float32)
    product = widened * noise
    square = product * widened
    folded = square[:, :LANES]
    for lane in range(LANES, square.shape[1], LANES):
        folded = folded + square[:, lane : lane + LANES]
    energy[...] += folded
    return product.astype(jnp.bfloat16)


def pick_words(sig_ref, words_ref):
    word = lax.broadcasted_iota(jnp.int32, words_ref.shape, 0)
    words = jnp.zeros(words_ref.shape, jnp.int32)
    for pick in range(sig_ref.shape[0]):
        chosen = sig_ref[pick : pick + 1, :]
        bit = jnp.left_shift(1, jnp.bitwise_and(chosen, 31))
        words = words | jnp.where(jnp.right_shift(chosen, 5) == word, bit, 0)
    words_ref[...] = words


def picked_rows(words_ref, source, height):
    bit = jnp.left_shift(1, lax.broadcasted_iota(jnp.int32, (32, 1), 0))
    rows = []
    for word in range(height // 32):
        rows.append((words_ref[pl.ds(source * (height // 32) + word, 1), :] & bit) != 0)
    return jnp.concatenate(rows, axis=0)


def add_rows(tags, hit, logs_ref, state, acc, energy):
    classes = logs_ref.shape[0]
    prior = jnp.zeros_like(tags[:, :1])
    for tag in range(classes):
        prior = jnp.where(tags[:, :1] == tag, logs_ref[tag], prior)
    bias = prior - 0.5 * jnp.sum(energy[...], axis=1, keepdims=True)
    scores = acc[...] + bias
    old_max, old_sum, old_top, weights = state
    new_max = jnp.maximum(old_max, jnp.max(scores, axis=0, keepdims=True))
    new_sum = old_sum * jnp.exp(old_max - new_max) + jnp.sum(
        jnp.exp(scores - new_max), axis=0, keepdims=True
    )
    new_top = jnp.maximum(
        old_top, jnp.max(jnp.where(hit, scores, LOWEST), axis=0, keepdims=True)
    )
    value = jnp.where(hit, jnp.exp(scores - new_top), 0.0)
    lane = lax.broadcasted_iota(jnp.int32, tags.shape, 1).astype(jnp.float32)
    onehot = jnp.transpose(jnp.where(tags == lane, 1.0, 0.0))[:classes, :].astype(jnp.bfloat16)
    weights = weights * jnp.exp(old_top - new_top)
    left = value
    for _ in range(3):
        piece = left.astype(jnp.bfloat16)
        left = left - piece.astype(jnp.float32)
        weights = weights + jnp.dot(onehot, piece, preferred_element_type=jnp.float32)
    return new_max, new_sum, new_top, weights


def put_state(state, out_ref):
    new_max, new_sum, new_top, weights = state
    out_ref[0:1, :] = new_max
    out_ref[1:2, :] = new_sum
    out_ref[2:3, :] = new_top
    out_ref[3:STATE_ROWS, :] = jnp.zeros_like(out_ref[3:STATE_ROWS, :])
    out_ref[STATE_ROWS:, :] = weights


def get_state(state_ref):
    return state_ref[0:1, :], state_ref[1:2, :], state_ref[2:3, :], state_ref[STATE_ROWS:, :]


def own_kernel(quarters, where_ref, noise_ref, tmpl_ref, far_ref, *rest):
    first, last = quarters[0] == 0, quarters[-1] == 3
    if first:
        sig_ref, words_ref, acc, energy, *turned_refs, next_ref, near, arrived, late = rest
    elif last:
        acc_in, energy_in, logs_ref, tags_ref, words_ref, near, out_ref, *rest = rest
        *turned_refs, acc, energy = rest
    else:
        acc_in, energy_in, near, acc, energy, *turned_refs, next_ref, late = rest
    span, height = turned_refs[0].shape[0], tmpl_ref.shape[0]
    steps, _, width = near.shape
    low = quarters[0] * span

    def copy(step):
        columns = pl.ds(pl.multiple_of(low + step * width, width), width)
        return pltpu.make_async_copy(far_ref.at[:, columns], near.at[step], arrived.at[step])

    def following(step):
        columns = pl.ds(low + (steps + step) * width, width)
        return pltpu.make_async_copy(far_ref.at[:, columns], next_ref.at[step], late.at[step])

    if first:
        for step in range(steps):
            copy(step).start()
    if not last:
        for step in range(next_ref.shape[0]):
            following(step).start()
    if first:
        pick_words(sig_ref, words_ref)
        acc[...] = jnp.zeros_like(acc)
        energy[...] = jnp.zeros_like(energy)
    else:
        acc[...] = acc_in[...]
        energy[...] = energy_in[...]
    for quarter, turned_ref in zip(quarters, turned_refs):

        @pl.loop(0, span // width)
        def _(inner):
            step = (quarter - quarters[0]) * (span // width) + inner
            if first:
                copy(step).wait()
            for strip in range(0, width, STRIP):
                there = pl.ds(pl.multiple_of(inner * width + strip, STRIP), STRIP)
                part = quarter % 2 * span + inner * width + strip
                here = pl.ds(pl.multiple_of(part, STRIP), STRIP)
                columns = pl.ds(pl.multiple_of(low + step * width + strip, STRIP), STRIP)
                weighted = weigh(tmpl_ref[:, here], noise_ref[:, columns], energy)
                turned = jnp.transpose(near[step, :, strip : strip + STRIP])
                turned_ref[there, :] = turned
                acc[...] += jnp.dot(weighted, turned, preferred_element_type=jnp.float32)

    if not last:
        for step in range(next_ref.shape[0]):
            following(step).wait()
        return
    tags = tag_rows(tags_ref, height)
    hit = picked_rows(words_ref, where_ref[0], height)
    lowest = jnp.full((1, acc.shape[1]), LOWEST, jnp.float32)
    none = jnp.zeros((1, acc.shape[1]), jnp.float32)
    weights = jnp.zeros((logs_ref.shape[0], acc.shape[1]), jnp.float32)
    state = (lowest, none, lowest, weights)
    put_state(add_rows(tags, hit, logs_ref, state, acc, energy), out_ref)


def own_scores(quarters, where, noise, particles, templates, rest, total=0):
    per_device, freqs = particles.shape
    height = templates.shape[0]
    width = freqs // STEPS
    span = freqs // 4
    steps = span // width
    first, last = quarters[0] == 0, quarters[-1] == 3
    sums = [
        jax.ShapeDtypeStruct((height, per_device), jnp.float32),
        jax.ShapeDtypeStruct((height, LANES), jnp.float32),
    ]
    turned = [pltpu.VMEM((span, per_device), particles.dtype)] * len(quarters)
    raw = pltpu.VMEM((steps, per_device, width), particles.dtype)
    if first:
        shapes = [jax.ShapeDtypeStruct((total // 32, per_device), jnp.int32)] + sums
        shapes += turned + [raw]
        rest_specs = [in_vmem()]
        scratch = [
            pltpu.VMEM((2 * steps, per_device, width), particles.dtype),
            pltpu.SemaphoreType.DMA((2 * steps,)),
            pltpu.SemaphoreType.DMA((steps,)),
        ]
    elif last:
        rows = STATE_ROWS + rest[2].shape[0]
        shapes = [jax.ShapeDtypeStruct((rows, per_device), jnp.float32)] + turned
        rest_specs = [in_vmem(), in_vmem(), in_smem(), in_vmem(), in_vmem(), in_vmem()]
        scratch = [pltpu.VMEM(array.shape, array.dtype) for array in sums]
    else:
        shapes = sums + turned + [raw]
        rest_specs = [in_vmem()] * 3
        scratch = [pltpu.SemaphoreType.DMA((steps,))]
    if not first:
        rest = (*rest[:-1], pltpu.with_memory_space_constraint(rest[-1], pltpu.VMEM))
    return pl.pallas_call(
        functools.partial(own_kernel, quarters),
        in_specs=[in_smem(), in_vmem(), in_vmem(), pl.BlockSpec(memory_space=pl.ANY)] + rest_specs,
        out_specs=[in_vmem()] * len(shapes),
        out_shape=shapes,
        scratch_shapes=scratch,
        compiler_params=pltpu.CompilerParams(vmem_limit_bytes=VMEM_LIMIT if first else SMALL_LIMIT),
        cost_estimate=pl.CostEstimate(
            flops=2 * 128 * per_device * freqs,
            bytes_accessed=per_device * freqs,
            transcendentals=0,
        ),
    )(where, noise, templates, pltpu.with_memory_space_constraint(particles, pltpu.HBM), *rest)


def near_copy(block, far_ref, near, arrived):
    width = near.shape[1]
    return pltpu.make_async_copy(far_ref.at[:, pl.ds(block * width, width)], near, arrived)


def swapped_bits(block, core):
    low, next_low = lax.rem(block, 2), lax.rem(lax.div(block, 2), 2)
    return block + jnp.where(core == 1, next_low - low, 0) + 2 * jnp.where(core == 1, low - next_low, 0)


def class_sums(state, core, nears, last_copy, loglik_ref, mine_ref, theirs_ref):
    top, total, _, weights = state
    loglik_ref[...] = top + jnp.log(total)
    per_owner = mine_ref.shape[1]
    width = nears[0].shape[1]
    weights = weights / jnp.sum(weights, axis=0, keepdims=True)
    turned = jnp.concatenate([weights[per_owner:], weights[:per_owner]], axis=0)
    weights = jnp.where(core == 0, weights, turned)
    rounded = weights.astype(jnp.bfloat16)
    totals = jnp.broadcast_to(
        jnp.sum(weights, axis=1, keepdims=True), (weights.shape[0], LANES)
    )
    for block, near in enumerate(nears):
        if block == len(nears) - 1:
            last_copy.wait()
        sums = jnp.dot(rounded, near[...], preferred_element_type=jnp.float32)
        for ref, rows, owner in ((mine_ref, slice(0, per_owner), core),
                                 (theirs_ref, slice(per_owner, None), 1 - core)):
            at = swapped_bits(jnp.int32(block), owner)
            ref[at, :, :width] = sums[rows]
            ref[at, :, width:] = totals[rows]


def ring_kernel(phase, ends, block, sources, where_ref, noise_ref, low_ref, high_ref, *rest):
    row_refs, rest = rest[: 2 * len(sources)], rest[2 * len(sources) :]
    far_ref, *rest = rest
    if phase == 0:
        acc, energy, near, arrived = rest
    else:
        acc_in, energy_in, logs_ref, words_ref, state_ref, *rest = rest
        if ends:
            *nears, loglik_ref, mine_ref, theirs_ref, acc, energy, near, arrived = rest
        else:
            out_ref, near, acc, energy, arrived = rest
    copy = near_copy(block, far_ref, near, arrived)
    copy.start()
    if phase == 0:
        acc[...] = jnp.zeros_like(acc)
        energy[...] = jnp.zeros_like(energy)
    else:
        acc[...] = acc_in[...]
        energy[...] = energy_in[...]
    quarter = low_ref.shape[0]
    core = where_ref[1]

    for at, part_ref in enumerate((low_ref, high_ref)):
        for step in range(quarter // WIDTH):
            there = pl.ds(step * WIDTH, WIDTH)
            columns = pl.ds((2 * phase + at) * quarter + step * WIDTH, WIDTH)
            if ends:
                rows = jnp.where(core == at, row_refs[0][:, there], row_refs[1][:, there])
            else:
                here = pl.ds(at * quarter + step * WIDTH, WIDTH)
                rows = jnp.concatenate([ref[:, here] for ref in row_refs], axis=0)
            weighted = weigh(rows, noise_ref[:, columns], energy)
            acc[...] += jnp.dot(weighted, part_ref[there, :], preferred_element_type=jnp.float32)

    if not (ends and phase == 1):
        copy.wait()
    if phase == 0:
        return
    height = row_refs[0].shape[0]
    span = quarter if ends else 2 * quarter
    tags = [ref[:, span:].astype(jnp.float32) for ref in row_refs]
    tags = jnp.where(core == 0, tags[1], tags[0]) if ends else jnp.concatenate(tags, axis=0)
    found = []
    for tables in sources:
        for table in tables:
            source = jnp.int32(table[0])
            for block in range(1, len(table)):
                source = jnp.where(where_ref[0] == block, table[block], source)
            found.append(source)
    if ends:
        found = found[:1]
    else:
        for at in range(0, len(found), 2):
            front, back = found[at : at + 2]
            found[at] = jnp.where(core == 0, front, back)
            found[at + 1] = jnp.where(core == 0, back, front)
    hit = jnp.concatenate([picked_rows(words_ref, source, height) for source in found], axis=0)
    state = add_rows(tags, hit, logs_ref, get_state(state_ref), acc, energy)
    if ends:
        class_sums(state, core, [*nears, near], copy, loglik_ref, mine_ref, theirs_ref)
    else:
        put_state(state, out_ref)


def ring_scores(phase, sources, where, noise, turned, arrays, rest, ends, particles, block, shape):
    quarter, per_device = turned[0].shape
    freqs = 4 * quarter
    rows = arrays[0].shape[0] * (1 if ends else len(arrays))
    sums = [
        jax.ShapeDtypeStruct((rows, per_device), jnp.float32),
        jax.ShapeDtypeStruct((rows, LANES), jnp.float32),
    ]
    scratch = [pltpu.VMEM(array.shape, array.dtype) for array in sums]
    raw = pltpu.VMEM((per_device, freqs // shape[0]), particles.dtype)
    specs = [pl.BlockSpec(memory_space=pl.ANY)]
    if phase == 0:
        shapes, scratch = sums + [raw], []
    else:
        specs += [in_vmem(), in_vmem(), in_smem(), in_vmem(), in_vmem()]
        if ends:
            piece = jax.ShapeDtypeStruct(shape, jnp.float32)
            shapes = [jax.ShapeDtypeStruct((1, per_device), jnp.float32), piece, piece]
            nears = [pltpu.with_memory_space_constraint(x, pltpu.VMEM) for x in rest[5:]]
            specs += [in_vmem()] * len(nears)
            rest = (*rest[:5], *nears)
            scratch.append(raw)
        else:
            shapes = [jax.ShapeDtypeStruct(rest[4].shape, jnp.float32), raw]
    scratch.append(pltpu.SemaphoreType.DMA)
    return pl.pallas_call(
        functools.partial(ring_kernel, phase, ends, block, sources),
        in_specs=[in_smem()] + [in_vmem()] * (3 + len(arrays)) + specs,
        out_specs=[in_vmem()] * len(shapes),
        out_shape=shapes,
        scratch_shapes=scratch,
        compiler_params=pltpu.CompilerParams(vmem_limit_bytes=SMALL_LIMIT),
        cost_estimate=pl.CostEstimate(
            flops=2 * 128 * per_device * freqs,
            bytes_accessed=per_device * freqs,
            transcendentals=0,
        ),
    )(
        where,
        noise,
        *(pltpu.with_memory_space_constraint(part, pltpu.VMEM) for part in turned),
        *arrays,
        pltpu.with_memory_space_constraint(particles, pltpu.HBM),
        *rest,
    )


def scatter_sum(pieces, blocks, block_id, core):
    tail = pieces.shape[1:]
    place = swapped_bits(block_id, core)
    for step in range(blocks.bit_length() - 1):
        bit = lax.rem(lax.div(place, 1 << step), 2)
        pairs = pieces.reshape((-1, 2) + tail)
        keep = lax.dynamic_index_in_dim(pairs, bit, 1, keepdims=False)
        send = lax.dynamic_index_in_dim(pairs, 1 - bit, 1, keepdims=False)
        swaps = []
        for block in range(blocks):
            for owner in range(2):
                change = (2, 1)[step] if owner == 1 and step < 2 else 1 << step
                swaps.append((2 * block + owner, 2 * (block ^ change) + owner))
        pieces = keep + lax.ppermute(send, ("blk", "cls"), swaps)
    return pieces[0]


def body(particles, significant, templates, template_class, class_counts, inv_noise):
    per_device, freqs = particles.shape
    classes = class_counts.shape[0]
    blocks = lax.axis_size("blk")
    owners = lax.axis_size("cls")
    order = ring_order(blocks)
    place = [order.index(block) for block in range(blocks)]
    block_id = lax.axis_index("blk")
    core = lax.axis_index("cls")
    ring = [(2 * order[i], 2 * order[(i + 1) % blocks]) for i in range(blocks)]
    ring += [(2 * order[(i + 1) % blocks] + 1, 2 * order[i] + 1) for i in range(blocks)]
    swap = [(i, owners - 1 - i) for i in range(owners)]

    noise = inv_noise[None, :]
    logs = jnp.log(class_counts.astype(jnp.float32))
    tags = template_class[None, :]
    *held, near_noise, picks = make_messages(tags, noise, significant, templates)
    where = jnp.stack([block_id, core])
    cut = freqs // 4
    where, cut_at = lax.optimization_barrier((where, core.astype(jnp.uint32) * cut))
    own = functools.partial(own_scores, where=where, noise=near_noise, particles=particles)
    total = blocks * templates.shape[0]
    words, *sums, low, high, raw = own([0, 1], templates=held[0], rest=(picks,), total=total)
    turned = [(low, high)]
    gates = [sums]
    *sums, low, raw = own([2], templates=held[1], rest=(*sums, raw))
    gates.append(sums)
    state, high = own([3], templates=held[1], rest=(*sums, logs, tags, words, raw))
    turned.append((low, high))
    gates.append(state)
    width = freqs // blocks
    per_owner = classes // owners
    shape = (blocks, per_owner, width + LANES)
    nears = []
    last = blocks // 2
    for distance in range(1, last + 1):
        ends = distance == last
        tables = [
            [
                tuple(order[(place[block] - sign * distance) % blocks] for block in range(blocks))
                for sign in (1, -1)
            ]
        ]
        arrived = []
        for phase in range(2):
            message = held[phase]
            if ends:
                message = lax.dynamic_slice(
                    message,
                    (jnp.uint32(0), cut_at),
                    (message.shape[0], message.shape[1] - cut),
                )
            own = lax.ppermute(message, ("blk", "cls"), ring)
            lag = 3 if distance == 2 else 2
            gate = phase if distance == 1 else len(gates) - lag
            own, _ = lax.optimization_barrier((own, gates[gate]))
            pair = (own, lax.ppermute(own, "cls", swap))
            arrived.append(own)
            rest = (*sums, logs, words, state) if phase else ()
            if ends and phase:
                rest += tuple(nears)
            *sums, near = ring_scores(
                phase, tables, where, near_noise, turned[phase], pair, rest,
                ends, particles, len(nears), shape,
            )
            gates.append(sums)
            nears.append(near)
        held = arrived
        if not ends:
            (state,) = sums

    loglik, mine, theirs = (*sums, near)
    reduced = mine + lax.ppermute(theirs, "cls", swap)
    total = scatter_sum(reduced, blocks, block_id, core)
    counts = lax.dynamic_slice_in_dim(class_counts, core * per_owner, per_owner, 0)
    class_avg = total[:, :width] / (total[:, width] + counts.astype(jnp.float32))[:, None]
    return loglik[0], class_avg


def solution(mesh):
    placed = (
        P(("grp", "blk", "cls"), None),
        P(None, ("grp", "blk", "cls")),
        P(("grp", "blk"), None),
        P(("grp", "blk")),
        P("grp"),
        P(),
    )
    return jax.shard_map(
        body,
        mesh=mesh,
        in_specs=placed,
        out_specs=(P(("grp", "blk", "cls")), P(("grp", "cls"), "blk")),
        check_vma=False,
    )
```

```python
import functools

import jax
import jax.numpy as jnp
from jax import lax
from jax.experimental import pallas as pl
from jax.experimental.pallas import tpu as pltpu
from jax.sharding import PartitionSpec as P

LOWEST = -1e30
STEPS = 16
WIDTH = 1024
STRIP = 256
LANES = 128
STATE_ROWS = 8
VMEM_LIMIT = 16 * 1024 * 1024
SMALL_LIMIT = 6 * 1024 * 1024


def ring_order(blocks):
    if blocks <= 8:
        return list(range(0, blocks, 2)) + list(range(blocks - 1, 0, -2))
    return list(range(blocks))


def spread_copies(source, target, sent):
    count = sent.shape[0]
    rows = target.shape[0] // count
    return [
        pltpu.make_async_copy(
            source.at[pl.ds(at * rows, rows)], target.at[pl.ds(at * rows, rows)], sent.at[at]
        )
        for at in range(count)
    ]


def message_kernel(
    tags_ref, noise_ref, sig_ref, rows_ref,
    first_ref, second_ref, near_noise_ref, near_sig_ref, tags, sent, spread,
):
    height, span = first_ref.shape
    copies = [
        pltpu.make_async_copy(tags_ref, tags, sent.at[0]),
        pltpu.make_async_copy(noise_ref, near_noise_ref, sent.at[1]),
        pltpu.make_async_copy(sig_ref, near_sig_ref, sent.at[2]),
        *spread_copies(rows_ref.at[:, :span], first_ref, spread.at[0]),
        *spread_copies(rows_ref.at[:, span:], second_ref.at[:, :span], spread.at[1]),
    ]
    for copy in copies:
        copy.start()
    copies[0].wait()
    second_ref[:, span:] = tag_rows(tags, height).astype(jnp.bfloat16)
    for copy in copies[1:]:
        copy.wait()


def make_messages(tags, noise, significant, templates):
    height, freqs = templates.shape
    span = freqs // 2
    return pl.pallas_call(
        message_kernel,
        in_specs=[pl.BlockSpec(memory_space=pl.ANY)] * 4,
        out_specs=[in_vmem()] * 4,
        out_shape=[
            pltpu.VMEM((height, span), jnp.bfloat16),
            pltpu.VMEM((height, span + LANES), jnp.bfloat16),
            pltpu.VMEM(noise.shape, noise.dtype),
            pltpu.VMEM(significant.shape, significant.dtype),
        ],
        scratch_shapes=[
            pltpu.VMEM(tags.shape, tags.dtype),
            pltpu.SemaphoreType.DMA((3,)),
            pltpu.SemaphoreType.DMA((2, 4)),
        ],
        compiler_params=pltpu.CompilerParams(vmem_limit_bytes=SMALL_LIMIT),
    )(
        *(
            pltpu.with_memory_space_constraint(x, pltpu.HBM)
            for x in (tags, noise, significant, templates)
        )
    )


def tag_rows(tags_ref, height):
    row = lax.broadcasted_iota(jnp.int32, (height, height), 0)
    lane = lax.broadcasted_iota(jnp.int32, (height, height), 1)
    spread = jnp.where(row == lane, tags_ref[...].astype(jnp.float32), 0.0)
    return jnp.broadcast_to(jnp.sum(spread, axis=1, keepdims=True), (height, LANES))


def in_smem():
    return pl.BlockSpec(memory_space=pltpu.SMEM)


def in_vmem():
    return pl.BlockSpec(memory_space=pltpu.VMEM)


def weigh(rows, noise, energy):
    widened = rows.astype(jnp.float32)
    product = widened * noise
    square = product * widened
    folded = square[:, :LANES]
    for lane in range(LANES, square.shape[1], LANES):
        folded = folded + square[:, lane : lane + LANES]
    energy[...] += folded
    return product.astype(jnp.bfloat16)


def pick_words(sig_ref, words_ref):
    word = lax.broadcasted_iota(jnp.int32, words_ref.shape, 0)
    words = jnp.zeros(words_ref.shape, jnp.int32)
    for pick in range(sig_ref.shape[0]):
        chosen = sig_ref[pick : pick + 1, :]
        bit = jnp.left_shift(1, jnp.bitwise_and(chosen, 31))
        words = words | jnp.where(jnp.right_shift(chosen, 5) == word, bit, 0)
    words_ref[...] = words


def picked_rows(words_ref, source, height):
    bit = jnp.left_shift(1, lax.broadcasted_iota(jnp.int32, (32, 1), 0))
    rows = []
    for word in range(height // 32):
        rows.append((words_ref[pl.ds(source * (height // 32) + word, 1), :] & bit) != 0)
    return jnp.concatenate(rows, axis=0)


def add_rows(tags, hit, logs_ref, state, acc, energy):
    classes = logs_ref.shape[0]
    prior = jnp.zeros_like(tags[:, :1])
    for tag in range(classes):
        prior = jnp.where(tags[:, :1] == tag, logs_ref[tag], prior)
    bias = prior - 0.5 * jnp.sum(energy[...], axis=1, keepdims=True)
    scores = acc[...] + bias
    old_max, old_sum, old_top, weights = state
    new_max = jnp.maximum(old_max, jnp.max(scores, axis=0, keepdims=True))
    new_sum = old_sum * jnp.exp(old_max - new_max) + jnp.sum(
        jnp.exp(scores - new_max), axis=0, keepdims=True
    )
    new_top = jnp.maximum(
        old_top, jnp.max(jnp.where(hit, scores, LOWEST), axis=0, keepdims=True)
    )
    value = jnp.where(hit, jnp.exp(scores - new_top), 0.0)
    lane = lax.broadcasted_iota(jnp.int32, tags.shape, 1).astype(jnp.float32)
    onehot = jnp.transpose(jnp.where(tags == lane, 1.0, 0.0))[:classes, :].astype(jnp.bfloat16)
    weights = weights * jnp.exp(old_top - new_top)
    left = value
    for _ in range(3):
        piece = left.astype(jnp.bfloat16)
        left = left - piece.astype(jnp.float32)
        weights = weights + jnp.dot(onehot, piece, preferred_element_type=jnp.float32)
    return new_max, new_sum, new_top, weights


def put_state(state, out_ref):
    new_max, new_sum, new_top, weights = state
    out_ref[0:1, :] = new_max
    out_ref[1:2, :] = new_sum
    out_ref[2:3, :] = new_top
    out_ref[3:STATE_ROWS, :] = jnp.zeros_like(out_ref[3:STATE_ROWS, :])
    out_ref[STATE_ROWS:, :] = weights


def get_state(state_ref):
    return state_ref[0:1, :], state_ref[1:2, :], state_ref[2:3, :], state_ref[STATE_ROWS:, :]


def own_kernel(quarters, where_ref, noise_ref, tmpl_ref, far_ref, *rest):
    first, last = quarters[0] == 0, quarters[-1] == 3
    if first:
        sig_ref, words_ref, acc, energy, *turned_refs, next_ref, near, arrived, late = rest
    elif last:
        acc_in, energy_in, logs_ref, tags_ref, words_ref, near, out_ref, *rest = rest
        *turned_refs, acc, energy = rest
    else:
        acc_in, energy_in, near, acc, energy, *turned_refs, next_ref, late = rest
    span, height = turned_refs[0].shape[0], tmpl_ref.shape[0]
    steps, _, width = near.shape
    low = quarters[0] * span

    def copies(step):
        columns = pl.ds(pl.multiple_of(low + step * width, width), width)
        return spread_copies(far_ref.at[:, columns], near.at[step], arrived.at[step])

    def following(step):
        columns = pl.ds(low + (steps + step) * width, width)
        return spread_copies(far_ref.at[:, columns], next_ref.at[step], late.at[step])

    if first:
        for step in range(steps):
            for copy in copies(step):
                copy.start()
    if not last:
        for step in range(next_ref.shape[0]):
            for copy in following(step):
                copy.start()
    if first:
        pick_words(sig_ref, words_ref)
        acc[...] = jnp.zeros_like(acc)
        energy[...] = jnp.zeros_like(energy)
    else:
        acc[...] = acc_in[...]
        energy[...] = energy_in[...]
    for quarter, turned_ref in zip(quarters, turned_refs):

        @pl.loop(0, span // width)
        def _(inner):
            step = (quarter - quarters[0]) * (span // width) + inner
            if first:
                for copy in copies(step):
                    copy.wait()
            for strip in range(0, width, STRIP):
                there = pl.ds(pl.multiple_of(inner * width + strip, STRIP), STRIP)
                part = quarter % 2 * span + inner * width + strip
                here = pl.ds(pl.multiple_of(part, STRIP), STRIP)
                columns = pl.ds(pl.multiple_of(low + step * width + strip, STRIP), STRIP)
                weighted = weigh(tmpl_ref[:, here], noise_ref[:, columns], energy)
                turned = jnp.transpose(near[step, :, strip : strip + STRIP])
                turned_ref[there, :] = turned
                acc[...] += jnp.dot(weighted, turned, preferred_element_type=jnp.float32)

    if not last:
        for step in range(next_ref.shape[0]):
            for copy in following(step):
                copy.wait()
        return
    tags = tag_rows(tags_ref, height)
    hit = picked_rows(words_ref, where_ref[0], height)
    lowest = jnp.full((1, acc.shape[1]), LOWEST, jnp.float32)
    none = jnp.zeros((1, acc.shape[1]), jnp.float32)
    weights = jnp.zeros((logs_ref.shape[0], acc.shape[1]), jnp.float32)
    state = (lowest, none, lowest, weights)
    put_state(add_rows(tags, hit, logs_ref, state, acc, energy), out_ref)


def own_scores(quarters, where, noise, particles, templates, rest, total=0):
    per_device, freqs = particles.shape
    height = templates.shape[0]
    width = freqs // STEPS
    span = freqs // 4
    steps = span // width
    first, last = quarters[0] == 0, quarters[-1] == 3
    sums = [
        jax.ShapeDtypeStruct((height, per_device), jnp.float32),
        jax.ShapeDtypeStruct((height, LANES), jnp.float32),
    ]
    turned = [pltpu.VMEM((span, per_device), particles.dtype)] * len(quarters)
    raw = pltpu.VMEM((steps, per_device, width), particles.dtype)
    if first:
        shapes = [jax.ShapeDtypeStruct((total // 32, per_device), jnp.int32)] + sums
        shapes += turned + [raw]
        rest_specs = [in_vmem()]
        scratch = [
            pltpu.VMEM((2 * steps, per_device, width), particles.dtype),
            pltpu.SemaphoreType.DMA((2 * steps, 4)),
            pltpu.SemaphoreType.DMA((steps, 4)),
        ]
    elif last:
        rows = STATE_ROWS + rest[2].shape[0]
        shapes = [jax.ShapeDtypeStruct((rows, per_device), jnp.float32)] + turned
        rest_specs = [in_vmem(), in_vmem(), in_smem(), in_vmem(), in_vmem(), in_vmem()]
        scratch = [pltpu.VMEM(array.shape, array.dtype) for array in sums]
    else:
        shapes = sums + turned + [raw]
        rest_specs = [in_vmem()] * 3
        scratch = [pltpu.SemaphoreType.DMA((steps, 4))]
    if not first:
        rest = (*rest[:-1], pltpu.with_memory_space_constraint(rest[-1], pltpu.VMEM))
    return pl.pallas_call(
        functools.partial(own_kernel, quarters),
        in_specs=[in_smem(), in_vmem(), in_vmem(), pl.BlockSpec(memory_space=pl.ANY)] + rest_specs,
        out_specs=[in_vmem()] * len(shapes),
        out_shape=shapes,
        scratch_shapes=scratch,
        compiler_params=pltpu.CompilerParams(vmem_limit_bytes=VMEM_LIMIT if first else SMALL_LIMIT),
        cost_estimate=pl.CostEstimate(
            flops=2 * 128 * per_device * freqs,
            bytes_accessed=per_device * freqs,
            transcendentals=0,
        ),
    )(where, noise, templates, pltpu.with_memory_space_constraint(particles, pltpu.HBM), *rest)


def class_weights(state, core, per_owner):
    _, _, _, weights = state
    weights = weights / jnp.sum(weights, axis=0, keepdims=True)
    turned = jnp.concatenate([weights[per_owner:], weights[:per_owner]], axis=0)
    weights = jnp.where(core == 0, weights, turned)
    totals = jnp.sum(weights, axis=1, keepdims=True)
    return weights.astype(jnp.bfloat16), jnp.broadcast_to(totals, (weights.shape[0], LANES))


def class_sums(rounded, totals, nears, mine_ref, theirs_ref):
    per_owner = mine_ref.shape[1]
    for block, near in enumerate(nears):
        width = near.shape[1]
        sums = jnp.dot(rounded, near[...], preferred_element_type=jnp.float32)
        mine_ref[block, :, :width] = sums[:per_owner]
        theirs_ref[block, :, :width] = sums[per_owner:]
        mine_ref[block, :, width:] = totals[:per_owner]
        theirs_ref[block, :, width:] = totals[per_owner:]


def rest_kernel(rounded_ref, totals_ref, *rest):
    *nears, mine_ref, theirs_ref = rest
    class_sums(rounded_ref[...], totals_ref[...], nears, mine_ref, theirs_ref)


def rest_sums(rounded, totals, nears, piece):
    per_device, width = nears[0].shape
    return pl.pallas_call(
        rest_kernel,
        in_specs=[in_vmem()] * (2 + len(nears)),
        out_specs=[in_vmem()] * 2,
        out_shape=[piece, piece],
        compiler_params=pltpu.CompilerParams(vmem_limit_bytes=SMALL_LIMIT),
        cost_estimate=pl.CostEstimate(
            flops=2 * 128 * per_device * width * len(nears),
            bytes_accessed=per_device * width * len(nears),
            transcendentals=0,
        ),
    )(rounded, totals, *(pltpu.with_memory_space_constraint(x, pltpu.VMEM) for x in nears))


def ring_kernel(phase, ends, slot, sources, where_ref, noise_ref, low_ref, high_ref, *rest):
    row_refs, rest = rest[: 2 * len(sources)], rest[2 * len(sources) :]
    far_ref, *rest = rest
    if phase == 0:
        acc, energy, near, arrived = rest
    else:
        acc_in, energy_in, logs_ref, words_ref, state_ref, *rest = rest
        if ends:
            *nears, loglik_ref, mine_ref, theirs_ref, rounded_ref, totals_ref = rest[:-4]
            near, acc, energy, arrived = rest[-4:]
        else:
            out_ref, near, acc, energy, arrived = rest
    width = near.shape[1]
    slots = len(sources[0][0])
    bit = lax.rem(where_ref[0], 2)
    block = 2 * (slot % (slots // 2)) + (1 - bit if slot < slots // 2 else bit)
    columns = pl.ds(pl.multiple_of(block * width, width), width)
    copies = spread_copies(far_ref.at[:, columns], near, arrived)
    for copy in copies:
        copy.start()
    if phase == 0:
        acc[...] = jnp.zeros_like(acc)
        energy[...] = jnp.zeros_like(energy)
    else:
        acc[...] = acc_in[...]
        energy[...] = energy_in[...]
    quarter = low_ref.shape[0]
    core = where_ref[1]

    for at, part_ref in enumerate((low_ref, high_ref)):
        for step in range(quarter // WIDTH):
            there = pl.ds(step * WIDTH, WIDTH)
            columns = pl.ds((2 * phase + at) * quarter + step * WIDTH, WIDTH)
            if ends:
                rows = jnp.where(core == at, row_refs[0][:, there], row_refs[1][:, there])
            else:
                here = pl.ds(at * quarter + step * WIDTH, WIDTH)
                rows = jnp.concatenate([ref[:, here] for ref in row_refs], axis=0)
            weighted = weigh(rows, noise_ref[:, columns], energy)
            acc[...] += jnp.dot(weighted, part_ref[there, :], preferred_element_type=jnp.float32)

    if phase == 0:
        for copy in copies:
            copy.wait()
        return
    height = row_refs[0].shape[0]
    span = quarter if ends else 2 * quarter
    tags = [ref[:, span:].astype(jnp.float32) for ref in row_refs]
    tags = jnp.where(core == 0, tags[1], tags[0]) if ends else jnp.concatenate(tags, axis=0)
    found = []
    for tables in sources:
        for table in tables:
            source = jnp.int32(table[0])
            for block in range(1, len(table)):
                source = jnp.where(where_ref[0] == block, table[block], source)
            found.append(source)
    if ends:
        found = found[:1]
    else:
        for at in range(0, len(found), 2):
            front, back = found[at : at + 2]
            found[at] = jnp.where(core == 0, front, back)
            found[at + 1] = jnp.where(core == 0, back, front)
    hit = jnp.concatenate([picked_rows(words_ref, source, height) for source in found], axis=0)
    state = add_rows(tags, hit, logs_ref, get_state(state_ref), acc, energy)
    if ends:
        loglik_ref[...] = state[0] + jnp.log(state[1])
        rounded, totals = class_weights(state, core, mine_ref.shape[1])
        rounded_ref[...] = rounded
        totals_ref[...] = totals
        class_sums(rounded, totals, nears, mine_ref, theirs_ref)
    else:
        put_state(state, out_ref)
    for copy in copies:
        copy.wait()


def ring_scores(phase, sources, where, noise, turned, arrays, rest, ends, particles, slot, piece):
    quarter, per_device = turned[0].shape
    freqs = 4 * quarter
    rows = arrays[0].shape[0] * (1 if ends else len(arrays))
    sums = [
        jax.ShapeDtypeStruct((rows, per_device), jnp.float32),
        jax.ShapeDtypeStruct((rows, LANES), jnp.float32),
    ]
    scratch = [pltpu.VMEM(array.shape, array.dtype) for array in sums]
    raw = pltpu.VMEM((per_device, freqs // len(sources[0][0])), particles.dtype)
    specs = [pl.BlockSpec(memory_space=pl.ANY)]
    if phase == 0:
        shapes, scratch = sums + [raw], []
    else:
        specs += [in_vmem(), in_vmem(), in_smem(), in_vmem(), in_vmem()]
        if ends:
            classes = rest[2].shape[0]
            shapes = [
                jax.ShapeDtypeStruct((1, per_device), jnp.float32),
                piece,
                piece,
                jax.ShapeDtypeStruct((classes, per_device), jnp.bfloat16),
                jax.ShapeDtypeStruct((classes, LANES), jnp.float32),
                raw,
            ]
            nears = [pltpu.with_memory_space_constraint(x, pltpu.VMEM) for x in rest[5:]]
            specs += [in_vmem()] * len(nears)
            rest = (*rest[:5], *nears)
        else:
            shapes = [jax.ShapeDtypeStruct(rest[4].shape, jnp.float32), raw]
    scratch.append(pltpu.SemaphoreType.DMA((8,)))
    return pl.pallas_call(
        functools.partial(ring_kernel, phase, ends, slot, sources),
        in_specs=[in_smem()] + [in_vmem()] * (3 + len(arrays)) + specs,
        out_specs=[in_vmem()] * len(shapes),
        out_shape=shapes,
        scratch_shapes=scratch,
        compiler_params=pltpu.CompilerParams(vmem_limit_bytes=SMALL_LIMIT),
        cost_estimate=pl.CostEstimate(
            flops=2 * 128 * per_device * freqs,
            bytes_accessed=per_device * freqs,
            transcendentals=0,
        ),
    )(
        where,
        noise,
        *(pltpu.with_memory_space_constraint(part, pltpu.VMEM) for part in turned),
        *arrays,
        pltpu.with_memory_space_constraint(particles, pltpu.HBM),
        *rest,
    )


def scatter_sum(pieces, blocks, bits):
    tail = pieces.shape[1:]
    zero = jnp.uint32(0)
    for step, (bit, other) in enumerate(bits):
        pairs = pieces.reshape((-1, 2) + tail)
        size = (pairs.shape[0], 1) + tail
        keep, send = (
            lax.dynamic_slice(pairs, (zero, which, zero, zero), size).reshape((-1,) + tail)
            for which in (bit, other)
        )
        swaps = [(block, block ^ (2 << step)) for block in range(blocks)]
        pieces = keep + lax.ppermute(send, "blk", swaps)
    return pieces[0]


def body(particles, significant, templates, template_class, class_counts, inv_noise):
    per_device, freqs = particles.shape
    classes = class_counts.shape[0]
    blocks = lax.axis_size("blk")
    owners = lax.axis_size("cls")
    order = ring_order(blocks)
    place = [order.index(block) for block in range(blocks)]
    block_id = lax.axis_index("blk")
    core = lax.axis_index("cls")
    ring = [(2 * order[i], 2 * order[(i + 1) % blocks]) for i in range(blocks)]
    ring += [(2 * order[(i + 1) % blocks] + 1, 2 * order[i] + 1) for i in range(blocks)]
    swap = [(i, owners - 1 - i) for i in range(owners)]

    noise = inv_noise[None, :]
    logs = jnp.log(class_counts.astype(jnp.float32))
    tags = template_class[None, :]
    *held, near_noise, picks = make_messages(tags, noise, significant, templates)
    where = jnp.stack([block_id, core])
    cut = freqs // 4
    per_owner = classes // owners
    counts = lax.dynamic_slice_in_dim(class_counts, core * per_owner, per_owner, 0)
    bits = [
        lax.rem(lax.div(block_id, 2 << step), 2) for step in range(blocks.bit_length() - 2)
    ]
    bits = [(bit.astype(jnp.uint32), (1 - bit).astype(jnp.uint32)) for bit in bits]
    cut_at = core.astype(jnp.uint32) * cut
    where, cut_at, bits, counts = lax.optimization_barrier((where, cut_at, bits, counts))
    own = functools.partial(own_scores, where=where, noise=near_noise, particles=particles)
    total = blocks * templates.shape[0]
    words, *sums, low, high, raw = own([0, 1], templates=held[0], rest=(picks,), total=total)
    turned = [(low, high)]
    gates = [sums]
    *sums, low, raw = own([2], templates=held[1], rest=(*sums, raw))
    gates.append(sums)
    state, high = own([3], templates=held[1], rest=(*sums, logs, tags, words, raw))
    turned.append((low, high))
    gates.append(state)
    width = freqs // blocks
    piece = jax.ShapeDtypeStruct((blocks // 2, per_owner, width + LANES), jnp.float32)
    nears = []
    last = blocks // 2
    for distance in range(1, last + 1):
        ends = distance == last
        tables = [
            [
                tuple(order[(place[block] - sign * distance) % blocks] for block in range(blocks))
                for sign in (1, -1)
            ]
        ]
        arrived = []
        for phase in range(2):
            message = held[phase]
            if ends:
                message = lax.dynamic_slice(
                    message,
                    (jnp.uint32(0), cut_at),
                    (message.shape[0], message.shape[1] - cut),
                )
            own = lax.ppermute(message, ("blk", "cls"), ring)
            lag = 3 if distance == 2 else 2
            gate = phase if distance == 1 else len(gates) - lag
            own, _ = lax.optimization_barrier((own, gates[gate]))
            pair = (own, lax.ppermute(own, "cls", swap))
            arrived.append(own)
            rest = (*sums, logs, words, state) if phase else ()
            if ends and phase:
                rest += tuple(nears[: blocks // 2])
            *sums, near = ring_scores(
                phase, tables, where, near_noise, turned[phase], pair, rest,
                ends, particles, len(nears), piece,
            )
            gates.append(sums)
            nears.append(near)
        held = arrived
        if not ends:
            (state,) = sums

    loglik, mine, theirs, rounded, totals = sums
    given = lax.ppermute(theirs, "cls", swap)
    across = lax.ppermute(mine + given, "blk", [(i, i ^ 1) for i in range(blocks)])
    rounded, _ = lax.optimization_barrier((rounded, given))
    mine, theirs = rest_sums(rounded, totals, nears[blocks // 2 :], piece)
    kept = lax.optimization_barrier(mine + across)
    total = scatter_sum(kept + lax.ppermute(theirs, "cls", swap), blocks, bits)
    class_avg = total[:, :width] / (total[:, width] + counts.astype(jnp.float32))[:, None]
    return loglik[0], class_avg


def solution(mesh):
    placed = (
        P(("grp", "blk", "cls"), None),
        P(None, ("grp", "blk", "cls")),
        P(("grp", "blk"), None),
        P(("grp", "blk")),
        P("grp"),
        P(),
    )
    return jax.shard_map(
        body,
        mesh=mesh,
        in_specs=placed,
        out_specs=(P(("grp", "blk", "cls")), P(("grp", "cls"), "blk")),
        check_vma=False,
    )
```

```python
import functools

import jax
import jax.numpy as jnp
from jax import lax
from jax.experimental import pallas as pl
from jax.experimental.pallas import tpu as pltpu
from jax.sharding import PartitionSpec as P

LOWEST = -1e30
STEPS = 16
WIDTH = 1024
STRIP = 256
LANES = 128
STATE_ROWS = 8
VMEM_LIMIT = 6 * 1024 * 1024


def ring_order(blocks):
    if blocks <= 8:
        return list(range(0, blocks, 2)) + list(range(blocks - 1, 0, -2))
    return list(range(blocks))


def spread_copies(source, target, sent):
    count = sent.shape[0]
    rows = target.shape[0] // count
    return [
        pltpu.make_async_copy(
            source.at[pl.ds(at * rows, rows)], target.at[pl.ds(at * rows, rows)], sent.at[at]
        )
        for at in range(count)
    ]


def message_kernel(
    tags_ref, noise_ref, sig_ref, rows_ref,
    first_ref, second_ref, near_noise_ref, near_sig_ref, tags, sent, spread,
):
    height, span = first_ref.shape
    copies = [
        pltpu.make_async_copy(tags_ref, tags, sent.at[0]),
        pltpu.make_async_copy(noise_ref, near_noise_ref, sent.at[1]),
        pltpu.make_async_copy(sig_ref, near_sig_ref, sent.at[2]),
        *spread_copies(rows_ref.at[:, :span], first_ref, spread.at[0]),
        *spread_copies(rows_ref.at[:, span:], second_ref.at[:, :span], spread.at[1]),
    ]
    for copy in copies:
        copy.start()
    copies[0].wait()
    second_ref[:, span:] = tag_rows(tags, height).astype(jnp.bfloat16)
    for copy in copies[1:]:
        copy.wait()


def make_messages(tags, noise, significant, templates):
    height, freqs = templates.shape
    span = freqs // 2
    return pl.pallas_call(
        message_kernel,
        in_specs=[pl.BlockSpec(memory_space=pl.ANY)] * 4,
        out_specs=[in_vmem()] * 4,
        out_shape=[
            pltpu.VMEM((height, span), jnp.bfloat16),
            pltpu.VMEM((height, span + LANES), jnp.bfloat16),
            pltpu.VMEM(noise.shape, noise.dtype),
            pltpu.VMEM(significant.shape, significant.dtype),
        ],
        scratch_shapes=[
            pltpu.VMEM(tags.shape, tags.dtype),
            pltpu.SemaphoreType.DMA((3,)),
            pltpu.SemaphoreType.DMA((2, 4)),
        ],
        compiler_params=pltpu.CompilerParams(vmem_limit_bytes=VMEM_LIMIT),
    )(
        *(
            pltpu.with_memory_space_constraint(x, pltpu.HBM)
            for x in (tags, noise, significant, templates)
        )
    )


def tag_rows(tags_ref, height):
    row = lax.broadcasted_iota(jnp.int32, (height, height), 0)
    lane = lax.broadcasted_iota(jnp.int32, (height, height), 1)
    spread = jnp.where(row == lane, tags_ref[...].astype(jnp.float32), 0.0)
    return jnp.broadcast_to(jnp.sum(spread, axis=1, keepdims=True), (height, LANES))


def in_smem():
    return pl.BlockSpec(memory_space=pltpu.SMEM)


def in_vmem():
    return pl.BlockSpec(memory_space=pltpu.VMEM)


def weigh(rows, noise, energy):
    widened = rows.astype(jnp.float32)
    product = widened * noise
    square = product * widened
    folded = square[:, :LANES]
    for lane in range(LANES, square.shape[1], LANES):
        folded = folded + square[:, lane : lane + LANES]
    energy[...] += folded
    return product.astype(jnp.bfloat16)


def pick_words(sig_ref, words_ref):
    word = lax.broadcasted_iota(jnp.int32, words_ref.shape, 0)
    words = jnp.zeros(words_ref.shape, jnp.int32)
    for pick in range(sig_ref.shape[0]):
        chosen = sig_ref[pick : pick + 1, :]
        bit = jnp.left_shift(1, jnp.bitwise_and(chosen, 31))
        words = words | jnp.where(jnp.right_shift(chosen, 5) == word, bit, 0)
    words_ref[...] = words


def picked_rows(words_ref, source, height):
    bit = jnp.left_shift(1, lax.broadcasted_iota(jnp.int32, (32, 1), 0))
    rows = []
    for word in range(height // 32):
        rows.append((words_ref[pl.ds(source * (height // 32) + word, 1), :] & bit) != 0)
    return jnp.concatenate(rows, axis=0)


def add_rows(tags, hit, logs_ref, state, acc, energy):
    classes = logs_ref.shape[0]
    prior = jnp.zeros_like(tags[:, :1])
    for tag in range(classes):
        prior = jnp.where(tags[:, :1] == tag, logs_ref[tag], prior)
    bias = prior - 0.5 * jnp.sum(energy[...], axis=1, keepdims=True)
    scores = acc[...] + bias
    old_max, old_sum, old_top, weights = state
    new_max = jnp.maximum(old_max, jnp.max(scores, axis=0, keepdims=True))
    new_sum = old_sum * jnp.exp(old_max - new_max) + jnp.sum(
        jnp.exp(scores - new_max), axis=0, keepdims=True
    )
    new_top = jnp.maximum(
        old_top, jnp.max(jnp.where(hit, scores, LOWEST), axis=0, keepdims=True)
    )
    value = jnp.where(hit, jnp.exp(scores - new_top), 0.0)
    lane = lax.broadcasted_iota(jnp.int32, tags.shape, 1).astype(jnp.float32)
    onehot = jnp.transpose(jnp.where(tags == lane, 1.0, 0.0))[:classes, :].astype(jnp.bfloat16)
    weights = weights * jnp.exp(old_top - new_top)
    left = value
    for _ in range(3):
        piece = left.astype(jnp.bfloat16)
        left = left - piece.astype(jnp.float32)
        weights = weights + jnp.dot(onehot, piece, preferred_element_type=jnp.float32)
    return new_max, new_sum, new_top, weights


def put_state(state, out_ref):
    new_max, new_sum, new_top, weights = state
    out_ref[0:1, :] = new_max
    out_ref[1:2, :] = new_sum
    out_ref[2:3, :] = new_top
    out_ref[3:STATE_ROWS, :] = jnp.zeros_like(out_ref[3:STATE_ROWS, :])
    out_ref[STATE_ROWS:, :] = weights


def get_state(state_ref):
    return state_ref[0:1, :], state_ref[1:2, :], state_ref[2:3, :], state_ref[STATE_ROWS:, :]


def own_kernel(quarters, where_ref, noise_ref, tmpl_ref, far_ref, *rest):
    first, last = quarters[0] == 0, quarters[-1] == 3
    if first:
        sig_ref, words_ref, acc, energy, *turned_refs, near, next_ref, arrived, late = rest
    elif last:
        acc_in, energy_in, logs_ref, tags_ref, words_ref, near, out_ref, *rest = rest
        *turned_refs, acc, energy = rest
    else:
        acc_in, energy_in, near, acc, energy, *turned_refs, next_ref, late = rest
    span, height = turned_refs[0].shape[0], tmpl_ref.shape[0]
    steps, _, width = near.shape
    low = quarters[0] * span

    def copies(step):
        columns = pl.ds(pl.multiple_of(low + step * width, width), width)
        return spread_copies(far_ref.at[:, columns], near.at[step], arrived.at[step])

    def following(step):
        columns = pl.ds(low + (steps + step) * width, width)
        return spread_copies(far_ref.at[:, columns], next_ref.at[step], late.at[step])

    if first:
        for step in range(steps):
            for copy in copies(step):
                copy.start()
    if not last:
        for step in range(next_ref.shape[0]):
            for copy in following(step):
                copy.start()
    if first:
        pick_words(sig_ref, words_ref)
        acc[...] = jnp.zeros_like(acc)
        energy[...] = jnp.zeros_like(energy)
    else:
        acc[...] = acc_in[...]
        energy[...] = energy_in[...]
    for quarter, turned_ref in zip(quarters, turned_refs):

        @pl.loop(0, span // width)
        def _(inner):
            step = (quarter - quarters[0]) * (span // width) + inner
            if first:
                for copy in copies(step):
                    copy.wait()
            for strip in range(0, width, STRIP):
                there = pl.ds(pl.multiple_of(inner * width + strip, STRIP), STRIP)
                part = quarter % 2 * span + inner * width + strip
                here = pl.ds(pl.multiple_of(part, STRIP), STRIP)
                columns = pl.ds(pl.multiple_of(low + step * width + strip, STRIP), STRIP)
                weighted = weigh(tmpl_ref[:, here], noise_ref[:, columns], energy)
                turned = jnp.transpose(near[step, :, strip : strip + STRIP])
                turned_ref[there, :] = turned
                acc[...] += jnp.dot(weighted, turned, preferred_element_type=jnp.float32)

    if not last:
        for step in range(next_ref.shape[0]):
            for copy in following(step):
                copy.wait()
        return
    tags = tag_rows(tags_ref, height)
    hit = picked_rows(words_ref, where_ref[0], height)
    lowest = jnp.full((1, acc.shape[1]), LOWEST, jnp.float32)
    none = jnp.zeros((1, acc.shape[1]), jnp.float32)
    weights = jnp.zeros((logs_ref.shape[0], acc.shape[1]), jnp.float32)
    state = (lowest, none, lowest, weights)
    put_state(add_rows(tags, hit, logs_ref, state, acc, energy), out_ref)


def own_scores(quarters, where, noise, particles, templates, rest, total=0):
    per_device, freqs = particles.shape
    height = templates.shape[0]
    width = freqs // STEPS
    span = freqs // 4
    steps = span // width
    first, last = quarters[0] == 0, quarters[-1] == 3
    sums = [
        jax.ShapeDtypeStruct((height, per_device), jnp.float32),
        jax.ShapeDtypeStruct((height, LANES), jnp.float32),
    ]
    turned = [pltpu.VMEM((span, per_device), particles.dtype)] * len(quarters)
    raw = pltpu.VMEM((steps, per_device, width), particles.dtype)
    if first:
        shapes = [jax.ShapeDtypeStruct((total // 32, per_device), jnp.int32)] + sums
        shapes += turned + [pltpu.VMEM((2 * steps, per_device, width), particles.dtype), raw]
        rest_specs = [in_vmem()]
        scratch = [
            pltpu.SemaphoreType.DMA((2 * steps, 4)),
            pltpu.SemaphoreType.DMA((steps, 4)),
        ]
    elif last:
        rows = STATE_ROWS + rest[2].shape[0]
        shapes = [jax.ShapeDtypeStruct((rows, per_device), jnp.float32)] + turned
        rest_specs = [in_vmem(), in_vmem(), in_smem(), in_vmem(), in_vmem(), in_vmem()]
        scratch = [pltpu.VMEM(array.shape, array.dtype) for array in sums]
    else:
        shapes = sums + turned + [raw]
        rest_specs = [in_vmem()] * 3
        scratch = [pltpu.SemaphoreType.DMA((steps, 4))]
    if not first:
        rest = (*rest[:-1], pltpu.with_memory_space_constraint(rest[-1], pltpu.VMEM))
    return pl.pallas_call(
        functools.partial(own_kernel, quarters),
        in_specs=[in_smem(), in_vmem(), in_vmem(), pl.BlockSpec(memory_space=pl.ANY)] + rest_specs,
        out_specs=[in_vmem()] * len(shapes),
        out_shape=shapes,
        scratch_shapes=scratch,
        compiler_params=pltpu.CompilerParams(vmem_limit_bytes=VMEM_LIMIT),
        cost_estimate=pl.CostEstimate(
            flops=2 * 128 * per_device * freqs,
            bytes_accessed=per_device * freqs,
            transcendentals=0,
        ),
    )(where, noise, templates, pltpu.with_memory_space_constraint(particles, pltpu.HBM), *rest)


def class_weights(state, where_ref, counts_ref, per_owner):
    _, _, _, weights = state
    classes = weights.shape[0]
    row = lax.broadcasted_iota(jnp.int32, (classes, LANES), 0)
    counts = jnp.zeros((classes, LANES), jnp.float32)
    for tag in range(classes):
        mine = (where_ref[0] == 0) & (where_ref[1] == tag // per_owner)
        count = jnp.where(mine, counts_ref[tag], 0).astype(jnp.float32)
        counts = jnp.where(row == tag, count, counts)
    weights = weights / jnp.sum(weights, axis=0, keepdims=True)
    totals = jnp.sum(weights, axis=1, keepdims=True) + counts

    def own_first(rows):
        turned = jnp.concatenate([rows[per_owner:], rows[:per_owner]], axis=0)
        return jnp.where(where_ref[1] == 0, rows, turned)

    return own_first(weights).astype(jnp.bfloat16), own_first(totals)


def class_sums(rounded, totals, bit, nears, mine_ref, theirs_ref):
    per_owner = mine_ref.shape[1]
    chunk = nears[0].shape[2]
    share = mine_ref.shape[2] // chunk
    piece = 0
    for near in nears:
        for pair in range(near.shape[0] // (2 * share)):
            for part in range(share):
                at = (2 * pair + bit) * share + part
                sums = jnp.dot(rounded, near[at], preferred_element_type=jnp.float32)
                columns = pl.ds(part * chunk, chunk)
                mine_ref[piece, :, columns] = sums[:per_owner]
                theirs_ref[piece, :, columns] = sums[per_owner:]
            mine_ref[piece, :, share * chunk :] = totals[:per_owner]
            theirs_ref[piece, :, share * chunk :] = totals[per_owner:]
            piece += 1


def rest_kernel(where_ref, rounded_ref, totals_ref, *rest):
    *nears, mine_ref, theirs_ref = rest
    bit = lax.rem(where_ref[0], 2)
    class_sums(rounded_ref[...], totals_ref[...], bit, nears, mine_ref, theirs_ref)


def rest_sums(where, rounded, totals, nears, piece):
    classes, per_device = rounded.shape
    blocks = 2 * piece.shape[0]
    freqs = blocks * (piece.shape[2] - LANES)
    return pl.pallas_call(
        rest_kernel,
        in_specs=[in_smem()] + [in_vmem()] * (2 + len(nears)),
        out_specs=[in_vmem()] * 2,
        out_shape=[piece, piece],
        compiler_params=pltpu.CompilerParams(vmem_limit_bytes=VMEM_LIMIT),
        cost_estimate=pl.CostEstimate(
            flops=128 * per_device * freqs,
            bytes_accessed=per_device * freqs // 2,
            transcendentals=0,
        ),
    )(where, rounded, totals, *(pltpu.with_memory_space_constraint(x, pltpu.VMEM) for x in nears))


def ring_kernel(phase, ends, sources, where_ref, noise_ref, low_ref, high_ref, *rest):
    row_refs, rest = rest[: 2 * len(sources)], rest[2 * len(sources) :]
    if phase == 0:
        acc, energy = rest
    else:
        acc_in, energy_in, logs_ref, words_ref, state_ref, *rest = rest
        if ends:
            counts_ref, *nears, loglik_ref, mine_ref, theirs_ref = rest[:-4]
            rounded_ref, totals_ref, acc, energy = rest[-4:]
        else:
            out_ref, acc, energy = rest
    if phase == 0:
        acc[...] = jnp.zeros_like(acc)
        energy[...] = jnp.zeros_like(energy)
    else:
        acc[...] = acc_in[...]
        energy[...] = energy_in[...]
    quarter = low_ref.shape[0]
    core = where_ref[1]

    for at, part_ref in enumerate((low_ref, high_ref)):
        for step in range(quarter // WIDTH):
            there = pl.ds(step * WIDTH, WIDTH)
            columns = pl.ds((2 * phase + at) * quarter + step * WIDTH, WIDTH)
            if ends:
                rows = jnp.where(core == at, row_refs[0][:, there], row_refs[1][:, there])
            else:
                here = pl.ds(at * quarter + step * WIDTH, WIDTH)
                rows = jnp.concatenate([ref[:, here] for ref in row_refs], axis=0)
            weighted = weigh(rows, noise_ref[:, columns], energy)
            acc[...] += jnp.dot(weighted, part_ref[there, :], preferred_element_type=jnp.float32)

    if phase == 0:
        return
    height = row_refs[0].shape[0]
    span = quarter if ends else 2 * quarter
    tags = [ref[:, span:].astype(jnp.float32) for ref in row_refs]
    tags = jnp.where(core == 0, tags[1], tags[0]) if ends else jnp.concatenate(tags, axis=0)
    found = []
    for tables in sources:
        for table in tables:
            source = jnp.int32(table[0])
            for block in range(1, len(table)):
                source = jnp.where(where_ref[0] == block, table[block], source)
            found.append(source)
    if ends:
        found = found[:1]
    else:
        for at in range(0, len(found), 2):
            front, back = found[at : at + 2]
            found[at] = jnp.where(core == 0, front, back)
            found[at + 1] = jnp.where(core == 0, back, front)
    hit = jnp.concatenate([picked_rows(words_ref, source, height) for source in found], axis=0)
    state = add_rows(tags, hit, logs_ref, get_state(state_ref), acc, energy)
    if ends:
        loglik_ref[...] = state[0] + jnp.log(state[1])
        rounded, totals = class_weights(state, where_ref, counts_ref, mine_ref.shape[1])
        rounded_ref[...] = rounded
        totals_ref[...] = totals
        bit = 1 - lax.rem(where_ref[0], 2)
        class_sums(rounded, totals, bit, nears, mine_ref, theirs_ref)
    else:
        put_state(state, out_ref)


def ring_scores(phase, sources, where, noise, turned, arrays, rest, ends, piece):
    quarter, per_device = turned[0].shape
    freqs = 4 * quarter
    rows = arrays[0].shape[0] * (1 if ends else len(arrays))
    sums = [
        jax.ShapeDtypeStruct((rows, per_device), jnp.float32),
        jax.ShapeDtypeStruct((rows, LANES), jnp.float32),
    ]
    scratch = [pltpu.VMEM(array.shape, array.dtype) for array in sums]
    specs = []
    if phase == 0:
        shapes, scratch = sums, []
    else:
        specs = [in_vmem(), in_vmem(), in_smem(), in_vmem(), in_vmem()]
        if ends:
            classes = rest[2].shape[0]
            shapes = [
                jax.ShapeDtypeStruct((1, per_device), jnp.float32),
                piece,
                piece,
                jax.ShapeDtypeStruct((classes, per_device), jnp.bfloat16),
                jax.ShapeDtypeStruct((classes, LANES), jnp.float32),
            ]
            nears = [pltpu.with_memory_space_constraint(x, pltpu.VMEM) for x in rest[6:]]
            specs += [in_smem()] + [in_vmem()] * len(nears)
            rest = (*rest[:6], *nears)
        else:
            shapes = [jax.ShapeDtypeStruct(rest[4].shape, jnp.float32)]
    return pl.pallas_call(
        functools.partial(ring_kernel, phase, ends, sources),
        in_specs=[in_smem()] + [in_vmem()] * (3 + len(arrays)) + specs,
        out_specs=[in_vmem()] * len(shapes),
        out_shape=shapes,
        scratch_shapes=scratch,
        compiler_params=pltpu.CompilerParams(vmem_limit_bytes=VMEM_LIMIT),
        cost_estimate=pl.CostEstimate(
            flops=2 * 128 * per_device * freqs,
            bytes_accessed=per_device * freqs,
            transcendentals=0,
        ),
    )(
        where,
        noise,
        *(pltpu.with_memory_space_constraint(part, pltpu.VMEM) for part in turned),
        *arrays,
        *rest,
    )


def scatter_sum(pieces, blocks, bits):
    tail = pieces.shape[1:]
    zero = jnp.uint32(0)
    for step, (bit, other) in enumerate(bits):
        pairs = pieces.reshape((-1, 2) + tail)
        size = (pairs.shape[0], 1) + tail
        keep, send = (
            lax.dynamic_slice(pairs, (zero, which, zero, zero), size).reshape((-1,) + tail)
            for which in (bit, other)
        )
        swaps = [(block, block ^ (2 << step)) for block in range(blocks)]
        pieces = keep + lax.ppermute(send, "blk", swaps)
    return pieces[0]


def body(particles, significant, templates, template_class, class_counts, inv_noise):
    per_device, freqs = particles.shape
    classes = class_counts.shape[0]
    blocks = lax.axis_size("blk")
    owners = lax.axis_size("cls")
    order = ring_order(blocks)
    place = [order.index(block) for block in range(blocks)]
    block_id = lax.axis_index("blk")
    core = lax.axis_index("cls")
    ring = [(2 * order[i], 2 * order[(i + 1) % blocks]) for i in range(blocks)]
    ring += [(2 * order[(i + 1) % blocks] + 1, 2 * order[i] + 1) for i in range(blocks)]
    swap = [(i, owners - 1 - i) for i in range(owners)]

    noise = inv_noise[None, :]
    logs = jnp.log(class_counts.astype(jnp.float32))
    tags = template_class[None, :]
    *held, near_noise, picks = make_messages(tags, noise, significant, templates)
    where = jnp.stack([block_id, core])
    cut = freqs // 4
    per_owner = classes // owners
    bits = [
        lax.rem(lax.div(block_id, 2 << step), 2) for step in range(blocks.bit_length() - 2)
    ]
    bits = [(bit.astype(jnp.uint32), (1 - bit).astype(jnp.uint32)) for bit in bits]
    cut_at = core.astype(jnp.uint32) * cut
    where, cut_at, bits = lax.optimization_barrier((where, cut_at, bits))
    own = functools.partial(own_scores, where=where, noise=near_noise, particles=particles)
    total = blocks * templates.shape[0]
    words, *sums, low, high, near, raw = own([0, 1], templates=held[0], rest=(picks,), total=total)
    turned, nears = [(low, high)], [near, raw]
    gates = [sums]
    *sums, low, raw = own([2], templates=held[1], rest=(*sums, raw))
    nears.append(raw)
    gates.append(sums)
    state, high = own([3], templates=held[1], rest=(*sums, logs, tags, words, raw))
    turned.append((low, high))
    gates.append(state)
    width = freqs // blocks
    piece = jax.ShapeDtypeStruct((blocks // 2, per_owner, width + LANES), jnp.float32)
    last = blocks // 2
    for distance in range(1, last + 1):
        ends = distance == last
        tables = [
            [
                tuple(order[(place[block] - sign * distance) % blocks] for block in range(blocks))
                for sign in (1, -1)
            ]
        ]
        arrived = []
        for phase in range(2):
            message = held[phase]
            if ends:
                message = lax.dynamic_slice(
                    message,
                    (jnp.uint32(0), cut_at),
                    (message.shape[0], message.shape[1] - cut),
                )
            own = lax.ppermute(message, ("blk", "cls"), ring)
            lag = 3 if distance == 2 else 2
            gate = phase if distance == 1 else len(gates) - lag
            own, _ = lax.optimization_barrier((own, gates[gate]))
            pair = (own, lax.ppermute(own, "cls", swap))
            arrived.append(own)
            rest = (*sums, logs, words, state) if phase else ()
            if ends and phase:
                rest += (class_counts, *nears)
            sums = ring_scores(
                phase, tables, where, near_noise, turned[phase], pair, rest, ends, piece
            )
            gates.append(sums)
        held = arrived
        if not ends:
            (state,) = sums

    loglik, mine, theirs, rounded, totals = sums
    given = lax.ppermute(theirs, "cls", swap)
    across = lax.ppermute(mine + given, "blk", [(i, i ^ 1) for i in range(blocks)])
    rounded, _ = lax.optimization_barrier((rounded, given))
    mine, theirs = rest_sums(where, rounded, totals, nears, piece)
    kept = lax.optimization_barrier(mine + across)
    total = scatter_sum(kept + lax.ppermute(theirs, "cls", swap), blocks, bits)
    class_avg = total[:, :width] / total[:, width][:, None]
    return loglik[0], class_avg


def solution(mesh):
    placed = (
        P(("grp", "blk", "cls"), None),
        P(None, ("grp", "blk", "cls")),
        P(("grp", "blk"), None),
        P(("grp", "blk")),
        P("grp"),
        P(),
    )
    return jax.shard_map(
        body,
        mesh=mesh,
        in_specs=placed,
        out_specs=(P(("grp", "blk", "cls")), P(("grp", "cls"), "blk")),
        check_vma=False,
    )
```

```python
import functools

import jax
import jax.numpy as jnp
from jax import lax
from jax.experimental import pallas as pl
from jax.experimental.pallas import tpu as pltpu
from jax.sharding import PartitionSpec as P

LOWEST = -1e30
STEPS = 16
WIDTH = 1024
STRIP = 256
LANES = 128
STATE_ROWS = 8
VMEM_LIMIT = 6 * 1024 * 1024


def ring_order(blocks):
    if blocks <= 8:
        return list(range(0, blocks, 2)) + list(range(blocks - 1, 0, -2))
    return list(range(blocks))


def spread_copies(source, target, sent):
    count = sent.shape[0]
    rows = target.shape[0] // count
    return [
        pltpu.make_async_copy(
            source.at[pl.ds(at * rows, rows)], target.at[pl.ds(at * rows, rows)], sent.at[at]
        )
        for at in range(count)
    ]


def message_kernel(
    tags_ref, noise_ref, sig_ref, rows_ref,
    first_ref, second_ref, near_noise_ref, near_sig_ref, tags, sent, spread,
):
    height, span = first_ref.shape
    copies = [
        pltpu.make_async_copy(tags_ref, tags, sent.at[0]),
        pltpu.make_async_copy(noise_ref, near_noise_ref, sent.at[1]),
        pltpu.make_async_copy(sig_ref, near_sig_ref, sent.at[2]),
        *spread_copies(rows_ref.at[:, :span], first_ref, spread.at[0]),
        *spread_copies(rows_ref.at[:, span:], second_ref.at[:, :span], spread.at[1]),
    ]
    for copy in copies:
        copy.start()
    copies[0].wait()
    second_ref[:, span:] = tag_rows(tags, height).astype(jnp.bfloat16)
    for copy in copies[1:]:
        copy.wait()


def make_messages(tags, noise, significant, templates):
    height, freqs = templates.shape
    span = freqs // 2
    return pl.pallas_call(
        message_kernel,
        in_specs=[pl.BlockSpec(memory_space=pl.ANY)] * 4,
        out_specs=[in_vmem()] * 4,
        out_shape=[
            pltpu.VMEM((height, span), jnp.bfloat16),
            pltpu.VMEM((height, span + LANES), jnp.bfloat16),
            pltpu.VMEM(noise.shape, noise.dtype),
            pltpu.VMEM(significant.shape, significant.dtype),
        ],
        scratch_shapes=[
            pltpu.VMEM(tags.shape, tags.dtype),
            pltpu.SemaphoreType.DMA((3,)),
            pltpu.SemaphoreType.DMA((2, 4)),
        ],
        compiler_params=pltpu.CompilerParams(vmem_limit_bytes=VMEM_LIMIT),
    )(
        *(
            pltpu.with_memory_space_constraint(x, pltpu.HBM)
            for x in (tags, noise, significant, templates)
        )
    )


def tag_rows(tags_ref, height):
    row = lax.broadcasted_iota(jnp.int32, (height, height), 0)
    lane = lax.broadcasted_iota(jnp.int32, (height, height), 1)
    spread = jnp.where(row == lane, tags_ref[...].astype(jnp.float32), 0.0)
    return jnp.broadcast_to(jnp.sum(spread, axis=1, keepdims=True), (height, LANES))


def in_smem():
    return pl.BlockSpec(memory_space=pltpu.SMEM)


def in_vmem():
    return pl.BlockSpec(memory_space=pltpu.VMEM)


def weigh(rows, noise, energy):
    widened = rows.astype(jnp.float32)
    product = widened * noise
    square = product * widened
    folded = square[:, :LANES]
    for lane in range(LANES, square.shape[1], LANES):
        folded = folded + square[:, lane : lane + LANES]
    energy[...] += folded
    return product.astype(jnp.bfloat16)


def pick_words(sig_ref, words_ref):
    word = lax.broadcasted_iota(jnp.int32, words_ref.shape, 0)
    words = jnp.zeros(words_ref.shape, jnp.int32)
    for pick in range(sig_ref.shape[0]):
        chosen = sig_ref[pick : pick + 1, :]
        bit = jnp.left_shift(1, jnp.bitwise_and(chosen, 31))
        words = words | jnp.where(jnp.right_shift(chosen, 5) == word, bit, 0)
    words_ref[...] = words


def picked_rows(words_ref, source, height):
    bit = jnp.left_shift(1, lax.broadcasted_iota(jnp.int32, (32, 1), 0))
    rows = []
    for word in range(height // 32):
        rows.append((words_ref[pl.ds(source * (height // 32) + word, 1), :] & bit) != 0)
    return jnp.concatenate(rows, axis=0)


def add_rows(tags, hit, logs_ref, state, acc, energy):
    classes = logs_ref.shape[0]
    prior = jnp.zeros_like(tags[:, :1])
    for tag in range(classes):
        prior = jnp.where(tags[:, :1] == tag, logs_ref[tag], prior)
    bias = prior - 0.5 * jnp.sum(energy[...], axis=1, keepdims=True)
    scores = acc[...] + bias
    old_max, old_sum, old_top, weights = state
    new_max = jnp.maximum(old_max, jnp.max(scores, axis=0, keepdims=True))
    new_sum = old_sum * jnp.exp(old_max - new_max) + jnp.sum(
        jnp.exp(scores - new_max), axis=0, keepdims=True
    )
    new_top = jnp.maximum(
        old_top, jnp.max(jnp.where(hit, scores, LOWEST), axis=0, keepdims=True)
    )
    value = jnp.where(hit, jnp.exp(scores - new_top), 0.0)
    lane = lax.broadcasted_iota(jnp.int32, tags.shape, 1).astype(jnp.float32)
    onehot = jnp.transpose(jnp.where(tags == lane, 1.0, 0.0))[:classes, :].astype(jnp.bfloat16)
    weights = weights * jnp.exp(old_top - new_top)
    left = value
    for _ in range(3):
        piece = left.astype(jnp.bfloat16)
        left = left - piece.astype(jnp.float32)
        weights = weights + jnp.dot(onehot, piece, preferred_element_type=jnp.float32)
    return new_max, new_sum, new_top, weights


def put_state(state, out_ref):
    new_max, new_sum, new_top, weights = state
    out_ref[0:1, :] = new_max
    out_ref[1:2, :] = new_sum
    out_ref[2:3, :] = new_top
    out_ref[3:STATE_ROWS, :] = jnp.zeros_like(out_ref[3:STATE_ROWS, :])
    out_ref[STATE_ROWS:, :] = weights


def get_state(state_ref):
    return state_ref[0:1, :], state_ref[1:2, :], state_ref[2:3, :], state_ref[STATE_ROWS:, :]


def own_kernel(quarters, where_ref, noise_ref, tmpl_ref, far_ref, *rest):
    first, last = quarters[0] == 0, quarters[-1] == 3
    if first:
        sig_ref, words_ref, acc, energy, *turned_refs, near, next_ref, arrived, late = rest
    elif last:
        acc_in, energy_in, logs_ref, tags_ref, words_ref, near, out_ref, *rest = rest
        *turned_refs, acc, energy = rest
    else:
        acc_in, energy_in, near, acc, energy, *turned_refs, next_ref, late = rest
    span, height = turned_refs[0].shape[0], tmpl_ref.shape[0]
    steps, _, width = near.shape
    low = quarters[0] * span

    def copies(step):
        columns = pl.ds(pl.multiple_of(low + step * width, width), width)
        return spread_copies(far_ref.at[:, columns], near.at[step], arrived.at[step])

    def following(step):
        columns = pl.ds(low + (steps + step) * width, width)
        return spread_copies(far_ref.at[:, columns], next_ref.at[step], late.at[step])

    if first:
        for step in range(steps):
            for copy in copies(step):
                copy.start()
    if not last:
        for step in range(next_ref.shape[0]):
            for copy in following(step):
                copy.start()
    if first:
        pick_words(sig_ref, words_ref)
        acc[...] = jnp.zeros_like(acc)
        energy[...] = jnp.zeros_like(energy)
    else:
        acc[...] = acc_in[...]
        energy[...] = energy_in[...]
    for quarter, turned_ref in zip(quarters, turned_refs):

        @pl.loop(0, span // width)
        def _(inner):
            step = (quarter - quarters[0]) * (span // width) + inner
            if first:
                for copy in copies(step):
                    copy.wait()
            for strip in range(0, width, STRIP):
                there = pl.ds(pl.multiple_of(inner * width + strip, STRIP), STRIP)
                part = quarter % 2 * span + inner * width + strip
                here = pl.ds(pl.multiple_of(part, STRIP), STRIP)
                columns = pl.ds(pl.multiple_of(low + step * width + strip, STRIP), STRIP)
                weighted = weigh(tmpl_ref[:, here], noise_ref[:, columns], energy)
                turned = jnp.transpose(near[step, :, strip : strip + STRIP])
                turned_ref[there, :] = turned
                acc[...] += jnp.dot(weighted, turned, preferred_element_type=jnp.float32)

    if not last:
        for step in range(next_ref.shape[0]):
            for copy in following(step):
                copy.wait()
        return
    tags = tag_rows(tags_ref, height)
    hit = picked_rows(words_ref, where_ref[0], height)
    lowest = jnp.full((1, acc.shape[1]), LOWEST, jnp.float32)
    none = jnp.zeros((1, acc.shape[1]), jnp.float32)
    weights = jnp.zeros((logs_ref.shape[0], acc.shape[1]), jnp.float32)
    state = (lowest, none, lowest, weights)
    put_state(add_rows(tags, hit, logs_ref, state, acc, energy), out_ref)


def own_scores(quarters, where, noise, particles, templates, rest, total=0):
    per_device, freqs = particles.shape
    height = templates.shape[0]
    width = freqs // STEPS
    span = freqs // 4
    steps = span // width
    first, last = quarters[0] == 0, quarters[-1] == 3
    sums = [
        jax.ShapeDtypeStruct((height, per_device), jnp.float32),
        jax.ShapeDtypeStruct((height, LANES), jnp.float32),
    ]
    turned = [pltpu.VMEM((span, per_device), particles.dtype)] * len(quarters)
    raw = pltpu.VMEM((steps, per_device, width), particles.dtype)
    if first:
        shapes = [jax.ShapeDtypeStruct((total // 32, per_device), jnp.int32)] + sums
        shapes += turned + [pltpu.VMEM((2 * steps, per_device, width), particles.dtype), raw]
        rest_specs = [in_vmem()]
        scratch = [
            pltpu.SemaphoreType.DMA((2 * steps, 4)),
            pltpu.SemaphoreType.DMA((steps, 4)),
        ]
    elif last:
        rows = STATE_ROWS + rest[2].shape[0]
        shapes = [jax.ShapeDtypeStruct((rows, per_device), jnp.float32)] + turned
        rest_specs = [in_vmem(), in_vmem(), in_smem(), in_vmem(), in_vmem(), in_vmem()]
        scratch = [pltpu.VMEM(array.shape, array.dtype) for array in sums]
    else:
        shapes = sums + turned + [raw]
        rest_specs = [in_vmem()] * 3
        scratch = [pltpu.SemaphoreType.DMA((steps, 4))]
    if not first:
        rest = (*rest[:-1], pltpu.with_memory_space_constraint(rest[-1], pltpu.VMEM))
    return pl.pallas_call(
        functools.partial(own_kernel, quarters),
        in_specs=[in_smem(), in_vmem(), in_vmem(), pl.BlockSpec(memory_space=pl.ANY)] + rest_specs,
        out_specs=[in_vmem()] * len(shapes),
        out_shape=shapes,
        scratch_shapes=scratch,
        compiler_params=pltpu.CompilerParams(vmem_limit_bytes=VMEM_LIMIT),
        cost_estimate=pl.CostEstimate(
            flops=2 * 128 * per_device * freqs,
            bytes_accessed=per_device * freqs,
            transcendentals=0,
        ),
    )(where, noise, templates, pltpu.with_memory_space_constraint(particles, pltpu.HBM), *rest)


def class_weights(state, where_ref, counts_ref):
    _, _, _, weights = state
    classes = weights.shape[0]
    row = lax.broadcasted_iota(jnp.int32, (classes, LANES), 0)
    counts = jnp.zeros((classes, LANES), jnp.float32)
    for tag in range(classes):
        count = jnp.where((where_ref[0] == 0) & (where_ref[1] == 1), counts_ref[tag], 0)
        counts = jnp.where(row == tag, count.astype(jnp.float32), counts)
    weights = weights / jnp.sum(weights, axis=0, keepdims=True)
    totals = jnp.sum(weights, axis=1, keepdims=True) + counts
    return weights.astype(jnp.bfloat16), totals


def class_sums(rounded, totals, bit, nears, sums_ref):
    chunk = nears[0].shape[2]
    share = sums_ref.shape[2] // chunk
    piece = 0
    for near in nears:
        for pair in range(near.shape[0] // (2 * share)):
            for part in range(share):
                at = (2 * pair + bit) * share + part
                sums_ref[piece, :, pl.ds(part * chunk, chunk)] = jnp.dot(
                    rounded, near[at], preferred_element_type=jnp.float32
                )
            sums_ref[piece, :, share * chunk :] = totals
            piece += 1


def rest_kernel(where_ref, rounded_ref, totals_ref, *rest):
    *nears, sums_ref = rest
    bit = lax.rem(where_ref[0], 2)
    class_sums(rounded_ref[...], totals_ref[...], bit, nears, sums_ref)


def rest_sums(where, rounded, totals, nears, piece):
    classes, per_device = rounded.shape
    blocks = 2 * piece.shape[0]
    freqs = blocks * (piece.shape[2] - LANES)
    return pl.pallas_call(
        rest_kernel,
        in_specs=[in_smem()] + [in_vmem()] * (2 + len(nears)),
        out_specs=in_vmem(),
        out_shape=piece,
        compiler_params=pltpu.CompilerParams(vmem_limit_bytes=VMEM_LIMIT),
        cost_estimate=pl.CostEstimate(
            flops=128 * per_device * freqs,
            bytes_accessed=per_device * freqs // 2,
            transcendentals=0,
        ),
    )(where, rounded, totals, *(pltpu.with_memory_space_constraint(x, pltpu.VMEM) for x in nears))


def ring_kernel(phase, ends, sources, where_ref, noise_ref, low_ref, high_ref, *rest):
    row_refs, rest = rest[: 2 * len(sources)], rest[2 * len(sources) :]
    if phase == 0:
        acc, energy = rest
    else:
        acc_in, energy_in, logs_ref, words_ref, state_ref, *rest = rest
        if ends:
            counts_ref, *nears, loglik_ref, sums_ref = rest[:-4]
            rounded_ref, totals_ref, acc, energy = rest[-4:]
        else:
            out_ref, acc, energy = rest
    if phase == 0:
        acc[...] = jnp.zeros_like(acc)
        energy[...] = jnp.zeros_like(energy)
    else:
        acc[...] = acc_in[...]
        energy[...] = energy_in[...]
    quarter = low_ref.shape[0]
    core = where_ref[1]

    for at, part_ref in enumerate((low_ref, high_ref)):
        for step in range(quarter // WIDTH):
            there = pl.ds(step * WIDTH, WIDTH)
            columns = pl.ds((2 * phase + at) * quarter + step * WIDTH, WIDTH)
            if ends:
                rows = jnp.where(core == at, row_refs[0][:, there], row_refs[1][:, there])
            else:
                here = pl.ds(at * quarter + step * WIDTH, WIDTH)
                rows = jnp.concatenate([ref[:, here] for ref in row_refs], axis=0)
            weighted = weigh(rows, noise_ref[:, columns], energy)
            acc[...] += jnp.dot(weighted, part_ref[there, :], preferred_element_type=jnp.float32)

    if phase == 0:
        return
    height = row_refs[0].shape[0]
    span = quarter if ends else 2 * quarter
    tags = [ref[:, span:].astype(jnp.float32) for ref in row_refs]
    tags = jnp.where(core == 0, tags[1], tags[0]) if ends else jnp.concatenate(tags, axis=0)
    found = []
    for tables in sources:
        for table in tables:
            source = jnp.int32(table[0])
            for block in range(1, len(table)):
                source = jnp.where(where_ref[0] == block, table[block], source)
            found.append(source)
    if ends:
        found = found[:1]
    else:
        for at in range(0, len(found), 2):
            front, back = found[at : at + 2]
            found[at] = jnp.where(core == 0, front, back)
            found[at + 1] = jnp.where(core == 0, back, front)
    hit = jnp.concatenate([picked_rows(words_ref, source, height) for source in found], axis=0)
    state = add_rows(tags, hit, logs_ref, get_state(state_ref), acc, energy)
    if ends:
        loglik_ref[...] = state[0] + jnp.log(state[1])
        rounded, totals = class_weights(state, where_ref, counts_ref)
        rounded_ref[...] = rounded
        totals_ref[...] = totals
        bit = 1 - lax.rem(where_ref[0], 2)
        class_sums(rounded, totals, bit, nears, sums_ref)
    else:
        put_state(state, out_ref)


def ring_scores(phase, sources, where, noise, turned, arrays, rest, ends, piece):
    quarter, per_device = turned[0].shape
    freqs = 4 * quarter
    rows = arrays[0].shape[0] * (1 if ends else len(arrays))
    sums = [
        jax.ShapeDtypeStruct((rows, per_device), jnp.float32),
        jax.ShapeDtypeStruct((rows, LANES), jnp.float32),
    ]
    scratch = [pltpu.VMEM(array.shape, array.dtype) for array in sums]
    specs = []
    if phase == 0:
        shapes, scratch = sums, []
    else:
        specs = [in_vmem(), in_vmem(), in_smem(), in_vmem(), in_vmem()]
        if ends:
            classes = rest[2].shape[0]
            shapes = [
                jax.ShapeDtypeStruct((1, per_device), jnp.float32),
                piece,
                jax.ShapeDtypeStruct((classes, per_device), jnp.bfloat16),
                jax.ShapeDtypeStruct((classes, LANES), jnp.float32),
            ]
            nears = [pltpu.with_memory_space_constraint(x, pltpu.VMEM) for x in rest[6:]]
            specs += [in_smem()] + [in_vmem()] * len(nears)
            rest = (*rest[:6], *nears)
        else:
            shapes = [jax.ShapeDtypeStruct(rest[4].shape, jnp.float32)]
    return pl.pallas_call(
        functools.partial(ring_kernel, phase, ends, sources),
        in_specs=[in_smem()] + [in_vmem()] * (3 + len(arrays)) + specs,
        out_specs=[in_vmem()] * len(shapes),
        out_shape=shapes,
        scratch_shapes=scratch,
        compiler_params=pltpu.CompilerParams(vmem_limit_bytes=VMEM_LIMIT),
        cost_estimate=pl.CostEstimate(
            flops=2 * 128 * per_device * freqs,
            bytes_accessed=per_device * freqs,
            transcendentals=0,
        ),
    )(
        where,
        noise,
        *(pltpu.with_memory_space_constraint(part, pltpu.VMEM) for part in turned),
        *arrays,
        *rest,
    )


def scatter_sum(pieces, blocks, bits):
    tail = pieces.shape[1:]
    zero = jnp.uint32(0)
    for step, (bit, other) in enumerate(bits):
        pairs = pieces.reshape((-1, 2) + tail)
        size = (pairs.shape[0], 1) + tail
        keep, send = (
            lax.dynamic_slice(pairs, (zero, which, zero, zero), size).reshape((-1,) + tail)
            for which in (bit, other)
        )
        pieces = keep + lax.ppermute(send, ("blk", "cls"), across_chips(blocks, 2 << step))
    return pieces[0]


def across_chips(blocks, change):
    return [(2 * block + 1, 2 * (block ^ change) + 1) for block in range(blocks)]


def body(particles, significant, templates, template_class, class_counts, inv_noise):
    per_device, freqs = particles.shape
    classes = class_counts.shape[0]
    blocks = lax.axis_size("blk")
    owners = lax.axis_size("cls")
    order = ring_order(blocks)
    place = [order.index(block) for block in range(blocks)]
    block_id = lax.axis_index("blk")
    core = lax.axis_index("cls")
    ring = [(2 * order[i], 2 * order[(i + 1) % blocks]) for i in range(blocks)]
    ring += [(2 * order[(i + 1) % blocks] + 1, 2 * order[i] + 1) for i in range(blocks)]
    swap = [(i, owners - 1 - i) for i in range(owners)]

    noise = inv_noise[None, :]
    logs = jnp.log(class_counts.astype(jnp.float32))
    tags = template_class[None, :]
    *held, near_noise, picks = make_messages(tags, noise, significant, templates)
    where = jnp.stack([block_id, core])
    cut = freqs // 4
    per_owner = classes // owners
    bits = [
        lax.rem(lax.div(block_id, 2 << step), 2) for step in range(blocks.bit_length() - 2)
    ]
    bits = [(bit.astype(jnp.uint32), (1 - bit).astype(jnp.uint32)) for bit in bits]
    cut_at = core.astype(jnp.uint32) * cut
    where, cut_at, bits = lax.optimization_barrier((where, cut_at, bits))
    own = functools.partial(own_scores, where=where, noise=near_noise, particles=particles)
    total = blocks * templates.shape[0]
    words, *sums, low, high, near, raw = own([0, 1], templates=held[0], rest=(picks,), total=total)
    turned, nears = [(low, high)], [near, raw]
    gates = [sums]
    *sums, low, raw = own([2], templates=held[1], rest=(*sums, raw))
    nears.append(raw)
    gates.append(sums)
    state, high = own([3], templates=held[1], rest=(*sums, logs, tags, words, raw))
    turned.append((low, high))
    gates.append(state)
    width = freqs // blocks
    piece = jax.ShapeDtypeStruct((blocks // 2, classes, width + LANES), jnp.float32)
    last = blocks // 2
    for distance in range(1, last + 1):
        ends = distance == last
        tables = [
            [
                tuple(order[(place[block] - sign * distance) % blocks] for block in range(blocks))
                for sign in (1, -1)
            ]
        ]
        arrived = []
        for phase in range(2):
            message = held[phase]
            if ends:
                message = lax.dynamic_slice(
                    message,
                    (jnp.uint32(0), cut_at),
                    (message.shape[0], message.shape[1] - cut),
                )
            own = lax.ppermute(message, ("blk", "cls"), ring)
            lag = 3 if distance == 2 else 2
            gate = phase if distance == 1 else len(gates) - lag
            own, _ = lax.optimization_barrier((own, gates[gate]))
            pair = (own, lax.ppermute(own, "cls", swap))
            arrived.append(own)
            rest = (*sums, logs, words, state) if phase else ()
            if ends and phase:
                rest += (class_counts, *nears)
            sums = ring_scores(
                phase, tables, where, near_noise, turned[phase], pair, rest, ends, piece
            )
            gates.append(sums)
        held = arrived
        if not ends:
            (state,) = sums

    loglik, sums, rounded, totals = sums
    given = lax.ppermute(sums, "cls", [(0, 1)])
    across = lax.ppermute(sums + given, ("blk", "cls"), across_chips(blocks, 1))
    rounded, _ = lax.optimization_barrier((rounded, given))
    rest = rest_sums(where, rounded, totals, nears, piece)
    kept = lax.optimization_barrier(rest + across)
    total = scatter_sum(kept + lax.ppermute(rest, "cls", [(0, 1)]), blocks, bits)
    handed = lax.ppermute(total[:per_owner], "cls", [(1, 0)])
    total = jnp.where(core == 0, handed, total[per_owner:])
    class_avg = total[:, :width] / total[:, width][:, None]
    return loglik[0], class_avg


def solution(mesh):
    placed = (
        P(("grp", "blk", "cls"), None),
        P(None, ("grp", "blk", "cls")),
        P(("grp", "blk"), None),
        P(("grp", "blk")),
        P("grp"),
        P(),
    )
    return jax.shard_map(
        body,
        mesh=mesh,
        in_specs=placed,
        out_specs=(P(("grp", "blk", "cls")), P(("grp", "cls"), "blk")),
        check_vma=False,
    )
```

```python
import functools

import jax
import jax.numpy as jnp
from jax import lax
from jax.experimental import pallas as pl
from jax.experimental.pallas import tpu as pltpu
from jax.sharding import PartitionSpec as P

LOWEST = -1e30
STEPS = 16
WIDTH = 1024
STRIP = 256
LANES = 128
STATE_ROWS = 8
VMEM_LIMIT = 6 * 1024 * 1024


def ring_order(blocks):
    if blocks <= 8:
        return list(range(0, blocks, 2)) + list(range(blocks - 1, 0, -2))
    return list(range(blocks))


def spread_copies(source, target, sent):
    count = sent.shape[0]
    rows = target.shape[0] // count
    return [
        pltpu.make_async_copy(
            source.at[pl.ds(at * rows, rows)], target.at[pl.ds(at * rows, rows)], sent.at[at]
        )
        for at in range(count)
    ]


def message_kernel(
    tags_ref, noise_ref, sig_ref, rows_ref,
    first_ref, second_ref, near_noise_ref, near_sig_ref, tags, sent, spread,
):
    height, span = first_ref.shape
    copies = [
        pltpu.make_async_copy(tags_ref, tags, sent.at[0]),
        pltpu.make_async_copy(noise_ref, near_noise_ref, sent.at[1]),
        pltpu.make_async_copy(sig_ref, near_sig_ref, sent.at[2]),
        *spread_copies(rows_ref.at[:, :span], first_ref, spread.at[0]),
        *spread_copies(rows_ref.at[:, span:], second_ref.at[:, :span], spread.at[1]),
    ]
    for copy in copies:
        copy.start()
    copies[0].wait()
    second_ref[:, span:] = tag_rows(tags, height).astype(jnp.bfloat16)
    for copy in copies[1:]:
        copy.wait()


def make_messages(tags, noise, significant, templates):
    height, freqs = templates.shape
    span = freqs // 2
    return pl.pallas_call(
        message_kernel,
        in_specs=[pl.BlockSpec(memory_space=pl.ANY)] * 4,
        out_specs=[in_vmem()] * 4,
        out_shape=[
            pltpu.VMEM((height, span), jnp.bfloat16),
            pltpu.VMEM((height, span + LANES), jnp.bfloat16),
            pltpu.VMEM(noise.shape, noise.dtype),
            pltpu.VMEM(significant.shape, significant.dtype),
        ],
        scratch_shapes=[
            pltpu.VMEM(tags.shape, tags.dtype),
            pltpu.SemaphoreType.DMA((3,)),
            pltpu.SemaphoreType.DMA((2, 4)),
        ],
        compiler_params=pltpu.CompilerParams(vmem_limit_bytes=VMEM_LIMIT),
    )(
        *(
            pltpu.with_memory_space_constraint(x, pltpu.HBM)
            for x in (tags, noise, significant, templates)
        )
    )


def tag_rows(tags_ref, height):
    row = lax.broadcasted_iota(jnp.int32, (height, height), 0)
    lane = lax.broadcasted_iota(jnp.int32, (height, height), 1)
    spread = jnp.where(row == lane, tags_ref[...].astype(jnp.float32), 0.0)
    return jnp.broadcast_to(jnp.sum(spread, axis=1, keepdims=True), (height, LANES))


def in_smem():
    return pl.BlockSpec(memory_space=pltpu.SMEM)


def in_vmem():
    return pl.BlockSpec(memory_space=pltpu.VMEM)


def weigh(rows, noise, energy):
    widened = rows.astype(jnp.float32)
    product = widened * noise
    square = product * widened
    folded = square[:, :LANES]
    for lane in range(LANES, square.shape[1], LANES):
        folded = folded + square[:, lane : lane + LANES]
    energy[...] += folded
    return product.astype(jnp.bfloat16)


def pick_words(sig_ref, words_ref):
    word = lax.broadcasted_iota(jnp.int32, words_ref.shape, 0)
    words = jnp.zeros(words_ref.shape, jnp.int32)
    for pick in range(sig_ref.shape[0]):
        chosen = sig_ref[pick : pick + 1, :]
        bit = jnp.left_shift(1, jnp.bitwise_and(chosen, 31))
        words = words | jnp.where(jnp.right_shift(chosen, 5) == word, bit, 0)
    words_ref[...] = words


def picked_rows(words_ref, source, height):
    bit = jnp.left_shift(1, lax.broadcasted_iota(jnp.int32, (32, 1), 0))
    rows = []
    for word in range(height // 32):
        rows.append((words_ref[pl.ds(source * (height // 32) + word, 1), :] & bit) != 0)
    return jnp.concatenate(rows, axis=0)


def add_rows(tags, hit, logs_ref, state, acc, energy):
    classes = logs_ref.shape[0]
    prior = jnp.zeros_like(tags[:, :1])
    for tag in range(classes):
        prior = jnp.where(tags[:, :1] == tag, logs_ref[tag], prior)
    bias = prior - 0.5 * jnp.sum(energy[...], axis=1, keepdims=True)
    scores = acc[...] + bias
    old_max, old_sum, old_top, weights = state
    new_max = jnp.maximum(old_max, jnp.max(scores, axis=0, keepdims=True))
    new_sum = old_sum * jnp.exp(old_max - new_max) + jnp.sum(
        jnp.exp(scores - new_max), axis=0, keepdims=True
    )
    new_top = jnp.maximum(
        old_top, jnp.max(jnp.where(hit, scores, LOWEST), axis=0, keepdims=True)
    )
    value = jnp.where(hit, jnp.exp(scores - new_top), 0.0)
    lane = lax.broadcasted_iota(jnp.int32, tags.shape, 1).astype(jnp.float32)
    onehot = jnp.transpose(jnp.where(tags == lane, 1.0, 0.0))[:classes, :].astype(jnp.bfloat16)
    weights = weights * jnp.exp(old_top - new_top)
    left = value
    for _ in range(3):
        piece = left.astype(jnp.bfloat16)
        left = left - piece.astype(jnp.float32)
        weights = weights + jnp.dot(onehot, piece, preferred_element_type=jnp.float32)
    return new_max, new_sum, new_top, weights


def put_state(state, out_ref):
    new_max, new_sum, new_top, weights = state
    out_ref[0:1, :] = new_max
    out_ref[1:2, :] = new_sum
    out_ref[2:3, :] = new_top
    out_ref[3:STATE_ROWS, :] = jnp.zeros_like(out_ref[3:STATE_ROWS, :])
    out_ref[STATE_ROWS:, :] = weights


def get_state(state_ref):
    return state_ref[0:1, :], state_ref[1:2, :], state_ref[2:3, :], state_ref[STATE_ROWS:, :]


def own_kernel(quarters, where_ref, noise_ref, tmpl_ref, far_ref, *rest):
    first, last = quarters[0] == 0, quarters[-1] == 3
    if first:
        sig_ref, words_ref, acc, energy, *turned_refs, near, next_ref, arrived, late = rest
    elif last:
        acc_in, energy_in, logs_ref, tags_ref, words_ref, near, out_ref, *rest = rest
        *turned_refs, acc, energy = rest
    else:
        acc_in, energy_in, near, acc, energy, *turned_refs, next_ref, late = rest
    span, height = turned_refs[0].shape[0], tmpl_ref.shape[0]
    steps, _, width = near.shape
    low = quarters[0] * span

    def copies(step):
        columns = pl.ds(pl.multiple_of(low + step * width, width), width)
        return spread_copies(far_ref.at[:, columns], near.at[step], arrived.at[step])

    def following(step):
        columns = pl.ds(low + (steps + step) * width, width)
        return spread_copies(far_ref.at[:, columns], next_ref.at[step], late.at[step])

    if first:
        for step in range(steps):
            for copy in copies(step):
                copy.start()
    if not last:
        for step in range(next_ref.shape[0]):
            for copy in following(step):
                copy.start()
    if first:
        pick_words(sig_ref, words_ref)
        acc[...] = jnp.zeros_like(acc)
        energy[...] = jnp.zeros_like(energy)
    else:
        acc[...] = acc_in[...]
        energy[...] = energy_in[...]
    for quarter, turned_ref in zip(quarters, turned_refs):

        @pl.loop(0, span // width)
        def _(inner):
            step = (quarter - quarters[0]) * (span // width) + inner
            if first:
                for copy in copies(step):
                    copy.wait()
            for strip in range(0, width, STRIP):
                there = pl.ds(pl.multiple_of(inner * width + strip, STRIP), STRIP)
                part = quarter % 2 * span + inner * width + strip
                here = pl.ds(pl.multiple_of(part, STRIP), STRIP)
                columns = pl.ds(pl.multiple_of(low + step * width + strip, STRIP), STRIP)
                weighted = weigh(tmpl_ref[:, here], noise_ref[:, columns], energy)
                turned = jnp.transpose(near[step, :, strip : strip + STRIP])
                turned_ref[there, :] = turned
                acc[...] += jnp.dot(weighted, turned, preferred_element_type=jnp.float32)

    if not last:
        for step in range(next_ref.shape[0]):
            for copy in following(step):
                copy.wait()
        return
    tags = tag_rows(tags_ref, height)
    hit = picked_rows(words_ref, where_ref[0], height)
    lowest = jnp.full((1, acc.shape[1]), LOWEST, jnp.float32)
    none = jnp.zeros((1, acc.shape[1]), jnp.float32)
    weights = jnp.zeros((logs_ref.shape[0], acc.shape[1]), jnp.float32)
    state = (lowest, none, lowest, weights)
    put_state(add_rows(tags, hit, logs_ref, state, acc, energy), out_ref)


def own_scores(quarters, where, noise, particles, templates, rest, total=0):
    per_device, freqs = particles.shape
    height = templates.shape[0]
    width = freqs // STEPS
    span = freqs // 4
    steps = span // width
    first, last = quarters[0] == 0, quarters[-1] == 3
    sums = [
        jax.ShapeDtypeStruct((height, per_device), jnp.float32),
        jax.ShapeDtypeStruct((height, LANES), jnp.float32),
    ]
    turned = [pltpu.VMEM((span, per_device), particles.dtype)] * len(quarters)
    raw = pltpu.VMEM((steps, per_device, width), particles.dtype)
    if first:
        shapes = [jax.ShapeDtypeStruct((total // 32, per_device), jnp.int32)] + sums
        shapes += turned + [pltpu.VMEM((2 * steps, per_device, width), particles.dtype), raw]
        rest_specs = [in_vmem()]
        scratch = [
            pltpu.SemaphoreType.DMA((2 * steps, 4)),
            pltpu.SemaphoreType.DMA((steps, 4)),
        ]
    elif last:
        rows = STATE_ROWS + rest[2].shape[0]
        shapes = [jax.ShapeDtypeStruct((rows, per_device), jnp.float32)] + turned
        rest_specs = [in_vmem(), in_vmem(), in_smem(), in_vmem(), in_vmem(), in_vmem()]
        scratch = [pltpu.VMEM(array.shape, array.dtype) for array in sums]
    else:
        shapes = sums + turned + [raw]
        rest_specs = [in_vmem()] * 3
        scratch = [pltpu.SemaphoreType.DMA((steps, 4))]
    if not first:
        rest = (*rest[:-1], pltpu.with_memory_space_constraint(rest[-1], pltpu.VMEM))
    return pl.pallas_call(
        functools.partial(own_kernel, quarters),
        in_specs=[in_smem(), in_vmem(), in_vmem(), pl.BlockSpec(memory_space=pl.ANY)] + rest_specs,
        out_specs=[in_vmem()] * len(shapes),
        out_shape=shapes,
        scratch_shapes=scratch,
        compiler_params=pltpu.CompilerParams(vmem_limit_bytes=VMEM_LIMIT),
        cost_estimate=pl.CostEstimate(
            flops=2 * 128 * per_device * freqs,
            bytes_accessed=per_device * freqs,
            transcendentals=0,
        ),
    )(where, noise, templates, pltpu.with_memory_space_constraint(particles, pltpu.HBM), *rest)


def class_weights(state, where_ref, counts_ref):
    _, _, _, weights = state
    classes = weights.shape[0]
    row = lax.broadcasted_iota(jnp.int32, (classes, LANES), 0)
    counts = jnp.zeros((classes, LANES), jnp.float32)
    for tag in range(classes):
        count = jnp.where((where_ref[0] == 0) & (where_ref[1] == 1), counts_ref[tag], 0)
        counts = jnp.where(row == tag, count.astype(jnp.float32), counts)
    weights = weights / jnp.sum(weights, axis=0, keepdims=True)
    totals = jnp.sum(weights, axis=1, keepdims=True) + counts
    return weights.astype(jnp.bfloat16), totals


def class_sums(rounded, totals, bit, nears, sums_ref):
    chunk = nears[0].shape[2]
    share = sums_ref.shape[2] // chunk
    piece = 0
    for near in nears:
        for pair in range(near.shape[0] // (2 * share)):
            for part in range(share):
                at = (2 * pair + bit) * share + part
                sums_ref[piece, :, pl.ds(part * chunk, chunk)] = jnp.dot(
                    rounded, near[at], preferred_element_type=jnp.float32
                )
            sums_ref[piece, :, share * chunk :] = totals
            piece += 1


def rest_kernel(where_ref, rounded_ref, totals_ref, *rest):
    *nears, sums_ref = rest
    bit = lax.rem(where_ref[0], 2)
    class_sums(rounded_ref[...], totals_ref[...], bit, nears, sums_ref)


def rest_sums(where, rounded, totals, nears, piece):
    classes, per_device = rounded.shape
    blocks = 2 * piece.shape[0]
    freqs = blocks * (piece.shape[2] - LANES)
    return pl.pallas_call(
        rest_kernel,
        in_specs=[in_smem()] + [in_vmem()] * (2 + len(nears)),
        out_specs=in_vmem(),
        out_shape=piece,
        compiler_params=pltpu.CompilerParams(vmem_limit_bytes=VMEM_LIMIT),
        cost_estimate=pl.CostEstimate(
            flops=128 * per_device * freqs,
            bytes_accessed=per_device * freqs // 2,
            transcendentals=0,
        ),
    )(where, rounded, totals, *(pltpu.with_memory_space_constraint(x, pltpu.VMEM) for x in nears))


def ring_kernel(phase, ends, sources, where_ref, noise_ref, low_ref, high_ref, *rest):
    row_refs, rest = rest[: 2 * len(sources)], rest[2 * len(sources) :]
    if phase == 0:
        acc, energy = rest
    else:
        acc_in, energy_in, logs_ref, words_ref, state_ref, *rest = rest
        if ends:
            counts_ref, *nears, loglik_ref, sums_ref = rest[:-4]
            rounded_ref, totals_ref, acc, energy = rest[-4:]
        else:
            out_ref, acc, energy = rest
    if phase == 0:
        acc[...] = jnp.zeros_like(acc)
        energy[...] = jnp.zeros_like(energy)
    else:
        acc[...] = acc_in[...]
        energy[...] = energy_in[...]
    quarter = low_ref.shape[0]
    core = where_ref[1]

    for at, part_ref in enumerate((low_ref, high_ref)):
        for step in range(quarter // WIDTH):
            there = pl.ds(step * WIDTH, WIDTH)
            columns = pl.ds((2 * phase + at) * quarter + step * WIDTH, WIDTH)
            if ends:
                rows = jnp.where(core == at, row_refs[0][:, there], row_refs[1][:, there])
            else:
                here = pl.ds(at * quarter + step * WIDTH, WIDTH)
                rows = jnp.concatenate([ref[:, here] for ref in row_refs], axis=0)
            weighted = weigh(rows, noise_ref[:, columns], energy)
            acc[...] += jnp.dot(weighted, part_ref[there, :], preferred_element_type=jnp.float32)

    if phase == 0:
        return
    height = row_refs[0].shape[0]
    span = quarter if ends else 2 * quarter
    tags = [ref[:, span:].astype(jnp.float32) for ref in row_refs]
    tags = jnp.where(core == 0, tags[1], tags[0]) if ends else jnp.concatenate(tags, axis=0)
    found = []
    for tables in sources:
        for table in tables:
            source = jnp.int32(table[0])
            for block in range(1, len(table)):
                source = jnp.where(where_ref[0] == block, table[block], source)
            found.append(source)
    if ends:
        found = found[:1]
    else:
        for at in range(0, len(found), 2):
            front, back = found[at : at + 2]
            found[at] = jnp.where(core == 0, front, back)
            found[at + 1] = jnp.where(core == 0, back, front)
    hit = jnp.concatenate([picked_rows(words_ref, source, height) for source in found], axis=0)
    state = add_rows(tags, hit, logs_ref, get_state(state_ref), acc, energy)
    if ends:
        loglik_ref[...] = state[0] + jnp.log(state[1])
        rounded, totals = class_weights(state, where_ref, counts_ref)
        rounded_ref[...] = rounded
        totals_ref[...] = totals
        bit = 1 - lax.rem(where_ref[0], 2)
        class_sums(rounded, totals, bit, nears, sums_ref)
    else:
        put_state(state, out_ref)


def ring_scores(phase, sources, where, noise, turned, arrays, rest, ends, piece):
    quarter, per_device = turned[0].shape
    freqs = 4 * quarter
    rows = arrays[0].shape[0] * (1 if ends else len(arrays))
    sums = [
        jax.ShapeDtypeStruct((rows, per_device), jnp.float32),
        jax.ShapeDtypeStruct((rows, LANES), jnp.float32),
    ]
    scratch = [pltpu.VMEM(array.shape, array.dtype) for array in sums]
    specs = []
    if phase == 0:
        shapes, scratch = sums, []
    else:
        specs = [in_vmem(), in_vmem(), in_smem(), in_vmem(), in_vmem()]
        if ends:
            classes = rest[2].shape[0]
            shapes = [
                jax.ShapeDtypeStruct((1, per_device), jnp.float32),
                piece,
                jax.ShapeDtypeStruct((classes, per_device), jnp.bfloat16),
                jax.ShapeDtypeStruct((classes, LANES), jnp.float32),
            ]
            nears = [pltpu.with_memory_space_constraint(x, pltpu.VMEM) for x in rest[6:]]
            specs += [in_smem()] + [in_vmem()] * len(nears)
            rest = (*rest[:6], *nears)
        else:
            shapes = [jax.ShapeDtypeStruct(rest[4].shape, jnp.float32)]
    return pl.pallas_call(
        functools.partial(ring_kernel, phase, ends, sources),
        in_specs=[in_smem()] + [in_vmem()] * (3 + len(arrays)) + specs,
        out_specs=[in_vmem()] * len(shapes),
        out_shape=shapes,
        scratch_shapes=scratch,
        compiler_params=pltpu.CompilerParams(vmem_limit_bytes=VMEM_LIMIT),
        cost_estimate=pl.CostEstimate(
            flops=2 * 128 * per_device * freqs,
            bytes_accessed=per_device * freqs,
            transcendentals=0,
        ),
    )(
        where,
        noise,
        *(pltpu.with_memory_space_constraint(part, pltpu.VMEM) for part in turned),
        *arrays,
        *rest,
    )


def scatter_sum(pieces, blocks, bits):
    tail = pieces.shape[1:]
    zero = jnp.uint32(0)
    for step, (bit, other) in enumerate(bits):
        pairs = pieces.reshape((-1, 2) + tail)
        size = (pairs.shape[0], 1) + tail
        keep, send = (
            lax.dynamic_slice(pairs, (zero, which, zero, zero), size).reshape((-1,) + tail)
            for which in (bit, other)
        )
        pieces = keep + lax.ppermute(send, ("blk", "cls"), across_chips(blocks, 2 << step))
    return pieces[0]


def across_chips(blocks, change):
    pairs = [(2 * block, 2 * block) for block in range(blocks)]
    return pairs + [(2 * block + 1, 2 * (block ^ change) + 1) for block in range(blocks)]


def body(particles, significant, templates, template_class, class_counts, inv_noise):
    per_device, freqs = particles.shape
    classes = class_counts.shape[0]
    blocks = lax.axis_size("blk")
    owners = lax.axis_size("cls")
    order = ring_order(blocks)
    place = [order.index(block) for block in range(blocks)]
    block_id = lax.axis_index("blk")
    core = lax.axis_index("cls")
    ring = [(2 * order[i], 2 * order[(i + 1) % blocks]) for i in range(blocks)]
    ring += [(2 * order[(i + 1) % blocks] + 1, 2 * order[i] + 1) for i in range(blocks)]
    swap = [(i, owners - 1 - i) for i in range(owners)]

    noise = inv_noise[None, :]
    logs = jnp.log(class_counts.astype(jnp.float32))
    tags = template_class[None, :]
    *held, near_noise, picks = make_messages(tags, noise, significant, templates)
    where = jnp.stack([block_id, core])
    cut = freqs // 4
    per_owner = classes // owners
    bits = [
        lax.rem(lax.div(block_id, 2 << step), 2) for step in range(blocks.bit_length() - 2)
    ]
    bits = [(bit.astype(jnp.uint32), (1 - bit).astype(jnp.uint32)) for bit in bits]
    cut_at = core.astype(jnp.uint32) * cut
    where, cut_at, bits = lax.optimization_barrier((where, cut_at, bits))
    own = functools.partial(own_scores, where=where, noise=near_noise, particles=particles)
    total = blocks * templates.shape[0]
    words, *sums, low, high, near, raw = own([0, 1], templates=held[0], rest=(picks,), total=total)
    turned, nears = [(low, high)], [near, raw]
    gates = [sums]
    *sums, low, raw = own([2], templates=held[1], rest=(*sums, raw))
    nears.append(raw)
    gates.append(sums)
    state, high = own([3], templates=held[1], rest=(*sums, logs, tags, words, raw))
    turned.append((low, high))
    gates.append(state)
    width = freqs // blocks
    piece = jax.ShapeDtypeStruct((blocks // 2, classes, width + LANES), jnp.float32)
    last = blocks // 2
    for distance in range(1, last + 1):
        ends = distance == last
        tables = [
            [
                tuple(order[(place[block] - sign * distance) % blocks] for block in range(blocks))
                for sign in (1, -1)
            ]
        ]
        arrived = []
        for phase in range(2):
            message = held[phase]
            if ends:
                message = lax.dynamic_slice(
                    message,
                    (jnp.uint32(0), cut_at),
                    (message.shape[0], message.shape[1] - cut),
                )
            own = lax.ppermute(message, ("blk", "cls"), ring)
            lag = 3 if distance == 2 else 2
            gate = phase if distance == 1 else len(gates) - lag
            own, _ = lax.optimization_barrier((own, gates[gate]))
            pair = (own, lax.ppermute(own, "cls", swap))
            arrived.append(own)
            rest = (*sums, logs, words, state) if phase else ()
            if ends and phase:
                rest += (class_counts, *nears)
            sums = ring_scores(
                phase, tables, where, near_noise, turned[phase], pair, rest, ends, piece
            )
            gates.append(sums)
        held = arrived
        if not ends:
            (state,) = sums

    loglik, sums, rounded, totals = sums
    given = lax.ppermute(sums, "cls", swap)
    across = lax.ppermute(sums + given, ("blk", "cls"), across_chips(blocks, 1))
    rounded, _ = lax.optimization_barrier((rounded, given))
    rest = rest_sums(where, rounded, totals, nears, piece)
    kept = lax.optimization_barrier(rest + across)
    total = scatter_sum(kept + lax.ppermute(rest, "cls", swap), blocks, bits)
    handed = lax.ppermute(total[:per_owner], "cls", swap)
    total = jnp.where(core == 0, handed, total[per_owner:])
    class_avg = total[:, :width] / total[:, width][:, None]
    return loglik[0], class_avg


def solution(mesh):
    placed = (
        P(("grp", "blk", "cls"), None),
        P(None, ("grp", "blk", "cls")),
        P(("grp", "blk"), None),
        P(("grp", "blk")),
        P("grp"),
        P(),
    )
    return jax.shard_map(
        body,
        mesh=mesh,
        in_specs=placed,
        out_specs=(P(("grp", "blk", "cls")), P(("grp", "cls"), "blk")),
        check_vma=False,
    )
```

```python
import functools

import jax
import jax.numpy as jnp
from jax import lax
from jax.experimental import pallas as pl
from jax.experimental.pallas import tpu as pltpu
from jax.sharding import PartitionSpec as P

LOWEST = -1e30
CHUNK = 1024
PIECES = 2
WIDTH = 1024
STRIP = 256
LANES = 128
STATE_ROWS = 8
VMEM_LIMIT = 6 * 1024 * 1024


def ring_order(blocks):
    if blocks <= 8:
        return list(range(0, blocks, 2)) + list(range(blocks - 1, 0, -2))
    return list(range(blocks))


def spread_copies(source, target, sent):
    count = sent.shape[0]
    rows = target.shape[0] // count
    return [
        pltpu.make_async_copy(
            source.at[pl.ds(at * rows, rows)], target.at[pl.ds(at * rows, rows)], sent.at[at]
        )
        for at in range(count)
    ]


def message_kernel(
    tags_ref, noise_ref, sig_ref, rows_ref,
    first_ref, second_ref, near_noise_ref, near_sig_ref, tags, sent, spread,
):
    height, span = first_ref.shape
    copies = [
        pltpu.make_async_copy(tags_ref, tags, sent.at[0]),
        pltpu.make_async_copy(noise_ref, near_noise_ref, sent.at[1]),
        pltpu.make_async_copy(sig_ref, near_sig_ref, sent.at[2]),
        *spread_copies(rows_ref.at[:, :span], first_ref, spread.at[0]),
        *spread_copies(rows_ref.at[:, span:], second_ref.at[:, :span], spread.at[1]),
    ]
    for copy in copies:
        copy.start()
    copies[0].wait()
    second_ref[:, span:] = tag_rows(tags, height).astype(jnp.bfloat16)
    for copy in copies[1:]:
        copy.wait()


def make_messages(tags, noise, significant, templates):
    height, freqs = templates.shape
    span = freqs // 2
    return pl.pallas_call(
        message_kernel,
        in_specs=[pl.BlockSpec(memory_space=pl.ANY)] * 4,
        out_specs=[in_vmem()] * 4,
        out_shape=[
            pltpu.VMEM((height, span), jnp.bfloat16),
            pltpu.VMEM((height, span + LANES), jnp.bfloat16),
            pltpu.VMEM(noise.shape, noise.dtype),
            pltpu.VMEM(significant.shape, significant.dtype),
        ],
        scratch_shapes=[
            pltpu.VMEM(tags.shape, tags.dtype),
            pltpu.SemaphoreType.DMA((3,)),
            pltpu.SemaphoreType.DMA((2, 4)),
        ],
        compiler_params=pltpu.CompilerParams(vmem_limit_bytes=VMEM_LIMIT),
    )(
        *(
            pltpu.with_memory_space_constraint(x, pltpu.HBM)
            for x in (tags, noise, significant, templates)
        )
    )


def tag_rows(tags_ref, height):
    row = lax.broadcasted_iota(jnp.int32, (height, height), 0)
    lane = lax.broadcasted_iota(jnp.int32, (height, height), 1)
    spread = jnp.where(row == lane, tags_ref[...].astype(jnp.float32), 0.0)
    return jnp.broadcast_to(jnp.sum(spread, axis=1, keepdims=True), (height, LANES))


def in_smem():
    return pl.BlockSpec(memory_space=pltpu.SMEM)


def in_vmem():
    return pl.BlockSpec(memory_space=pltpu.VMEM)


def weigh(rows, noise, energy):
    widened = rows.astype(jnp.float32)
    product = widened * noise
    square = product * widened
    folded = square[:, :LANES]
    for lane in range(LANES, square.shape[1], LANES):
        folded = folded + square[:, lane : lane + LANES]
    energy[...] += folded
    return product.astype(jnp.bfloat16)


def pick_words(sig_ref, words_ref):
    word = lax.broadcasted_iota(jnp.int32, words_ref.shape, 0)
    words = jnp.zeros(words_ref.shape, jnp.int32)
    for pick in range(sig_ref.shape[0]):
        chosen = sig_ref[pick : pick + 1, :]
        bit = jnp.left_shift(1, jnp.bitwise_and(chosen, 31))
        words = words | jnp.where(jnp.right_shift(chosen, 5) == word, bit, 0)
    words_ref[...] = words


def picked_rows(words_ref, source, height):
    bit = jnp.left_shift(1, lax.broadcasted_iota(jnp.int32, (32, 1), 0))
    rows = []
    for word in range(height // 32):
        rows.append((words_ref[pl.ds(source * (height // 32) + word, 1), :] & bit) != 0)
    return jnp.concatenate(rows, axis=0)


def add_rows(tags, hit, logs_ref, state, acc, energy):
    classes = logs_ref.shape[0]
    prior = jnp.zeros_like(tags[:, :1])
    for tag in range(classes):
        prior = jnp.where(tags[:, :1] == tag, logs_ref[tag], prior)
    bias = prior - 0.5 * jnp.sum(energy[...], axis=1, keepdims=True)
    scores = acc[...] + bias
    old_max, old_sum, old_top, weights = state
    new_max = jnp.maximum(old_max, jnp.max(scores, axis=0, keepdims=True))
    new_sum = old_sum * jnp.exp(old_max - new_max) + jnp.sum(
        jnp.exp(scores - new_max), axis=0, keepdims=True
    )
    new_top = jnp.maximum(
        old_top, jnp.max(jnp.where(hit, scores, LOWEST), axis=0, keepdims=True)
    )
    value = jnp.where(hit, jnp.exp(scores - new_top), 0.0)
    lane = lax.broadcasted_iota(jnp.int32, tags.shape, 1).astype(jnp.float32)
    onehot = jnp.transpose(jnp.where(tags == lane, 1.0, 0.0))[:classes, :].astype(jnp.bfloat16)
    weights = weights * jnp.exp(old_top - new_top)
    left = value
    for _ in range(3):
        piece = left.astype(jnp.bfloat16)
        left = left - piece.astype(jnp.float32)
        weights = weights + jnp.dot(onehot, piece, preferred_element_type=jnp.float32)
    return new_max, new_sum, new_top, weights


def put_state(state, out_ref):
    new_max, new_sum, new_top, weights = state
    out_ref[0:1, :] = new_max
    out_ref[1:2, :] = new_sum
    out_ref[2:3, :] = new_top
    out_ref[3:STATE_ROWS, :] = jnp.zeros_like(out_ref[3:STATE_ROWS, :])
    out_ref[STATE_ROWS:, :] = weights


def get_state(state_ref):
    return state_ref[0:1, :], state_ref[1:2, :], state_ref[2:3, :], state_ref[STATE_ROWS:, :]


def own_kernel(quarters, where_ref, noise_ref, tmpl_ref, far_ref, *rest):
    first, last = quarters[0] == 0, quarters[-1] == 3
    if first:
        sig_ref, words_ref, acc, energy, *turned_refs, near, next_ref, arrived, late = rest
    elif last:
        acc_in, energy_in, logs_ref, tags_ref, words_ref, near, out_ref, *rest = rest
        *turned_refs, acc, energy = rest
    else:
        acc_in, energy_in, near, acc, energy, *turned_refs, next_ref, late = rest
    span, height = turned_refs[0].shape[0], tmpl_ref.shape[0]
    chunks, _, chunk = near.shape
    steps = chunks * PIECES
    width = chunk // PIECES
    low = quarters[0] * span

    def part(ref, step):
        columns = pl.ds(pl.multiple_of(lax.rem(step, PIECES) * width, width), width)
        return ref.at[lax.div(step, PIECES), :, columns]

    def copies(step):
        columns = pl.ds(pl.multiple_of(low + step * width, width), width)
        return spread_copies(far_ref.at[:, columns], part(near, step), arrived.at[step])

    def following(step):
        columns = pl.ds(low + (steps + step) * width, width)
        return spread_copies(far_ref.at[:, columns], part(next_ref, step), late.at[step])

    if first:
        for step in range(steps):
            for copy in copies(step):
                copy.start()
    if not last:
        for step in range(next_ref.shape[0] * PIECES):
            for copy in following(step):
                copy.start()
    if first:
        pick_words(sig_ref, words_ref)
        acc[...] = jnp.zeros_like(acc)
        energy[...] = jnp.zeros_like(energy)
    else:
        acc[...] = acc_in[...]
        energy[...] = energy_in[...]
    for quarter, turned_ref in zip(quarters, turned_refs):

        @pl.loop(0, span // width)
        def _(inner):
            step = (quarter - quarters[0]) * (span // width) + inner
            if first:
                for copy in copies(step):
                    copy.wait()
            for strip in range(0, width, STRIP):
                there = pl.ds(pl.multiple_of(inner * width + strip, STRIP), STRIP)
                start = quarter % 2 * span + inner * width + strip
                here = pl.ds(pl.multiple_of(start, STRIP), STRIP)
                columns = pl.ds(pl.multiple_of(low + step * width + strip, STRIP), STRIP)
                weighted = weigh(tmpl_ref[:, here], noise_ref[:, columns], energy)
                turned = jnp.transpose(part(near, step)[:, strip : strip + STRIP])
                turned_ref[there, :] = turned
                acc[...] += jnp.dot(weighted, turned, preferred_element_type=jnp.float32)

    if not last:
        for step in range(next_ref.shape[0] * PIECES):
            for copy in following(step):
                copy.wait()
        return
    tags = tag_rows(tags_ref, height)
    hit = picked_rows(words_ref, where_ref[0], height)
    lowest = jnp.full((1, acc.shape[1]), LOWEST, jnp.float32)
    none = jnp.zeros((1, acc.shape[1]), jnp.float32)
    weights = jnp.zeros((logs_ref.shape[0], acc.shape[1]), jnp.float32)
    state = (lowest, none, lowest, weights)
    put_state(add_rows(tags, hit, logs_ref, state, acc, energy), out_ref)


def own_scores(quarters, where, noise, particles, templates, rest, total=0):
    per_device, freqs = particles.shape
    height = templates.shape[0]
    span = freqs // 4
    chunks = span // CHUNK
    steps = chunks * PIECES
    first, last = quarters[0] == 0, quarters[-1] == 3
    sums = [
        jax.ShapeDtypeStruct((height, per_device), jnp.float32),
        jax.ShapeDtypeStruct((height, LANES), jnp.float32),
    ]
    turned = [pltpu.VMEM((span, per_device), particles.dtype)] * len(quarters)
    raw = pltpu.VMEM((chunks, per_device, CHUNK), particles.dtype)
    if first:
        shapes = [jax.ShapeDtypeStruct((total // 32, per_device), jnp.int32)] + sums
        shapes += turned + [pltpu.VMEM((2 * chunks, per_device, CHUNK), particles.dtype), raw]
        rest_specs = [in_vmem()]
        scratch = [
            pltpu.SemaphoreType.DMA((2 * steps, 4)),
            pltpu.SemaphoreType.DMA((steps, 4)),
        ]
    elif last:
        rows = STATE_ROWS + rest[2].shape[0]
        shapes = [jax.ShapeDtypeStruct((rows, per_device), jnp.float32)] + turned
        rest_specs = [in_vmem(), in_vmem(), in_smem(), in_vmem(), in_vmem(), in_vmem()]
        scratch = [pltpu.VMEM(array.shape, array.dtype) for array in sums]
    else:
        shapes = sums + turned + [raw]
        rest_specs = [in_vmem()] * 3
        scratch = [pltpu.SemaphoreType.DMA((steps, 4))]
    if not first:
        rest = (*rest[:-1], pltpu.with_memory_space_constraint(rest[-1], pltpu.VMEM))
    return pl.pallas_call(
        functools.partial(own_kernel, quarters),
        in_specs=[in_smem(), in_vmem(), in_vmem(), pl.BlockSpec(memory_space=pl.ANY)] + rest_specs,
        out_specs=[in_vmem()] * len(shapes),
        out_shape=shapes,
        scratch_shapes=scratch,
        compiler_params=pltpu.CompilerParams(vmem_limit_bytes=VMEM_LIMIT),
        cost_estimate=pl.CostEstimate(
            flops=2 * 128 * per_device * freqs,
            bytes_accessed=per_device * freqs,
            transcendentals=0,
        ),
    )(where, noise, templates, pltpu.with_memory_space_constraint(particles, pltpu.HBM), *rest)


def class_weights(state, where_ref, counts_ref, per_owner):
    _, _, _, weights = state
    classes = weights.shape[0]
    row = lax.broadcasted_iota(jnp.int32, (classes, LANES), 0)
    counts = jnp.zeros((classes, LANES), jnp.float32)
    for tag in range(classes):
        mine = (where_ref[0] == 0) & (where_ref[1] == tag // per_owner)
        count = jnp.where(mine, counts_ref[tag], 0).astype(jnp.float32)
        counts = jnp.where(row == tag, count, counts)
    weights = weights / jnp.sum(weights, axis=0, keepdims=True)
    totals = jnp.sum(weights, axis=1, keepdims=True) + counts

    def own_first(rows):
        turned = jnp.concatenate([rows[per_owner:], rows[:per_owner]], axis=0)
        return jnp.where(where_ref[1] == 0, rows, turned)

    return own_first(weights).astype(jnp.bfloat16), own_first(totals)


def class_sums(rounded, totals, bit, nears, mine_ref, theirs_ref):
    per_owner = mine_ref.shape[1]
    chunk = nears[0].shape[2]
    width = mine_ref.shape[2] - LANES
    piece = 0
    for near in nears:
        for pair in range(near.shape[0] * chunk // (2 * width)):
            start = (2 * pair + bit) * width
            at, low = lax.div(start, chunk), lax.rem(start, chunk)
            columns = pl.ds(pl.multiple_of(low, width), width) if width < chunk else slice(None)
            sums = jnp.dot(rounded, near[at, :, columns], preferred_element_type=jnp.float32)
            mine_ref[piece, :, :width] = sums[:per_owner]
            theirs_ref[piece, :, :width] = sums[per_owner:]
            mine_ref[piece, :, width:] = totals[:per_owner]
            theirs_ref[piece, :, width:] = totals[per_owner:]
            piece += 1


def rest_kernel(where_ref, rounded_ref, totals_ref, *rest):
    *nears, mine_ref, theirs_ref = rest
    bit = lax.rem(where_ref[0], 2)
    class_sums(rounded_ref[...], totals_ref[...], bit, nears, mine_ref, theirs_ref)


def rest_sums(where, rounded, totals, nears, piece):
    classes, per_device = rounded.shape
    blocks = 2 * piece.shape[0]
    freqs = blocks * (piece.shape[2] - LANES)
    return pl.pallas_call(
        rest_kernel,
        in_specs=[in_smem()] + [in_vmem()] * (2 + len(nears)),
        out_specs=[in_vmem()] * 2,
        out_shape=[piece, piece],
        compiler_params=pltpu.CompilerParams(vmem_limit_bytes=VMEM_LIMIT),
        cost_estimate=pl.CostEstimate(
            flops=128 * per_device * freqs,
            bytes_accessed=per_device * freqs // 2,
            transcendentals=0,
        ),
    )(where, rounded, totals, *(pltpu.with_memory_space_constraint(x, pltpu.VMEM) for x in nears))


def ring_kernel(phase, ends, sources, where_ref, noise_ref, low_ref, high_ref, *rest):
    row_refs, rest = rest[: 2 * len(sources)], rest[2 * len(sources) :]
    if phase == 0:
        acc, energy = rest
    else:
        acc_in, energy_in, logs_ref, words_ref, state_ref, *rest = rest
        if ends:
            counts_ref, *nears, loglik_ref, mine_ref, theirs_ref = rest[:-4]
            rounded_ref, totals_ref, acc, energy = rest[-4:]
        else:
            out_ref, acc, energy = rest
    if phase == 0:
        acc[...] = jnp.zeros_like(acc)
        energy[...] = jnp.zeros_like(energy)
    else:
        acc[...] = acc_in[...]
        energy[...] = energy_in[...]
    quarter = low_ref.shape[0]
    core = where_ref[1]

    for at, part_ref in enumerate((low_ref, high_ref)):
        for step in range(quarter // WIDTH):
            there = pl.ds(step * WIDTH, WIDTH)
            columns = pl.ds((2 * phase + at) * quarter + step * WIDTH, WIDTH)
            if ends:
                rows = jnp.where(core == at, row_refs[0][:, there], row_refs[1][:, there])
            else:
                here = pl.ds(at * quarter + step * WIDTH, WIDTH)
                rows = jnp.concatenate([ref[:, here] for ref in row_refs], axis=0)
            weighted = weigh(rows, noise_ref[:, columns], energy)
            acc[...] += jnp.dot(weighted, part_ref[there, :], preferred_element_type=jnp.float32)

    if phase == 0:
        return
    height = row_refs[0].shape[0]
    span = quarter if ends else 2 * quarter
    tags = [ref[:, span:].astype(jnp.float32) for ref in row_refs]
    tags = jnp.where(core == 0, tags[1], tags[0]) if ends else jnp.concatenate(tags, axis=0)
    found = []
    for tables in sources:
        for table in tables:
            source = jnp.int32(table[0])
            for block in range(1, len(table)):
                source = jnp.where(where_ref[0] == block, table[block], source)
            found.append(source)
    if ends:
        found = found[:1]
    else:
        for at in range(0, len(found), 2):
            front, back = found[at : at + 2]
            found[at] = jnp.where(core == 0, front, back)
            found[at + 1] = jnp.where(core == 0, back, front)
    hit = jnp.concatenate([picked_rows(words_ref, source, height) for source in found], axis=0)
    state = add_rows(tags, hit, logs_ref, get_state(state_ref), acc, energy)
    if ends:
        loglik_ref[...] = state[0] + jnp.log(state[1])
        rounded, totals = class_weights(state, where_ref, counts_ref, mine_ref.shape[1])
        rounded_ref[...] = rounded
        totals_ref[...] = totals
        bit = 1 - lax.rem(where_ref[0], 2)
        class_sums(rounded, totals, bit, nears, mine_ref, theirs_ref)
    else:
        put_state(state, out_ref)


def ring_scores(phase, sources, where, noise, turned, arrays, rest, ends, piece):
    quarter, per_device = turned[0].shape
    freqs = 4 * quarter
    rows = arrays[0].shape[0] * (1 if ends else len(arrays))
    sums = [
        jax.ShapeDtypeStruct((rows, per_device), jnp.float32),
        jax.ShapeDtypeStruct((rows, LANES), jnp.float32),
    ]
    scratch = [pltpu.VMEM(array.shape, array.dtype) for array in sums]
    specs = []
    if phase == 0:
        shapes, scratch = sums, []
    else:
        specs = [in_vmem(), in_vmem(), in_smem(), in_vmem(), in_vmem()]
        if ends:
            classes = rest[2].shape[0]
            shapes = [
                jax.ShapeDtypeStruct((1, per_device), jnp.float32),
                piece,
                piece,
                jax.ShapeDtypeStruct((classes, per_device), jnp.bfloat16),
                jax.ShapeDtypeStruct((classes, LANES), jnp.float32),
            ]
            nears = [pltpu.with_memory_space_constraint(x, pltpu.VMEM) for x in rest[6:]]
            specs += [in_smem()] + [in_vmem()] * len(nears)
            rest = (*rest[:6], *nears)
        else:
            shapes = [jax.ShapeDtypeStruct(rest[4].shape, jnp.float32)]
    return pl.pallas_call(
        functools.partial(ring_kernel, phase, ends, sources),
        in_specs=[in_smem()] + [in_vmem()] * (3 + len(arrays)) + specs,
        out_specs=[in_vmem()] * len(shapes),
        out_shape=shapes,
        scratch_shapes=scratch,
        compiler_params=pltpu.CompilerParams(vmem_limit_bytes=VMEM_LIMIT),
        cost_estimate=pl.CostEstimate(
            flops=2 * 128 * per_device * freqs,
            bytes_accessed=per_device * freqs,
            transcendentals=0,
        ),
    )(
        where,
        noise,
        *(pltpu.with_memory_space_constraint(part, pltpu.VMEM) for part in turned),
        *arrays,
        *rest,
    )


def scatter_sum(pieces, blocks, bits):
    tail = pieces.shape[1:]
    zero = jnp.uint32(0)
    for step, (bit, other) in enumerate(bits):
        pairs = pieces.reshape((-1, 2) + tail)
        size = (pairs.shape[0], 1) + tail
        keep, send = (
            lax.dynamic_slice(pairs, (zero, which, zero, zero), size).reshape((-1,) + tail)
            for which in (bit, other)
        )
        swaps = [(block, block ^ (2 << step)) for block in range(blocks)]
        pieces = keep + lax.ppermute(send, "blk", swaps)
    return pieces[0]


def body(particles, significant, templates, template_class, class_counts, inv_noise):
    per_device, freqs = particles.shape
    classes = class_counts.shape[0]
    blocks = lax.axis_size("blk")
    owners = lax.axis_size("cls")
    order = ring_order(blocks)
    place = [order.index(block) for block in range(blocks)]
    block_id = lax.axis_index("blk")
    core = lax.axis_index("cls")
    ring = [(2 * order[i], 2 * order[(i + 1) % blocks]) for i in range(blocks)]
    ring += [(2 * order[(i + 1) % blocks] + 1, 2 * order[i] + 1) for i in range(blocks)]
    swap = [(i, owners - 1 - i) for i in range(owners)]

    noise = inv_noise[None, :]
    logs = jnp.log(class_counts.astype(jnp.float32))
    tags = template_class[None, :]
    *held, near_noise, picks = make_messages(tags, noise, significant, templates)
    where = jnp.stack([block_id, core])
    cut = freqs // 4
    per_owner = classes // owners
    bits = [
        lax.rem(lax.div(block_id, 2 << step), 2) for step in range(blocks.bit_length() - 2)
    ]
    bits = [(bit.astype(jnp.uint32), (1 - bit).astype(jnp.uint32)) for bit in bits]
    cut_at = core.astype(jnp.uint32) * cut
    where, cut_at, bits = lax.optimization_barrier((where, cut_at, bits))
    own = functools.partial(own_scores, where=where, noise=near_noise, particles=particles)
    total = blocks * templates.shape[0]
    words, *sums, low, high, near, raw = own([0, 1], templates=held[0], rest=(picks,), total=total)
    turned, nears = [(low, high)], [near, raw]
    gates = [sums]
    *sums, low, raw = own([2], templates=held[1], rest=(*sums, raw))
    nears.append(raw)
    gates.append(sums)
    state, high = own([3], templates=held[1], rest=(*sums, logs, tags, words, raw))
    turned.append((low, high))
    gates.append(state)
    width = freqs // blocks
    piece = jax.ShapeDtypeStruct((blocks // 2, per_owner, width + LANES), jnp.float32)
    last = blocks // 2
    for distance in range(1, last + 1):
        ends = distance == last
        tables = [
            [
                tuple(order[(place[block] - sign * distance) % blocks] for block in range(blocks))
                for sign in (1, -1)
            ]
        ]
        arrived = []
        for phase in range(2):
            message = held[phase]
            if ends:
                message = lax.dynamic_slice(
                    message,
                    (jnp.uint32(0), cut_at),
                    (message.shape[0], message.shape[1] - cut),
                )
            own = lax.ppermute(message, ("blk", "cls"), ring)
            lag = 3 if distance == 2 else 2
            gate = phase if distance == 1 else len(gates) - lag
            own, _ = lax.optimization_barrier((own, gates[gate]))
            pair = (own, lax.ppermute(own, "cls", swap))
            arrived.append(own)
            rest = (*sums, logs, words, state) if phase else ()
            if ends and phase:
                rest += (class_counts, *nears)
            sums = ring_scores(
                phase, tables, where, near_noise, turned[phase], pair, rest, ends, piece
            )
            gates.append(sums)
        held = arrived
        if not ends:
            (state,) = sums

    loglik, mine, theirs, rounded, totals = sums
    given = lax.ppermute(theirs, "cls", swap)
    across = lax.ppermute(mine + given, "blk", [(i, i ^ 1) for i in range(blocks)])
    rounded, _ = lax.optimization_barrier((rounded, given))
    mine, theirs = rest_sums(where, rounded, totals, nears, piece)
    kept = lax.optimization_barrier(mine + across)
    total = scatter_sum(kept + lax.ppermute(theirs, "cls", swap), blocks, bits)
    class_avg = total[:, :width] / total[:, width][:, None]
    return loglik[0], class_avg


def solution(mesh):
    placed = (
        P(("grp", "blk", "cls"), None),
        P(None, ("grp", "blk", "cls")),
        P(("grp", "blk"), None),
        P(("grp", "blk")),
        P("grp"),
        P(),
    )
    return jax.shard_map(
        body,
        mesh=mesh,
        in_specs=placed,
        out_specs=(P(("grp", "blk", "cls")), P(("grp", "cls"), "blk")),
        check_vma=False,
    )
```

```python
import functools

import jax
import jax.numpy as jnp
from jax import lax
from jax.experimental import pallas as pl
from jax.experimental.pallas import tpu as pltpu
from jax.sharding import PartitionSpec as P

LOWEST = -1e30
CHUNK = 1024
PIECES = 2
WIDTH = 1024
STRIP = 256
LANES = 128
STATE_ROWS = 8
VMEM_LIMIT = 6 * 1024 * 1024


def ring_order(blocks):
    if blocks <= 8:
        return list(range(0, blocks, 2)) + list(range(blocks - 1, 0, -2))
    return list(range(blocks))


def spread_copies(source, target, sent):
    count = sent.shape[0]
    rows = target.shape[0] // count
    return [
        pltpu.make_async_copy(
            source.at[pl.ds(at * rows, rows)], target.at[pl.ds(at * rows, rows)], sent.at[at]
        )
        for at in range(count)
    ]


def message_kernel(
    tags_ref, noise_ref, sig_ref, rows_ref,
    first_ref, second_ref, near_noise_ref, near_sig_ref, tags, sent, spread,
):
    height, span = first_ref.shape
    copies = [
        pltpu.make_async_copy(tags_ref, tags, sent.at[0]),
        pltpu.make_async_copy(noise_ref, near_noise_ref, sent.at[1]),
        pltpu.make_async_copy(sig_ref, near_sig_ref, sent.at[2]),
        *spread_copies(rows_ref.at[:, :span], first_ref, spread.at[0]),
        *spread_copies(rows_ref.at[:, span:], second_ref.at[:, :span], spread.at[1]),
    ]
    for copy in copies:
        copy.start()
    copies[0].wait()
    second_ref[:, span:] = tag_rows(tags, height).astype(jnp.bfloat16)
    for copy in copies[1:]:
        copy.wait()


def make_messages(tags, noise, significant, templates):
    height, freqs = templates.shape
    span = freqs // 2
    return pl.pallas_call(
        message_kernel,
        in_specs=[pl.BlockSpec(memory_space=pl.ANY)] * 4,
        out_specs=[in_vmem()] * 4,
        out_shape=[
            pltpu.VMEM((height, span), jnp.bfloat16),
            pltpu.VMEM((height, span + LANES), jnp.bfloat16),
            pltpu.VMEM(noise.shape, noise.dtype),
            pltpu.VMEM(significant.shape, significant.dtype),
        ],
        scratch_shapes=[
            pltpu.VMEM(tags.shape, tags.dtype),
            pltpu.SemaphoreType.DMA((3,)),
            pltpu.SemaphoreType.DMA((2, 4)),
        ],
        compiler_params=pltpu.CompilerParams(vmem_limit_bytes=VMEM_LIMIT),
    )(
        *(
            pltpu.with_memory_space_constraint(x, pltpu.HBM)
            for x in (tags, noise, significant, templates)
        )
    )


def tag_rows(tags_ref, height):
    row = lax.broadcasted_iota(jnp.int32, (height, height), 0)
    lane = lax.broadcasted_iota(jnp.int32, (height, height), 1)
    spread = jnp.where(row == lane, tags_ref[...].astype(jnp.float32), 0.0)
    return jnp.broadcast_to(jnp.sum(spread, axis=1, keepdims=True), (height, LANES))


def in_smem():
    return pl.BlockSpec(memory_space=pltpu.SMEM)


def in_vmem():
    return pl.BlockSpec(memory_space=pltpu.VMEM)


def weigh(rows, noise, energy):
    widened = rows.astype(jnp.float32)
    product = widened * noise
    square = product * widened
    folded = square[:, :LANES]
    for lane in range(LANES, square.shape[1], LANES):
        folded = folded + square[:, lane : lane + LANES]
    energy[...] += folded
    return product.astype(jnp.bfloat16)


def pick_words(sig_ref, words_ref):
    word = lax.broadcasted_iota(jnp.int32, words_ref.shape, 0)
    words = jnp.zeros(words_ref.shape, jnp.int32)
    for pick in range(sig_ref.shape[0]):
        chosen = sig_ref[pick : pick + 1, :]
        bit = jnp.left_shift(1, jnp.bitwise_and(chosen, 31))
        words = words | jnp.where(jnp.right_shift(chosen, 5) == word, bit, 0)
    words_ref[...] = words


def picked_rows(words_ref, source, height):
    bit = jnp.left_shift(1, lax.broadcasted_iota(jnp.int32, (32, 1), 0))
    rows = []
    for word in range(height // 32):
        rows.append((words_ref[pl.ds(source * (height // 32) + word, 1), :] & bit) != 0)
    return jnp.concatenate(rows, axis=0)


def add_rows(tags, hit, logs_ref, state, acc, energy):
    classes = logs_ref.shape[0]
    prior = jnp.zeros_like(tags[:, :1])
    for tag in range(classes):
        prior = jnp.where(tags[:, :1] == tag, logs_ref[tag], prior)
    bias = prior - 0.5 * jnp.sum(energy[...], axis=1, keepdims=True)
    scores = acc[...] + bias
    old_max, old_sum, old_top, weights = state
    new_max = jnp.maximum(old_max, jnp.max(scores, axis=0, keepdims=True))
    new_sum = old_sum * jnp.exp(old_max - new_max) + jnp.sum(
        jnp.exp(scores - new_max), axis=0, keepdims=True
    )
    new_top = jnp.maximum(
        old_top, jnp.max(jnp.where(hit, scores, LOWEST), axis=0, keepdims=True)
    )
    value = jnp.where(hit, jnp.exp(scores - new_top), 0.0)
    lane = lax.broadcasted_iota(jnp.int32, tags.shape, 1).astype(jnp.float32)
    onehot = jnp.transpose(jnp.where(tags == lane, 1.0, 0.0))[:classes, :].astype(jnp.bfloat16)
    weights = weights * jnp.exp(old_top - new_top)
    left = value
    for _ in range(3):
        piece = left.astype(jnp.bfloat16)
        left = left - piece.astype(jnp.float32)
        weights = weights + jnp.dot(onehot, piece, preferred_element_type=jnp.float32)
    return new_max, new_sum, new_top, weights


def put_state(state, out_ref):
    new_max, new_sum, new_top, weights = state
    out_ref[0:1, :] = new_max
    out_ref[1:2, :] = new_sum
    out_ref[2:3, :] = new_top
    out_ref[3:STATE_ROWS, :] = jnp.zeros_like(out_ref[3:STATE_ROWS, :])
    out_ref[STATE_ROWS:, :] = weights


def get_state(state_ref):
    return state_ref[0:1, :], state_ref[1:2, :], state_ref[2:3, :], state_ref[STATE_ROWS:, :]


def own_kernel(quarters, where_ref, noise_ref, tmpl_ref, far_ref, *rest):
    first, last = quarters[0] == 0, quarters[-1] == 3
    if first:
        sig_ref, words_ref, acc, energy, *turned_refs, near, next_ref, arrived, late = rest
    elif last:
        acc_in, energy_in, logs_ref, tags_ref, words_ref, near, out_ref, *rest = rest
        *turned_refs, acc, energy = rest
    else:
        acc_in, energy_in, near, acc, energy, *turned_refs, next_ref, late = rest
    span, height = turned_refs[0].shape[0], tmpl_ref.shape[0]
    chunks, _, chunk = near.shape
    steps = chunks * PIECES
    width = chunk // PIECES
    low = quarters[0] * span

    def part(ref, step):
        columns = pl.ds(pl.multiple_of(lax.rem(step, PIECES) * width, width), width)
        return ref.at[lax.div(step, PIECES), :, columns]

    def copies(step):
        columns = pl.ds(pl.multiple_of(low + step * width, width), width)
        return spread_copies(far_ref.at[:, columns], part(near, step), arrived.at[step])

    def following(step):
        columns = pl.ds(low + (steps + step) * width, width)
        return spread_copies(far_ref.at[:, columns], part(next_ref, step), late.at[step])

    if first:
        for step in range(steps):
            for copy in copies(step):
                copy.start()
    if not last:
        for step in range(next_ref.shape[0] * PIECES):
            for copy in following(step):
                copy.start()
    if first:
        pick_words(sig_ref, words_ref)
        acc[...] = jnp.zeros_like(acc)
        energy[...] = jnp.zeros_like(energy)
    else:
        acc[...] = acc_in[...]
        energy[...] = energy_in[...]
    for quarter, turned_ref in zip(quarters, turned_refs):

        @pl.loop(0, span // width)
        def _(inner):
            step = (quarter - quarters[0]) * (span // width) + inner
            if first:
                for copy in copies(step):
                    copy.wait()
            for strip in range(0, width, STRIP):
                there = pl.ds(pl.multiple_of(inner * width + strip, STRIP), STRIP)
                start = quarter % 2 * span + inner * width + strip
                here = pl.ds(pl.multiple_of(start, STRIP), STRIP)
                columns = pl.ds(pl.multiple_of(low + step * width + strip, STRIP), STRIP)
                weighted = weigh(tmpl_ref[:, here], noise_ref[:, columns], energy)
                turned = jnp.transpose(part(near, step)[:, strip : strip + STRIP])
                turned_ref[there, :] = turned
                acc[...] += jnp.dot(weighted, turned, preferred_element_type=jnp.float32)

    if not last:
        for step in range(next_ref.shape[0] * PIECES):
            for copy in following(step):
                copy.wait()
        return
    tags = tag_rows(tags_ref, height)
    hit = picked_rows(words_ref, where_ref[0], height)
    lowest = jnp.full((1, acc.shape[1]), LOWEST, jnp.float32)
    none = jnp.zeros((1, acc.shape[1]), jnp.float32)
    weights = jnp.zeros((logs_ref.shape[0], acc.shape[1]), jnp.float32)
    state = (lowest, none, lowest, weights)
    put_state(add_rows(tags, hit, logs_ref, state, acc, energy), out_ref)


def own_scores(quarters, where, noise, particles, templates, rest, total=0):
    per_device, freqs = particles.shape
    height = templates.shape[0]
    span = freqs // 4
    chunks = span // CHUNK
    steps = chunks * PIECES
    first, last = quarters[0] == 0, quarters[-1] == 3
    sums = [
        jax.ShapeDtypeStruct((height, per_device), jnp.float32),
        jax.ShapeDtypeStruct((height, LANES), jnp.float32),
    ]
    turned = [pltpu.VMEM((span, per_device), particles.dtype)] * len(quarters)
    raw = pltpu.VMEM((chunks, per_device, CHUNK), particles.dtype)
    if first:
        shapes = [jax.ShapeDtypeStruct((total // 32, per_device), jnp.int32)] + sums
        shapes += turned + [pltpu.VMEM((2 * chunks, per_device, CHUNK), particles.dtype), raw]
        rest_specs = [in_vmem()]
        scratch = [
            pltpu.SemaphoreType.DMA((2 * steps, 4)),
            pltpu.SemaphoreType.DMA((steps, 4)),
        ]
    elif last:
        rows = STATE_ROWS + rest[2].shape[0]
        shapes = [jax.ShapeDtypeStruct((rows, per_device), jnp.float32)] + turned
        rest_specs = [in_vmem(), in_vmem(), in_smem(), in_vmem(), in_vmem(), in_vmem()]
        scratch = [pltpu.VMEM(array.shape, array.dtype) for array in sums]
    else:
        shapes = sums + turned + [raw]
        rest_specs = [in_vmem()] * 3
        scratch = [pltpu.SemaphoreType.DMA((steps, 4))]
    if not first:
        rest = (*rest[:-1], pltpu.with_memory_space_constraint(rest[-1], pltpu.VMEM))
    return pl.pallas_call(
        functools.partial(own_kernel, quarters),
        in_specs=[in_smem(), in_vmem(), in_vmem(), pl.BlockSpec(memory_space=pl.ANY)] + rest_specs,
        out_specs=[in_vmem()] * len(shapes),
        out_shape=shapes,
        scratch_shapes=scratch,
        compiler_params=pltpu.CompilerParams(vmem_limit_bytes=VMEM_LIMIT),
        cost_estimate=pl.CostEstimate(
            flops=2 * 128 * per_device * freqs,
            bytes_accessed=per_device * freqs,
            transcendentals=0,
        ),
    )(where, noise, templates, pltpu.with_memory_space_constraint(particles, pltpu.HBM), *rest)


def class_weights(state, where_ref, counts_ref, per_owner):
    _, _, _, weights = state
    classes = weights.shape[0]
    row = lax.broadcasted_iota(jnp.int32, (classes, LANES), 0)
    counts = jnp.zeros((classes, LANES), jnp.float32)
    for tag in range(classes):
        mine = (where_ref[0] == 0) & (where_ref[1] == tag // per_owner)
        count = jnp.where(mine, counts_ref[tag], 0).astype(jnp.float32)
        counts = jnp.where(row == tag, count, counts)
    weights = weights / jnp.sum(weights, axis=0, keepdims=True)
    totals = jnp.sum(weights, axis=1, keepdims=True) + counts

    def own_first(rows):
        turned = jnp.concatenate([rows[per_owner:], rows[:per_owner]], axis=0)
        return jnp.where(where_ref[1] == 0, rows, turned)

    return own_first(weights).astype(jnp.bfloat16), own_first(totals)


def class_sums(rounded, totals, bit, nears, mine_ref, theirs_ref):
    per_owner = mine_ref.shape[1]
    chunk = nears[0].shape[2]
    width = mine_ref.shape[2] - LANES

    def sums_of(which):
        piece = 0
        for near in nears:
            for pair in range(near.shape[0] * chunk // (2 * width)):
                at, low = divmod((2 * pair + which) * width, chunk)
                sums = jnp.dot(
                    rounded, near[at, :, low : low + width], preferred_element_type=jnp.float32
                )
                mine_ref[piece, :, :width] = sums[:per_owner]
                theirs_ref[piece, :, :width] = sums[per_owner:]
                mine_ref[piece, :, width:] = totals[:per_owner]
                theirs_ref[piece, :, width:] = totals[per_owner:]
                piece += 1

    for which in range(2):
        pl.when(bit == which)(functools.partial(sums_of, which))


def rest_kernel(where_ref, rounded_ref, totals_ref, *rest):
    *nears, mine_ref, theirs_ref = rest
    bit = lax.rem(where_ref[0], 2)
    class_sums(rounded_ref[...], totals_ref[...], bit, nears, mine_ref, theirs_ref)


def rest_sums(where, rounded, totals, nears, piece):
    classes, per_device = rounded.shape
    blocks = 2 * piece.shape[0]
    freqs = blocks * (piece.shape[2] - LANES)
    return pl.pallas_call(
        rest_kernel,
        in_specs=[in_smem()] + [in_vmem()] * (2 + len(nears)),
        out_specs=[in_vmem()] * 2,
        out_shape=[piece, piece],
        compiler_params=pltpu.CompilerParams(vmem_limit_bytes=VMEM_LIMIT),
        cost_estimate=pl.CostEstimate(
            flops=128 * per_device * freqs,
            bytes_accessed=per_device * freqs // 2,
            transcendentals=0,
        ),
    )(where, rounded, totals, *(pltpu.with_memory_space_constraint(x, pltpu.VMEM) for x in nears))


def ring_kernel(phase, ends, sources, where_ref, noise_ref, low_ref, high_ref, *rest):
    row_refs, rest = rest[: 2 * len(sources)], rest[2 * len(sources) :]
    if phase == 0:
        acc, energy = rest
    else:
        acc_in, energy_in, logs_ref, words_ref, state_ref, *rest = rest
        if ends:
            counts_ref, *nears, loglik_ref, mine_ref, theirs_ref = rest[:-4]
            rounded_ref, totals_ref, acc, energy = rest[-4:]
        else:
            out_ref, acc, energy = rest
    if phase == 0:
        acc[...] = jnp.zeros_like(acc)
        energy[...] = jnp.zeros_like(energy)
    else:
        acc[...] = acc_in[...]
        energy[...] = energy_in[...]
    quarter = low_ref.shape[0]
    core = where_ref[1]

    for at, part_ref in enumerate((low_ref, high_ref)):
        for step in range(quarter // WIDTH):
            there = pl.ds(step * WIDTH, WIDTH)
            columns = pl.ds((2 * phase + at) * quarter + step * WIDTH, WIDTH)
            if ends:
                rows = jnp.where(core == at, row_refs[0][:, there], row_refs[1][:, there])
            else:
                here = pl.ds(at * quarter + step * WIDTH, WIDTH)
                rows = jnp.concatenate([ref[:, here] for ref in row_refs], axis=0)
            weighted = weigh(rows, noise_ref[:, columns], energy)
            acc[...] += jnp.dot(weighted, part_ref[there, :], preferred_element_type=jnp.float32)

    if phase == 0:
        return
    height = row_refs[0].shape[0]
    span = quarter if ends else 2 * quarter
    tags = [ref[:, span:].astype(jnp.float32) for ref in row_refs]
    tags = jnp.where(core == 0, tags[1], tags[0]) if ends else jnp.concatenate(tags, axis=0)
    found = []
    for tables in sources:
        for table in tables:
            source = jnp.int32(table[0])
            for block in range(1, len(table)):
                source = jnp.where(where_ref[0] == block, table[block], source)
            found.append(source)
    if ends:
        found = found[:1]
    else:
        for at in range(0, len(found), 2):
            front, back = found[at : at + 2]
            found[at] = jnp.where(core == 0, front, back)
            found[at + 1] = jnp.where(core == 0, back, front)
    hit = jnp.concatenate([picked_rows(words_ref, source, height) for source in found], axis=0)
    state = add_rows(tags, hit, logs_ref, get_state(state_ref), acc, energy)
    if ends:
        loglik_ref[...] = state[0] + jnp.log(state[1])
        rounded, totals = class_weights(state, where_ref, counts_ref, mine_ref.shape[1])
        rounded_ref[...] = rounded
        totals_ref[...] = totals
        bit = 1 - lax.rem(where_ref[0], 2)
        class_sums(rounded, totals, bit, nears, mine_ref, theirs_ref)
    else:
        put_state(state, out_ref)


def ring_scores(phase, sources, where, noise, turned, arrays, rest, ends, piece):
    quarter, per_device = turned[0].shape
    freqs = 4 * quarter
    rows = arrays[0].shape[0] * (1 if ends else len(arrays))
    sums = [
        jax.ShapeDtypeStruct((rows, per_device), jnp.float32),
        jax.ShapeDtypeStruct((rows, LANES), jnp.float32),
    ]
    scratch = [pltpu.VMEM(array.shape, array.dtype) for array in sums]
    specs = []
    if phase == 0:
        shapes, scratch = sums, []
    else:
        specs = [in_vmem(), in_vmem(), in_smem(), in_vmem(), in_vmem()]
        if ends:
            classes = rest[2].shape[0]
            shapes = [
                jax.ShapeDtypeStruct((1, per_device), jnp.float32),
                piece,
                piece,
                jax.ShapeDtypeStruct((classes, per_device), jnp.bfloat16),
                jax.ShapeDtypeStruct((classes, LANES), jnp.float32),
            ]
            nears = [pltpu.with_memory_space_constraint(x, pltpu.VMEM) for x in rest[6:]]
            specs += [in_smem()] + [in_vmem()] * len(nears)
            rest = (*rest[:6], *nears)
        else:
            shapes = [jax.ShapeDtypeStruct(rest[4].shape, jnp.float32)]
    return pl.pallas_call(
        functools.partial(ring_kernel, phase, ends, sources),
        in_specs=[in_smem()] + [in_vmem()] * (3 + len(arrays)) + specs,
        out_specs=[in_vmem()] * len(shapes),
        out_shape=shapes,
        scratch_shapes=scratch,
        compiler_params=pltpu.CompilerParams(vmem_limit_bytes=VMEM_LIMIT),
        cost_estimate=pl.CostEstimate(
            flops=2 * 128 * per_device * freqs,
            bytes_accessed=per_device * freqs,
            transcendentals=0,
        ),
    )(
        where,
        noise,
        *(pltpu.with_memory_space_constraint(part, pltpu.VMEM) for part in turned),
        *arrays,
        *rest,
    )


def scatter_sum(pieces, blocks, bits):
    tail = pieces.shape[1:]
    zero = jnp.uint32(0)
    for step, (bit, other) in enumerate(bits):
        pairs = pieces.reshape((-1, 2) + tail)
        size = (pairs.shape[0], 1) + tail
        keep, send = (
            lax.dynamic_slice(pairs, (zero, which, zero, zero), size).reshape((-1,) + tail)
            for which in (bit, other)
        )
        swaps = [(block, block ^ (2 << step)) for block in range(blocks)]
        pieces = keep + lax.ppermute(send, "blk", swaps)
    return pieces[0]


def body(particles, significant, templates, template_class, class_counts, inv_noise):
    per_device, freqs = particles.shape
    classes = class_counts.shape[0]
    blocks = lax.axis_size("blk")
    owners = lax.axis_size("cls")
    order = ring_order(blocks)
    place = [order.index(block) for block in range(blocks)]
    block_id = lax.axis_index("blk")
    core = lax.axis_index("cls")
    ring = [(2 * order[i], 2 * order[(i + 1) % blocks]) for i in range(blocks)]
    ring += [(2 * order[(i + 1) % blocks] + 1, 2 * order[i] + 1) for i in range(blocks)]
    swap = [(i, owners - 1 - i) for i in range(owners)]

    noise = inv_noise[None, :]
    logs = jnp.log(class_counts.astype(jnp.float32))
    tags = template_class[None, :]
    *held, near_noise, picks = make_messages(tags, noise, significant, templates)
    where = jnp.stack([block_id, core])
    cut = freqs // 4
    per_owner = classes // owners
    bits = [
        lax.rem(lax.div(block_id, 2 << step), 2) for step in range(blocks.bit_length() - 2)
    ]
    bits = [(bit.astype(jnp.uint32), (1 - bit).astype(jnp.uint32)) for bit in bits]
    cut_at = core.astype(jnp.uint32) * cut
    where, cut_at, bits = lax.optimization_barrier((where, cut_at, bits))
    own = functools.partial(own_scores, where=where, noise=near_noise, particles=particles)
    total = blocks * templates.shape[0]
    words, *sums, low, high, near, raw = own([0, 1], templates=held[0], rest=(picks,), total=total)
    turned, nears = [(low, high)], [near, raw]
    gates = [sums]
    *sums, low, raw = own([2], templates=held[1], rest=(*sums, raw))
    nears.append(raw)
    gates.append(sums)
    state, high = own([3], templates=held[1], rest=(*sums, logs, tags, words, raw))
    turned.append((low, high))
    gates.append(state)
    width = freqs // blocks
    piece = jax.ShapeDtypeStruct((blocks // 2, per_owner, width + LANES), jnp.float32)
    last = blocks // 2
    for distance in range(1, last + 1):
        ends = distance == last
        tables = [
            [
                tuple(order[(place[block] - sign * distance) % blocks] for block in range(blocks))
                for sign in (1, -1)
            ]
        ]
        arrived = []
        for phase in range(2):
            message = held[phase]
            if ends:
                message = lax.dynamic_slice(
                    message,
                    (jnp.uint32(0), cut_at),
                    (message.shape[0], message.shape[1] - cut),
                )
            own = lax.ppermute(message, ("blk", "cls"), ring)
            lag = 3 if distance == 2 else 2
            gate = phase if distance == 1 else len(gates) - lag
            own, _ = lax.optimization_barrier((own, gates[gate]))
            pair = (own, lax.ppermute(own, "cls", swap))
            arrived.append(own)
            rest = (*sums, logs, words, state) if phase else ()
            if ends and phase:
                rest += (class_counts, *nears)
            sums = ring_scores(
                phase, tables, where, near_noise, turned[phase], pair, rest, ends, piece
            )
            gates.append(sums)
        held = arrived
        if not ends:
            (state,) = sums

    loglik, mine, theirs, rounded, totals = sums
    given = lax.ppermute(theirs, "cls", swap)
    across = lax.ppermute(mine + given, "blk", [(i, i ^ 1) for i in range(blocks)])
    rounded, _ = lax.optimization_barrier((rounded, given))
    mine, theirs = rest_sums(where, rounded, totals, nears, piece)
    kept = lax.optimization_barrier(mine + across)
    total = scatter_sum(kept + lax.ppermute(theirs, "cls", swap), blocks, bits)
    class_avg = total[:, :width] / total[:, width][:, None]
    return loglik[0], class_avg


def solution(mesh):
    placed = (
        P(("grp", "blk", "cls"), None),
        P(None, ("grp", "blk", "cls")),
        P(("grp", "blk"), None),
        P(("grp", "blk")),
        P("grp"),
        P(),
    )
    return jax.shard_map(
        body,
        mesh=mesh,
        in_specs=placed,
        out_specs=(P(("grp", "blk", "cls")), P(("grp", "cls"), "blk")),
        check_vma=False,
    )
```

```python
import functools

import jax
import jax.numpy as jnp
from jax import lax
from jax.experimental import pallas as pl
from jax.experimental.pallas import tpu as pltpu
from jax.sharding import PartitionSpec as P

LOWEST = -1e30
CHUNK = 1024
PIECES = 2
WIDTH = 1024
STRIP = 256
LANES = 128
STATE_ROWS = 8
VMEM_LIMIT = 6 * 1024 * 1024


def ring_order(blocks):
    if blocks <= 8:
        return list(range(0, blocks, 2)) + list(range(blocks - 1, 0, -2))
    return list(range(blocks))


def spread_copies(source, target, sent):
    count = sent.shape[0]
    rows = target.shape[0] // count
    return [
        pltpu.make_async_copy(
            source.at[pl.ds(at * rows, rows)], target.at[pl.ds(at * rows, rows)], sent.at[at]
        )
        for at in range(count)
    ]


def message_kernel(
    tags_ref, noise_ref, sig_ref, rows_ref,
    first_ref, second_ref, near_noise_ref, near_sig_ref, tags, sent, spread,
):
    height, span = first_ref.shape
    copies = [
        pltpu.make_async_copy(tags_ref, tags, sent.at[0]),
        pltpu.make_async_copy(noise_ref, near_noise_ref, sent.at[1]),
        pltpu.make_async_copy(sig_ref, near_sig_ref, sent.at[2]),
        *spread_copies(rows_ref.at[:, :span], first_ref, spread.at[0]),
        *spread_copies(rows_ref.at[:, span:], second_ref.at[:, :span], spread.at[1]),
    ]
    for copy in copies:
        copy.start()
    copies[0].wait()
    second_ref[:, span:] = tag_rows(tags, height).astype(jnp.bfloat16)
    for copy in copies[1:]:
        copy.wait()


def make_messages(tags, noise, significant, templates):
    height, freqs = templates.shape
    span = freqs // 2
    return pl.pallas_call(
        message_kernel,
        in_specs=[pl.BlockSpec(memory_space=pl.ANY)] * 4,
        out_specs=[in_vmem()] * 4,
        out_shape=[
            pltpu.VMEM((height, span), jnp.bfloat16),
            pltpu.VMEM((height, span + LANES), jnp.bfloat16),
            pltpu.VMEM(noise.shape, noise.dtype),
            pltpu.VMEM(significant.shape, significant.dtype),
        ],
        scratch_shapes=[
            pltpu.VMEM(tags.shape, tags.dtype),
            pltpu.SemaphoreType.DMA((3,)),
            pltpu.SemaphoreType.DMA((2, 4)),
        ],
        compiler_params=pltpu.CompilerParams(vmem_limit_bytes=VMEM_LIMIT),
    )(
        *(
            pltpu.with_memory_space_constraint(x, pltpu.HBM)
            for x in (tags, noise, significant, templates)
        )
    )


def tag_rows(tags_ref, height):
    row = lax.broadcasted_iota(jnp.int32, (height, height), 0)
    lane = lax.broadcasted_iota(jnp.int32, (height, height), 1)
    spread = jnp.where(row == lane, tags_ref[...].astype(jnp.float32), 0.0)
    return jnp.broadcast_to(jnp.sum(spread, axis=1, keepdims=True), (height, LANES))


def in_smem():
    return pl.BlockSpec(memory_space=pltpu.SMEM)


def in_vmem():
    return pl.BlockSpec(memory_space=pltpu.VMEM)


def weigh(rows, noise, energy):
    widened = rows.astype(jnp.float32)
    product = widened * noise
    square = product * widened
    folded = square[:, :LANES]
    for lane in range(LANES, square.shape[1], LANES):
        folded = folded + square[:, lane : lane + LANES]
    energy[...] += folded
    return product.astype(jnp.bfloat16)


def pick_words(sig_ref, words_ref):
    word = lax.broadcasted_iota(jnp.int32, words_ref.shape, 0)
    words = jnp.zeros(words_ref.shape, jnp.int32)
    for pick in range(sig_ref.shape[0]):
        chosen = sig_ref[pick : pick + 1, :]
        bit = jnp.left_shift(1, jnp.bitwise_and(chosen, 31))
        words = words | jnp.where(jnp.right_shift(chosen, 5) == word, bit, 0)
    words_ref[...] = words


def picked_rows(words_ref, source, height):
    bit = jnp.left_shift(1, lax.broadcasted_iota(jnp.int32, (32, 1), 0))
    rows = []
    for word in range(height // 32):
        rows.append((words_ref[pl.ds(source * (height // 32) + word, 1), :] & bit) != 0)
    return jnp.concatenate(rows, axis=0)


def add_rows(tags, hit, logs_ref, state, acc, energy):
    classes = logs_ref.shape[0]
    prior = jnp.zeros_like(tags[:, :1])
    for tag in range(classes):
        prior = jnp.where(tags[:, :1] == tag, logs_ref[tag], prior)
    bias = prior - 0.5 * jnp.sum(energy[...], axis=1, keepdims=True)
    scores = acc[...] + bias
    old_max, old_sum, old_top, weights = state
    new_max = jnp.maximum(old_max, jnp.max(scores, axis=0, keepdims=True))
    new_sum = old_sum * jnp.exp(old_max - new_max) + jnp.sum(
        jnp.exp(scores - new_max), axis=0, keepdims=True
    )
    new_top = jnp.maximum(
        old_top, jnp.max(jnp.where(hit, scores, LOWEST), axis=0, keepdims=True)
    )
    value = jnp.where(hit, jnp.exp(scores - new_top), 0.0)
    lane = lax.broadcasted_iota(jnp.int32, tags.shape, 1).astype(jnp.float32)
    onehot = jnp.transpose(jnp.where(tags == lane, 1.0, 0.0))[:classes, :].astype(jnp.bfloat16)
    weights = weights * jnp.exp(old_top - new_top)
    left = value
    for _ in range(3):
        piece = left.astype(jnp.bfloat16)
        left = left - piece.astype(jnp.float32)
        weights = weights + jnp.dot(onehot, piece, preferred_element_type=jnp.float32)
    return new_max, new_sum, new_top, weights


def put_state(state, out_ref):
    new_max, new_sum, new_top, weights = state
    out_ref[0:1, :] = new_max
    out_ref[1:2, :] = new_sum
    out_ref[2:3, :] = new_top
    out_ref[3:STATE_ROWS, :] = jnp.zeros_like(out_ref[3:STATE_ROWS, :])
    out_ref[STATE_ROWS:, :] = weights


def get_state(state_ref):
    return state_ref[0:1, :], state_ref[1:2, :], state_ref[2:3, :], state_ref[STATE_ROWS:, :]


def own_kernel(quarters, blocks, where_ref, noise_ref, tmpl_ref, far_ref, *rest):
    first, last = quarters[0] == 0, quarters[-1] == 3
    if first:
        sig_ref, words_ref, acc, energy, *turned_refs, near, next_ref, arrived, late = rest
    elif last:
        acc_in, energy_in, logs_ref, tags_ref, words_ref, near, out_ref, *rest = rest
        *turned_refs, acc, energy = rest
    else:
        acc_in, energy_in, near, acc, energy, *turned_refs, next_ref, late = rest
    span, height = turned_refs[0].shape[0], tmpl_ref.shape[0]
    chunks, _, chunk = near.shape
    steps = chunks * PIECES
    width = chunk // PIECES
    low = quarters[0] * span

    share = 4 * span // (blocks * width)
    bit = lax.rem(where_ref[0], 2)

    def part(ref, step):
        block, rest = lax.div(step, share), lax.rem(step, share)
        place = block - lax.rem(block, 2) + jnp.where(lax.rem(block, 2) == bit, 1, 0)
        piece = place * share + rest
        columns = pl.ds(pl.multiple_of(lax.rem(piece, PIECES) * width, width), width)
        return ref.at[lax.div(piece, PIECES), :, columns]

    def copies(step):
        columns = pl.ds(pl.multiple_of(low + step * width, width), width)
        return spread_copies(far_ref.at[:, columns], part(near, step), arrived.at[step])

    def following(step):
        columns = pl.ds(low + (steps + step) * width, width)
        return spread_copies(far_ref.at[:, columns], part(next_ref, step), late.at[step])

    if first:
        for step in range(steps):
            for copy in copies(step):
                copy.start()
    if not last:
        for step in range(next_ref.shape[0] * PIECES):
            for copy in following(step):
                copy.start()
    if first:
        pick_words(sig_ref, words_ref)
        acc[...] = jnp.zeros_like(acc)
        energy[...] = jnp.zeros_like(energy)
    else:
        acc[...] = acc_in[...]
        energy[...] = energy_in[...]
    for quarter, turned_ref in zip(quarters, turned_refs):

        @pl.loop(0, span // width)
        def _(inner):
            step = (quarter - quarters[0]) * (span // width) + inner
            if first:
                for copy in copies(step):
                    copy.wait()
            for strip in range(0, width, STRIP):
                there = pl.ds(pl.multiple_of(inner * width + strip, STRIP), STRIP)
                start = quarter % 2 * span + inner * width + strip
                here = pl.ds(pl.multiple_of(start, STRIP), STRIP)
                columns = pl.ds(pl.multiple_of(low + step * width + strip, STRIP), STRIP)
                weighted = weigh(tmpl_ref[:, here], noise_ref[:, columns], energy)
                turned = jnp.transpose(part(near, step)[:, strip : strip + STRIP])
                turned_ref[there, :] = turned
                acc[...] += jnp.dot(weighted, turned, preferred_element_type=jnp.float32)

    if not last:
        for step in range(next_ref.shape[0] * PIECES):
            for copy in following(step):
                copy.wait()
        return
    tags = tag_rows(tags_ref, height)
    hit = picked_rows(words_ref, where_ref[0], height)
    lowest = jnp.full((1, acc.shape[1]), LOWEST, jnp.float32)
    none = jnp.zeros((1, acc.shape[1]), jnp.float32)
    weights = jnp.zeros((logs_ref.shape[0], acc.shape[1]), jnp.float32)
    state = (lowest, none, lowest, weights)
    put_state(add_rows(tags, hit, logs_ref, state, acc, energy), out_ref)


def own_scores(quarters, blocks, where, noise, particles, templates, rest, total=0):
    per_device, freqs = particles.shape
    height = templates.shape[0]
    span = freqs // 4
    chunks = span // CHUNK
    steps = chunks * PIECES
    first, last = quarters[0] == 0, quarters[-1] == 3
    sums = [
        jax.ShapeDtypeStruct((height, per_device), jnp.float32),
        jax.ShapeDtypeStruct((height, LANES), jnp.float32),
    ]
    turned = [pltpu.VMEM((span, per_device), particles.dtype)] * len(quarters)
    raw = pltpu.VMEM((chunks, per_device, CHUNK), particles.dtype)
    if first:
        shapes = [jax.ShapeDtypeStruct((total // 32, per_device), jnp.int32)] + sums
        shapes += turned + [pltpu.VMEM((2 * chunks, per_device, CHUNK), particles.dtype), raw]
        rest_specs = [in_vmem()]
        scratch = [
            pltpu.SemaphoreType.DMA((2 * steps, 4)),
            pltpu.SemaphoreType.DMA((steps, 4)),
        ]
    elif last:
        rows = STATE_ROWS + rest[2].shape[0]
        shapes = [jax.ShapeDtypeStruct((rows, per_device), jnp.float32)] + turned
        rest_specs = [in_vmem(), in_vmem(), in_smem(), in_vmem(), in_vmem(), in_vmem()]
        scratch = [pltpu.VMEM(array.shape, array.dtype) for array in sums]
    else:
        shapes = sums + turned + [raw]
        rest_specs = [in_vmem()] * 3
        scratch = [pltpu.SemaphoreType.DMA((steps, 4))]
    if not first:
        rest = (*rest[:-1], pltpu.with_memory_space_constraint(rest[-1], pltpu.VMEM))
    return pl.pallas_call(
        functools.partial(own_kernel, quarters, blocks),
        in_specs=[in_smem(), in_vmem(), in_vmem(), pl.BlockSpec(memory_space=pl.ANY)] + rest_specs,
        out_specs=[in_vmem()] * len(shapes),
        out_shape=shapes,
        scratch_shapes=scratch,
        compiler_params=pltpu.CompilerParams(vmem_limit_bytes=VMEM_LIMIT),
        cost_estimate=pl.CostEstimate(
            flops=2 * 128 * per_device * freqs,
            bytes_accessed=per_device * freqs,
            transcendentals=0,
        ),
    )(where, noise, templates, pltpu.with_memory_space_constraint(particles, pltpu.HBM), *rest)


def class_weights(state, where_ref, counts_ref, per_owner):
    _, _, _, weights = state
    classes = weights.shape[0]
    row = lax.broadcasted_iota(jnp.int32, (classes, LANES), 0)
    counts = jnp.zeros((classes, LANES), jnp.float32)
    for tag in range(classes):
        mine = (where_ref[0] == 0) & (where_ref[1] == tag // per_owner)
        count = jnp.where(mine, counts_ref[tag], 0).astype(jnp.float32)
        counts = jnp.where(row == tag, count, counts)
    weights = weights / jnp.sum(weights, axis=0, keepdims=True)
    totals = jnp.sum(weights, axis=1, keepdims=True) + counts

    def own_first(rows):
        turned = jnp.concatenate([rows[per_owner:], rows[:per_owner]], axis=0)
        return jnp.where(where_ref[1] == 0, rows, turned)

    return own_first(weights).astype(jnp.bfloat16), own_first(totals)


def class_sums(rounded, totals, which, nears, mine_ref, theirs_ref):
    per_owner = mine_ref.shape[1]
    chunk = nears[0].shape[2]
    width = mine_ref.shape[2] - LANES
    piece = 0
    for near in nears:
        for pair in range(near.shape[0] * chunk // (2 * width)):
            at, low = divmod((2 * pair + which) * width, chunk)
            sums = jnp.dot(
                rounded, near[at, :, low : low + width], preferred_element_type=jnp.float32
            )
            mine_ref[piece, :, :width] = sums[:per_owner]
            theirs_ref[piece, :, :width] = sums[per_owner:]
            mine_ref[piece, :, width:] = totals[:per_owner]
            theirs_ref[piece, :, width:] = totals[per_owner:]
            piece += 1


def rest_kernel(rounded_ref, totals_ref, *rest):
    *nears, mine_ref, theirs_ref = rest
    class_sums(rounded_ref[...], totals_ref[...], 1, nears, mine_ref, theirs_ref)


def rest_sums(rounded, totals, nears, piece):
    classes, per_device = rounded.shape
    blocks = 2 * piece.shape[0]
    freqs = blocks * (piece.shape[2] - LANES)
    return pl.pallas_call(
        rest_kernel,
        in_specs=[in_vmem()] * (2 + len(nears)),
        out_specs=[in_vmem()] * 2,
        out_shape=[piece, piece],
        compiler_params=pltpu.CompilerParams(vmem_limit_bytes=VMEM_LIMIT),
        cost_estimate=pl.CostEstimate(
            flops=128 * per_device * freqs,
            bytes_accessed=per_device * freqs // 2,
            transcendentals=0,
        ),
    )(rounded, totals, *(pltpu.with_memory_space_constraint(x, pltpu.VMEM) for x in nears))


def ring_kernel(phase, ends, sources, where_ref, noise_ref, low_ref, high_ref, *rest):
    row_refs, rest = rest[: 2 * len(sources)], rest[2 * len(sources) :]
    if phase == 0:
        acc, energy = rest
    else:
        acc_in, energy_in, logs_ref, words_ref, state_ref, *rest = rest
        if ends:
            counts_ref, *nears, loglik_ref, mine_ref, theirs_ref = rest[:-4]
            rounded_ref, totals_ref, acc, energy = rest[-4:]
        else:
            out_ref, acc, energy = rest
    if phase == 0:
        acc[...] = jnp.zeros_like(acc)
        energy[...] = jnp.zeros_like(energy)
    else:
        acc[...] = acc_in[...]
        energy[...] = energy_in[...]
    quarter = low_ref.shape[0]
    core = where_ref[1]

    for at, part_ref in enumerate((low_ref, high_ref)):
        for step in range(quarter // WIDTH):
            there = pl.ds(step * WIDTH, WIDTH)
            columns = pl.ds((2 * phase + at) * quarter + step * WIDTH, WIDTH)
            if ends:
                rows = jnp.where(core == at, row_refs[0][:, there], row_refs[1][:, there])
            else:
                here = pl.ds(at * quarter + step * WIDTH, WIDTH)
                rows = jnp.concatenate([ref[:, here] for ref in row_refs], axis=0)
            weighted = weigh(rows, noise_ref[:, columns], energy)
            acc[...] += jnp.dot(weighted, part_ref[there, :], preferred_element_type=jnp.float32)

    if phase == 0:
        return
    height = row_refs[0].shape[0]
    span = quarter if ends else 2 * quarter
    tags = [ref[:, span:].astype(jnp.float32) for ref in row_refs]
    tags = jnp.where(core == 0, tags[1], tags[0]) if ends else jnp.concatenate(tags, axis=0)
    found = []
    for tables in sources:
        for table in tables:
            source = jnp.int32(table[0])
            for block in range(1, len(table)):
                source = jnp.where(where_ref[0] == block, table[block], source)
            found.append(source)
    if ends:
        found = found[:1]
    else:
        for at in range(0, len(found), 2):
            front, back = found[at : at + 2]
            found[at] = jnp.where(core == 0, front, back)
            found[at + 1] = jnp.where(core == 0, back, front)
    hit = jnp.concatenate([picked_rows(words_ref, source, height) for source in found], axis=0)
    state = add_rows(tags, hit, logs_ref, get_state(state_ref), acc, energy)
    if ends:
        loglik_ref[...] = state[0] + jnp.log(state[1])
        rounded, totals = class_weights(state, where_ref, counts_ref, mine_ref.shape[1])
        rounded_ref[...] = rounded
        totals_ref[...] = totals
        class_sums(rounded, totals, 0, nears, mine_ref, theirs_ref)
    else:
        put_state(state, out_ref)


def ring_scores(phase, sources, where, noise, turned, arrays, rest, ends, piece):
    quarter, per_device = turned[0].shape
    freqs = 4 * quarter
    rows = arrays[0].shape[0] * (1 if ends else len(arrays))
    sums = [
        jax.ShapeDtypeStruct((rows, per_device), jnp.float32),
        jax.ShapeDtypeStruct((rows, LANES), jnp.float32),
    ]
    scratch = [pltpu.VMEM(array.shape, array.dtype) for array in sums]
    specs = []
    if phase == 0:
        shapes, scratch = sums, []
    else:
        specs = [in_vmem(), in_vmem(), in_smem(), in_vmem(), in_vmem()]
        if ends:
            classes = rest[2].shape[0]
            shapes = [
                jax.ShapeDtypeStruct((1, per_device), jnp.float32),
                piece,
                piece,
                jax.ShapeDtypeStruct((classes, per_device), jnp.bfloat16),
                jax.ShapeDtypeStruct((classes, LANES), jnp.float32),
            ]
            nears = [pltpu.with_memory_space_constraint(x, pltpu.VMEM) for x in rest[6:]]
            specs += [in_smem()] + [in_vmem()] * len(nears)
            rest = (*rest[:6], *nears)
        else:
            shapes = [jax.ShapeDtypeStruct(rest[4].shape, jnp.float32)]
    return pl.pallas_call(
        functools.partial(ring_kernel, phase, ends, sources),
        in_specs=[in_smem()] + [in_vmem()] * (3 + len(arrays)) + specs,
        out_specs=[in_vmem()] * len(shapes),
        out_shape=shapes,
        scratch_shapes=scratch,
        compiler_params=pltpu.CompilerParams(vmem_limit_bytes=VMEM_LIMIT),
        cost_estimate=pl.CostEstimate(
            flops=2 * 128 * per_device * freqs,
            bytes_accessed=per_device * freqs,
            transcendentals=0,
        ),
    )(
        where,
        noise,
        *(pltpu.with_memory_space_constraint(part, pltpu.VMEM) for part in turned),
        *arrays,
        *rest,
    )


def scatter_sum(pieces, blocks, bits):
    tail = pieces.shape[1:]
    zero = jnp.uint32(0)
    for step, (bit, other) in enumerate(bits):
        pairs = pieces.reshape((-1, 2) + tail)
        size = (pairs.shape[0], 1) + tail
        keep, send = (
            lax.dynamic_slice(pairs, (zero, which, zero, zero), size).reshape((-1,) + tail)
            for which in (bit, other)
        )
        swaps = [(block, block ^ (2 << step)) for block in range(blocks)]
        pieces = keep + lax.ppermute(send, "blk", swaps)
    return pieces[0]


def body(particles, significant, templates, template_class, class_counts, inv_noise):
    per_device, freqs = particles.shape
    classes = class_counts.shape[0]
    blocks = lax.axis_size("blk")
    owners = lax.axis_size("cls")
    order = ring_order(blocks)
    place = [order.index(block) for block in range(blocks)]
    block_id = lax.axis_index("blk")
    core = lax.axis_index("cls")
    ring = [(2 * order[i], 2 * order[(i + 1) % blocks]) for i in range(blocks)]
    ring += [(2 * order[(i + 1) % blocks] + 1, 2 * order[i] + 1) for i in range(blocks)]
    swap = [(i, owners - 1 - i) for i in range(owners)]

    noise = inv_noise[None, :]
    logs = jnp.log(class_counts.astype(jnp.float32))
    tags = template_class[None, :]
    *held, near_noise, picks = make_messages(tags, noise, significant, templates)
    where = jnp.stack([block_id, core])
    cut = freqs // 4
    per_owner = classes // owners
    bits = [
        lax.rem(lax.div(block_id, 2 << step), 2) for step in range(blocks.bit_length() - 2)
    ]
    bits = [(bit.astype(jnp.uint32), (1 - bit).astype(jnp.uint32)) for bit in bits]
    cut_at = core.astype(jnp.uint32) * cut
    where, cut_at, bits = lax.optimization_barrier((where, cut_at, bits))
    own = functools.partial(
        own_scores, blocks=blocks, where=where, noise=near_noise, particles=particles
    )
    total = blocks * templates.shape[0]
    words, *sums, low, high, near, raw = own([0, 1], templates=held[0], rest=(picks,), total=total)
    turned, nears = [(low, high)], [near, raw]
    gates = [sums]
    *sums, low, raw = own([2], templates=held[1], rest=(*sums, raw))
    nears.append(raw)
    gates.append(sums)
    state, high = own([3], templates=held[1], rest=(*sums, logs, tags, words, raw))
    turned.append((low, high))
    gates.append(state)
    width = freqs // blocks
    piece = jax.ShapeDtypeStruct((blocks // 2, per_owner, width + LANES), jnp.float32)
    last = blocks // 2
    for distance in range(1, last + 1):
        ends = distance == last
        tables = [
            [
                tuple(order[(place[block] - sign * distance) % blocks] for block in range(blocks))
                for sign in (1, -1)
            ]
        ]
        arrived = []
        for phase in range(2):
            message = held[phase]
            if ends:
                message = lax.dynamic_slice(
                    message,
                    (jnp.uint32(0), cut_at),
                    (message.shape[0], message.shape[1] - cut),
                )
            own = lax.ppermute(message, ("blk", "cls"), ring)
            lag = 3 if distance == 2 else 2
            gate = phase if distance == 1 else len(gates) - lag
            own, _ = lax.optimization_barrier((own, gates[gate]))
            pair = (own, lax.ppermute(own, "cls", swap))
            arrived.append(own)
            rest = (*sums, logs, words, state) if phase else ()
            if ends and phase:
                rest += (class_counts, *nears)
            sums = ring_scores(
                phase, tables, where, near_noise, turned[phase], pair, rest, ends, piece
            )
            gates.append(sums)
        held = arrived
        if not ends:
            (state,) = sums

    loglik, mine, theirs, rounded, totals = sums
    given = lax.ppermute(theirs, "cls", swap)
    across = lax.ppermute(mine + given, "blk", [(i, i ^ 1) for i in range(blocks)])
    rounded, _ = lax.optimization_barrier((rounded, given))
    mine, theirs = rest_sums(rounded, totals, nears, piece)
    kept = lax.optimization_barrier(mine + across)
    total = scatter_sum(kept + lax.ppermute(theirs, "cls", swap), blocks, bits)
    class_avg = total[:, :width] / total[:, width][:, None]
    return loglik[0], class_avg


def solution(mesh):
    placed = (
        P(("grp", "blk", "cls"), None),
        P(None, ("grp", "blk", "cls")),
        P(("grp", "blk"), None),
        P(("grp", "blk")),
        P("grp"),
        P(),
    )
    return jax.shard_map(
        body,
        mesh=mesh,
        in_specs=placed,
        out_specs=(P(("grp", "blk", "cls")), P(("grp", "cls"), "blk")),
        check_vma=False,
    )
```

```python
import functools

import jax
import jax.numpy as jnp
from jax import lax
from jax.experimental import pallas as pl
from jax.experimental.pallas import tpu as pltpu
from jax.sharding import PartitionSpec as P

LOWEST = -1e30
CHUNK = 1024
PIECES = 2
WIDTH = 1024
STRIP = 256
LANES = 128
STATE_ROWS = 8
VMEM_LIMIT = 6 * 1024 * 1024


def ring_order(blocks):
    if blocks <= 8:
        return list(range(0, blocks, 2)) + list(range(blocks - 1, 0, -2))
    return list(range(blocks))


def spread_copies(source, target, sent):
    count = sent.shape[0]
    rows = target.shape[0] // count
    return [
        pltpu.make_async_copy(
            source.at[pl.ds(at * rows, rows)], target.at[pl.ds(at * rows, rows)], sent.at[at]
        )
        for at in range(count)
    ]


def message_kernel(
    tags_ref, noise_ref, sig_ref, rows_ref,
    first_ref, second_ref, near_noise_ref, near_sig_ref, tags, sent, spread,
):
    height, span = first_ref.shape
    copies = [
        pltpu.make_async_copy(tags_ref, tags, sent.at[0]),
        pltpu.make_async_copy(noise_ref, near_noise_ref, sent.at[1]),
        pltpu.make_async_copy(sig_ref, near_sig_ref, sent.at[2]),
        *spread_copies(rows_ref.at[:, :span], first_ref, spread.at[0]),
        *spread_copies(rows_ref.at[:, span:], second_ref.at[:, :span], spread.at[1]),
    ]
    for copy in copies:
        copy.start()
    copies[0].wait()
    second_ref[:, span:] = tag_rows(tags, height).astype(jnp.bfloat16)
    for copy in copies[1:]:
        copy.wait()


def make_messages(tags, noise, significant, templates):
    height, freqs = templates.shape
    span = freqs // 2
    return pl.pallas_call(
        message_kernel,
        in_specs=[pl.BlockSpec(memory_space=pl.ANY)] * 4,
        out_specs=[in_vmem()] * 4,
        out_shape=[
            pltpu.VMEM((height, span), jnp.bfloat16),
            pltpu.VMEM((height, span + LANES), jnp.bfloat16),
            pltpu.VMEM(noise.shape, noise.dtype),
            pltpu.VMEM(significant.shape, significant.dtype),
        ],
        scratch_shapes=[
            pltpu.VMEM(tags.shape, tags.dtype),
            pltpu.SemaphoreType.DMA((3,)),
            pltpu.SemaphoreType.DMA((2, 4)),
        ],
        compiler_params=pltpu.CompilerParams(vmem_limit_bytes=VMEM_LIMIT),
    )(
        *(
            pltpu.with_memory_space_constraint(x, pltpu.HBM)
            for x in (tags, noise, significant, templates)
        )
    )


def tag_rows(tags_ref, height):
    row = lax.broadcasted_iota(jnp.int32, (height, height), 0)
    lane = lax.broadcasted_iota(jnp.int32, (height, height), 1)
    spread = jnp.where(row == lane, tags_ref[...].astype(jnp.float32), 0.0)
    return jnp.broadcast_to(jnp.sum(spread, axis=1, keepdims=True), (height, LANES))


def in_smem():
    return pl.BlockSpec(memory_space=pltpu.SMEM)


def in_vmem():
    return pl.BlockSpec(memory_space=pltpu.VMEM)


def weigh(rows, noise, energy):
    widened = rows.astype(jnp.float32)
    product = widened * noise
    square = product * widened
    folded = square[:, :LANES]
    for lane in range(LANES, square.shape[1], LANES):
        folded = folded + square[:, lane : lane + LANES]
    energy[...] += folded
    return product.astype(jnp.bfloat16)


def pick_words(sig_ref, words_ref):
    word = lax.broadcasted_iota(jnp.int32, words_ref.shape, 0)
    words = jnp.zeros(words_ref.shape, jnp.int32)
    for pick in range(sig_ref.shape[0]):
        chosen = sig_ref[pick : pick + 1, :]
        bit = jnp.left_shift(1, jnp.bitwise_and(chosen, 31))
        words = words | jnp.where(jnp.right_shift(chosen, 5) == word, bit, 0)
    words_ref[...] = words


def picked_rows(words_ref, source, height):
    bit = jnp.left_shift(1, lax.broadcasted_iota(jnp.int32, (32, 1), 0))
    rows = []
    for word in range(height // 32):
        rows.append((words_ref[pl.ds(source * (height // 32) + word, 1), :] & bit) != 0)
    return jnp.concatenate(rows, axis=0)


def add_rows(tags, hit, logs_ref, state, acc, energy):
    classes = logs_ref.shape[0]
    prior = jnp.zeros_like(tags[:, :1])
    for tag in range(classes):
        prior = jnp.where(tags[:, :1] == tag, logs_ref[tag], prior)
    bias = prior - 0.5 * jnp.sum(energy[...], axis=1, keepdims=True)
    scores = acc[...] + bias
    old_max, old_sum, old_top, weights = state
    new_max = jnp.maximum(old_max, jnp.max(scores, axis=0, keepdims=True))
    new_sum = old_sum * jnp.exp(old_max - new_max) + jnp.sum(
        jnp.exp(scores - new_max), axis=0, keepdims=True
    )
    new_top = jnp.maximum(
        old_top, jnp.max(jnp.where(hit, scores, LOWEST), axis=0, keepdims=True)
    )
    value = jnp.where(hit, jnp.exp(scores - new_top), 0.0)
    lane = lax.broadcasted_iota(jnp.int32, tags.shape, 1).astype(jnp.float32)
    onehot = jnp.transpose(jnp.where(tags == lane, 1.0, 0.0))[:classes, :].astype(jnp.bfloat16)
    weights = weights * jnp.exp(old_top - new_top)
    left = value
    for _ in range(3):
        piece = left.astype(jnp.bfloat16)
        left = left - piece.astype(jnp.float32)
        weights = weights + jnp.dot(onehot, piece, preferred_element_type=jnp.float32)
    return new_max, new_sum, new_top, weights


def put_state(state, out_ref):
    new_max, new_sum, new_top, weights = state
    out_ref[0:1, :] = new_max
    out_ref[1:2, :] = new_sum
    out_ref[2:3, :] = new_top
    out_ref[3:STATE_ROWS, :] = jnp.zeros_like(out_ref[3:STATE_ROWS, :])
    out_ref[STATE_ROWS:, :] = weights


def get_state(state_ref):
    return state_ref[0:1, :], state_ref[1:2, :], state_ref[2:3, :], state_ref[STATE_ROWS:, :]


def own_kernel(quarters, blocks, where_ref, noise_ref, tmpl_ref, far_ref, *rest):
    first, last = quarters[0] == 0, quarters[-1] == 3
    if first:
        sig_ref, words_ref, acc, energy, *turned_refs, near, next_ref, arrived, late = rest
    elif last:
        acc_in, energy_in, logs_ref, tags_ref, words_ref, near, out_ref, *rest = rest
        *turned_refs, acc, energy = rest
    else:
        acc_in, energy_in, near, acc, energy, *turned_refs, next_ref, late = rest
    span, height = turned_refs[0].shape[0], tmpl_ref.shape[0]
    chunks, _, chunk = near.shape
    steps = chunks * PIECES
    width = chunk // PIECES
    low = quarters[0] * span

    share = 4 * span // (blocks * width)
    bit = lax.rem(where_ref[0], 2)

    def part(ref, step):
        block, rest = lax.div(step, share), lax.rem(step, share)
        place = block - lax.rem(block, 2) + jnp.where(lax.rem(block, 2) == bit, 1, 0)
        piece = place * share + rest
        columns = pl.ds(pl.multiple_of(lax.rem(piece, PIECES) * width, width), width)
        return ref.at[lax.div(piece, PIECES), :, columns]

    def copies(step):
        columns = pl.ds(pl.multiple_of(low + step * width, width), width)
        return spread_copies(far_ref.at[:, columns], part(near, step), arrived.at[step])

    def following(step):
        columns = pl.ds(low + (steps + step) * width, width)
        return spread_copies(far_ref.at[:, columns], part(next_ref, step), late.at[step])

    if first:
        for step in range(steps):
            for copy in copies(step):
                copy.start()
    if not last:
        for step in range(next_ref.shape[0] * PIECES):
            for copy in following(step):
                copy.start()
    if first:
        pick_words(sig_ref, words_ref)
        acc[...] = jnp.zeros_like(acc)
        energy[...] = jnp.zeros_like(energy)
    else:
        acc[...] = acc_in[...]
        energy[...] = energy_in[...]
    for quarter, turned_ref in zip(quarters, turned_refs):

        @pl.loop(0, span // width)
        def _(inner):
            step = (quarter - quarters[0]) * (span // width) + inner
            if first:
                for copy in copies(step):
                    copy.wait()
            for strip in range(0, width, STRIP):
                there = pl.ds(pl.multiple_of(inner * width + strip, STRIP), STRIP)
                start = quarter % 2 * span + inner * width + strip
                here = pl.ds(pl.multiple_of(start, STRIP), STRIP)
                columns = pl.ds(pl.multiple_of(low + step * width + strip, STRIP), STRIP)
                weighted = weigh(tmpl_ref[:, here], noise_ref[:, columns], energy)
                turned = jnp.transpose(part(near, step)[:, strip : strip + STRIP])
                turned_ref[there, :] = turned
                acc[...] += jnp.dot(weighted, turned, preferred_element_type=jnp.float32)

    if not last:
        for step in range(next_ref.shape[0] * PIECES):
            for copy in following(step):
                copy.wait()
        return
    tags = tag_rows(tags_ref, height)
    hit = picked_rows(words_ref, where_ref[0], height)
    lowest = jnp.full((1, acc.shape[1]), LOWEST, jnp.float32)
    none = jnp.zeros((1, acc.shape[1]), jnp.float32)
    weights = jnp.zeros((logs_ref.shape[0], acc.shape[1]), jnp.float32)
    state = (lowest, none, lowest, weights)
    put_state(add_rows(tags, hit, logs_ref, state, acc, energy), out_ref)


def own_scores(quarters, blocks, where, noise, particles, templates, rest, total=0):
    per_device, freqs = particles.shape
    height = templates.shape[0]
    span = freqs // 4
    chunks = span // CHUNK
    steps = chunks * PIECES
    first, last = quarters[0] == 0, quarters[-1] == 3
    sums = [
        jax.ShapeDtypeStruct((height, per_device), jnp.float32),
        jax.ShapeDtypeStruct((height, LANES), jnp.float32),
    ]
    turned = [pltpu.VMEM((span, per_device), particles.dtype)] * len(quarters)
    raw = pltpu.VMEM((chunks, per_device, CHUNK), particles.dtype)
    if first:
        shapes = [jax.ShapeDtypeStruct((total // 32, per_device), jnp.int32)] + sums
        shapes += turned + [pltpu.VMEM((2 * chunks, per_device, CHUNK), particles.dtype), raw]
        rest_specs = [in_vmem()]
        scratch = [
            pltpu.SemaphoreType.DMA((2 * steps, 4)),
            pltpu.SemaphoreType.DMA((steps, 4)),
        ]
    elif last:
        rows = STATE_ROWS + rest[2].shape[0]
        shapes = [jax.ShapeDtypeStruct((rows, per_device), jnp.float32)] + turned
        rest_specs = [in_vmem(), in_vmem(), in_smem(), in_vmem(), in_vmem(), in_vmem()]
        scratch = [pltpu.VMEM(array.shape, array.dtype) for array in sums]
    else:
        shapes = sums + turned + [raw]
        rest_specs = [in_vmem()] * 3
        scratch = [pltpu.SemaphoreType.DMA((steps, 4))]
    if not first:
        rest = (*rest[:-1], pltpu.with_memory_space_constraint(rest[-1], pltpu.VMEM))
    return pl.pallas_call(
        functools.partial(own_kernel, quarters, blocks),
        in_specs=[in_smem(), in_vmem(), in_vmem(), pl.BlockSpec(memory_space=pl.ANY)] + rest_specs,
        out_specs=[in_vmem()] * len(shapes),
        out_shape=shapes,
        scratch_shapes=scratch,
        compiler_params=pltpu.CompilerParams(vmem_limit_bytes=VMEM_LIMIT),
        cost_estimate=pl.CostEstimate(
            flops=2 * 128 * per_device * freqs,
            bytes_accessed=per_device * freqs,
            transcendentals=0,
        ),
    )(where, noise, templates, pltpu.with_memory_space_constraint(particles, pltpu.HBM), *rest)


def class_weights(state, where_ref, counts_ref, per_owner):
    _, _, _, weights = state
    classes = weights.shape[0]
    row = lax.broadcasted_iota(jnp.int32, (classes, LANES), 0)
    counts = jnp.zeros((classes, LANES), jnp.float32)
    for tag in range(classes):
        mine = (where_ref[0] == 0) & (where_ref[1] == tag // per_owner)
        count = jnp.where(mine, counts_ref[tag], 0).astype(jnp.float32)
        counts = jnp.where(row == tag, count, counts)
    weights = weights / jnp.sum(weights, axis=0, keepdims=True)
    totals = jnp.sum(weights, axis=1, keepdims=True) + counts

    def own_first(rows):
        turned = jnp.concatenate([rows[per_owner:], rows[:per_owner]], axis=0)
        return jnp.where(where_ref[1] == 0, rows, turned)

    return own_first(weights).astype(jnp.bfloat16), own_first(totals)


def class_sums(rounded, totals, which, nears, mine_ref, theirs_ref):
    per_owner = mine_ref.shape[1]
    chunk = nears[0].shape[2]
    width = mine_ref.shape[2] - LANES
    piece = 0
    for near in nears:
        for pair in range(near.shape[0] * chunk // (2 * width)):
            at, low = divmod((2 * pair + which) * width, chunk)
            sums = jnp.dot(
                rounded, near[at, :, low : low + width], preferred_element_type=jnp.float32
            )
            mine_ref[piece, :, :width] = sums[:per_owner]
            theirs_ref[piece, :, :width] = sums[per_owner:]
            mine_ref[piece, :, width:] = totals[:per_owner]
            theirs_ref[piece, :, width:] = totals[per_owner:]
            piece += 1


def rest_kernel(rounded_ref, totals_ref, *rest):
    *nears, mine_ref, theirs_ref = rest
    class_sums(rounded_ref[...], totals_ref[...], 1, nears, mine_ref, theirs_ref)


def rest_sums(rounded, totals, nears, piece):
    classes, per_device = rounded.shape
    blocks = 2 * piece.shape[0]
    freqs = blocks * (piece.shape[2] - LANES)
    return pl.pallas_call(
        rest_kernel,
        in_specs=[in_vmem()] * (2 + len(nears)),
        out_specs=[in_vmem()] * 2,
        out_shape=[piece, piece],
        compiler_params=pltpu.CompilerParams(vmem_limit_bytes=VMEM_LIMIT),
        cost_estimate=pl.CostEstimate(
            flops=128 * per_device * freqs,
            bytes_accessed=per_device * freqs // 2,
            transcendentals=0,
        ),
    )(rounded, totals, *(pltpu.with_memory_space_constraint(x, pltpu.VMEM) for x in nears))


def ring_kernel(phase, ends, sources, where_ref, noise_ref, low_ref, high_ref, *rest):
    row_refs, rest = rest[: 2 * len(sources)], rest[2 * len(sources) :]
    if phase == 0:
        acc, energy = rest
    else:
        acc_in, energy_in, logs_ref, words_ref, state_ref, *rest = rest
        if ends:
            counts_ref, *nears, loglik_ref, mine_ref, theirs_ref = rest[:-4]
            rounded_ref, totals_ref, acc, energy = rest[-4:]
        else:
            out_ref, acc, energy = rest
    if phase == 0:
        acc[...] = jnp.zeros_like(acc)
        energy[...] = jnp.zeros_like(energy)
    else:
        acc[...] = acc_in[...]
        energy[...] = energy_in[...]
    quarter = low_ref.shape[0]
    core = where_ref[1]

    for at, part_ref in enumerate((low_ref, high_ref)):
        for step in range(quarter // WIDTH):
            there = pl.ds(step * WIDTH, WIDTH)
            columns = pl.ds((2 * phase + at) * quarter + step * WIDTH, WIDTH)
            if ends:
                rows = jnp.where(core == at, row_refs[0][:, there], row_refs[1][:, there])
            else:
                here = pl.ds(at * quarter + step * WIDTH, WIDTH)
                rows = jnp.concatenate([ref[:, here] for ref in row_refs], axis=0)
            weighted = weigh(rows, noise_ref[:, columns], energy)
            acc[...] += jnp.dot(weighted, part_ref[there, :], preferred_element_type=jnp.float32)

    if phase == 0:
        return
    height = row_refs[0].shape[0]
    span = quarter if ends else 2 * quarter
    tags = [ref[:, span:].astype(jnp.float32) for ref in row_refs]
    tags = jnp.where(core == 0, tags[1], tags[0]) if ends else jnp.concatenate(tags, axis=0)
    found = []
    for tables in sources:
        for table in tables:
            source = jnp.int32(table[0])
            for block in range(1, len(table)):
                source = jnp.where(where_ref[0] == block, table[block], source)
            found.append(source)
    if ends:
        found = found[:1]
    else:
        for at in range(0, len(found), 2):
            front, back = found[at : at + 2]
            found[at] = jnp.where(core == 0, front, back)
            found[at + 1] = jnp.where(core == 0, back, front)
    hit = jnp.concatenate([picked_rows(words_ref, source, height) for source in found], axis=0)
    state = add_rows(tags, hit, logs_ref, get_state(state_ref), acc, energy)
    if ends:
        loglik_ref[...] = state[0] + jnp.log(state[1])
        rounded, totals = class_weights(state, where_ref, counts_ref, mine_ref.shape[1])
        rounded_ref[...] = rounded
        totals_ref[...] = totals

        @pl.when(core >= 0)
        def _():
            class_sums(rounded_ref[...], totals_ref[...], 0, nears, mine_ref, theirs_ref)

    else:
        put_state(state, out_ref)


def ring_scores(phase, sources, where, noise, turned, arrays, rest, ends, piece):
    quarter, per_device = turned[0].shape
    freqs = 4 * quarter
    rows = arrays[0].shape[0] * (1 if ends else len(arrays))
    sums = [
        jax.ShapeDtypeStruct((rows, per_device), jnp.float32),
        jax.ShapeDtypeStruct((rows, LANES), jnp.float32),
    ]
    scratch = [pltpu.VMEM(array.shape, array.dtype) for array in sums]
    specs = []
    if phase == 0:
        shapes, scratch = sums, []
    else:
        specs = [in_vmem(), in_vmem(), in_smem(), in_vmem(), in_vmem()]
        if ends:
            classes = rest[2].shape[0]
            shapes = [
                jax.ShapeDtypeStruct((1, per_device), jnp.float32),
                piece,
                piece,
                jax.ShapeDtypeStruct((classes, per_device), jnp.bfloat16),
                jax.ShapeDtypeStruct((classes, LANES), jnp.float32),
            ]
            nears = [pltpu.with_memory_space_constraint(x, pltpu.VMEM) for x in rest[6:]]
            specs += [in_smem()] + [in_vmem()] * len(nears)
            rest = (*rest[:6], *nears)
        else:
            shapes = [jax.ShapeDtypeStruct(rest[4].shape, jnp.float32)]
    return pl.pallas_call(
        functools.partial(ring_kernel, phase, ends, sources),
        in_specs=[in_smem()] + [in_vmem()] * (3 + len(arrays)) + specs,
        out_specs=[in_vmem()] * len(shapes),
        out_shape=shapes,
        scratch_shapes=scratch,
        compiler_params=pltpu.CompilerParams(vmem_limit_bytes=VMEM_LIMIT),
        cost_estimate=pl.CostEstimate(
            flops=2 * 128 * per_device * freqs,
            bytes_accessed=per_device * freqs,
            transcendentals=0,
        ),
    )(
        where,
        noise,
        *(pltpu.with_memory_space_constraint(part, pltpu.VMEM) for part in turned),
        *arrays,
        *rest,
    )


def scatter_sum(pieces, blocks, bits):
    tail = pieces.shape[1:]
    zero = jnp.uint32(0)
    for step, (bit, other) in enumerate(bits):
        pairs = pieces.reshape((-1, 2) + tail)
        size = (pairs.shape[0], 1) + tail
        keep, send = (
            lax.dynamic_slice(pairs, (zero, which, zero, zero), size).reshape((-1,) + tail)
            for which in (bit, other)
        )
        swaps = [(block, block ^ (2 << step)) for block in range(blocks)]
        pieces = keep + lax.ppermute(send, "blk", swaps)
    return pieces[0]


def body(particles, significant, templates, template_class, class_counts, inv_noise):
    per_device, freqs = particles.shape
    classes = class_counts.shape[0]
    blocks = lax.axis_size("blk")
    owners = lax.axis_size("cls")
    order = ring_order(blocks)
    place = [order.index(block) for block in range(blocks)]
    block_id = lax.axis_index("blk")
    core = lax.axis_index("cls")
    ring = [(2 * order[i], 2 * order[(i + 1) % blocks]) for i in range(blocks)]
    ring += [(2 * order[(i + 1) % blocks] + 1, 2 * order[i] + 1) for i in range(blocks)]
    swap = [(i, owners - 1 - i) for i in range(owners)]

    noise = inv_noise[None, :]
    logs = jnp.log(class_counts.astype(jnp.float32))
    tags = template_class[None, :]
    *held, near_noise, picks = make_messages(tags, noise, significant, templates)
    where = jnp.stack([block_id, core])
    cut = freqs // 4
    per_owner = classes // owners
    bits = [
        lax.rem(lax.div(block_id, 2 << step), 2) for step in range(blocks.bit_length() - 2)
    ]
    bits = [(bit.astype(jnp.uint32), (1 - bit).astype(jnp.uint32)) for bit in bits]
    cut_at = core.astype(jnp.uint32) * cut
    where, cut_at, bits = lax.optimization_barrier((where, cut_at, bits))
    own = functools.partial(
        own_scores, blocks=blocks, where=where, noise=near_noise, particles=particles
    )
    total = blocks * templates.shape[0]
    words, *sums, low, high, near, raw = own([0, 1], templates=held[0], rest=(picks,), total=total)
    turned, nears = [(low, high)], [near, raw]
    gates = [sums]
    *sums, low, raw = own([2], templates=held[1], rest=(*sums, raw))
    nears.append(raw)
    gates.append(sums)
    state, high = own([3], templates=held[1], rest=(*sums, logs, tags, words, raw))
    turned.append((low, high))
    gates.append(state)
    width = freqs // blocks
    piece = jax.ShapeDtypeStruct((blocks // 2, per_owner, width + LANES), jnp.float32)
    last = blocks // 2
    for distance in range(1, last + 1):
        ends = distance == last
        tables = [
            [
                tuple(order[(place[block] - sign * distance) % blocks] for block in range(blocks))
                for sign in (1, -1)
            ]
        ]
        arrived = []
        for phase in range(2):
            message = held[phase]
            if ends:
                message = lax.dynamic_slice(
                    message,
                    (jnp.uint32(0), cut_at),
                    (message.shape[0], message.shape[1] - cut),
                )
            own = lax.ppermute(message, ("blk", "cls"), ring)
            lag = 3 if distance == 2 else 2
            gate = phase if distance == 1 else len(gates) - lag
            own, _ = lax.optimization_barrier((own, gates[gate]))
            pair = (own, lax.ppermute(own, "cls", swap))
            arrived.append(own)
            rest = (*sums, logs, words, state) if phase else ()
            if ends and phase:
                rest += (class_counts, *nears)
            sums = ring_scores(
                phase, tables, where, near_noise, turned[phase], pair, rest, ends, piece
            )
            gates.append(sums)
        held = arrived
        if not ends:
            (state,) = sums

    loglik, mine, theirs, rounded, totals = sums
    given = lax.ppermute(theirs, "cls", swap)
    across = lax.ppermute(mine + given, "blk", [(i, i ^ 1) for i in range(blocks)])
    rounded, _ = lax.optimization_barrier((rounded, given))
    mine, theirs = rest_sums(rounded, totals, nears, piece)
    kept = lax.optimization_barrier(mine + across)
    total = scatter_sum(kept + lax.ppermute(theirs, "cls", swap), blocks, bits)
    class_avg = total[:, :width] / total[:, width][:, None]
    return loglik[0], class_avg


def solution(mesh):
    placed = (
        P(("grp", "blk", "cls"), None),
        P(None, ("grp", "blk", "cls")),
        P(("grp", "blk"), None),
        P(("grp", "blk")),
        P("grp"),
        P(),
    )
    return jax.shard_map(
        body,
        mesh=mesh,
        in_specs=placed,
        out_specs=(P(("grp", "blk", "cls")), P(("grp", "cls"), "blk")),
        check_vma=False,
    )
```

```python
import functools

import jax
import jax.numpy as jnp
from jax import lax
from jax.experimental import pallas as pl
from jax.experimental.pallas import tpu as pltpu
from jax.sharding import PartitionSpec as P

LOWEST = -1e30
CHUNK = 1024
PIECES = 2
WIDTH = 1024
STRIP = 256
LANES = 128
STATE_ROWS = 8
VMEM_LIMIT = 6 * 1024 * 1024


def ring_order(blocks):
    if blocks <= 8:
        return list(range(0, blocks, 2)) + list(range(blocks - 1, 0, -2))
    return list(range(blocks))


def spread_copies(source, target, sent):
    count = sent.shape[0]
    rows = target.shape[0] // count
    return [
        pltpu.make_async_copy(
            source.at[pl.ds(at * rows, rows)], target.at[pl.ds(at * rows, rows)], sent.at[at]
        )
        for at in range(count)
    ]


def message_kernel(
    tags_ref, noise_ref, sig_ref, rows_ref,
    first_ref, second_ref, near_noise_ref, near_sig_ref, tags, sent, spread,
):
    height, span = first_ref.shape
    copies = [
        pltpu.make_async_copy(tags_ref, tags, sent.at[0]),
        pltpu.make_async_copy(noise_ref, near_noise_ref, sent.at[1]),
        pltpu.make_async_copy(sig_ref, near_sig_ref, sent.at[2]),
        *spread_copies(rows_ref.at[:, :span], first_ref, spread.at[0]),
        *spread_copies(rows_ref.at[:, span:], second_ref.at[:, :span], spread.at[1]),
    ]
    for copy in copies:
        copy.start()
    copies[0].wait()
    second_ref[:, span:] = tag_rows(tags, height).astype(jnp.bfloat16)
    for copy in copies[1:]:
        copy.wait()


def make_messages(tags, noise, significant, templates):
    height, freqs = templates.shape
    span = freqs // 2
    return pl.pallas_call(
        message_kernel,
        in_specs=[pl.BlockSpec(memory_space=pl.ANY)] * 4,
        out_specs=[in_vmem()] * 4,
        out_shape=[
            pltpu.VMEM((height, span), jnp.bfloat16),
            pltpu.VMEM((height, span + LANES), jnp.bfloat16),
            pltpu.VMEM(noise.shape, noise.dtype),
            pltpu.VMEM(significant.shape, significant.dtype),
        ],
        scratch_shapes=[
            pltpu.VMEM(tags.shape, tags.dtype),
            pltpu.SemaphoreType.DMA((3,)),
            pltpu.SemaphoreType.DMA((2, 4)),
        ],
        compiler_params=pltpu.CompilerParams(vmem_limit_bytes=VMEM_LIMIT),
    )(
        *(
            pltpu.with_memory_space_constraint(x, pltpu.HBM)
            for x in (tags, noise, significant, templates)
        )
    )


def tag_rows(tags_ref, height):
    row = lax.broadcasted_iota(jnp.int32, (height, height), 0)
    lane = lax.broadcasted_iota(jnp.int32, (height, height), 1)
    spread = jnp.where(row == lane, tags_ref[...].astype(jnp.float32), 0.0)
    return jnp.broadcast_to(jnp.sum(spread, axis=1, keepdims=True), (height, LANES))


def in_smem():
    return pl.BlockSpec(memory_space=pltpu.SMEM)


def in_vmem():
    return pl.BlockSpec(memory_space=pltpu.VMEM)


def weigh(rows, noise, energy):
    widened = rows.astype(jnp.float32)
    product = widened * noise
    square = product * widened
    folded = square[:, :LANES]
    for lane in range(LANES, square.shape[1], LANES):
        folded = folded + square[:, lane : lane + LANES]
    energy[...] += folded
    return product.astype(jnp.bfloat16)


def pick_words(sig_ref, words_ref):
    word = lax.broadcasted_iota(jnp.int32, words_ref.shape, 0)
    words = jnp.zeros(words_ref.shape, jnp.int32)
    for pick in range(sig_ref.shape[0]):
        chosen = sig_ref[pick : pick + 1, :]
        bit = jnp.left_shift(1, jnp.bitwise_and(chosen, 31))
        words = words | jnp.where(jnp.right_shift(chosen, 5) == word, bit, 0)
    words_ref[...] = words


def picked_rows(words_ref, source, height):
    bit = jnp.left_shift(1, lax.broadcasted_iota(jnp.int32, (32, 1), 0))
    rows = []
    for word in range(height // 32):
        rows.append((words_ref[pl.ds(source * (height // 32) + word, 1), :] & bit) != 0)
    return jnp.concatenate(rows, axis=0)


def add_rows(tags, hit, logs_ref, state, acc, energy):
    classes = logs_ref.shape[0]
    prior = jnp.zeros_like(tags[:, :1])
    for tag in range(classes):
        prior = jnp.where(tags[:, :1] == tag, logs_ref[tag], prior)
    bias = prior - 0.5 * jnp.sum(energy[...], axis=1, keepdims=True)
    scores = acc[...] + bias
    old_max, old_sum, old_top, weights = state
    new_max = jnp.maximum(old_max, jnp.max(scores, axis=0, keepdims=True))
    new_sum = old_sum * jnp.exp(old_max - new_max) + jnp.sum(
        jnp.exp(scores - new_max), axis=0, keepdims=True
    )
    new_top = jnp.maximum(
        old_top, jnp.max(jnp.where(hit, scores, LOWEST), axis=0, keepdims=True)
    )
    value = jnp.where(hit, jnp.exp(scores - new_top), 0.0)
    lane = lax.broadcasted_iota(jnp.int32, tags.shape, 1).astype(jnp.float32)
    onehot = jnp.transpose(jnp.where(tags == lane, 1.0, 0.0))[:classes, :].astype(jnp.bfloat16)
    weights = weights * jnp.exp(old_top - new_top)
    left = value
    for _ in range(3):
        piece = left.astype(jnp.bfloat16)
        left = left - piece.astype(jnp.float32)
        weights = weights + jnp.dot(onehot, piece, preferred_element_type=jnp.float32)
    return new_max, new_sum, new_top, weights


def put_state(state, out_ref):
    new_max, new_sum, new_top, weights = state
    out_ref[0:1, :] = new_max
    out_ref[1:2, :] = new_sum
    out_ref[2:3, :] = new_top
    out_ref[3:STATE_ROWS, :] = jnp.zeros_like(out_ref[3:STATE_ROWS, :])
    out_ref[STATE_ROWS:, :] = weights


def get_state(state_ref):
    return state_ref[0:1, :], state_ref[1:2, :], state_ref[2:3, :], state_ref[STATE_ROWS:, :]


def own_kernel(quarters, blocks, where_ref, noise_ref, tmpl_ref, far_ref, *rest):
    first, last = quarters[0] == 0, quarters[-1] == 3
    if first:
        sig_ref, words_ref, acc, energy, *turned_refs, near, next_ref, arrived, late = rest
    elif last:
        acc_in, energy_in, logs_ref, tags_ref, words_ref, near, out_ref, *rest = rest
        *turned_refs, acc, energy = rest
    else:
        acc_in, energy_in, near, acc, energy, *turned_refs, next_ref, late = rest
    span, height = turned_refs[0].shape[0], tmpl_ref.shape[0]
    chunks, _, chunk = near.shape
    steps = chunks * PIECES
    width = chunk // PIECES
    low = quarters[0] * span

    share = 4 * span // (blocks * width)
    bit = lax.rem(where_ref[0], 2)

    def part(ref, step):
        block, rest = lax.div(step, share), lax.rem(step, share)
        place = block - lax.rem(block, 2) + jnp.where(lax.rem(block, 2) == bit, 1, 0)
        piece = place * share + rest
        columns = pl.ds(pl.multiple_of(lax.rem(piece, PIECES) * width, width), width)
        return ref.at[lax.div(piece, PIECES), :, columns]

    def copies(step):
        columns = pl.ds(pl.multiple_of(low + step * width, width), width)
        return spread_copies(far_ref.at[:, columns], part(near, step), arrived.at[step])

    def following(step):
        columns = pl.ds(low + (steps + step) * width, width)
        return spread_copies(far_ref.at[:, columns], part(next_ref, step), late.at[step])

    if first:
        for step in range(steps):
            for copy in copies(step):
                copy.start()
    if not last:
        for step in range(next_ref.shape[0] * PIECES):
            for copy in following(step):
                copy.start()
    if first:
        pick_words(sig_ref, words_ref)
        acc[...] = jnp.zeros_like(acc)
        energy[...] = jnp.zeros_like(energy)
    else:
        acc[...] = acc_in[...]
        energy[...] = energy_in[...]
    for quarter, turned_ref in zip(quarters, turned_refs):

        @pl.loop(0, span // width)
        def _(inner):
            step = (quarter - quarters[0]) * (span // width) + inner
            if first:
                for copy in copies(step):
                    copy.wait()
            for strip in range(0, width, STRIP):
                there = pl.ds(pl.multiple_of(inner * width + strip, STRIP), STRIP)
                start = quarter % 2 * span + inner * width + strip
                here = pl.ds(pl.multiple_of(start, STRIP), STRIP)
                columns = pl.ds(pl.multiple_of(low + step * width + strip, STRIP), STRIP)
                weighted = weigh(tmpl_ref[:, here], noise_ref[:, columns], energy)
                turned = jnp.transpose(part(near, step)[:, strip : strip + STRIP])
                turned_ref[there, :] = turned
                acc[...] += jnp.dot(weighted, turned, preferred_element_type=jnp.float32)

    if not last:
        for step in range(next_ref.shape[0] * PIECES):
            for copy in following(step):
                copy.wait()
        return
    tags = tag_rows(tags_ref, height)
    hit = picked_rows(words_ref, where_ref[0], height)
    lowest = jnp.full((1, acc.shape[1]), LOWEST, jnp.float32)
    none = jnp.zeros((1, acc.shape[1]), jnp.float32)
    weights = jnp.zeros((logs_ref.shape[0], acc.shape[1]), jnp.float32)
    state = (lowest, none, lowest, weights)
    put_state(add_rows(tags, hit, logs_ref, state, acc, energy), out_ref)


def own_scores(quarters, blocks, where, noise, particles, templates, rest, total=0):
    per_device, freqs = particles.shape
    height = templates.shape[0]
    span = freqs // 4
    chunks = span // CHUNK
    steps = chunks * PIECES
    first, last = quarters[0] == 0, quarters[-1] == 3
    sums = [
        jax.ShapeDtypeStruct((height, per_device), jnp.float32),
        jax.ShapeDtypeStruct((height, LANES), jnp.float32),
    ]
    turned = [pltpu.VMEM((span, per_device), particles.dtype)] * len(quarters)
    raw = pltpu.VMEM((chunks, per_device, CHUNK), particles.dtype)
    if first:
        shapes = [jax.ShapeDtypeStruct((total // 32, per_device), jnp.int32)] + sums
        shapes += turned + [pltpu.VMEM((2 * chunks, per_device, CHUNK), particles.dtype), raw]
        rest_specs = [in_vmem()]
        scratch = [
            pltpu.SemaphoreType.DMA((2 * steps, 4)),
            pltpu.SemaphoreType.DMA((steps, 4)),
        ]
    elif last:
        rows = STATE_ROWS + rest[2].shape[0]
        shapes = [jax.ShapeDtypeStruct((rows, per_device), jnp.float32)] + turned
        rest_specs = [in_vmem(), in_vmem(), in_smem(), in_vmem(), in_vmem(), in_vmem()]
        scratch = [pltpu.VMEM(array.shape, array.dtype) for array in sums]
    else:
        shapes = sums + turned + [raw]
        rest_specs = [in_vmem()] * 3
        scratch = [pltpu.SemaphoreType.DMA((steps, 4))]
    if not first:
        rest = (*rest[:-1], pltpu.with_memory_space_constraint(rest[-1], pltpu.VMEM))
    return pl.pallas_call(
        functools.partial(own_kernel, quarters, blocks),
        in_specs=[in_smem(), in_vmem(), in_vmem(), pl.BlockSpec(memory_space=pl.ANY)] + rest_specs,
        out_specs=[in_vmem()] * len(shapes),
        out_shape=shapes,
        scratch_shapes=scratch,
        compiler_params=pltpu.CompilerParams(vmem_limit_bytes=VMEM_LIMIT),
        cost_estimate=pl.CostEstimate(
            flops=2 * 128 * per_device * freqs,
            bytes_accessed=per_device * freqs,
            transcendentals=0,
        ),
    )(where, noise, templates, pltpu.with_memory_space_constraint(particles, pltpu.HBM), *rest)


def class_weights(state, where_ref, counts_ref, per_owner):
    _, _, _, weights = state
    classes = weights.shape[0]
    row = lax.broadcasted_iota(jnp.int32, (classes, LANES), 0)
    counts = jnp.zeros((classes, LANES), jnp.float32)
    for tag in range(classes):
        mine = (where_ref[0] == 0) & (where_ref[1] == tag // per_owner)
        count = jnp.where(mine, counts_ref[tag], 0).astype(jnp.float32)
        counts = jnp.where(row == tag, count, counts)
    weights = weights / jnp.sum(weights, axis=0, keepdims=True)
    totals = jnp.sum(weights, axis=1, keepdims=True) + counts

    def own_first(rows):
        turned = jnp.concatenate([rows[per_owner:], rows[:per_owner]], axis=0)
        return jnp.where(where_ref[1] == 0, rows, turned)

    return own_first(weights).astype(jnp.bfloat16), own_first(totals)


def class_sums(rounded, totals, which, nears, mine_ref, theirs_ref):
    per_owner = mine_ref.shape[1]
    chunk = nears[0].shape[2]
    width = mine_ref.shape[2] - LANES
    piece = 0
    for near in nears:
        for pair in range(near.shape[0] * chunk // (2 * width)):
            at, low = divmod((2 * pair + which) * width, chunk)
            sums = jnp.dot(
                rounded, near[at, :, low : low + width], preferred_element_type=jnp.float32
            )
            mine_ref[piece, :, :width] = sums[:per_owner]
            theirs_ref[piece, :, :width] = sums[per_owner:]
            mine_ref[piece, :, width:] = totals[:per_owner]
            theirs_ref[piece, :, width:] = totals[per_owner:]
            piece += 1


def rest_kernel(rounded_ref, totals_ref, *rest):
    *nears, mine_ref, theirs_ref = rest
    class_sums(rounded_ref[...], totals_ref[...], 1, nears, mine_ref, theirs_ref)


def rest_sums(rounded, totals, nears, piece):
    classes, per_device = rounded.shape
    blocks = 2 * piece.shape[0]
    freqs = blocks * (piece.shape[2] - LANES)
    return pl.pallas_call(
        rest_kernel,
        in_specs=[in_vmem()] * (2 + len(nears)),
        out_specs=[in_vmem()] * 2,
        out_shape=[piece, piece],
        compiler_params=pltpu.CompilerParams(vmem_limit_bytes=VMEM_LIMIT),
        cost_estimate=pl.CostEstimate(
            flops=128 * per_device * freqs,
            bytes_accessed=per_device * freqs // 2,
            transcendentals=0,
        ),
    )(rounded, totals, *(pltpu.with_memory_space_constraint(x, pltpu.VMEM) for x in nears))


def ring_kernel(phase, ends, sources, where_ref, noise_ref, low_ref, high_ref, *rest):
    row_refs, rest = rest[: 2 * len(sources)], rest[2 * len(sources) :]
    if phase == 0:
        acc, energy = rest
    else:
        acc_in, energy_in, logs_ref, words_ref, state_ref, *rest = rest
        if ends:
            counts_ref, *nears, loglik_ref, mine_ref, theirs_ref = rest[:-4]
            rounded_ref, totals_ref, acc, energy = rest[-4:]
        else:
            out_ref, acc, energy = rest
    if phase == 0:
        acc[...] = jnp.zeros_like(acc)
        energy[...] = jnp.zeros_like(energy)
    else:
        acc[...] = acc_in[...]
        energy[...] = energy_in[...]
    quarter = low_ref.shape[0]
    core = where_ref[1]

    for at, part_ref in enumerate((low_ref, high_ref)):

        def add(step):
            there = pl.ds(pl.multiple_of(step * WIDTH, WIDTH), WIDTH)
            begin = (2 * phase + at) * quarter + step * WIDTH
            columns = pl.ds(pl.multiple_of(begin, WIDTH), WIDTH)
            if ends:
                rows = jnp.where(core == at, row_refs[0][:, there], row_refs[1][:, there])
            else:
                here = pl.ds(pl.multiple_of(at * quarter + step * WIDTH, WIDTH), WIDTH)
                rows = jnp.concatenate([ref[:, here] for ref in row_refs], axis=0)
            weighted = weigh(rows, noise_ref[:, columns], energy)
            acc[...] += jnp.dot(weighted, part_ref[there, :], preferred_element_type=jnp.float32)

        if ends and phase == 1:
            pl.loop(0, quarter // WIDTH)(add)
        else:
            for step in range(quarter // WIDTH):
                add(step)

    if phase == 0:
        return
    height = row_refs[0].shape[0]
    span = quarter if ends else 2 * quarter
    tags = [ref[:, span:].astype(jnp.float32) for ref in row_refs]
    tags = jnp.where(core == 0, tags[1], tags[0]) if ends else jnp.concatenate(tags, axis=0)
    found = []
    for tables in sources:
        for table in tables:
            source = jnp.int32(table[0])
            for block in range(1, len(table)):
                source = jnp.where(where_ref[0] == block, table[block], source)
            found.append(source)
    if ends:
        found = found[:1]
    else:
        for at in range(0, len(found), 2):
            front, back = found[at : at + 2]
            found[at] = jnp.where(core == 0, front, back)
            found[at + 1] = jnp.where(core == 0, back, front)
    hit = jnp.concatenate([picked_rows(words_ref, source, height) for source in found], axis=0)
    state = add_rows(tags, hit, logs_ref, get_state(state_ref), acc, energy)
    if ends:
        loglik_ref[...] = state[0] + jnp.log(state[1])
        rounded, totals = class_weights(state, where_ref, counts_ref, mine_ref.shape[1])
        rounded_ref[...] = rounded
        totals_ref[...] = totals
        class_sums(rounded, totals, 0, nears, mine_ref, theirs_ref)
    else:
        put_state(state, out_ref)


def ring_scores(phase, sources, where, noise, turned, arrays, rest, ends, piece):
    quarter, per_device = turned[0].shape
    freqs = 4 * quarter
    rows = arrays[0].shape[0] * (1 if ends else len(arrays))
    sums = [
        jax.ShapeDtypeStruct((rows, per_device), jnp.float32),
        jax.ShapeDtypeStruct((rows, LANES), jnp.float32),
    ]
    scratch = [pltpu.VMEM(array.shape, array.dtype) for array in sums]
    specs = []
    if phase == 0:
        shapes, scratch = sums, []
    else:
        specs = [in_vmem(), in_vmem(), in_smem(), in_vmem(), in_vmem()]
        if ends:
            classes = rest[2].shape[0]
            shapes = [
                jax.ShapeDtypeStruct((1, per_device), jnp.float32),
                piece,
                piece,
                jax.ShapeDtypeStruct((classes, per_device), jnp.bfloat16),
                jax.ShapeDtypeStruct((classes, LANES), jnp.float32),
            ]
            nears = [pltpu.with_memory_space_constraint(x, pltpu.VMEM) for x in rest[6:]]
            specs += [in_smem()] + [in_vmem()] * len(nears)
            rest = (*rest[:6], *nears)
        else:
            shapes = [jax.ShapeDtypeStruct(rest[4].shape, jnp.float32)]
    return pl.pallas_call(
        functools.partial(ring_kernel, phase, ends, sources),
        in_specs=[in_smem()] + [in_vmem()] * (3 + len(arrays)) + specs,
        out_specs=[in_vmem()] * len(shapes),
        out_shape=shapes,
        scratch_shapes=scratch,
        compiler_params=pltpu.CompilerParams(vmem_limit_bytes=VMEM_LIMIT),
        cost_estimate=pl.CostEstimate(
            flops=2 * 128 * per_device * freqs,
            bytes_accessed=per_device * freqs,
            transcendentals=0,
        ),
    )(
        where,
        noise,
        *(pltpu.with_memory_space_constraint(part, pltpu.VMEM) for part in turned),
        *arrays,
        *rest,
    )


def scatter_sum(pieces, blocks, bits):
    tail = pieces.shape[1:]
    zero = jnp.uint32(0)
    for step, (bit, other) in enumerate(bits):
        pairs = pieces.reshape((-1, 2) + tail)
        size = (pairs.shape[0], 1) + tail
        keep, send = (
            lax.dynamic_slice(pairs, (zero, which, zero, zero), size).reshape((-1,) + tail)
            for which in (bit, other)
        )
        swaps = [(block, block ^ (2 << step)) for block in range(blocks)]
        pieces = keep + lax.ppermute(send, "blk", swaps)
    return pieces[0]


def body(particles, significant, templates, template_class, class_counts, inv_noise):
    per_device, freqs = particles.shape
    classes = class_counts.shape[0]
    blocks = lax.axis_size("blk")
    owners = lax.axis_size("cls")
    order = ring_order(blocks)
    place = [order.index(block) for block in range(blocks)]
    block_id = lax.axis_index("blk")
    core = lax.axis_index("cls")
    ring = [(2 * order[i], 2 * order[(i + 1) % blocks]) for i in range(blocks)]
    ring += [(2 * order[(i + 1) % blocks] + 1, 2 * order[i] + 1) for i in range(blocks)]
    swap = [(i, owners - 1 - i) for i in range(owners)]

    noise = inv_noise[None, :]
    logs = jnp.log(class_counts.astype(jnp.float32))
    tags = template_class[None, :]
    *held, near_noise, picks = make_messages(tags, noise, significant, templates)
    where = jnp.stack([block_id, core])
    cut = freqs // 4
    per_owner = classes // owners
    bits = [
        lax.rem(lax.div(block_id, 2 << step), 2) for step in range(blocks.bit_length() - 2)
    ]
    bits = [(bit.astype(jnp.uint32), (1 - bit).astype(jnp.uint32)) for bit in bits]
    cut_at = core.astype(jnp.uint32) * cut
    where, cut_at, bits = lax.optimization_barrier((where, cut_at, bits))
    own = functools.partial(
        own_scores, blocks=blocks, where=where, noise=near_noise, particles=particles
    )
    total = blocks * templates.shape[0]
    words, *sums, low, high, near, raw = own([0, 1], templates=held[0], rest=(picks,), total=total)
    turned, nears = [(low, high)], [near, raw]
    gates = [sums]
    *sums, low, raw = own([2], templates=held[1], rest=(*sums, raw))
    nears.append(raw)
    gates.append(sums)
    state, high = own([3], templates=held[1], rest=(*sums, logs, tags, words, raw))
    turned.append((low, high))
    gates.append(state)
    width = freqs // blocks
    piece = jax.ShapeDtypeStruct((blocks // 2, per_owner, width + LANES), jnp.float32)
    last = blocks // 2
    for distance in range(1, last + 1):
        ends = distance == last
        tables = [
            [
                tuple(order[(place[block] - sign * distance) % blocks] for block in range(blocks))
                for sign in (1, -1)
            ]
        ]
        arrived = []
        for phase in range(2):
            message = held[phase]
            if ends:
                message = lax.dynamic_slice(
                    message,
                    (jnp.uint32(0), cut_at),
                    (message.shape[0], message.shape[1] - cut),
                )
            own = lax.ppermute(message, ("blk", "cls"), ring)
            lag = 3 if distance == 2 else 2
            gate = phase if distance == 1 else len(gates) - lag
            own, _ = lax.optimization_barrier((own, gates[gate]))
            pair = (own, lax.ppermute(own, "cls", swap))
            arrived.append(own)
            rest = (*sums, logs, words, state) if phase else ()
            if ends and phase:
                rest += (class_counts, *nears)
            sums = ring_scores(
                phase, tables, where, near_noise, turned[phase], pair, rest, ends, piece
            )
            gates.append(sums)
        held = arrived
        if not ends:
            (state,) = sums

    loglik, mine, theirs, rounded, totals = sums
    given = lax.ppermute(theirs, "cls", swap)
    across = lax.ppermute(mine + given, "blk", [(i, i ^ 1) for i in range(blocks)])
    rounded, _ = lax.optimization_barrier((rounded, given))
    mine, theirs = rest_sums(rounded, totals, nears, piece)
    kept = lax.optimization_barrier(mine + across)
    total = scatter_sum(kept + lax.ppermute(theirs, "cls", swap), blocks, bits)
    class_avg = total[:, :width] / total[:, width][:, None]
    return loglik[0], class_avg


def solution(mesh):
    placed = (
        P(("grp", "blk", "cls"), None),
        P(None, ("grp", "blk", "cls")),
        P(("grp", "blk"), None),
        P(("grp", "blk")),
        P("grp"),
        P(),
    )
    return jax.shard_map(
        body,
        mesh=mesh,
        in_specs=placed,
        out_specs=(P(("grp", "blk", "cls")), P(("grp", "cls"), "blk")),
        check_vma=False,
    )
```

```python
import functools

import jax
import jax.numpy as jnp
from jax import lax
from jax.experimental import pallas as pl
from jax.experimental.pallas import tpu as pltpu
from jax.sharding import PartitionSpec as P

LOWEST = -1e30
STEPS = 16
WIDTH = 1024
STRIP = 256
LANES = 128
STATE_ROWS = 8
VMEM_LIMIT = 6 * 1024 * 1024


def ring_order(blocks):
    if blocks <= 8:
        return list(range(0, blocks, 2)) + list(range(blocks - 1, 0, -2))
    return list(range(blocks))


def spread_copies(source, target, sent):
    count = sent.shape[0]
    rows = target.shape[0] // count
    return [
        pltpu.make_async_copy(
            source.at[pl.ds(at * rows, rows)], target.at[pl.ds(at * rows, rows)], sent.at[at]
        )
        for at in range(count)
    ]


def message_kernel(
    tags_ref, noise_ref, sig_ref, rows_ref,
    first_ref, second_ref, near_noise_ref, near_sig_ref, tags, sent, spread,
):
    height, span = first_ref.shape
    copies = [
        pltpu.make_async_copy(tags_ref, tags, sent.at[0]),
        pltpu.make_async_copy(noise_ref, near_noise_ref, sent.at[1]),
        pltpu.make_async_copy(sig_ref, near_sig_ref, sent.at[2]),
        *spread_copies(rows_ref.at[:, :span], first_ref, spread.at[0]),
        *spread_copies(rows_ref.at[:, span:], second_ref.at[:, :span], spread.at[1]),
    ]
    for copy in copies:
        copy.start()
    copies[0].wait()
    second_ref[:, span:] = tag_rows(tags, height).astype(jnp.bfloat16)
    for copy in copies[1:]:
        copy.wait()


def make_messages(tags, noise, significant, templates):
    height, freqs = templates.shape
    span = freqs // 2
    return pl.pallas_call(
        message_kernel,
        in_specs=[pl.BlockSpec(memory_space=pl.ANY)] * 4,
        out_specs=[in_vmem()] * 4,
        out_shape=[
            pltpu.VMEM((height, span), jnp.bfloat16),
            pltpu.VMEM((height, span + LANES), jnp.bfloat16),
            pltpu.VMEM(noise.shape, noise.dtype),
            pltpu.VMEM(significant.shape, significant.dtype),
        ],
        scratch_shapes=[
            pltpu.VMEM(tags.shape, tags.dtype),
            pltpu.SemaphoreType.DMA((3,)),
            pltpu.SemaphoreType.DMA((2, 4)),
        ],
        compiler_params=pltpu.CompilerParams(vmem_limit_bytes=VMEM_LIMIT),
    )(
        *(
            pltpu.with_memory_space_constraint(x, pltpu.HBM)
            for x in (tags, noise, significant, templates)
        )
    )


def tag_rows(tags_ref, height):
    row = lax.broadcasted_iota(jnp.int32, (height, height), 0)
    lane = lax.broadcasted_iota(jnp.int32, (height, height), 1)
    spread = jnp.where(row == lane, tags_ref[...].astype(jnp.float32), 0.0)
    return jnp.broadcast_to(jnp.sum(spread, axis=1, keepdims=True), (height, LANES))


def in_smem():
    return pl.BlockSpec(memory_space=pltpu.SMEM)


def in_vmem():
    return pl.BlockSpec(memory_space=pltpu.VMEM)


def weigh(rows, noise, energy):
    widened = rows.astype(jnp.float32)
    product = widened * noise
    square = product * widened
    folded = square[:, :LANES]
    for lane in range(LANES, square.shape[1], LANES):
        folded = folded + square[:, lane : lane + LANES]
    energy[...] += folded
    return product.astype(jnp.bfloat16)


def pick_words(sig_ref, words_ref):
    word = lax.broadcasted_iota(jnp.int32, words_ref.shape, 0)
    words = jnp.zeros(words_ref.shape, jnp.int32)
    for pick in range(sig_ref.shape[0]):
        chosen = sig_ref[pick : pick + 1, :]
        bit = jnp.left_shift(1, jnp.bitwise_and(chosen, 31))
        words = words | jnp.where(jnp.right_shift(chosen, 5) == word, bit, 0)
    words_ref[...] = words


def picked_rows(words_ref, source, height):
    bit = jnp.left_shift(1, lax.broadcasted_iota(jnp.int32, (32, 1), 0))
    rows = []
    for word in range(height // 32):
        rows.append((words_ref[pl.ds(source * (height // 32) + word, 1), :] & bit) != 0)
    return jnp.concatenate(rows, axis=0)


def add_rows(tags, hit, logs_ref, state, acc, energy):
    classes = logs_ref.shape[0]
    prior = jnp.zeros_like(tags[:, :1])
    for tag in range(classes):
        prior = jnp.where(tags[:, :1] == tag, logs_ref[tag], prior)
    bias = prior - 0.5 * jnp.sum(energy[...], axis=1, keepdims=True)
    scores = acc[...] + bias
    old_max, old_sum, old_top, weights = state
    new_max = jnp.maximum(old_max, jnp.max(scores, axis=0, keepdims=True))
    new_sum = old_sum * jnp.exp(old_max - new_max) + jnp.sum(
        jnp.exp(scores - new_max), axis=0, keepdims=True
    )
    new_top = jnp.maximum(
        old_top, jnp.max(jnp.where(hit, scores, LOWEST), axis=0, keepdims=True)
    )
    value = jnp.where(hit, jnp.exp(scores - new_top), 0.0)
    lane = lax.broadcasted_iota(jnp.int32, tags.shape, 1).astype(jnp.float32)
    onehot = jnp.transpose(jnp.where(tags == lane, 1.0, 0.0))[:classes, :].astype(jnp.bfloat16)
    weights = weights * jnp.exp(old_top - new_top)
    left = value
    for _ in range(3):
        piece = left.astype(jnp.bfloat16)
        left = left - piece.astype(jnp.float32)
        weights = weights + jnp.dot(onehot, piece, preferred_element_type=jnp.float32)
    return new_max, new_sum, new_top, weights


def put_state(state, out_ref):
    new_max, new_sum, new_top, weights = state
    out_ref[0:1, :] = new_max
    out_ref[1:2, :] = new_sum
    out_ref[2:3, :] = new_top
    out_ref[3:STATE_ROWS, :] = jnp.zeros_like(out_ref[3:STATE_ROWS, :])
    out_ref[STATE_ROWS:, :] = weights


def get_state(state_ref):
    return state_ref[0:1, :], state_ref[1:2, :], state_ref[2:3, :], state_ref[STATE_ROWS:, :]


def own_kernel(quarters, where_ref, noise_ref, tmpl_ref, far_ref, *rest):
    first, last = quarters[0] == 0, quarters[-1] == 3
    if first:
        sig_ref, words_ref, acc, energy, *turned_refs, near, next_ref, arrived, late = rest
    elif last:
        acc_in, energy_in, logs_ref, tags_ref, words_ref, near, out_ref, *rest = rest
        *turned_refs, acc, energy = rest
    else:
        acc_in, energy_in, near, acc, energy, *turned_refs, next_ref, late = rest
    span, height = turned_refs[0].shape[0], tmpl_ref.shape[0]
    steps, _, width = near.shape
    low = quarters[0] * span

    def copies(step):
        columns = pl.ds(pl.multiple_of(low + step * width, width), width)
        return spread_copies(far_ref.at[:, columns], near.at[step], arrived.at[step])

    def following(step):
        columns = pl.ds(low + (steps + step) * width, width)
        return spread_copies(far_ref.at[:, columns], next_ref.at[step], late.at[step])

    if first:
        for step in range(steps):
            for copy in copies(step):
                copy.start()
    if not last:
        for step in range(next_ref.shape[0]):
            for copy in following(step):
                copy.start()
    if first:
        pick_words(sig_ref, words_ref)
        acc[...] = jnp.zeros_like(acc)
        energy[...] = jnp.zeros_like(energy)
    else:
        acc[...] = acc_in[...]
        energy[...] = energy_in[...]
    for quarter, turned_ref in zip(quarters, turned_refs):

        @pl.loop(0, span // width)
        def _(inner):
            step = (quarter - quarters[0]) * (span // width) + inner
            if first:
                for copy in copies(step):
                    copy.wait()
            for strip in range(0, width, STRIP):
                there = pl.ds(pl.multiple_of(inner * width + strip, STRIP), STRIP)
                part = quarter % 2 * span + inner * width + strip
                here = pl.ds(pl.multiple_of(part, STRIP), STRIP)
                columns = pl.ds(pl.multiple_of(low + step * width + strip, STRIP), STRIP)
                weighted = weigh(tmpl_ref[:, here], noise_ref[:, columns], energy)
                turned = jnp.transpose(near[step, :, strip : strip + STRIP])
                turned_ref[there, :] = turned
                acc[...] += jnp.dot(weighted, turned, preferred_element_type=jnp.float32)

    if not last:
        for step in range(next_ref.shape[0]):
            for copy in following(step):
                copy.wait()
        return
    tags = tag_rows(tags_ref, height)
    hit = picked_rows(words_ref, where_ref[0], height)
    lowest = jnp.full((1, acc.shape[1]), LOWEST, jnp.float32)
    none = jnp.zeros((1, acc.shape[1]), jnp.float32)
    weights = jnp.zeros((logs_ref.shape[0], acc.shape[1]), jnp.float32)
    state = (lowest, none, lowest, weights)
    put_state(add_rows(tags, hit, logs_ref, state, acc, energy), out_ref)


def own_scores(quarters, where, noise, particles, templates, rest, total=0):
    per_device, freqs = particles.shape
    height = templates.shape[0]
    width = freqs // STEPS
    span = freqs // 4
    steps = span // width
    first, last = quarters[0] == 0, quarters[-1] == 3
    sums = [
        jax.ShapeDtypeStruct((height, per_device), jnp.float32),
        jax.ShapeDtypeStruct((height, LANES), jnp.float32),
    ]
    turned = [pltpu.VMEM((span, per_device), particles.dtype)] * len(quarters)
    raw = pltpu.VMEM((steps, per_device, width), particles.dtype)
    if first:
        shapes = [jax.ShapeDtypeStruct((total // 32, per_device), jnp.int32)] + sums
        shapes += turned + [pltpu.VMEM((2 * steps, per_device, width), particles.dtype), raw]
        rest_specs = [in_vmem()]
        scratch = [
            pltpu.SemaphoreType.DMA((2 * steps, 4)),
            pltpu.SemaphoreType.DMA((steps, 4)),
        ]
    elif last:
        rows = STATE_ROWS + rest[2].shape[0]
        shapes = [jax.ShapeDtypeStruct((rows, per_device), jnp.float32)] + turned
        rest_specs = [in_vmem(), in_vmem(), in_smem(), in_vmem(), in_vmem(), in_vmem()]
        scratch = [pltpu.VMEM(array.shape, array.dtype) for array in sums]
    else:
        shapes = sums + turned + [raw]
        rest_specs = [in_vmem()] * 3
        scratch = [pltpu.SemaphoreType.DMA((steps, 4))]
    if not first:
        rest = (*rest[:-1], pltpu.with_memory_space_constraint(rest[-1], pltpu.VMEM))
    return pl.pallas_call(
        functools.partial(own_kernel, quarters),
        in_specs=[in_smem(), in_vmem(), in_vmem(), pl.BlockSpec(memory_space=pl.ANY)] + rest_specs,
        out_specs=[in_vmem()] * len(shapes),
        out_shape=shapes,
        scratch_shapes=scratch,
        compiler_params=pltpu.CompilerParams(vmem_limit_bytes=VMEM_LIMIT),
        cost_estimate=pl.CostEstimate(
            flops=2 * 128 * per_device * freqs,
            bytes_accessed=per_device * freqs,
            transcendentals=0,
        ),
    )(where, noise, templates, pltpu.with_memory_space_constraint(particles, pltpu.HBM), *rest)


def class_weights(state, where_ref, counts_ref, per_owner):
    _, _, _, weights = state
    classes = weights.shape[0]
    row = lax.broadcasted_iota(jnp.int32, (classes, LANES), 0)
    counts = jnp.zeros((classes, LANES), jnp.float32)
    for tag in range(classes):
        mine = (where_ref[0] == 0) & (where_ref[1] == tag // per_owner)
        count = jnp.where(mine, counts_ref[tag], 0).astype(jnp.float32)
        counts = jnp.where(row == tag, count, counts)
    weights = weights / jnp.sum(weights, axis=0, keepdims=True)
    totals = jnp.sum(weights, axis=1, keepdims=True) + counts

    def own_first(rows):
        turned = jnp.concatenate([rows[per_owner:], rows[:per_owner]], axis=0)
        return jnp.where(where_ref[1] == 0, rows, turned)

    return own_first(weights).astype(jnp.bfloat16), own_first(totals)


def class_sums(rounded, totals, bit, nears, mine_ref, theirs_ref):
    per_owner = mine_ref.shape[1]
    chunk = nears[0].shape[2]
    share = mine_ref.shape[2] // chunk
    piece = 0
    for near in nears:
        for pair in range(near.shape[0] // (2 * share)):
            for part in range(share):
                at = (2 * pair + bit) * share + part
                sums = jnp.dot(rounded, near[at], preferred_element_type=jnp.float32)
                columns = pl.ds(part * chunk, chunk)
                mine_ref[piece, :, columns] = sums[:per_owner]
                theirs_ref[piece, :, columns] = sums[per_owner:]
            mine_ref[piece, :, share * chunk :] = totals[:per_owner]
            theirs_ref[piece, :, share * chunk :] = totals[per_owner:]
            piece += 1


def rest_kernel(where_ref, rounded_ref, totals_ref, *rest):
    *nears, mine_ref, theirs_ref = rest
    bit = lax.rem(where_ref[0], 2)
    class_sums(rounded_ref[...], totals_ref[...], bit, nears, mine_ref, theirs_ref)


def rest_sums(where, rounded, totals, nears, piece):
    classes, per_device = rounded.shape
    blocks = 2 * piece.shape[0]
    freqs = blocks * (piece.shape[2] - LANES)
    return pl.pallas_call(
        rest_kernel,
        in_specs=[in_smem()] + [in_vmem()] * (2 + len(nears)),
        out_specs=[in_vmem()] * 2,
        out_shape=[piece, piece],
        compiler_params=pltpu.CompilerParams(vmem_limit_bytes=VMEM_LIMIT),
        cost_estimate=pl.CostEstimate(
            flops=128 * per_device * freqs,
            bytes_accessed=per_device * freqs // 2,
            transcendentals=0,
        ),
    )(where, rounded, totals, *(pltpu.with_memory_space_constraint(x, pltpu.VMEM) for x in nears))


def ring_kernel(phase, ends, sources, *rest):
    where_ref = None
    if phase or ends:
        where_ref, *rest = rest
    noise_ref, low_ref, high_ref, *rest = rest
    row_refs, rest = rest[: 2 * len(sources)], rest[2 * len(sources) :]
    if phase == 0:
        acc, energy = rest
    else:
        acc_in, energy_in, logs_ref, words_ref, state_ref, *rest = rest
        if ends:
            counts_ref, *nears, loglik_ref, mine_ref, theirs_ref = rest[:-4]
            rounded_ref, totals_ref, acc, energy = rest[-4:]
        else:
            out_ref, acc, energy = rest
    if phase == 0:
        acc[...] = jnp.zeros_like(acc)
        energy[...] = jnp.zeros_like(energy)
    else:
        acc[...] = acc_in[...]
        energy[...] = energy_in[...]
    quarter = low_ref.shape[0]
    core = where_ref[1] if phase or ends else None

    for at, part_ref in enumerate((low_ref, high_ref)):
        for step in range(quarter // WIDTH):
            there = pl.ds(step * WIDTH, WIDTH)
            columns = pl.ds((2 * phase + at) * quarter + step * WIDTH, WIDTH)
            if ends:
                rows = jnp.where(core == at, row_refs[0][:, there], row_refs[1][:, there])
            else:
                here = pl.ds(at * quarter + step * WIDTH, WIDTH)
                rows = jnp.concatenate([ref[:, here] for ref in row_refs], axis=0)
            weighted = weigh(rows, noise_ref[:, columns], energy)
            acc[...] += jnp.dot(weighted, part_ref[there, :], preferred_element_type=jnp.float32)

    if phase == 0:
        return
    height = row_refs[0].shape[0]
    span = quarter if ends else 2 * quarter
    tags = [ref[:, span:].astype(jnp.float32) for ref in row_refs]
    tags = jnp.where(core == 0, tags[1], tags[0]) if ends else jnp.concatenate(tags, axis=0)
    found = []
    for tables in sources:
        for table in tables:
            source = jnp.int32(table[0])
            for block in range(1, len(table)):
                source = jnp.where(where_ref[0] == block, table[block], source)
            found.append(source)
    if ends:
        found = found[:1]
    else:
        for at in range(0, len(found), 2):
            front, back = found[at : at + 2]
            found[at] = jnp.where(core == 0, front, back)
            found[at + 1] = jnp.where(core == 0, back, front)
    hit = jnp.concatenate([picked_rows(words_ref, source, height) for source in found], axis=0)
    state = add_rows(tags, hit, logs_ref, get_state(state_ref), acc, energy)
    if ends:
        loglik_ref[...] = state[0] + jnp.log(state[1])
        rounded, totals = class_weights(state, where_ref, counts_ref, mine_ref.shape[1])
        rounded_ref[...] = rounded
        totals_ref[...] = totals
        bit = 1 - lax.rem(where_ref[0], 2)
        class_sums(rounded, totals, bit, nears, mine_ref, theirs_ref)
    else:
        put_state(state, out_ref)


def ring_scores(phase, sources, where, noise, turned, arrays, rest, ends, piece):
    quarter, per_device = turned[0].shape
    freqs = 4 * quarter
    rows = arrays[0].shape[0] * (1 if ends else len(arrays))
    sums = [
        jax.ShapeDtypeStruct((rows, per_device), jnp.float32),
        jax.ShapeDtypeStruct((rows, LANES), jnp.float32),
    ]
    scratch = [pltpu.VMEM(array.shape, array.dtype) for array in sums]
    specs = []
    places = [where] if phase or ends else []
    if phase == 0:
        shapes, scratch = sums, []
    else:
        specs = [in_vmem(), in_vmem(), in_smem(), in_vmem(), in_vmem()]
        if ends:
            classes = rest[2].shape[0]
            shapes = [
                jax.ShapeDtypeStruct((1, per_device), jnp.float32),
                piece,
                piece,
                jax.ShapeDtypeStruct((classes, per_device), jnp.bfloat16),
                jax.ShapeDtypeStruct((classes, LANES), jnp.float32),
            ]
            nears = [pltpu.with_memory_space_constraint(x, pltpu.VMEM) for x in rest[6:]]
            specs += [in_smem()] + [in_vmem()] * len(nears)
            rest = (*rest[:6], *nears)
        else:
            shapes = [jax.ShapeDtypeStruct(rest[4].shape, jnp.float32)]
    return pl.pallas_call(
        functools.partial(ring_kernel, phase, ends, sources),
        in_specs=[in_smem()] * len(places) + [in_vmem()] * (3 + len(arrays)) + specs,
        out_specs=[in_vmem()] * len(shapes),
        out_shape=shapes,
        scratch_shapes=scratch,
        compiler_params=pltpu.CompilerParams(vmem_limit_bytes=VMEM_LIMIT),
        cost_estimate=pl.CostEstimate(
            flops=2 * 128 * per_device * freqs,
            bytes_accessed=per_device * freqs,
            transcendentals=0,
        ),
    )(
        *places,
        noise,
        *(pltpu.with_memory_space_constraint(part, pltpu.VMEM) for part in turned),
        *arrays,
        *rest,
    )


def scatter_sum(pieces, blocks, bits):
    tail = pieces.shape[1:]
    zero = jnp.uint32(0)
    for step, (bit, other) in enumerate(bits):
        pairs = pieces.reshape((-1, 2) + tail)
        size = (pairs.shape[0], 1) + tail
        keep, send = (
            lax.dynamic_slice(pairs, (zero, which, zero, zero), size).reshape((-1,) + tail)
            for which in (bit, other)
        )
        swaps = [(block, block ^ (2 << step)) for block in range(blocks)]
        pieces = keep + lax.ppermute(send, "blk", swaps)
    return pieces[0]


def body(particles, significant, templates, template_class, class_counts, inv_noise):
    per_device, freqs = particles.shape
    classes = class_counts.shape[0]
    blocks = lax.axis_size("blk")
    owners = lax.axis_size("cls")
    order = ring_order(blocks)
    place = [order.index(block) for block in range(blocks)]
    block_id = lax.axis_index("blk")
    core = lax.axis_index("cls")
    ring = [(2 * order[i], 2 * order[(i + 1) % blocks]) for i in range(blocks)]
    ring += [(2 * order[(i + 1) % blocks] + 1, 2 * order[i] + 1) for i in range(blocks)]
    swap = [(i, owners - 1 - i) for i in range(owners)]

    noise = inv_noise[None, :]
    logs = jnp.log(class_counts.astype(jnp.float32))
    tags = template_class[None, :]
    *held, near_noise, picks = make_messages(tags, noise, significant, templates)
    where = jnp.stack([block_id, core])
    cut = freqs // 4
    per_owner = classes // owners
    bits = [
        lax.rem(lax.div(block_id, 2 << step), 2) for step in range(blocks.bit_length() - 2)
    ]
    bits = [(bit.astype(jnp.uint32), (1 - bit).astype(jnp.uint32)) for bit in bits]
    cut_at = core.astype(jnp.uint32) * cut
    where, cut_at, bits = lax.optimization_barrier((where, cut_at, bits))
    own = functools.partial(own_scores, where=where, noise=near_noise, particles=particles)
    total = blocks * templates.shape[0]
    words, *sums, low, high, near, raw = own([0, 1], templates=held[0], rest=(picks,), total=total)
    turned, nears = [(low, high)], [near, raw]
    gates = [sums]
    *sums, low, raw = own([2], templates=held[1], rest=(*sums, raw))
    nears.append(raw)
    gates.append(sums)
    state, high = own([3], templates=held[1], rest=(*sums, logs, tags, words, raw))
    turned.append((low, high))
    gates.append(state)
    width = freqs // blocks
    piece = jax.ShapeDtypeStruct((blocks // 2, per_owner, width + LANES), jnp.float32)
    last = blocks // 2
    for distance in range(1, last + 1):
        ends = distance == last
        tables = [
            [
                tuple(order[(place[block] - sign * distance) % blocks] for block in range(blocks))
                for sign in (1, -1)
            ]
        ]
        arrived = []
        for phase in range(2):
            message = held[phase]
            if ends:
                message = lax.dynamic_slice(
                    message,
                    (jnp.uint32(0), cut_at),
                    (message.shape[0], message.shape[1] - cut),
                )
            own = lax.ppermute(message, ("blk", "cls"), ring)
            lag = 3 if distance == 2 else 2
            gate = phase if distance == 1 else len(gates) - lag
            own, _ = lax.optimization_barrier((own, gates[gate]))
            pair = (own, lax.ppermute(own, "cls", swap))
            arrived.append(own)
            rest = (*sums, logs, words, state) if phase else ()
            if ends and phase:
                rest += (class_counts, *nears)
            sums = ring_scores(
                phase, tables, where, near_noise, turned[phase], pair, rest, ends, piece
            )
            gates.append(sums)
        held = arrived
        if not ends:
            (state,) = sums

    loglik, mine, theirs, rounded, totals = sums
    given = lax.ppermute(theirs, "cls", swap)
    across = lax.ppermute(mine + given, "blk", [(i, i ^ 1) for i in range(blocks)])
    rounded, _ = lax.optimization_barrier((rounded, given))
    mine, theirs = rest_sums(where, rounded, totals, nears, piece)
    kept = lax.optimization_barrier(mine + across)
    total = scatter_sum(kept + lax.ppermute(theirs, "cls", swap), blocks, bits)
    class_avg = total[:, :width] / total[:, width][:, None]
    return loglik[0], class_avg


def solution(mesh):
    placed = (
        P(("grp", "blk", "cls"), None),
        P(None, ("grp", "blk", "cls")),
        P(("grp", "blk"), None),
        P(("grp", "blk")),
        P("grp"),
        P(),
    )
    return jax.shard_map(
        body,
        mesh=mesh,
        in_specs=placed,
        out_specs=(P(("grp", "blk", "cls")), P(("grp", "cls"), "blk")),
        check_vma=False,
    )
```

```python
import functools

import jax
import jax.numpy as jnp
from jax import lax
from jax.experimental import pallas as pl
from jax.experimental.pallas import tpu as pltpu
from jax.sharding import PartitionSpec as P

LOWEST = -1e30
STEPS = 16
WIDTH = 1024
STRIP = 256
LANES = 128
STATE_ROWS = 8
VMEM_LIMIT = 6 * 1024 * 1024


def ring_order(blocks):
    if blocks <= 8:
        return list(range(0, blocks, 2)) + list(range(blocks - 1, 0, -2))
    return list(range(blocks))


def spread_copies(source, target, sent):
    count = sent.shape[0]
    rows = target.shape[0] // count
    return [
        pltpu.make_async_copy(
            source.at[pl.ds(at * rows, rows)], target.at[pl.ds(at * rows, rows)], sent.at[at]
        )
        for at in range(count)
    ]


def message_kernel(
    tags_ref, noise_ref, sig_ref, rows_ref,
    first_ref, second_ref, near_noise_ref, near_sig_ref, tags, sent, spread,
):
    height, span = first_ref.shape
    copies = [
        pltpu.make_async_copy(tags_ref, tags, sent.at[0]),
        pltpu.make_async_copy(noise_ref, near_noise_ref, sent.at[1]),
        pltpu.make_async_copy(sig_ref, near_sig_ref, sent.at[2]),
        *spread_copies(rows_ref.at[:, :span], first_ref, spread.at[0]),
        *spread_copies(rows_ref.at[:, span:], second_ref.at[:, :span], spread.at[1]),
    ]
    for copy in copies:
        copy.start()
    copies[0].wait()
    second_ref[:, span:] = tag_rows(tags, height).astype(jnp.bfloat16)
    for copy in copies[1:]:
        copy.wait()


def make_messages(tags, noise, significant, templates):
    height, freqs = templates.shape
    span = freqs // 2
    return pl.pallas_call(
        message_kernel,
        in_specs=[pl.BlockSpec(memory_space=pl.ANY)] * 4,
        out_specs=[in_vmem()] * 4,
        out_shape=[
            pltpu.VMEM((height, span), jnp.bfloat16),
            pltpu.VMEM((height, span + LANES), jnp.bfloat16),
            pltpu.VMEM(noise.shape, noise.dtype),
            pltpu.VMEM(significant.shape, significant.dtype),
        ],
        scratch_shapes=[
            pltpu.VMEM(tags.shape, tags.dtype),
            pltpu.SemaphoreType.DMA((3,)),
            pltpu.SemaphoreType.DMA((2, 4)),
        ],
        compiler_params=pltpu.CompilerParams(vmem_limit_bytes=VMEM_LIMIT),
    )(
        *(
            pltpu.with_memory_space_constraint(x, pltpu.HBM)
            for x in (tags, noise, significant, templates)
        )
    )


def tag_rows(tags_ref, height):
    row = lax.broadcasted_iota(jnp.int32, (height, height), 0)
    lane = lax.broadcasted_iota(jnp.int32, (height, height), 1)
    spread = jnp.where(row == lane, tags_ref[...].astype(jnp.float32), 0.0)
    return jnp.broadcast_to(jnp.sum(spread, axis=1, keepdims=True), (height, LANES))


def in_smem():
    return pl.BlockSpec(memory_space=pltpu.SMEM)


def in_vmem():
    return pl.BlockSpec(memory_space=pltpu.VMEM)


def weigh(rows, noise, energy):
    widened = rows.astype(jnp.float32)
    product = widened * noise
    square = product * widened
    folded = square[:, :LANES]
    for lane in range(LANES, square.shape[1], LANES):
        folded = folded + square[:, lane : lane + LANES]
    energy[...] += folded
    return product.astype(jnp.bfloat16)


def pick_words(sig_ref, words_ref):
    word = lax.broadcasted_iota(jnp.int32, words_ref.shape, 0)
    words = jnp.zeros(words_ref.shape, jnp.int32)
    for pick in range(sig_ref.shape[0]):
        chosen = sig_ref[pick : pick + 1, :]
        bit = jnp.left_shift(1, jnp.bitwise_and(chosen, 31))
        words = words | jnp.where(jnp.right_shift(chosen, 5) == word, bit, 0)
    words_ref[...] = words


def picked_rows(words_ref, source, height):
    bit = jnp.left_shift(1, lax.broadcasted_iota(jnp.int32, (32, 1), 0))
    rows = []
    for word in range(height // 32):
        rows.append((words_ref[pl.ds(source * (height // 32) + word, 1), :] & bit) != 0)
    return jnp.concatenate(rows, axis=0)


def add_rows(tags, hit, logs_ref, state, acc, energy):
    lane = lax.broadcasted_iota(jnp.int32, tags.shape, 1).astype(jnp.float32)
    own_lane = tags == lane
    prior = jnp.sum(jnp.where(own_lane, logs_ref[...], 0.0), axis=1, keepdims=True)
    bias = prior - 0.5 * jnp.sum(energy[...], axis=1, keepdims=True)
    scores = acc[...] + bias
    old_max, old_sum, old_top, weights = state
    classes = weights.shape[0]
    new_max = jnp.maximum(old_max, jnp.max(scores, axis=0, keepdims=True))
    new_sum = old_sum * jnp.exp(old_max - new_max) + jnp.sum(
        jnp.exp(scores - new_max), axis=0, keepdims=True
    )
    new_top = jnp.maximum(
        old_top, jnp.max(jnp.where(hit, scores, LOWEST), axis=0, keepdims=True)
    )
    value = jnp.where(hit, jnp.exp(scores - new_top), 0.0)
    onehot = jnp.transpose(jnp.where(own_lane, 1.0, 0.0))[:classes, :].astype(jnp.bfloat16)
    weights = weights * jnp.exp(old_top - new_top)
    left = value
    for _ in range(3):
        piece = left.astype(jnp.bfloat16)
        left = left - piece.astype(jnp.float32)
        weights = weights + jnp.dot(onehot, piece, preferred_element_type=jnp.float32)
    return new_max, new_sum, new_top, weights


def put_state(state, out_ref):
    new_max, new_sum, new_top, weights = state
    out_ref[0:1, :] = new_max
    out_ref[1:2, :] = new_sum
    out_ref[2:3, :] = new_top
    out_ref[3:STATE_ROWS, :] = jnp.zeros_like(out_ref[3:STATE_ROWS, :])
    out_ref[STATE_ROWS:, :] = weights


def get_state(state_ref):
    return state_ref[0:1, :], state_ref[1:2, :], state_ref[2:3, :], state_ref[STATE_ROWS:, :]


def own_kernel(quarters, where_ref, noise_ref, tmpl_ref, far_ref, *rest):
    first, last = quarters[0] == 0, quarters[-1] == 3
    if first:
        sig_ref, words_ref, acc, energy, *turned_refs, near, next_ref, arrived, late = rest
    elif last:
        acc_in, energy_in, logs_ref, tags_ref, words_ref, near, out_ref, *rest = rest
        *turned_refs, acc, energy = rest
    else:
        acc_in, energy_in, near, acc, energy, *turned_refs, next_ref, late = rest
    span, height = turned_refs[0].shape[0], tmpl_ref.shape[0]
    steps, _, width = near.shape
    low = quarters[0] * span

    def copies(step):
        columns = pl.ds(pl.multiple_of(low + step * width, width), width)
        return spread_copies(far_ref.at[:, columns], near.at[step], arrived.at[step])

    def following(step):
        columns = pl.ds(low + (steps + step) * width, width)
        return spread_copies(far_ref.at[:, columns], next_ref.at[step], late.at[step])

    if first:
        for step in range(steps):
            for copy in copies(step):
                copy.start()
    if not last:
        for step in range(next_ref.shape[0]):
            for copy in following(step):
                copy.start()
    if first:
        pick_words(sig_ref, words_ref)
        acc[...] = jnp.zeros_like(acc)
        energy[...] = jnp.zeros_like(energy)
    else:
        acc[...] = acc_in[...]
        energy[...] = energy_in[...]
    for quarter, turned_ref in zip(quarters, turned_refs):

        @pl.loop(0, span // width)
        def _(inner):
            step = (quarter - quarters[0]) * (span // width) + inner
            if first:
                for copy in copies(step):
                    copy.wait()
            for strip in range(0, width, STRIP):
                there = pl.ds(pl.multiple_of(inner * width + strip, STRIP), STRIP)
                part = quarter % 2 * span + inner * width + strip
                here = pl.ds(pl.multiple_of(part, STRIP), STRIP)
                columns = pl.ds(pl.multiple_of(low + step * width + strip, STRIP), STRIP)
                weighted = weigh(tmpl_ref[:, here], noise_ref[:, columns], energy)
                turned = jnp.transpose(near[step, :, strip : strip + STRIP])
                turned_ref[there, :] = turned
                acc[...] += jnp.dot(weighted, turned, preferred_element_type=jnp.float32)

    if not last:
        for step in range(next_ref.shape[0]):
            for copy in following(step):
                copy.wait()
        return
    tags = tag_rows(tags_ref, height)
    hit = picked_rows(words_ref, where_ref[0], height)
    lowest = jnp.full((1, acc.shape[1]), LOWEST, jnp.float32)
    none = jnp.zeros((1, acc.shape[1]), jnp.float32)
    weights = jnp.zeros((out_ref.shape[0] - STATE_ROWS, acc.shape[1]), jnp.float32)
    state = (lowest, none, lowest, weights)
    put_state(add_rows(tags, hit, logs_ref, state, acc, energy), out_ref)


def own_scores(quarters, where, noise, particles, templates, rest, total=0, classes=0):
    per_device, freqs = particles.shape
    height = templates.shape[0]
    width = freqs // STEPS
    span = freqs // 4
    steps = span // width
    first, last = quarters[0] == 0, quarters[-1] == 3
    sums = [
        jax.ShapeDtypeStruct((height, per_device), jnp.float32),
        jax.ShapeDtypeStruct((height, LANES), jnp.float32),
    ]
    turned = [pltpu.VMEM((span, per_device), particles.dtype)] * len(quarters)
    raw = pltpu.VMEM((steps, per_device, width), particles.dtype)
    if first:
        shapes = [jax.ShapeDtypeStruct((total // 32, per_device), jnp.int32)] + sums
        shapes += turned + [pltpu.VMEM((2 * steps, per_device, width), particles.dtype), raw]
        rest_specs = [in_vmem()]
        scratch = [
            pltpu.SemaphoreType.DMA((2 * steps, 4)),
            pltpu.SemaphoreType.DMA((steps, 4)),
        ]
    elif last:
        rows = STATE_ROWS + classes
        shapes = [jax.ShapeDtypeStruct((rows, per_device), jnp.float32)] + turned
        rest_specs = [in_vmem()] * 6
        scratch = [pltpu.VMEM(array.shape, array.dtype) for array in sums]
    else:
        shapes = sums + turned + [raw]
        rest_specs = [in_vmem()] * 3
        scratch = [pltpu.SemaphoreType.DMA((steps, 4))]
    if not first:
        rest = (*rest[:-1], pltpu.with_memory_space_constraint(rest[-1], pltpu.VMEM))
    return pl.pallas_call(
        functools.partial(own_kernel, quarters),
        in_specs=[in_smem(), in_vmem(), in_vmem(), pl.BlockSpec(memory_space=pl.ANY)] + rest_specs,
        out_specs=[in_vmem()] * len(shapes),
        out_shape=shapes,
        scratch_shapes=scratch,
        compiler_params=pltpu.CompilerParams(vmem_limit_bytes=VMEM_LIMIT),
        cost_estimate=pl.CostEstimate(
            flops=2 * 128 * per_device * freqs,
            bytes_accessed=per_device * freqs,
            transcendentals=0,
        ),
    )(where, noise, templates, pltpu.with_memory_space_constraint(particles, pltpu.HBM), *rest)


def class_weights(state, where_ref, counts_ref, per_owner):
    _, _, _, weights = state
    classes = weights.shape[0]
    row = lax.broadcasted_iota(jnp.int32, (classes, LANES), 0)
    lane = lax.broadcasted_iota(jnp.int32, (classes, LANES), 1)
    mine = (lax.div(row, per_owner) == where_ref[1]) & (where_ref[0] == 0)
    counts = jnp.where(mine & (row == lane), counts_ref[...], 0.0)
    counts = jnp.broadcast_to(jnp.sum(counts, axis=1, keepdims=True), (classes, LANES))
    weights = weights / jnp.sum(weights, axis=0, keepdims=True)
    totals = jnp.sum(weights, axis=1, keepdims=True) + counts

    def own_first(rows):
        turned = jnp.concatenate([rows[per_owner:], rows[:per_owner]], axis=0)
        return jnp.where(where_ref[1] == 0, rows, turned)

    return own_first(weights).astype(jnp.bfloat16), own_first(totals)


def class_sums(rounded, totals, bit, nears, mine_ref, theirs_ref):
    per_owner = mine_ref.shape[1]
    chunk = nears[0].shape[2]
    share = mine_ref.shape[2] // chunk
    piece = 0
    for near in nears:
        for pair in range(near.shape[0] // (2 * share)):
            for part in range(share):
                at = (2 * pair + bit) * share + part
                sums = jnp.dot(rounded, near[at], preferred_element_type=jnp.float32)
                columns = pl.ds(part * chunk, chunk)
                mine_ref[piece, :, columns] = sums[:per_owner]
                theirs_ref[piece, :, columns] = sums[per_owner:]
            mine_ref[piece, :, share * chunk :] = totals[:per_owner]
            theirs_ref[piece, :, share * chunk :] = totals[per_owner:]
            piece += 1


def rest_kernel(where_ref, rounded_ref, totals_ref, *rest):
    *nears, mine_ref, theirs_ref = rest
    bit = lax.rem(where_ref[0], 2)
    class_sums(rounded_ref[...], totals_ref[...], bit, nears, mine_ref, theirs_ref)


def rest_sums(where, rounded, totals, nears, piece):
    classes, per_device = rounded.shape
    blocks = 2 * piece.shape[0]
    freqs = blocks * (piece.shape[2] - LANES)
    return pl.pallas_call(
        rest_kernel,
        in_specs=[in_smem()] + [in_vmem()] * (2 + len(nears)),
        out_specs=[in_vmem()] * 2,
        out_shape=[piece, piece],
        compiler_params=pltpu.CompilerParams(vmem_limit_bytes=VMEM_LIMIT),
        cost_estimate=pl.CostEstimate(
            flops=128 * per_device * freqs,
            bytes_accessed=per_device * freqs // 2,
            transcendentals=0,
        ),
    )(where, rounded, totals, *(pltpu.with_memory_space_constraint(x, pltpu.VMEM) for x in nears))


def ring_kernel(phase, ends, sources, *rest):
    where_ref = None
    if phase or ends:
        where_ref, *rest = rest
    noise_ref, low_ref, high_ref, *rest = rest
    row_refs, rest = rest[: 2 * len(sources)], rest[2 * len(sources) :]
    if phase == 0:
        acc, energy = rest
    else:
        acc_in, energy_in, logs_ref, words_ref, state_ref, *rest = rest
        if ends:
            counts_ref, *nears, loglik_ref, mine_ref, theirs_ref = rest[:-4]
            rounded_ref, totals_ref, acc, energy = rest[-4:]
        else:
            out_ref, acc, energy = rest
    if phase == 0:
        acc[...] = jnp.zeros_like(acc)
        energy[...] = jnp.zeros_like(energy)
    else:
        acc[...] = acc_in[...]
        energy[...] = energy_in[...]
    quarter = low_ref.shape[0]
    core = where_ref[1] if phase or ends else None

    for at, part_ref in enumerate((low_ref, high_ref)):
        for step in range(quarter // WIDTH):
            there = pl.ds(step * WIDTH, WIDTH)
            columns = pl.ds((2 * phase + at) * quarter + step * WIDTH, WIDTH)
            if ends:
                rows = jnp.where(core == at, row_refs[0][:, there], row_refs[1][:, there])
            else:
                here = pl.ds(at * quarter + step * WIDTH, WIDTH)
                rows = jnp.concatenate([ref[:, here] for ref in row_refs], axis=0)
            weighted = weigh(rows, noise_ref[:, columns], energy)
            acc[...] += jnp.dot(weighted, part_ref[there, :], preferred_element_type=jnp.float32)

    if phase == 0:
        return
    height = row_refs[0].shape[0]
    span = quarter if ends else 2 * quarter
    tags = [ref[:, span:].astype(jnp.float32) for ref in row_refs]
    tags = jnp.where(core == 0, tags[1], tags[0]) if ends else jnp.concatenate(tags, axis=0)
    found = []
    for tables in sources:
        for table in tables:
            source = jnp.int32(table[0])
            for block in range(1, len(table)):
                source = jnp.where(where_ref[0] == block, table[block], source)
            found.append(source)
    if ends:
        found = found[:1]
    else:
        for at in range(0, len(found), 2):
            front, back = found[at : at + 2]
            found[at] = jnp.where(core == 0, front, back)
            found[at + 1] = jnp.where(core == 0, back, front)
    hit = jnp.concatenate([picked_rows(words_ref, source, height) for source in found], axis=0)
    state = add_rows(tags, hit, logs_ref, get_state(state_ref), acc, energy)
    if ends:
        loglik_ref[...] = state[0] + jnp.log(state[1])
        rounded, totals = class_weights(state, where_ref, counts_ref, mine_ref.shape[1])
        rounded_ref[...] = rounded
        totals_ref[...] = totals
        bit = 1 - lax.rem(where_ref[0], 2)
        class_sums(rounded, totals, bit, nears, mine_ref, theirs_ref)
    else:
        put_state(state, out_ref)


def ring_scores(phase, sources, where, noise, turned, arrays, rest, ends, piece):
    quarter, per_device = turned[0].shape
    freqs = 4 * quarter
    rows = arrays[0].shape[0] * (1 if ends else len(arrays))
    sums = [
        jax.ShapeDtypeStruct((rows, per_device), jnp.float32),
        jax.ShapeDtypeStruct((rows, LANES), jnp.float32),
    ]
    scratch = [pltpu.VMEM(array.shape, array.dtype) for array in sums]
    specs = []
    places = [where] if phase or ends else []
    if phase == 0:
        shapes, scratch = sums, []
    else:
        specs = [in_vmem()] * 5
        if ends:
            classes = rest[4].shape[0] - STATE_ROWS
            shapes = [
                jax.ShapeDtypeStruct((1, per_device), jnp.float32),
                piece,
                piece,
                jax.ShapeDtypeStruct((classes, per_device), jnp.bfloat16),
                jax.ShapeDtypeStruct((classes, LANES), jnp.float32),
            ]
            nears = [pltpu.with_memory_space_constraint(x, pltpu.VMEM) for x in rest[6:]]
            specs += [in_vmem()] * (1 + len(nears))
            rest = (*rest[:6], *nears)
        else:
            shapes = [jax.ShapeDtypeStruct(rest[4].shape, jnp.float32)]
    return pl.pallas_call(
        functools.partial(ring_kernel, phase, ends, sources),
        in_specs=[in_smem()] * len(places) + [in_vmem()] * (3 + len(arrays)) + specs,
        out_specs=[in_vmem()] * len(shapes),
        out_shape=shapes,
        scratch_shapes=scratch,
        compiler_params=pltpu.CompilerParams(vmem_limit_bytes=VMEM_LIMIT),
        cost_estimate=pl.CostEstimate(
            flops=2 * 128 * per_device * freqs,
            bytes_accessed=per_device * freqs,
            transcendentals=0,
        ),
    )(
        *places,
        noise,
        *(pltpu.with_memory_space_constraint(part, pltpu.VMEM) for part in turned),
        *arrays,
        *rest,
    )


def scatter_sum(pieces, blocks, bits):
    tail = pieces.shape[1:]
    zero = jnp.uint32(0)
    for step, (bit, other) in enumerate(bits):
        pairs = pieces.reshape((-1, 2) + tail)
        size = (pairs.shape[0], 1) + tail
        keep, send = (
            lax.dynamic_slice(pairs, (zero, which, zero, zero), size).reshape((-1,) + tail)
            for which in (bit, other)
        )
        swaps = [(block, block ^ (2 << step)) for block in range(blocks)]
        pieces = keep + lax.ppermute(send, "blk", swaps)
    return pieces[0]


def body(particles, significant, templates, template_class, class_counts, inv_noise):
    per_device, freqs = particles.shape
    classes = class_counts.shape[0]
    blocks = lax.axis_size("blk")
    owners = lax.axis_size("cls")
    order = ring_order(blocks)
    place = [order.index(block) for block in range(blocks)]
    block_id = lax.axis_index("blk")
    core = lax.axis_index("cls")
    ring = [(2 * order[i], 2 * order[(i + 1) % blocks]) for i in range(blocks)]
    ring += [(2 * order[(i + 1) % blocks] + 1, 2 * order[i] + 1) for i in range(blocks)]
    swap = [(i, owners - 1 - i) for i in range(owners)]

    noise = inv_noise[None, :]
    counts = jnp.pad(class_counts.astype(jnp.float32), (0, LANES - classes), constant_values=1.0)
    counts = counts[None, :]
    logs = jnp.log(counts)
    tags = template_class[None, :]
    *held, near_noise, picks = make_messages(tags, noise, significant, templates)
    where = jnp.stack([block_id, core])
    cut = freqs // 4
    per_owner = classes // owners
    bits = [
        lax.rem(lax.div(block_id, 2 << step), 2) for step in range(blocks.bit_length() - 2)
    ]
    bits = [(bit.astype(jnp.uint32), (1 - bit).astype(jnp.uint32)) for bit in bits]
    cut_at = core.astype(jnp.uint32) * cut
    where, cut_at, bits = lax.optimization_barrier((where, cut_at, bits))
    own = functools.partial(own_scores, where=where, noise=near_noise, particles=particles)
    total = blocks * templates.shape[0]
    words, *sums, low, high, near, raw = own([0, 1], templates=held[0], rest=(picks,), total=total)
    turned, nears = [(low, high)], [near, raw]
    gates = [sums]
    *sums, low, raw = own([2], templates=held[1], rest=(*sums, raw))
    nears.append(raw)
    gates.append(sums)
    state, high = own([3], templates=held[1], rest=(*sums, logs, tags, words, raw), classes=classes)
    turned.append((low, high))
    gates.append(state)
    width = freqs // blocks
    piece = jax.ShapeDtypeStruct((blocks // 2, per_owner, width + LANES), jnp.float32)
    last = blocks // 2
    for distance in range(1, last + 1):
        ends = distance == last
        tables = [
            [
                tuple(order[(place[block] - sign * distance) % blocks] for block in range(blocks))
                for sign in (1, -1)
            ]
        ]
        arrived = []
        for phase in range(2):
            message = held[phase]
            if ends:
                message = lax.dynamic_slice(
                    message,
                    (jnp.uint32(0), cut_at),
                    (message.shape[0], message.shape[1] - cut),
                )
            own = lax.ppermute(message, ("blk", "cls"), ring)
            lag = 3 if distance == 2 else 2
            gate = phase if distance == 1 else len(gates) - lag
            own, _ = lax.optimization_barrier((own, gates[gate]))
            pair = (own, lax.ppermute(own, "cls", swap))
            arrived.append(own)
            rest = (*sums, logs, words, state) if phase else ()
            if ends and phase:
                rest += (counts, *nears)
            sums = ring_scores(
                phase, tables, where, near_noise, turned[phase], pair, rest, ends, piece
            )
            gates.append(sums)
        held = arrived
        if not ends:
            (state,) = sums

    loglik, mine, theirs, rounded, totals = sums
    given = lax.ppermute(theirs, "cls", swap)
    across = lax.ppermute(mine + given, "blk", [(i, i ^ 1) for i in range(blocks)])
    rounded, _ = lax.optimization_barrier((rounded, given))
    mine, theirs = rest_sums(where, rounded, totals, nears, piece)
    kept = lax.optimization_barrier(mine + across)
    total = scatter_sum(kept + lax.ppermute(theirs, "cls", swap), blocks, bits)
    class_avg = total[:, :width] / total[:, width][:, None]
    return loglik[0], class_avg


def solution(mesh):
    placed = (
        P(("grp", "blk", "cls"), None),
        P(None, ("grp", "blk", "cls")),
        P(("grp", "blk"), None),
        P(("grp", "blk")),
        P("grp"),
        P(),
    )
    return jax.shard_map(
        body,
        mesh=mesh,
        in_specs=placed,
        out_specs=(P(("grp", "blk", "cls")), P(("grp", "cls"), "blk")),
        check_vma=False,
    )
```
